32 devices in a mesh: seq: 4 (over x, core), fsdp: 8 (over z, y).
Axes of the slice: x: 2, y: 2, z: 4, core: 2. Of those that a mesh axis runs over, the one named last changes fastest.
Arguments:
- tokens: bfloat16 [8, 1024, 1536], P('fsdp', 'seq'), may hold values from -6 to 6
- norm_gain: bfloat16 [1536], P('fsdp'), may hold values from 0.5 to 1.5
- query_weight: bfloat16 [1536, 1536], P('fsdp'), may hold values from -0.15625 to 0.15625
- key_weight: bfloat16 [1536, 512], P('fsdp'), may hold values from -0.15625 to 0.15625
- value_weight: bfloat16 [1536, 512], P('fsdp'), may hold values from -0.15625 to 0.15625
- query_gain: bfloat16 [64], P('fsdp'), may hold values from 0.5 to 1.5
- key_gain: bfloat16 [64], P('fsdp'), may hold values from 0.5 to 1.5
- out_weight: bfloat16 [1536, 1536], P('fsdp'), may hold values from -0.625 to 0.625
- ffn_gain: bfloat16 [1536], P('fsdp'), may hold values from 0.5 to 1.5
- gate_weight: bfloat16 [1536, 6912], P('fsdp'), may hold values from -0.15625 to 0.15625
- up_weight: bfloat16 [1536, 6912], P('fsdp'), may hold values from -0.15625 to 0.15625
- down_weight: bfloat16 [6912, 1536], P('fsdp'), may hold values from -0.078125 to 0.078125
- cotangent: bfloat16 [8, 1024, 1536], P('fsdp', 'seq'), may hold values from -6 to 6
Outputs:
- output: bfloat16 [8, 1024, 1536], P('fsdp', 'seq')
- tokens_grad: bfloat16 [8, 1024, 1536], P('fsdp', 'seq')
- norm_gain_grad: float32 [1536], P('fsdp')
- query_weight_grad: float32 [1536, 1536], P('fsdp')
- key_weight_grad: float32 [1536, 512], P('fsdp')
- value_weight_grad: float32 [1536, 512], P('fsdp')
- query_gain_grad: float32 [64], P('fsdp')
- key_gain_grad: float32 [64], P('fsdp')
- out_weight_grad: float32 [1536, 1536], P('fsdp')
- ffn_gain_grad: float32 [1536], P('fsdp')
- gate_weight_grad: float32 [1536, 6912], P('fsdp')
- up_weight_grad: float32 [1536, 6912], P('fsdp')
- down_weight_grad: float32 [6912, 1536], P('fsdp')
The draws below stay inside these ranges and needn't reach their ends.
All inputs are finite; a program needn't handle non-finite values.
Results may differ from the reference program's by a relative error of at most 0.024.
Values may be sent and summed in bfloat16 or wider, within the bound.
No kernel may reach another device: no remote copies, remote signals or barrier semaphores. Data moves between devices by JAX's collectives and lax.ppermute only.
A program may use at most 320 MiB of HBM per device.

```python
import math
import jax
import jax.numpy as jnp
from jax import lax

D = 1536
HEADS = 24
KV_HEADS = 8
HEAD = 64
FF = 6912
BLOCK = 512
LENGTH = 1024
SEQS = 8
KV = 512


def levels(own_key, dims, cuts, low, largest):
    factor_of = 1.0
    for dim, parts in cuts:
        draws = jax.random.uniform(jax.random.fold_in(jax.random.fold_in(own_key, 6), dim), (parts,), jnp.float32, low / len(cuts), largest / len(cuts))
        factor_of = factor_of * jnp.repeat(jnp.exp(draws), dims[dim] // parts).reshape((-1,) + (1,) * (len(dims) - 1 - dim))
    return factor_of


def gaussian(key, dims, scale, reach, pieces=(), kind=jnp.bfloat16):
    level = levels(key, dims, pieces, -0.22, 0.18) if pieces else 1.0
    array = jax.random.normal(key, dims, jnp.float32) * scale * level
    return jnp.minimum(jnp.maximum(array, -reach), reach).astype(kind)


def setup_inputs(seed: int = 0) -> dict:
    arg_keys = jax.random.split(jax.random.key(seed), 14)
    tokens = gaussian(arg_keys[0], (SEQS, LENGTH, D), 1.0, 6.0, ((0, 8), (1, 4)))
    norm_gain = jnp.clip(1.0 + 0.1 * jax.random.normal(arg_keys[1], (D,), jnp.float32), 0.5, 1.5).astype(jnp.bfloat16)
    query_weight = gaussian(arg_keys[2], (D, D), D ** -0.5, 0.15625, ((0, 8),))
    key_weight = gaussian(arg_keys[3], (D, KV), D ** -0.5, 0.15625, ((0, 8),))
    value_weight = gaussian(arg_keys[4], (D, KV), D ** -0.5, 0.15625, ((0, 8),))
    query_gain = jnp.clip(1.0 + 0.1 * jax.random.normal(arg_keys[5], (HEAD,), jnp.float32), 0.5, 1.5).astype(jnp.bfloat16)
    key_gain = jnp.clip(1.0 + 0.1 * jax.random.normal(arg_keys[6], (HEAD,), jnp.float32), 0.5, 1.5).astype(jnp.bfloat16)
    out_weight = gaussian(arg_keys[7], (D, D), (D // 16) ** -0.5, 0.625, ((0, 8),))
    ffn_gain = jnp.clip(1.0 + 0.1 * jax.random.normal(arg_keys[8], (D,), jnp.float32), 0.5, 1.5).astype(jnp.bfloat16)
    gate_weight = gaussian(arg_keys[9], (D, FF), D ** -0.5, 0.15625, ((0, 8),))
    up_weight = gaussian(arg_keys[10], (D, FF), D ** -0.5, 0.15625, ((0, 8),))
    down_weight = gaussian(arg_keys[11], (FF, D), FF ** -0.5, 0.078125, ((0, 8),))
    cotangent = gaussian(arg_keys[12], (SEQS, LENGTH, D), 1.0, 6.0, ((0, 8), (1, 4)))
    return {"tokens": tokens, "norm_gain": norm_gain, "query_weight": query_weight, "key_weight": key_weight, "value_weight": value_weight, "query_gain": query_gain, "key_gain": key_gain, "out_weight": out_weight, "ffn_gain": ffn_gain, "gate_weight": gate_weight, "up_weight": up_weight, "down_weight": down_weight, "cotangent": cotangent}


norm_epsilon = 1e-05
rope_base = 1000000.0
masked_score = -1e+30
highest = lax.Precision.HIGHEST

@jax.custom_vjp
def low(v):
    return lax.optimization_barrier(v.astype(jnp.bfloat16)).astype(jnp.float32)

@jax.custom_vjp
def low_back(v):
    return v

def low_keep(v):
    return (low(v), None)

def low_pass(kept, grad):
    return (grad,)

def back_keep(v):
    return (v, None)

def back_low(kept, grad):
    return (low(grad),)
low.defvjp(low_keep, low_pass)
low_back.defvjp(back_keep, back_low)

def rms_scale(values, gain):
    return values * lax.rsqrt(lax.optimization_barrier(jnp.mean(values * values, axis=-1, keepdims=True)) + norm_epsilon) * gain

def rope_tables(positions, width):
    half_width = width // 2
    inverse = jnp.exp(jnp.arange(half_width, dtype=jnp.float32) * (-2.0 * math.log(rope_base) / width))
    angles = positions[:, None] * inverse[None, :]
    return (jnp.cos(angles), jnp.sin(angles))

def rotate(values, cosine_table, sine_table):
    half_width = values.shape[-1] // 2
    lower_half = values[..., :half_width]
    upper_half = values[..., half_width:]
    return jnp.concatenate([lower_half * cosine_table - upper_half * sine_table, upper_half * cosine_table + lower_half * sine_table], axis=-1)

def layer(inputs, norm_gain, query_weight, key_weight, value_weight, query_gain, key_gain, out_weight, ffn_gain, gate_weight, up_weight, down_weight):
    length = inputs.shape[0]
    normed = low(rms_scale(inputs, norm_gain))
    query_pre = low_back(jnp.dot(normed, query_weight, precision=highest)).reshape(length, HEADS, HEAD)
    key_pre = low_back(jnp.dot(normed, key_weight, precision=highest)).reshape(length, KV_HEADS, HEAD)
    value_rows = low_back(low(jnp.dot(normed, value_weight, precision=highest))).reshape(length, KV_HEADS, HEAD)
    cosine_table, sine_table = rope_tables(jnp.arange(length, dtype=jnp.float32), HEAD)
    cosine_table = cosine_table[:, None, :]
    sine_table = sine_table[:, None, :]
    queries = low_back(low(rotate(rms_scale(query_pre, query_gain), cosine_table, sine_table)))
    key_rows = low_back(low(rotate(rms_scale(key_pre, key_gain), cosine_table, sine_table)))
    group_ratio = HEADS // KV_HEADS
    wide_keys = jnp.repeat(key_rows, group_ratio, axis=1)
    wide_values = jnp.repeat(value_rows, group_ratio, axis=1)
    score_scale = HEAD ** (-0.5)
    key_places = jnp.arange(length, dtype=jnp.int32)

    def one_block(first_row):
        query_block = lax.dynamic_slice_in_dim(queries, first_row, BLOCK, 0)
        scores = low_back(jnp.einsum('qhd,khd->hqk', query_block, wide_keys, precision=highest) * score_scale)
        places = first_row + jnp.arange(BLOCK, dtype=jnp.int32)
        scores = jnp.where(key_places[None, None, :] <= places[None, :, None], scores, masked_score)
        row_max = lax.optimization_barrier(jnp.max(scores, axis=-1, keepdims=True))
        log_total = row_max + jnp.log(lax.optimization_barrier(jnp.sum(jnp.exp(scores - row_max), axis=-1, keepdims=True)))
        weights = low(jnp.exp(scores - log_total))
        return jnp.einsum('hqk,khd->qhd', weights, wide_values, precision=highest)
    starts = (jnp.arange(length // BLOCK, dtype=jnp.int32) * BLOCK).astype(jnp.int32)
    mixed = lax.map(jax.checkpoint(one_block), starts).reshape(length, D)
    mixed = low_back(low(mixed))
    attended = low_back(jnp.dot(mixed, out_weight, precision=highest))
    middle = inputs + attended
    normed_two = low(rms_scale(middle, ffn_gain))
    gate_act = low_back(jnp.dot(normed_two, gate_weight, precision=highest))
    up_act = low_back(jnp.dot(normed_two, up_weight, precision=highest))
    hidden = low(jax.nn.silu(gate_act) * up_act)
    return middle + jnp.dot(hidden, down_weight, precision=highest)

def reference(tokens, norm_gain, query_weight, key_weight, value_weight, query_gain, key_gain, out_weight, ffn_gain, gate_weight, up_weight, down_weight, cotangent):
    params = tuple((w.astype(jnp.float32) for w in (norm_gain, query_weight, key_weight, value_weight, query_gain, key_gain, out_weight, ffn_gain, gate_weight, up_weight, down_weight)))

    def per_sequence(totals, sequence_pair):
        inputs, out_grad = sequence_pair
        result, pullback = jax.vjp(layer, inputs.astype(jnp.float32), *params)
        gradients = pullback(out_grad.astype(jnp.float32))
        totals = tuple((a + b for a, b in zip(totals, gradients[1:])))
        return (totals, (result.astype(jnp.bfloat16), gradients[0].astype(jnp.bfloat16)))
    zero_sums = tuple((jnp.zeros(w.shape, jnp.float32) for w in params))
    totals, (output, tokens_grad) = lax.scan(per_sequence, zero_sums, (tokens, cotangent))
    return (output, tokens_grad, totals[0], totals[1], totals[2], totals[3], totals[4], totals[5], totals[6], totals[7], totals[8], totals[9], totals[10])
```

```python
import math

import jax
import jax.numpy as jnp
from jax import lax
from jax.sharding import PartitionSpec as P

BLOCK = 512


norm_epsilon = 1e-05
rope_base = 1000000.0
masked_score = -1e30


def rope_tables(positions, width):
    half_width = width // 2
    inverse = jnp.exp(
        jnp.arange(half_width, dtype=jnp.float32) * (-2.0 * math.log(rope_base) / width)
    )
    angles = positions[:, None] * inverse[None, :]
    return (jnp.cos(angles), jnp.sin(angles))


def rotate(values, cosine_table, sine_table):
    half_width = values.shape[-1] // 2
    lower_half = values[..., :half_width]
    upper_half = values[..., half_width:]
    return jnp.concatenate(
        [
            lower_half * cosine_table - upper_half * sine_table,
            upper_half * cosine_table + lower_half * sine_table,
        ],
        axis=-1,
    )


def rotate_back(values, cosine_table, sine_table):
    half_width = values.shape[-1] // 2
    lower_half = values[..., :half_width]
    upper_half = values[..., half_width:]
    return jnp.concatenate(
        [
            lower_half * cosine_table + upper_half * sine_table,
            upper_half * cosine_table - lower_half * sine_table,
        ],
        axis=-1,
    )


def norm_forward(values, gain):
    inverse = lax.rsqrt(jnp.mean(values * values, axis=-1, keepdims=True) + norm_epsilon)
    unit = values * inverse
    return (unit * gain, unit, inverse)


def norm_backward(grad_in, unit, inverse, gain):
    scaled = grad_in * gain
    return inverse * (scaled - unit * jnp.mean(scaled * unit, axis=-1, keepdims=True))


def transpose_dot(left, right):
    return lax.dot_general(
        left, right, (((0,), (0,)), ((), ())), preferred_element_type=jnp.float32
    )


def dot_transposed(left, right):
    return lax.dot_general(
        left, right, (((1,), (1,)), ((), ())), preferred_element_type=jnp.float32
    )


def block_scores(query_block, key_three, first_row, length, score_scale):
    scores = (
        jnp.einsum("qgrd,kgd->grqk", query_block, key_three, preferred_element_type=jnp.float32)
        * score_scale
    )
    places = first_row + jnp.arange(BLOCK, dtype=jnp.int32)
    key_places = jnp.arange(length, dtype=jnp.int32)
    return jnp.where(
        key_places[None, None, None, :] <= places[None, None, :, None], scores, masked_score
    )


def attend_forward(queries, key_rows, value_rows, group_ratio, head_width):
    length = queries.shape[0]
    groups = key_rows.shape[1] // head_width
    query_four = queries.reshape(length, groups, group_ratio, head_width)
    key_three = key_rows.reshape(length, groups, head_width)
    value_three = value_rows.reshape(length, groups, head_width)
    score_scale = head_width ** (-0.5)

    def one_block(block_index):
        first_row = block_index * BLOCK
        query_block = lax.dynamic_slice_in_dim(query_four, first_row, BLOCK, 0)
        scores = block_scores(query_block, key_three, first_row, length, score_scale)
        row_max = jnp.max(scores, axis=-1, keepdims=True)
        log_total = row_max + jnp.log(jnp.sum(jnp.exp(scores - row_max), axis=-1, keepdims=True))
        weights = jnp.exp(scores - log_total).astype(jnp.bfloat16)
        result = jnp.einsum(
            "grqk,kgd->qgrd", weights, value_three, preferred_element_type=jnp.float32
        )
        return (result.astype(jnp.bfloat16).reshape(BLOCK, -1), log_total)

    results, log_totals = lax.map(one_block, jnp.arange(length // BLOCK, dtype=jnp.int32))
    return (results.reshape(length, -1), log_totals)


def attend_backward(queries, key_rows, value_rows, mixed_grad, log_totals, group_ratio, head_width):
    length = queries.shape[0]
    groups = key_rows.shape[1] // head_width
    query_four = queries.reshape(length, groups, group_ratio, head_width)
    grad_four = mixed_grad.reshape(length, groups, group_ratio, head_width)
    key_three = key_rows.reshape(length, groups, head_width)
    value_three = value_rows.reshape(length, groups, head_width)
    score_scale = head_width ** (-0.5)

    def one_block(carry, block_index):
        key_grad, value_grad = carry
        first_row = block_index * BLOCK
        query_block = lax.dynamic_slice_in_dim(query_four, first_row, BLOCK, 0)
        grad_block = lax.dynamic_slice_in_dim(grad_four, first_row, BLOCK, 0)
        scores = block_scores(query_block, key_three, first_row, length, score_scale)
        weights = jnp.exp(scores - log_totals[block_index])
        low_weights = weights.astype(jnp.bfloat16)
        weight_grad = jnp.einsum(
            "qgrd,kgd->grqk", grad_block, value_three, preferred_element_type=jnp.float32
        )
        inner = jnp.sum(weights * weight_grad, axis=-1, keepdims=True)
        score_grad = (weights * (weight_grad - inner)).astype(jnp.bfloat16)
        query_grad = (
            jnp.einsum("grqk,kgd->qgrd", score_grad, key_three, preferred_element_type=jnp.float32)
            * score_scale
        )
        key_grad = (
            key_grad
            + jnp.einsum(
                "grqk,qgrd->kgd", score_grad, query_block, preferred_element_type=jnp.float32
            )
            * score_scale
        )
        value_grad = value_grad + jnp.einsum(
            "grqk,qgrd->kgd", low_weights, grad_block, preferred_element_type=jnp.float32
        )
        return ((key_grad, value_grad), query_grad.astype(jnp.bfloat16).reshape(BLOCK, -1))

    zero_grad = jnp.zeros((length, groups, head_width), jnp.float32)
    (key_grad, value_grad), query_grads = lax.scan(
        one_block, (zero_grad, zero_grad), jnp.arange(length // BLOCK, dtype=jnp.int32)
    )
    return (
        query_grads.reshape(length, -1),
        key_grad.reshape(length, -1).astype(jnp.bfloat16),
        value_grad.reshape(length, -1).astype(jnp.bfloat16),
    )


def ring_ids(size):
    return list(range(0, size, 2)) + [i for i in range(size - 1, 0, -1) if i % 2]


def ring_place(index, size):
    return jnp.where(index % 2 == 0, index // 2, size - 1 - index // 2)


def ring_id(place, size):
    place = place % size
    half = (size + 1) // 2
    return jnp.where(place < half, 2 * place, 2 * (size - 1 - place) + 1)


def ring_perms(size):
    ids = ring_ids(size)
    forward = [(ids[i], ids[(i + 1) % size]) for i in range(size)]
    return forward, [(b, a) for a, b in forward]


def split_rows(rows):
    return (rows // 32) * 16


def ring_gather(block, size, place):
    forward, backward = ring_perms(size)
    rows, columns = block.shape
    top = split_rows(rows)
    ahead, behind = block[:top], block[top:]
    whole = jnp.zeros((size, rows, columns), block.dtype)

    def put(whole, piece, step, first):
        return lax.dynamic_update_slice(whole, piece[None], (ring_id(place + step, size), first, 0))

    whole = put(whole, ahead, 0, 0)
    whole = put(whole, behind, 0, top)
    for step in range(1, size):
        ahead = lax.ppermute(ahead, "fsdp", forward)
        behind = lax.ppermute(behind, "fsdp", backward)
        whole = put(whole, ahead, size - step, 0)
        whole = put(whole, behind, step, top)
    return whole


def ring_scatter(blocks, size, place):
    forward, backward = ring_perms(size)
    _, rows, columns = blocks.shape
    top = split_rows(rows)

    def own(step, first, count):
        return lax.dynamic_slice(
            blocks, (ring_id(place + step, size), first, 0), (1, count, columns)
        )[0]

    ahead = own(size - 1, 0, top).astype(jnp.bfloat16)
    behind = own(1, top, rows - top).astype(jnp.bfloat16)
    for step in range(1, size):
        ahead = lax.ppermute(ahead, "fsdp", forward)
        behind = lax.ppermute(behind, "fsdp", backward)
        ahead = (ahead.astype(jnp.float32) + own(2 * size - 1 - step, 0, top)).astype(jnp.bfloat16)
        behind = (behind.astype(jnp.float32) + own(1 + step, top, rows - top)).astype(jnp.bfloat16)
    return jnp.concatenate([ahead, behind], axis=0)


def exchange(values, mask):
    return lax.ppermute(values, "seq", [(i, i ^ mask) for i in range(4)])


def gather_seq(block):
    other = exchange(block, 2)
    pair = exchange(jnp.stack([block, other]), 1)
    return [block, other, pair[0], pair[1]]


def in_order(pieces, seq_index):
    high, low = seq_index // 2, seq_index % 2

    def pick(first, second, flag):
        return jnp.where(flag == 0, first, second), jnp.where(flag == 0, second, first)

    mine = pick(pieces[0], pieces[1], high)
    theirs = pick(pieces[2], pieces[3], high)
    return [*pick(mine[0], theirs[0], low), *pick(mine[1], theirs[1], low)]


def scatter_seq(blocks):
    came = exchange(blocks[2:].astype(jnp.bfloat16), 1).astype(jnp.float32)
    here = blocks[:2].astype(jnp.float32) + came
    return here[0] + exchange(here[1].astype(jnp.bfloat16), 2).astype(jnp.float32)


def swap_rows(values, seq_index):
    rows = values.shape[0] // 4

    def block(mask):
        return lax.dynamic_slice_in_dim(values, (seq_index ^ mask) * rows, rows, 0)

    return [block(0), exchange(block(2), 2), exchange(block(1), 1), exchange(block(3), 3)]


def swap_columns(values, seq_index):
    columns = values.shape[1] // 4

    def block(mask):
        return lax.dynamic_slice_in_dim(values, (seq_index ^ mask) * columns, columns, 1)

    return [block(0), exchange(block(2), 2), exchange(block(1), 1), exchange(block(3), 3)]


def body(
    tokens,
    norm_gain,
    query_weight,
    key_weight,
    value_weight,
    query_gain,
    key_gain,
    out_weight,
    ffn_gain,
    gate_weight,
    up_weight,
    down_weight,
    cotangent,
):
    bf16, f32 = jnp.bfloat16, jnp.float32
    size = lax.axis_size("fsdp")
    seq_index = lax.axis_index("seq")
    place = ring_place(lax.axis_index("fsdp"), size)
    own_rows, width = query_weight.shape
    head_part = query_gain.shape[0]
    head_width = head_part * size
    query_columns = width // 4
    key_columns = key_weight.shape[1] // 4
    ff_part = down_weight.shape[0]
    window = -(-ff_part // 64) * 16

    def columns_of(weight, count):
        return lax.dynamic_slice_in_dim(weight, seq_index * count, count, 1)

    def hidden_columns(weight):
        wide = jnp.pad(
            weight.reshape(own_rows, size, ff_part), ((0, 0), (0, 0), (0, 4 * window - ff_part))
        )
        return lax.dynamic_slice_in_dim(wide, seq_index * window, window, 2).reshape(
            own_rows, size * window
        )

    def hidden_rows(weight):
        tall = jnp.pad(weight, ((0, 4 * window - ff_part), (0, 0)))
        return lax.dynamic_slice_in_dim(tall, seq_index * window, window, 0)

    gains = jnp.concatenate([norm_gain, ffn_gain, query_gain, key_gain])
    packed_columns = 2 * query_columns + 2 * key_columns
    gain_rows = jnp.pad(gains[None], ((0, 15), (0, packed_columns - gains.shape[0])))
    packed = jnp.concatenate(
        [
            jnp.concatenate(
                [
                    columns_of(query_weight, query_columns),
                    columns_of(key_weight, key_columns),
                    columns_of(value_weight, key_columns),
                    columns_of(out_weight, query_columns),
                ],
                axis=1,
            ),
            gain_rows,
        ],
        axis=0,
    )
    packed_all = ring_gather(packed, size, place)
    gate_all = lax.all_gather(hidden_columns(gate_weight), "fsdp", axis=0, tiled=True)
    up_all = ring_gather(hidden_columns(up_weight), size, place).reshape(width, size * window)
    down_all = ring_gather(hidden_rows(down_weight), size, place).reshape(size * window, width)

    gains_all = packed_all[:, own_rows].astype(f32)
    first_gain = gains_all[:, :own_rows].reshape(-1)
    second_gain = gains_all[:, own_rows : 2 * own_rows].reshape(-1)
    q_gain_f = gains_all[:, 2 * own_rows : 2 * own_rows + head_part].reshape(-1)
    k_gain_f = gains_all[:, 2 * own_rows + head_part : 2 * (own_rows + head_part)].reshape(-1)
    attention_all = packed_all[:, :own_rows].reshape(width, packed_columns)
    qkv_all = attention_all[:, : query_columns + 2 * key_columns]
    out_all = jnp.concatenate(
        in_order(gather_seq(attention_all[:, query_columns + 2 * key_columns :]), seq_index), axis=1
    )

    inputs = tokens[0]
    tok_rows = inputs.shape[0]
    length = 4 * tok_rows
    inputs_all = jnp.concatenate(in_order(gather_seq(inputs), seq_index), axis=0).astype(f32)
    out_grad = cotangent[0]
    out_grad_all = jnp.concatenate(gather_seq(out_grad), axis=0)

    normed, norm_unit, norm_inverse = norm_forward(inputs_all, first_gain)
    normed_low = normed.astype(bf16)
    qkv = jnp.dot(normed_low, qkv_all, preferred_element_type=f32)
    query_pre = qkv[:, :query_columns]
    key_pre = qkv[:, query_columns : query_columns + key_columns]
    value_heads = qkv[:, query_columns + key_columns :].astype(bf16)
    group_ratio = query_columns // key_columns
    head_count = query_columns // head_width
    kv_count = key_columns // head_width
    positions = jnp.arange(length, dtype=jnp.int32).astype(f32)
    cosine_table, sine_table = rope_tables(positions, head_width)
    cosine_table = cosine_table[:, None, :]
    sine_table = sine_table[:, None, :]
    query_normed, query_unit, query_inverse = norm_forward(
        query_pre.reshape(length, head_count, head_width), q_gain_f
    )
    key_normed, key_unit, key_inverse = norm_forward(
        key_pre.reshape(length, kv_count, head_width), k_gain_f
    )
    query_heads = rotate(query_normed, cosine_table, sine_table).reshape(length, -1).astype(bf16)
    key_heads = rotate(key_normed, cosine_table, sine_table).reshape(length, -1).astype(bf16)
    mixed_heads, log_totals = attend_forward(
        query_heads, key_heads, value_heads, group_ratio, head_width
    )
    mixed = jnp.concatenate(in_order(swap_rows(mixed_heads, seq_index), seq_index), axis=1)
    attended = jnp.dot(mixed, out_all, preferred_element_type=f32)
    middle = inputs.astype(f32) + attended
    normed_two, middle_unit, middle_inverse = norm_forward(middle, second_gain)
    normed_two_all = jnp.concatenate(gather_seq(normed_two.astype(bf16)), axis=0)
    mixed_all = jnp.concatenate(in_order(gather_seq(mixed_heads), seq_index), axis=1)

    gate_act = jnp.dot(normed_two_all, gate_all, preferred_element_type=f32)
    up_act = jnp.dot(normed_two_all, up_all, preferred_element_type=f32)
    gate_sigmoid = jax.nn.sigmoid(gate_act)
    gate_silu = gate_act * gate_sigmoid
    hidden = (gate_silu * up_act).astype(bf16)
    down_weight_grad = transpose_dot(hidden, out_grad_all)
    down_share = ring_scatter(down_weight_grad.reshape(size, window, width), size, place)
    output = middle + scatter_seq(
        jnp.dot(hidden, down_all, preferred_element_type=f32).reshape(4, tok_rows, width)
    )

    hidden_grad = dot_transposed(out_grad_all, down_all)
    gate_grad = (
        hidden_grad * up_act * gate_sigmoid * (1.0 + gate_act * (1.0 - gate_sigmoid))
    ).astype(bf16)
    up_grad = (hidden_grad * gate_silu).astype(bf16)
    normed_two_grad = scatter_seq(
        (dot_transposed(gate_grad, gate_all) + dot_transposed(up_grad, up_all)).reshape(
            4, tok_rows, width
        )
    )
    gate_weight_grad = transpose_dot(normed_two_all, gate_grad)
    up_weight_grad = transpose_dot(normed_two_all, up_grad)
    up_share = ring_scatter(up_weight_grad.reshape(size, own_rows, size * window), size, place)
    gate_share = lax.psum_scatter(
        gate_weight_grad.astype(bf16), "fsdp", scatter_dimension=0, tiled=True
    )
    ffn_gain_grad = jnp.sum(normed_two_grad * middle_unit, axis=0)
    middle_grad = out_grad.astype(f32) + norm_backward(
        normed_two_grad, middle_unit, middle_inverse, second_gain
    )
    attended_low = middle_grad.astype(bf16)
    mixed_grad = dot_transposed(attended_low, out_all).astype(bf16)
    mixed_grad_heads = jnp.concatenate(in_order(swap_columns(mixed_grad, seq_index), seq_index), axis=0)
    attended_columns = jnp.concatenate(
        in_order(swap_columns(attended_low, seq_index), seq_index), axis=0
    )
    out_weight_grad = transpose_dot(mixed_all, attended_columns)
    query_grad_rot, key_grad_rot, value_grad = attend_backward(
        query_heads, key_heads, value_heads, mixed_grad_heads, log_totals, group_ratio, head_width
    )
    query_grad_normed = rotate_back(
        query_grad_rot.astype(f32).reshape(length, head_count, head_width), cosine_table, sine_table
    )
    key_grad_normed = rotate_back(
        key_grad_rot.astype(f32).reshape(length, kv_count, head_width), cosine_table, sine_table
    )
    query_gain_grad = jnp.sum(query_grad_normed * query_unit, axis=(0, 1))
    key_gain_grad = jnp.sum(key_grad_normed * key_unit, axis=(0, 1))
    query_pre_grad = norm_backward(query_grad_normed, query_unit, query_inverse, q_gain_f)
    key_pre_grad = norm_backward(key_grad_normed, key_unit, key_inverse, k_gain_f)
    qkv_grad = jnp.concatenate(
        [
            query_pre_grad.reshape(length, -1).astype(bf16),
            key_pre_grad.reshape(length, -1).astype(bf16),
            value_grad,
        ],
        axis=1,
    )
    qkv_weight_grad = transpose_dot(normed_low, qkv_grad)
    normed_partial = dot_transposed(qkv_grad, qkv_all)
    norm_gain_grad = jnp.sum(normed_partial * norm_unit, axis=0)
    partial_blocks = normed_partial.reshape(4, tok_rows, width)
    normed_grad = scatter_seq(
        jnp.concatenate(
            [
                lax.dynamic_slice_in_dim(partial_blocks, seq_index ^ mask, 1, 0)
                for mask in (0, 2, 1, 3)
            ],
            axis=0,
        )
    )
    _, own_unit, own_inverse = norm_forward(inputs.astype(f32), first_gain)
    inputs_grad = middle_grad + norm_backward(normed_grad, own_unit, own_inverse, first_gain)

    gain_grads = jnp.concatenate(
        [
            norm_gain_grad.reshape(size, -1),
            ffn_gain_grad.reshape(size, -1),
            query_gain_grad.reshape(size, -1),
            key_gain_grad.reshape(size, -1),
        ],
        axis=1,
    )
    gain_count = gain_grads.shape[1]
    gain_blocks = jnp.pad(
        gain_grads[:, None], ((0, 0), (0, 15), (0, packed_columns - gain_count))
    )
    packed_grad = jnp.concatenate(
        [
            jnp.concatenate([qkv_weight_grad, out_weight_grad], axis=1).reshape(
                size, own_rows, packed_columns
            ),
            gain_blocks,
        ],
        axis=1,
    )
    packed_share = ring_scatter(packed_grad, size, place)

    down_full = jnp.concatenate(in_order(gather_seq(down_share), seq_index), axis=0)[
        :ff_part
    ].astype(f32)

    def full_columns(share):
        parts = in_order(gather_seq(share), seq_index)
        wide = jnp.concatenate([p.reshape(own_rows, size, window) for p in parts], axis=2)
        return wide[:, :, :ff_part].reshape(own_rows, size * ff_part).astype(f32)

    gate_full = full_columns(gate_share)
    up_full = full_columns(up_share)
    packs = in_order(gather_seq(packed_share), seq_index)

    def unpack(first, count):
        return jnp.concatenate(
            [p[:own_rows, first : first + count] for p in packs], axis=1
        ).astype(f32)

    gain_sum = sum(p[own_rows, :gain_count].astype(f32) for p in packs)
    return (
        output[None].astype(bf16),
        inputs_grad[None].astype(bf16),
        gain_sum[:own_rows],
        unpack(0, query_columns),
        unpack(query_columns, key_columns),
        unpack(query_columns + key_columns, key_columns),
        gain_sum[2 * own_rows : 2 * own_rows + head_part],
        gain_sum[2 * own_rows + head_part :],
        unpack(query_columns + 2 * key_columns, query_columns),
        gain_sum[own_rows : 2 * own_rows],
        gate_full,
        up_full,
        down_full,
    )


def solution(mesh):
    in_specs = (
        P("fsdp", "seq", None),
        P("fsdp"),
        P("fsdp", None),
        P("fsdp", None),
        P("fsdp", None),
        P("fsdp"),
        P("fsdp"),
        P("fsdp", None),
        P("fsdp"),
        P("fsdp", None),
        P("fsdp", None),
        P("fsdp", None),
        P("fsdp", "seq", None),
    )
    out_specs = (
        P("fsdp", "seq", None),
        P("fsdp", "seq", None),
        P("fsdp"),
        P("fsdp", None),
        P("fsdp", None),
        P("fsdp", None),
        P("fsdp"),
        P("fsdp"),
        P("fsdp", None),
        P("fsdp"),
        P("fsdp", None),
        P("fsdp", None),
        P("fsdp", None),
    )
    return jax.shard_map(body, mesh=mesh, in_specs=in_specs, out_specs=out_specs, check_vma=False)
```

```python
import functools
import math

import jax
import jax.numpy as jnp
from jax import lax
from jax.experimental import pallas as pl
from jax.experimental.pallas import tpu as pltpu
from jax.sharding import PartitionSpec as P

norm_epsilon = 1e-05
TILE = 256
log2_e = math.log2(math.e)


def rope_rows(length, width):
    half_width = width // 2
    inverse = jnp.exp(
        jnp.arange(half_width, dtype=jnp.float32) * (-2.0 * math.log(1000000.0) / width)
    )
    angles = inverse[:, None] * jnp.arange(length, dtype=jnp.int32).astype(jnp.float32)[None, :]
    return jnp.cos(angles), jnp.sin(angles)


def head_norm(values):
    inverse = lax.rsqrt(jnp.mean(values * values, axis=0, keepdims=True) + norm_epsilon)
    return values * inverse, inverse


def head_turn(values, cosine, sine):
    half = values.shape[0] // 2
    first, second = values[:half], values[half:]
    return jnp.concatenate(
        [first * cosine - second * sine, second * cosine + first * sine], axis=0
    )


def head_turn_back(values, cosine, sine):
    half = values.shape[0] // 2
    first, second = values[:half], values[half:]
    return jnp.concatenate(
        [first * cosine + second * sine, second * cosine - first * sine], axis=0
    )


def fill_heads(qkv_ref, q_gain_ref, k_gain_ref, cos_ref, sin_ref, queries, keys, keys_t, values, values_t, sizes):
    heads, groups, width = sizes
    cosine, sine = cos_ref[...], sin_ref[...]

    @pl.loop(0, heads)
    def _(head):
        unit, _ = head_norm(qkv_ref[pl.ds(head * width, width), :])
        turned = head_turn(unit * q_gain_ref[...], cosine, sine)
        queries[head] = (turned * (width**-0.5 * log2_e)).astype(jnp.bfloat16)

    @pl.loop(0, groups)
    def _(group):
        unit, _ = head_norm(qkv_ref[pl.ds((heads + group) * width, width), :])
        turned = head_turn(unit * k_gain_ref[...], cosine, sine)
        keys[group] = turned.T.astype(jnp.bfloat16)
        if keys_t is not None:
            keys_t[group] = turned.astype(jnp.bfloat16)
        value = qkv_ref[pl.ds((heads + groups + group) * width, width), :]
        if values is not None:
            values[group] = value.T.astype(jnp.bfloat16)
        if values_t is not None:
            values_t[group] = value.astype(jnp.bfloat16)


def diagonal_mask():
    key_place = lax.broadcasted_iota(jnp.int32, (TILE, TILE), 0)
    query_place = lax.broadcasted_iota(jnp.int32, (TILE, TILE), 1)
    return key_place <= query_place


def causal_exp(scores, count):
    weights = jnp.exp2(scores)
    last = jnp.where(diagonal_mask(), weights[count - TILE :], 0.0)
    if count == TILE:
        return last
    return jnp.concatenate([weights[: count - TILE], last], axis=0)


def dot(left, right):
    return jnp.dot(left, right, preferred_element_type=jnp.float32)


def dot_nt(left, right):
    return lax.dot_general(
        left, right, (((1,), (1,)), ((), ())), preferred_element_type=jnp.float32
    )


def forward_kernel(sizes, qkv_ref, q_gain_ref, k_gain_ref, cos_ref, sin_ref, mixed_ref, mixed_t_ref, total_ref, queries, keys, values_t, mixed_f):
    heads, groups, width = sizes
    ratio = heads // groups
    length = qkv_ref.shape[1]
    fill_heads(qkv_ref, q_gain_ref, k_gain_ref, cos_ref, sin_ref, queries, keys, None, None, values_t, sizes)

    @pl.loop(0, heads)
    def _(head):
        group = head // ratio
        for tile in range(length // TILE):
            count = (tile + 1) * TILE
            columns = pl.ds(tile * TILE, TILE)
            scores = dot(keys[group, pl.ds(0, count), :], queries[head, :, columns])
            weights = causal_exp(scores, count)
            total = jnp.sum(weights, axis=0, keepdims=True)
            result = dot(values_t[group, :, pl.ds(0, count)], weights.astype(jnp.bfloat16))
            mixed_f[pl.ds(head * width, width), columns] = result * (1.0 / total)
            total_ref[pl.ds(head, 1), columns] = jnp.log2(total)

    for block in range(heads * width // 128):
        rows = mixed_f[pl.ds(block * 128, 128), :]
        mixed_t_ref[pl.ds(block * 128, 128), :] = rows.astype(jnp.bfloat16)
        mixed_ref[:, pl.ds(block * 128, 128)] = rows.T.astype(jnp.bfloat16)


def backward_kernel(sizes, qkv_ref, q_gain_ref, k_gain_ref, cos_ref, sin_ref, mixed_t_ref, total_ref, grad_ref, out_ref, gain_ref, queries, keys, keys_t, values, grads, key_sum, value_sum):
    heads, groups, width = sizes
    ratio = heads // groups
    length = qkv_ref.shape[1]
    fill_heads(qkv_ref, q_gain_ref, k_gain_ref, cos_ref, sin_ref, queries, keys, keys_t, values, None, sizes)
    for block in range(heads * width // 128):
        turned = grad_ref[:, pl.ds(block * 128, 128)].astype(jnp.float32).T
        grads[pl.ds(block * 128, 128), :] = turned.astype(jnp.bfloat16)
    key_sum[...] = jnp.zeros_like(key_sum)
    value_sum[...] = jnp.zeros_like(value_sum)
    gain_ref[...] = jnp.zeros_like(gain_ref)
    cosine, sine = cos_ref[...], sin_ref[...]

    def finish(grad_turned, rows, gain, first):
        grad = head_turn_back(grad_turned, cosine, sine)
        unit, inverse = head_norm(qkv_ref[rows, :])
        product = grad * unit
        part = product[:, :128]
        for lane in range(128, length, 128):
            part = part + product[:, lane : lane + 128]
        gain_ref[pl.ds(first, width), :] += part
        scaled = grad * gain
        before = inverse * (scaled - unit * jnp.mean(scaled * unit, axis=0, keepdims=True))
        out_ref[rows, :] = before.astype(jnp.bfloat16)

    @pl.loop(0, heads)
    def _(head):
        group = head // ratio
        rows = pl.ds(head * width, width)
        query_parts = []
        for tile in range(length // TILE):
            count = (tile + 1) * TILE
            columns = pl.ds(tile * TILE, TILE)
            query = queries[head, :, columns]
            grad = grads[rows, columns]
            scores = dot(keys[group, pl.ds(0, count), :], query) - total_ref[pl.ds(head, 1), columns]
            weights = causal_exp(scores, count)
            inner = jnp.sum(
                grad.astype(jnp.float32) * mixed_t_ref[rows, columns].astype(jnp.float32),
                axis=0,
                keepdims=True,
            )
            weight_grad = dot(values[group, pl.ds(0, count), :], grad)
            score_grad = (weights * (weight_grad - inner)).astype(jnp.bfloat16)
            query_parts.append(dot(keys_t[group, :, pl.ds(0, count)], score_grad))
            key_sum[group, pl.ds(0, count), :] += dot_nt(score_grad, query)
            value_sum[group, pl.ds(0, count), :] += dot_nt(weights.astype(jnp.bfloat16), grad)
        query_grad = jnp.concatenate(query_parts, axis=1) * width**-0.5
        finish(query_grad, rows, q_gain_ref[...], 0)

    for group in range(groups):
        key_grad = key_sum[group].T * (1.0 / log2_e)
        finish(key_grad, pl.ds((heads + group) * width, width), k_gain_ref[...], width)
        out_ref[pl.ds((heads + groups + group) * width, width), :] = value_sum[group].T.astype(
            jnp.bfloat16
        )


def attention_forward(qkv_t, q_gain, k_gain, cosine, sine, sizes):
    heads, groups, width = sizes
    length = qkv_t.shape[1]
    bf16, f32 = jnp.bfloat16, jnp.float32
    pairs = heads * length * length
    return pl.pallas_call(
        functools.partial(forward_kernel, sizes),
        out_shape=(
            jax.ShapeDtypeStruct((length, heads * width), bf16),
            jax.ShapeDtypeStruct((heads * width, length), bf16),
            jax.ShapeDtypeStruct((-(-heads // 8) * 8, length), f32),
        ),
        scratch_shapes=[
            pltpu.VMEM((heads, width, length), bf16),
            pltpu.VMEM((groups, length, width), bf16),
            pltpu.VMEM((groups, width, length), bf16),
            pltpu.VMEM((heads * width, length), f32),
        ],
        compiler_params=pltpu.CompilerParams(vmem_limit_bytes=32 * 2**20),
        cost_estimate=pl.CostEstimate(
            flops=8 * pairs * width, bytes_accessed=6 * 2**20, transcendentals=pairs
        ),
    )(qkv_t, q_gain, k_gain, cosine, sine)


def attention_backward(qkv_t, q_gain, k_gain, cosine, sine, mixed_t, total, mixed_grad, sizes):
    heads, groups, width = sizes
    length = qkv_t.shape[1]
    bf16, f32 = jnp.bfloat16, jnp.float32
    pairs = heads * length * length
    return pl.pallas_call(
        functools.partial(backward_kernel, sizes),
        out_shape=(
            jax.ShapeDtypeStruct(qkv_t.shape, bf16),
            jax.ShapeDtypeStruct((2 * width, 128), f32),
        ),
        scratch_shapes=[
            pltpu.VMEM((heads, width, length), bf16),
            pltpu.VMEM((groups, length, width), bf16),
            pltpu.VMEM((groups, width, length), bf16),
            pltpu.VMEM((groups, length, width), bf16),
            pltpu.VMEM((heads * width, length), bf16),
            pltpu.VMEM((groups, length, width), f32),
            pltpu.VMEM((groups, length, width), f32),
        ],
        compiler_params=pltpu.CompilerParams(vmem_limit_bytes=40 * 2**20),
        cost_estimate=pl.CostEstimate(
            flops=20 * pairs * width, bytes_accessed=8 * 2**20, transcendentals=pairs
        ),
    )(qkv_t, q_gain, k_gain, cosine, sine, mixed_t, total, mixed_grad)


def pick_kernel(sizes, index_ref, gate_ref, up_ref, gate_out, up_out):
    size, part, window = sizes
    rows = gate_ref.shape[0]
    for source, target in ((gate_ref, gate_out), (up_ref, up_out)):
        for index in range(4):
            count = min(window, part - index * window)

            @pl.when(index_ref[0] == index)
            def _():
                parts = []
                for owner in range(size):
                    first = owner * part + index * window
                    low, high = first // 128 * 128, -(-(first + count) // 128) * 128
                    wide = source[:, low:high].astype(jnp.float32)
                    parts.append(wide[:, first - low : first - low + count])
                    if count < window:
                        parts.append(jnp.zeros((rows, window - count), jnp.float32))
                target[...] = jnp.concatenate(parts, axis=1).astype(target.dtype)


def pick_hidden(gate, up, seq_index, size, part, window):
    rows, columns = gate.shape
    block = 48 if rows % 48 == 0 else rows
    wide = pl.BlockSpec((block, columns), lambda i, index: (i, 0))
    narrow = pl.BlockSpec((block, size * window), lambda i, index: (i, 0))
    out = jax.ShapeDtypeStruct((rows, size * window), gate.dtype)
    return pl.pallas_call(
        functools.partial(pick_kernel, (size, part, window)),
        grid_spec=pltpu.PrefetchScalarGridSpec(
            num_scalar_prefetch=1,
            grid=(rows // block,),
            in_specs=[wide, wide],
            out_specs=[narrow, narrow],
        ),
        out_shape=(out, out),
        compiler_params=pltpu.CompilerParams(vmem_limit_bytes=32 * 2**20),
        cost_estimate=pl.CostEstimate(flops=0, bytes_accessed=8 * 2**20, transcendentals=0),
    )(jnp.reshape(seq_index, (1,)).astype(jnp.int32), gate, up)


def spread_kernel(sizes, index_ref, own_ref, other_ref, pair_ref, out_ref, parts):
    size, part, window = sizes
    me = index_ref[0]
    parts[me] = own_ref[...]
    parts[me ^ 2] = other_ref[...]
    parts[me ^ 1] = pair_ref[0]
    parts[me ^ 3] = pair_ref[1]
    pieces = []
    for owner in range(size):
        for index in range(4):
            count = min(window, part - index * window)
            first = owner * window
            low, high = first // 128 * 128, -(-(first + count) // 128) * 128
            wide = parts[index, :, low:high].astype(jnp.float32)
            pieces.append(wide[:, first - low : first - low + count])
    out_ref[...] = jnp.concatenate(pieces, axis=1)


def spread_hidden(own, other, pair, seq_index, size, part, window):
    rows, columns = own.shape
    block = 48 if rows % 48 == 0 else rows
    narrow = pl.BlockSpec((block, columns), lambda i, index: (i, 0))
    return pl.pallas_call(
        functools.partial(spread_kernel, (size, part, window)),
        grid_spec=pltpu.PrefetchScalarGridSpec(
            num_scalar_prefetch=1,
            grid=(rows // block,),
            in_specs=[
                narrow,
                narrow,
                pl.BlockSpec((2, block, columns), lambda i, index: (0, i, 0)),
            ],
            out_specs=pl.BlockSpec((block, size * part), lambda i, index: (i, 0)),
            scratch_shapes=[pltpu.VMEM((4, block, columns), own.dtype)],
        ),
        out_shape=jax.ShapeDtypeStruct((rows, size * part), jnp.float32),
        compiler_params=pltpu.CompilerParams(vmem_limit_bytes=32 * 2**20),
        cost_estimate=pl.CostEstimate(flops=0, bytes_accessed=8 * 2**20, transcendentals=0),
    )(jnp.reshape(seq_index, (1,)).astype(jnp.int32), own, other, pair)


def norm_forward(values, gain):
    inverse = lax.rsqrt(jnp.mean(values * values, axis=-1, keepdims=True) + norm_epsilon)
    unit = values * inverse
    return (unit * gain, unit, inverse)


def norm_backward(grad_in, unit, inverse, gain):
    scaled = grad_in * gain
    return inverse * (scaled - unit * jnp.mean(scaled * unit, axis=-1, keepdims=True))


def transpose_dot(left, right):
    return lax.dot_general(
        left, right, (((0,), (0,)), ((), ())), preferred_element_type=jnp.float32
    )


def dot_transposed(left, right):
    return lax.dot_general(
        left, right, (((1,), (1,)), ((), ())), preferred_element_type=jnp.float32
    )


def split_rows(rows):
    return (rows // 32) * 16


def ring_ids(size):
    return list(range(0, size, 2)) + [i for i in range(size - 1, 0, -1) if i % 2]


def ring_place(index, size):
    return jnp.where(index % 2 == 0, index // 2, size - 1 - index // 2)


def ring_id(place, size):
    place = place % size
    half = (size + 1) // 2
    return jnp.where(place < half, 2 * place, 2 * (size - 1 - place) + 1)


def ring_perms(size):
    ids = ring_ids(size)
    forward = [(ids[i], ids[(i + 1) % size]) for i in range(size)]
    return forward, [(b, a) for a, b in forward]


def after(value, *needed):
    return lax.optimization_barrier((value, *needed))[0] if needed else value


def ring_gather(ahead, behind, size, place):
    forward, backward = ring_perms(size)
    ahead_all = jnp.zeros((size, *ahead.shape), ahead.dtype)
    behind_all = jnp.zeros((size, *behind.shape), behind.dtype)

    def put(whole, piece, step):
        return lax.dynamic_update_slice(whole, piece[None], (ring_id(place + step, size), 0, 0))

    ahead_all = put(ahead_all, ahead, 0)
    behind_all = put(behind_all, behind, 0)
    for step in range(1, size):
        ahead = lax.ppermute(ahead, "fsdp", forward)
        behind = lax.ppermute(behind, "fsdp", backward)
        ahead_all = put(ahead_all, ahead, size - step)
        behind_all = put(behind_all, behind, step)
    return ahead_all, behind_all


def ring_scatter(ahead_blocks, behind_blocks, size, place, needed={}):
    forward, backward = ring_perms(size)

    def own(blocks, step):
        shape = (1, *blocks.shape[1:])
        return lax.dynamic_slice(blocks, (ring_id(place + step, size), 0, 0), shape)[0]

    ahead = own(ahead_blocks, size - 1).astype(jnp.bfloat16)
    behind = own(behind_blocks, 1).astype(jnp.bfloat16)
    for step in range(1, size):
        values = needed.get(step, ())
        ahead = lax.ppermute(after(ahead, *values), "fsdp", forward)
        behind = lax.ppermute(after(behind, *values), "fsdp", backward)
        ahead = (ahead.astype(jnp.float32) + own(ahead_blocks, 2 * size - 1 - step)).astype(
            jnp.bfloat16
        )
        behind = (behind.astype(jnp.float32) + own(behind_blocks, 1 + step)).astype(jnp.bfloat16)
    return ahead, behind


def exchange(values, mask):
    return lax.ppermute(values, "seq", [(i, i ^ mask) for i in range(4)])


def gather_pair(block):
    other = exchange(block, 2)
    return other, exchange(jnp.stack([block, other]), 1)


def gather_seq(block):
    other, pair = gather_pair(block)
    return [block, other, pair[0], pair[1]]


def in_order(pieces, seq_index):
    high, low = seq_index // 2, seq_index % 2

    def pick(first, second, flag):
        return jnp.where(flag == 0, first, second), jnp.where(flag == 0, second, first)

    mine = pick(pieces[0], pieces[1], high)
    theirs = pick(pieces[2], pieces[3], high)
    return [*pick(mine[0], theirs[0], low), *pick(mine[1], theirs[1], low)]


def scatter_seq(blocks):
    came = exchange(blocks[2:].astype(jnp.bfloat16), 1).astype(jnp.float32)
    here = blocks[:2].astype(jnp.float32) + came
    sent = here[1].astype(jnp.bfloat16)
    return here[0] + exchange(sent, 2).astype(jnp.float32), sent


def swap_rows(values, seq_index):
    rows = values.shape[0] // 4

    def block(mask):
        return lax.dynamic_slice_in_dim(values, (seq_index ^ mask) * rows, rows, 0)

    return [block(0), exchange(block(2), 2), exchange(block(1), 1), exchange(block(3), 3)]


def swap_columns(values, seq_index):
    columns = values.shape[1] // 4

    def block(mask):
        return lax.dynamic_slice_in_dim(values, (seq_index ^ mask) * columns, columns, 1)

    return [block(0), exchange(block(2), 2), exchange(block(1), 1), exchange(block(3), 3)]


def body(
    tokens,
    norm_gain,
    query_weight,
    key_weight,
    value_weight,
    query_gain,
    key_gain,
    out_weight,
    ffn_gain,
    gate_weight,
    up_weight,
    down_weight,
    cotangent,
):
    bf16, f32 = jnp.bfloat16, jnp.float32
    size = lax.axis_size("fsdp")
    seq_index = lax.axis_index("seq")
    place = ring_place(lax.axis_index("fsdp"), size)
    own_rows, width = query_weight.shape
    head_part = query_gain.shape[0]
    head_width = head_part * size
    query_columns = width // 4
    key_columns = key_weight.shape[1] // 4
    ff_part = down_weight.shape[0]
    window = -(-ff_part // 64) * 16

    def columns_of(weight, count):
        return lax.dynamic_slice_in_dim(weight, seq_index * count, count, 1)

    def hidden_rows(weight):
        tall = jnp.pad(weight, ((0, 4 * window - ff_part), (0, 0)))
        return lax.dynamic_slice_in_dim(tall, seq_index * window, window, 0)

    gains = jnp.concatenate([norm_gain, ffn_gain, query_gain, key_gain])
    packed_columns = 2 * query_columns + 2 * key_columns
    gain_rows = jnp.pad(gains[None], ((0, 15), (0, packed_columns - gains.shape[0])))
    packed = jnp.concatenate(
        [
            jnp.concatenate(
                [
                    columns_of(query_weight, query_columns),
                    columns_of(key_weight, key_columns),
                    columns_of(value_weight, key_columns),
                    columns_of(out_weight, query_columns),
                ],
                axis=1,
            ),
            gain_rows,
        ],
        axis=0,
    )
    top = split_rows(packed.shape[0])
    top_all, bottom_all = ring_gather(packed[:top], packed[top:], size, place)
    down_all = lax.all_gather(hidden_rows(down_weight), "fsdp", axis=0, tiled=True)
    gate_all, up_all = ring_gather(
        *pick_hidden(gate_weight, up_weight, seq_index, size, ff_part, window), size, place
    )
    gate_all = gate_all.reshape(width, size * window)
    up_all = up_all.reshape(width, size * window)

    gains_all = bottom_all[:, own_rows - top].astype(f32)
    first_gain = gains_all[:, :own_rows].reshape(-1)
    second_gain = gains_all[:, own_rows : 2 * own_rows].reshape(-1)
    q_gain_f = gains_all[:, 2 * own_rows : 2 * own_rows + head_part].reshape(-1)
    k_gain_f = gains_all[:, 2 * own_rows + head_part : 2 * (own_rows + head_part)].reshape(-1)
    attention_all = jnp.concatenate([top_all, bottom_all[:, : own_rows - top]], axis=1).reshape(
        width, packed_columns
    )
    qkv_all = attention_all[:, : query_columns + 2 * key_columns]
    out_all = jnp.concatenate(
        in_order(gather_seq(attention_all[:, query_columns + 2 * key_columns :]), seq_index), axis=1
    )

    inputs = tokens[0]
    tok_rows = inputs.shape[0]
    length = 4 * tok_rows
    inputs_all = jnp.concatenate(in_order(gather_seq(inputs), seq_index), axis=0).astype(f32)
    out_grad = cotangent[0]
    out_grad_all = jnp.concatenate(gather_seq(out_grad), axis=0)

    normed, norm_unit, norm_inverse = norm_forward(inputs_all, first_gain)
    normed_low = normed.astype(bf16)
    qkv_t = lax.dot_general(
        qkv_all, normed_low, (((0,), (1,)), ((), ())), preferred_element_type=f32
    )
    sizes = (query_columns // head_width, key_columns // head_width, head_width)
    cosine, sine = rope_rows(length, head_width)
    tables = (q_gain_f[:, None], k_gain_f[:, None], cosine, sine)
    mixed_heads, mixed_t, totals = attention_forward(qkv_t, *tables, sizes)
    mixed = jnp.concatenate(in_order(swap_rows(mixed_heads, seq_index), seq_index), axis=1)
    attended = jnp.dot(mixed, out_all, preferred_element_type=f32)
    middle = inputs.astype(f32) + attended
    normed_two, middle_unit, middle_inverse = norm_forward(middle, second_gain)
    normed_two_all = jnp.concatenate(gather_seq(normed_two.astype(bf16)), axis=0)
    mixed_all = jnp.concatenate(in_order(gather_seq(mixed_heads), seq_index), axis=1)

    gate_act = jnp.dot(normed_two_all, gate_all, preferred_element_type=f32)
    up_act = jnp.dot(normed_two_all, up_all, preferred_element_type=f32)
    gate_sigmoid = jax.nn.sigmoid(gate_act)
    gate_silu = gate_act * gate_sigmoid
    hidden = (gate_silu * up_act).astype(bf16)
    down_weight_grad = transpose_dot(hidden, out_grad_all)
    down_share = lax.psum_scatter(
        down_weight_grad.astype(bf16), "fsdp", scatter_dimension=0, tiled=True
    )

    hidden_grad = dot_transposed(out_grad_all, down_all)
    gate_grad = (
        hidden_grad * up_act * gate_sigmoid * (1.0 + gate_act * (1.0 - gate_sigmoid))
    ).astype(bf16)
    up_grad = (hidden_grad * gate_silu).astype(bf16)
    normed_two_grad, half_sum = scatter_seq(
        (dot_transposed(gate_grad, gate_all) + dot_transposed(up_grad, up_all)).reshape(
            4, tok_rows, width
        )
    )
    gate_weight_grad = transpose_dot(normed_two_all, gate_grad)
    up_weight_grad = transpose_dot(normed_two_all, up_grad)
    down_sum, _ = scatter_seq(
        jnp.dot(hidden, down_all, preferred_element_type=f32).reshape(4, tok_rows, width)
    )
    output = middle + down_sum
    ffn_gain_grad = jnp.sum(normed_two_grad * middle_unit, axis=0)
    middle_grad = out_grad.astype(f32) + norm_backward(
        normed_two_grad, middle_unit, middle_inverse, second_gain
    )
    attended_low = middle_grad.astype(bf16)
    mixed_grad = dot_transposed(attended_low, out_all).astype(bf16)
    mixed_grad_heads = jnp.concatenate(in_order(swap_columns(mixed_grad, seq_index), seq_index), axis=0)
    attended_columns = jnp.concatenate(
        in_order(swap_columns(attended_low, seq_index), seq_index), axis=0
    )
    out_weight_grad = transpose_dot(mixed_all, attended_columns)
    out_share = lax.psum_scatter(
        out_weight_grad.astype(bf16), "fsdp", scatter_dimension=0, tiled=True
    )
    gate_share, up_share = ring_scatter(
        gate_weight_grad.reshape(size, own_rows, size * window),
        up_weight_grad.reshape(size, own_rows, size * window),
        size,
        place,
        {2: (half_sum,), 3: (mixed_grad,)},
    )
    qkv_grad_t, head_gains = attention_backward(
        qkv_t, *tables, mixed_t, totals, mixed_grad_heads, sizes
    )
    head_gains = jnp.sum(head_gains, axis=1)
    query_gain_grad, key_gain_grad = head_gains[:head_width], head_gains[head_width:]
    qkv_weight_grad = lax.dot_general(
        normed_low, qkv_grad_t, (((0,), (1,)), ((), ())), preferred_element_type=f32
    )
    normed_partial = lax.dot_general(
        qkv_grad_t, qkv_all, (((0,), (1,)), ((), ())), preferred_element_type=f32
    )
    norm_gain_grad = jnp.sum(normed_partial * norm_unit, axis=0)
    partial_blocks = normed_partial.reshape(4, tok_rows, width)
    normed_grad, _ = scatter_seq(
        jnp.concatenate(
            [
                lax.dynamic_slice_in_dim(partial_blocks, seq_index ^ mask, 1, 0)
                for mask in (0, 2, 1, 3)
            ],
            axis=0,
        )
    )
    _, own_unit, own_inverse = norm_forward(inputs.astype(f32), first_gain)
    inputs_grad = middle_grad + norm_backward(normed_grad, own_unit, own_inverse, first_gain)

    gain_grads = jnp.concatenate(
        [
            norm_gain_grad.reshape(size, -1),
            ffn_gain_grad.reshape(size, -1),
            query_gain_grad.reshape(size, -1),
            key_gain_grad.reshape(size, -1),
        ],
        axis=1,
    )
    gain_count = gain_grads.shape[1]
    qkv_columns = query_columns + 2 * key_columns
    gain_blocks = jnp.pad(gain_grads[:, None], ((0, 0), (0, 15), (0, qkv_columns - gain_count)))
    qkv_blocks = qkv_weight_grad.reshape(size, own_rows, qkv_columns)
    packed_share = jnp.concatenate(
        ring_scatter(
            qkv_blocks[:, :top],
            jnp.concatenate([qkv_blocks[:, top:], gain_blocks], axis=1),
            size,
            place,
        ),
        axis=0,
    )

    down_full = jnp.concatenate(in_order(gather_seq(down_share), seq_index), axis=0)[
        :ff_part
    ].astype(f32)

    def full_columns(share):
        return spread_hidden(share, *gather_pair(share), seq_index, size, ff_part, window)

    gate_full = full_columns(gate_share)
    up_full = full_columns(up_share)
    out_full = jnp.concatenate(in_order(gather_seq(out_share), seq_index), axis=1).astype(f32)
    packs = in_order(gather_seq(packed_share), seq_index)

    def unpack(first, count):
        return jnp.concatenate(
            [p[:own_rows, first : first + count] for p in packs], axis=1
        ).astype(f32)

    gain_sum = sum(p[own_rows, :gain_count].astype(f32) for p in packs)
    return (
        output[None].astype(bf16),
        inputs_grad[None].astype(bf16),
        gain_sum[:own_rows],
        unpack(0, query_columns),
        unpack(query_columns, key_columns),
        unpack(query_columns + key_columns, key_columns),
        gain_sum[2 * own_rows : 2 * own_rows + head_part],
        gain_sum[2 * own_rows + head_part :],
        out_full,
        gain_sum[own_rows : 2 * own_rows],
        gate_full,
        up_full,
        down_full,
    )


def solution(mesh):
    in_specs = (
        P("fsdp", "seq", None),
        P("fsdp"),
        P("fsdp", None),
        P("fsdp", None),
        P("fsdp", None),
        P("fsdp"),
        P("fsdp"),
        P("fsdp", None),
        P("fsdp"),
        P("fsdp", None),
        P("fsdp", None),
        P("fsdp", None),
        P("fsdp", "seq", None),
    )
    out_specs = (
        P("fsdp", "seq", None),
        P("fsdp", "seq", None),
        P("fsdp"),
        P("fsdp", None),
        P("fsdp", None),
        P("fsdp", None),
        P("fsdp"),
        P("fsdp"),
        P("fsdp", None),
        P("fsdp"),
        P("fsdp", None),
        P("fsdp", None),
        P("fsdp", None),
    )
    return jax.shard_map(body, mesh=mesh, in_specs=in_specs, out_specs=out_specs, check_vma=False)
```

```python
import functools
import math

import jax
import jax.numpy as jnp
from jax import lax
from jax.experimental import pallas as pl
from jax.experimental.pallas import tpu as pltpu
from jax.sharding import PartitionSpec as P

norm_epsilon = 1e-05
TILE = 256
log2_e = math.log2(math.e)


def rope_rows(length, width):
    half_width = width // 2
    inverse = jnp.exp(
        jnp.arange(half_width, dtype=jnp.float32) * (-2.0 * math.log(1000000.0) / width)
    )
    angles = inverse[:, None] * jnp.arange(length, dtype=jnp.int32).astype(jnp.float32)[None, :]
    return jnp.cos(angles), jnp.sin(angles)


def head_norm(values):
    inverse = lax.rsqrt(jnp.mean(values * values, axis=0, keepdims=True) + norm_epsilon)
    return values * inverse, inverse


def head_turn(values, cosine, sine):
    half = values.shape[0] // 2
    first, second = values[:half], values[half:]
    return jnp.concatenate(
        [first * cosine - second * sine, second * cosine + first * sine], axis=0
    )


def head_turn_back(values, cosine, sine):
    half = values.shape[0] // 2
    first, second = values[:half], values[half:]
    return jnp.concatenate(
        [first * cosine + second * sine, second * cosine - first * sine], axis=0
    )


def fill_heads(qkv_ref, q_gain_ref, k_gain_ref, cos_ref, sin_ref, queries, keys, keys_t, values, values_t, sizes):
    heads, groups, width = sizes
    cosine, sine = cos_ref[...], sin_ref[...]

    @pl.loop(0, heads)
    def _(head):
        unit, _ = head_norm(qkv_ref[pl.ds(head * width, width), :])
        turned = head_turn(unit * q_gain_ref[...], cosine, sine)
        queries[head] = (turned * (width**-0.5 * log2_e)).astype(jnp.bfloat16)

    @pl.loop(0, groups)
    def _(group):
        unit, _ = head_norm(qkv_ref[pl.ds((heads + group) * width, width), :])
        turned = head_turn(unit * k_gain_ref[...], cosine, sine)
        keys[group] = turned.T.astype(jnp.bfloat16)
        if keys_t is not None:
            keys_t[group] = turned.astype(jnp.bfloat16)
        value = qkv_ref[pl.ds((heads + groups + group) * width, width), :]
        if values is not None:
            values[group] = value.T.astype(jnp.bfloat16)
        if values_t is not None:
            values_t[group] = value.astype(jnp.bfloat16)


def diagonal_mask():
    key_place = lax.broadcasted_iota(jnp.int32, (TILE, TILE), 0)
    query_place = lax.broadcasted_iota(jnp.int32, (TILE, TILE), 1)
    return key_place <= query_place


def causal_exp(scores, count):
    weights = jnp.exp2(scores)
    last = jnp.where(diagonal_mask(), weights[count - TILE :], 0.0)
    if count == TILE:
        return last
    return jnp.concatenate([weights[: count - TILE], last], axis=0)


def dot(left, right):
    return jnp.dot(left, right, preferred_element_type=jnp.float32)


def dot_nt(left, right):
    return lax.dot_general(
        left, right, (((1,), (1,)), ((), ())), preferred_element_type=jnp.float32
    )


def forward_kernel(sizes, qkv_ref, q_gain_ref, k_gain_ref, cos_ref, sin_ref, mixed_ref, mixed_t_ref, total_ref, queries, keys, values_t, mixed_f):
    heads, groups, width = sizes
    ratio = heads // groups
    length = qkv_ref.shape[1]
    fill_heads(qkv_ref, q_gain_ref, k_gain_ref, cos_ref, sin_ref, queries, keys, None, None, values_t, sizes)

    @pl.loop(0, heads)
    def _(head):
        group = head // ratio
        for tile in range(length // TILE):
            count = (tile + 1) * TILE
            columns = pl.ds(tile * TILE, TILE)
            scores = dot(keys[group, pl.ds(0, count), :], queries[head, :, columns])
            weights = causal_exp(scores, count)
            total = jnp.sum(weights, axis=0, keepdims=True)
            result = dot(values_t[group, :, pl.ds(0, count)], weights.astype(jnp.bfloat16))
            mixed_f[pl.ds(head * width, width), columns] = result * (1.0 / total)
            total_ref[pl.ds(head, 1), columns] = jnp.log2(total)

    for block in range(heads * width // 128):
        rows = mixed_f[pl.ds(block * 128, 128), :]
        mixed_t_ref[pl.ds(block * 128, 128), :] = rows.astype(jnp.bfloat16)
        mixed_ref[:, pl.ds(block * 128, 128)] = rows.T.astype(jnp.bfloat16)


def backward_kernel(sizes, qkv_ref, q_gain_ref, k_gain_ref, cos_ref, sin_ref, mixed_t_ref, total_ref, grad_ref, out_ref, gain_ref, queries, keys, keys_t, values, grads, key_sum, value_sum):
    heads, groups, width = sizes
    ratio = heads // groups
    length = qkv_ref.shape[1]
    fill_heads(qkv_ref, q_gain_ref, k_gain_ref, cos_ref, sin_ref, queries, keys, keys_t, values, None, sizes)
    for block in range(heads * width // 128):
        turned = grad_ref[:, pl.ds(block * 128, 128)].astype(jnp.float32).T
        grads[pl.ds(block * 128, 128), :] = turned.astype(jnp.bfloat16)
    key_sum[...] = jnp.zeros_like(key_sum)
    value_sum[...] = jnp.zeros_like(value_sum)
    gain_ref[...] = jnp.zeros_like(gain_ref)
    cosine, sine = cos_ref[...], sin_ref[...]

    def finish(grad_turned, rows, gain, first):
        grad = head_turn_back(grad_turned, cosine, sine)
        unit, inverse = head_norm(qkv_ref[rows, :])
        product = grad * unit
        part = product[:, :128]
        for lane in range(128, length, 128):
            part = part + product[:, lane : lane + 128]
        gain_ref[pl.ds(first, width), :] += part
        scaled = grad * gain
        before = inverse * (scaled - unit * jnp.mean(scaled * unit, axis=0, keepdims=True))
        out_ref[rows, :] = before.astype(jnp.bfloat16)

    @pl.loop(0, heads)
    def _(head):
        group = head // ratio
        rows = pl.ds(head * width, width)
        query_parts = []
        for tile in range(length // TILE):
            count = (tile + 1) * TILE
            columns = pl.ds(tile * TILE, TILE)
            query = queries[head, :, columns]
            grad = grads[rows, columns]
            scores = dot(keys[group, pl.ds(0, count), :], query) - total_ref[pl.ds(head, 1), columns]
            weights = causal_exp(scores, count)
            inner = jnp.sum(
                grad.astype(jnp.float32) * mixed_t_ref[rows, columns].astype(jnp.float32),
                axis=0,
                keepdims=True,
            )
            weight_grad = dot(values[group, pl.ds(0, count), :], grad)
            score_grad = (weights * (weight_grad - inner)).astype(jnp.bfloat16)
            query_parts.append(dot(keys_t[group, :, pl.ds(0, count)], score_grad))
            key_sum[group, pl.ds(0, count), :] += dot_nt(score_grad, query)
            value_sum[group, pl.ds(0, count), :] += dot_nt(weights.astype(jnp.bfloat16), grad)
        query_grad = jnp.concatenate(query_parts, axis=1) * width**-0.5
        finish(query_grad, rows, q_gain_ref[...], 0)

    for group in range(groups):
        key_grad = key_sum[group].T * (1.0 / log2_e)
        finish(key_grad, pl.ds((heads + group) * width, width), k_gain_ref[...], width)
        out_ref[pl.ds((heads + groups + group) * width, width), :] = value_sum[group].T.astype(
            jnp.bfloat16
        )


def attention_forward(qkv_t, q_gain, k_gain, cosine, sine, sizes):
    heads, groups, width = sizes
    length = qkv_t.shape[1]
    bf16, f32 = jnp.bfloat16, jnp.float32
    pairs = heads * length * length
    return pl.pallas_call(
        functools.partial(forward_kernel, sizes),
        out_shape=(
            jax.ShapeDtypeStruct((length, heads * width), bf16),
            jax.ShapeDtypeStruct((heads * width, length), bf16),
            jax.ShapeDtypeStruct((-(-heads // 8) * 8, length), f32),
        ),
        scratch_shapes=[
            pltpu.VMEM((heads, width, length), bf16),
            pltpu.VMEM((groups, length, width), bf16),
            pltpu.VMEM((groups, width, length), bf16),
            pltpu.VMEM((heads * width, length), f32),
        ],
        compiler_params=pltpu.CompilerParams(vmem_limit_bytes=32 * 2**20),
        cost_estimate=pl.CostEstimate(
            flops=8 * pairs * width, bytes_accessed=6 * 2**20, transcendentals=pairs
        ),
    )(qkv_t, q_gain, k_gain, cosine, sine)


def attention_backward(qkv_t, q_gain, k_gain, cosine, sine, mixed_t, total, mixed_grad, sizes):
    heads, groups, width = sizes
    length = qkv_t.shape[1]
    bf16, f32 = jnp.bfloat16, jnp.float32
    pairs = heads * length * length
    return pl.pallas_call(
        functools.partial(backward_kernel, sizes),
        out_shape=(
            jax.ShapeDtypeStruct(qkv_t.shape, bf16),
            jax.ShapeDtypeStruct((2 * width, 128), f32),
        ),
        scratch_shapes=[
            pltpu.VMEM((heads, width, length), bf16),
            pltpu.VMEM((groups, length, width), bf16),
            pltpu.VMEM((groups, width, length), bf16),
            pltpu.VMEM((groups, length, width), bf16),
            pltpu.VMEM((heads * width, length), bf16),
            pltpu.VMEM((groups, length, width), f32),
            pltpu.VMEM((groups, length, width), f32),
        ],
        compiler_params=pltpu.CompilerParams(vmem_limit_bytes=40 * 2**20),
        cost_estimate=pl.CostEstimate(
            flops=20 * pairs * width, bytes_accessed=8 * 2**20, transcendentals=pairs
        ),
    )(qkv_t, q_gain, k_gain, cosine, sine, mixed_t, total, mixed_grad)


def hidden_kernel(size, ids_ref, rows_ref, *refs):
    chunks, refs = refs[: 2 * size], refs[2 * size :]
    slope_ref, silu_ref, hidden_ref, gate_out, up_out, gate, up, in_sems, out_sems = refs
    step = pl.program_id(0)
    steps = pl.num_programs(0)
    rows = chunks[0].shape[0]

    @pl.when(step == 0)
    def _():
        @pl.loop(0, steps)
        def _(tile):
            columns = pl.ds(pl.multiple_of(tile * TILE, TILE), TILE)
            for which, target in ((0, gate), (1, up)):
                for index in range(size):
                    first = pl.multiple_of(ids_ref[which, index] * rows, 16)
                    pltpu.make_async_copy(
                        chunks[which * size + index].at[:, columns],
                        target.at[pl.ds(first, rows), columns],
                        in_sems.at[which, tile],
                    ).start()

    columns = pl.ds(pl.multiple_of(step * TILE, TILE), TILE)
    for which, target, result in ((0, gate, gate_out), (1, up, up_out)):
        part = target.at[:, columns]
        pltpu.make_async_copy(part, part, in_sems.at[which, step]).wait()
        pltpu.make_async_copy(part, result.at[:, columns], out_sems.at[which, step]).start()
    gate_act = dot(rows_ref[...], gate[:, columns])
    up_act = dot(rows_ref[...], up[:, columns])
    sigmoid = 1.0 / (1.0 + jnp.exp(-gate_act))
    silu = gate_act * sigmoid
    hidden_ref[...] = (silu * up_act).astype(hidden_ref.dtype)
    silu_ref[...] = silu.astype(silu_ref.dtype)
    slope_ref[...] = (up_act * sigmoid * (1.0 + gate_act * (1.0 - sigmoid))).astype(slope_ref.dtype)

    @pl.when(step == steps - 1)
    def _():
        @pl.loop(0, steps)
        def _(tile):
            columns = pl.ds(pl.multiple_of(tile * TILE, TILE), TILE)
            for which, target, result in ((0, gate, gate_out), (1, up, up_out)):
                pltpu.make_async_copy(
                    target.at[:, columns], result.at[:, columns], out_sems.at[which, tile]
                ).wait()


def ffn_hidden(rows, gate_chunks, up_chunks, ids):
    size = len(gate_chunks)
    part, columns = gate_chunks[0].shape
    length, width = rows.shape
    bf16 = jnp.bfloat16
    tall = pl.BlockSpec((length, TILE), lambda i, ids: (0, i))
    act = jax.ShapeDtypeStruct((length, columns), bf16)
    weight = jax.ShapeDtypeStruct((width, columns), bf16)
    anywhere = pl.BlockSpec(memory_space=pl.ANY)
    return pl.pallas_call(
        functools.partial(hidden_kernel, size),
        grid_spec=pltpu.PrefetchScalarGridSpec(
            num_scalar_prefetch=1,
            grid=(columns // TILE,),
            in_specs=[pl.BlockSpec((length, width), lambda i, ids: (0, 0))] + [anywhere] * (2 * size),
            out_specs=[tall, tall, tall, anywhere, anywhere],
            scratch_shapes=[
                pltpu.VMEM((width, columns), bf16),
                pltpu.VMEM((width, columns), bf16),
                pltpu.SemaphoreType.DMA((2, columns // TILE)),
                pltpu.SemaphoreType.DMA((2, columns // TILE)),
            ],
        ),
        out_shape=(act, act, act, weight, weight),
        compiler_params=pltpu.CompilerParams(vmem_limit_bytes=40 * 2**20),
        cost_estimate=pl.CostEstimate(
            flops=4 * length * width * columns,
            bytes_accessed=36 * 2**20,
            transcendentals=length * columns,
        ),
    )(ids, rows, *gate_chunks, *up_chunks)


def hidden_grad_kernel(steps, grad_ref, down_ref, slope_ref, silu_ref, gate_ref, up_ref, gate_out, up_out, own_ref, sent_ref, gate_grads, up_grads):
    step = pl.program_id(0)
    half = own_ref.shape[0]

    @pl.when(step < steps)
    def _():
        hidden_grad = dot_nt(grad_ref[...], down_ref[...])
        gate_grad = (hidden_grad * slope_ref[...].astype(jnp.float32)).astype(jnp.bfloat16)
        up_grad = (hidden_grad * silu_ref[...].astype(jnp.float32)).astype(jnp.bfloat16)
        columns = pl.ds(pl.multiple_of(step * TILE, TILE), TILE)
        gate_out[...] = gate_grad
        up_out[...] = up_grad
        gate_grads[:, columns] = gate_grad
        up_grads[:, columns] = up_grad

    @pl.when(step >= steps)
    def _():
        total = dot_nt(gate_grads[...], gate_ref[...]) + dot_nt(up_grads[...], up_ref[...])
        own_ref[...] = total[:half].astype(own_ref.dtype)
        sent_ref[...] = total[half:].astype(sent_ref.dtype)


def ffn_hidden_grad(out_grad, down, slope, silu, gate, up):
    length, width = out_grad.shape
    columns = down.shape[0]
    steps = columns // TILE
    bf16 = jnp.bfloat16
    tall = pl.BlockSpec((length, TILE), lambda i: (0, jnp.minimum(i, steps - 1)))
    weight = pl.BlockSpec((TILE, columns), lambda i: (jnp.maximum(i - steps, 0), 0))
    half = pl.BlockSpec((length // 2, TILE), lambda i: (0, jnp.maximum(i - steps, 0)))
    act = jax.ShapeDtypeStruct((length, columns), bf16)
    part = jax.ShapeDtypeStruct((length // 2, width), bf16)
    return pl.pallas_call(
        functools.partial(hidden_grad_kernel, steps),
        grid=(steps + width // TILE,),
        in_specs=[
            pl.BlockSpec((length, width), lambda i: (0, 0)),
            pl.BlockSpec((TILE, width), lambda i: (jnp.minimum(i, steps - 1), 0)),
            tall,
            tall,
            weight,
            weight,
        ],
        out_specs=[tall, tall, half, half],
        out_shape=(act, act, part, part),
        scratch_shapes=[pltpu.VMEM((length, columns), bf16), pltpu.VMEM((length, columns), bf16)],
        compiler_params=pltpu.CompilerParams(vmem_limit_bytes=40 * 2**20),
        cost_estimate=pl.CostEstimate(
            flops=6 * length * width * columns, bytes_accessed=40 * 2**20, transcendentals=0
        ),
    )(out_grad, down, slope, silu, gate, up)


def pick_kernel(sizes, index_ref, gate_ref, up_ref, gate_out, up_out):
    size, part, window = sizes
    rows = gate_ref.shape[0]
    for source, target in ((gate_ref, gate_out), (up_ref, up_out)):
        for index in range(4):
            count = min(window, part - index * window)

            @pl.when(index_ref[0] == index)
            def _():
                parts = []
                for owner in range(size):
                    first = owner * part + index * window
                    low, high = first // 128 * 128, -(-(first + count) // 128) * 128
                    wide = source[:, low:high].astype(jnp.float32)
                    parts.append(wide[:, first - low : first - low + count])
                    if count < window:
                        parts.append(jnp.zeros((rows, window - count), jnp.float32))
                target[...] = jnp.concatenate(parts, axis=1).astype(target.dtype)


def pick_hidden(gate, up, seq_index, size, part, window):
    rows, columns = gate.shape
    block = 48 if rows % 48 == 0 else rows
    wide = pl.BlockSpec((block, columns), lambda i, index: (i, 0))
    narrow = pl.BlockSpec((block, size * window), lambda i, index: (i, 0))
    out = jax.ShapeDtypeStruct((rows, size * window), gate.dtype)
    return pl.pallas_call(
        functools.partial(pick_kernel, (size, part, window)),
        grid_spec=pltpu.PrefetchScalarGridSpec(
            num_scalar_prefetch=1,
            grid=(rows // block,),
            in_specs=[wide, wide],
            out_specs=[narrow, narrow],
        ),
        out_shape=(out, out),
        compiler_params=pltpu.CompilerParams(vmem_limit_bytes=32 * 2**20),
        cost_estimate=pl.CostEstimate(flops=0, bytes_accessed=8 * 2**20, transcendentals=0),
    )(jnp.reshape(seq_index, (1,)).astype(jnp.int32), gate, up)


def spread_kernel(sizes, index_ref, own_ref, other_ref, pair_ref, out_ref, parts):
    size, part, window = sizes
    me = index_ref[0]
    parts[me] = own_ref[...]
    parts[me ^ 2] = other_ref[...]
    parts[me ^ 1] = pair_ref[0]
    parts[me ^ 3] = pair_ref[1]
    pieces = []
    for owner in range(size):
        for index in range(4):
            count = min(window, part - index * window)
            first = owner * window
            low, high = first // 128 * 128, -(-(first + count) // 128) * 128
            wide = parts[index, :, low:high].astype(jnp.float32)
            pieces.append(wide[:, first - low : first - low + count])
    out_ref[...] = jnp.concatenate(pieces, axis=1)


def spread_hidden(own, other, pair, seq_index, size, part, window):
    rows, columns = own.shape
    block = 48 if rows % 48 == 0 else rows
    narrow = pl.BlockSpec((block, columns), lambda i, index: (i, 0))
    return pl.pallas_call(
        functools.partial(spread_kernel, (size, part, window)),
        grid_spec=pltpu.PrefetchScalarGridSpec(
            num_scalar_prefetch=1,
            grid=(rows // block,),
            in_specs=[
                narrow,
                narrow,
                pl.BlockSpec((2, block, columns), lambda i, index: (0, i, 0)),
            ],
            out_specs=pl.BlockSpec((block, size * part), lambda i, index: (i, 0)),
            scratch_shapes=[pltpu.VMEM((4, block, columns), own.dtype)],
        ),
        out_shape=jax.ShapeDtypeStruct((rows, size * part), jnp.float32),
        compiler_params=pltpu.CompilerParams(vmem_limit_bytes=32 * 2**20),
        cost_estimate=pl.CostEstimate(flops=0, bytes_accessed=8 * 2**20, transcendentals=0),
    )(jnp.reshape(seq_index, (1,)).astype(jnp.int32), own, other, pair)


def norm_forward(values, gain):
    inverse = lax.rsqrt(jnp.mean(values * values, axis=-1, keepdims=True) + norm_epsilon)
    unit = values * inverse
    return (unit * gain, unit, inverse)


def norm_backward(grad_in, unit, inverse, gain):
    scaled = grad_in * gain
    return inverse * (scaled - unit * jnp.mean(scaled * unit, axis=-1, keepdims=True))


def transpose_dot(left, right):
    return lax.dot_general(
        left, right, (((0,), (0,)), ((), ())), preferred_element_type=jnp.float32
    )


def dot_transposed(left, right):
    return lax.dot_general(
        left, right, (((1,), (1,)), ((), ())), preferred_element_type=jnp.float32
    )


def split_rows(rows):
    return (rows // 32) * 16


def ring_ids(size):
    return list(range(0, size, 2)) + [i for i in range(size - 1, 0, -1) if i % 2]


def ring_place(index, size):
    return jnp.where(index % 2 == 0, index // 2, size - 1 - index // 2)


def ring_id(place, size):
    place = place % size
    half = (size + 1) // 2
    return jnp.where(place < half, 2 * place, 2 * (size - 1 - place) + 1)


def ring_perms(size):
    ids = ring_ids(size)
    forward = [(ids[i], ids[(i + 1) % size]) for i in range(size)]
    return forward, [(b, a) for a, b in forward]


def after(value, *needed):
    return lax.optimization_barrier((value, *needed))[0] if needed else value


class GatherRing:
    def __init__(self, ahead, behind, size):
        self.perms = ring_perms(size)
        self.ahead, self.behind = [ahead], [behind]

    def step(self, *needed):
        forward, backward = self.perms
        self.ahead.append(lax.ppermute(after(self.ahead[-1], *needed), "fsdp", forward))
        self.behind.append(lax.ppermute(after(self.behind[-1], *needed), "fsdp", backward))
        return self.ahead[-1], self.behind[-1]


def ring_owners(size, place):
    steps = jnp.arange(size, dtype=jnp.int32)
    return jnp.stack([ring_id(place + size - steps, size), ring_id(place + steps, size)])


def lay_out(blocks, owners):
    whole = jnp.zeros((len(blocks), *blocks[0].shape), blocks[0].dtype)
    for index, block in enumerate(blocks):
        whole = lax.dynamic_update_slice(whole, block[None], (owners[index], 0, 0))
    return whole


class ScatterRing:
    def __init__(self, ahead_blocks, behind_blocks, size, place):
        self.perms = ring_perms(size)
        self.size, self.place, self.count = size, place, 0
        self.ahead_blocks, self.behind_blocks = ahead_blocks, behind_blocks
        self.ahead = self.own(ahead_blocks, size - 1).astype(jnp.bfloat16)
        self.behind = self.own(behind_blocks, 1).astype(jnp.bfloat16)

    def own(self, blocks, step):
        start = (ring_id(self.place + step, self.size), 0, 0)
        return lax.dynamic_slice(blocks, start, (1, *blocks.shape[1:]))[0].astype(jnp.float32)

    def step(self, *needed):
        forward, backward = self.perms
        self.count += 1
        ahead = lax.ppermute(after(self.ahead, *needed), "fsdp", forward)
        behind = lax.ppermute(after(self.behind, *needed), "fsdp", backward)
        ahead_own = self.own(self.ahead_blocks, 2 * self.size - 1 - self.count)
        behind_own = self.own(self.behind_blocks, 1 + self.count)
        self.ahead = (ahead.astype(jnp.float32) + ahead_own).astype(jnp.bfloat16)
        self.behind = (behind.astype(jnp.float32) + behind_own).astype(jnp.bfloat16)
        return self.ahead, self.behind


def exchange(values, mask):
    return lax.ppermute(values, "seq", [(i, i ^ mask) for i in range(4)])


def gather_pair(block, *needed):
    other = exchange(after(block, *needed), 2)
    return other, exchange(jnp.stack([block, other]), 1)


def gather_seq(block, *needed):
    other, pair = gather_pair(block, *needed)
    return [block, other, pair[0], pair[1]]


def in_order(pieces, seq_index):
    high, low = seq_index // 2, seq_index % 2

    def pick(first, second, flag):
        return jnp.where(flag == 0, first, second), jnp.where(flag == 0, second, first)

    mine = pick(pieces[0], pieces[1], high)
    theirs = pick(pieces[2], pieces[3], high)
    return [*pick(mine[0], theirs[0], low), *pick(mine[1], theirs[1], low)]


def scatter_seq(here, there):
    came = exchange(there.astype(jnp.bfloat16), 1).astype(jnp.float32)
    total = here.astype(jnp.float32) + came
    rows = total.shape[0] // 2
    sent = total[rows:].astype(jnp.bfloat16)
    return total[:rows] + exchange(sent, 2).astype(jnp.float32), sent


def swap_rows(values, seq_index):
    rows = values.shape[0] // 4

    def block(mask):
        return lax.dynamic_slice_in_dim(values, (seq_index ^ mask) * rows, rows, 0)

    return [block(0), exchange(block(2), 2), exchange(block(1), 1), exchange(block(3), 3)]


def swap_columns(values, seq_index):
    columns = values.shape[1] // 4

    def block(mask):
        return lax.dynamic_slice_in_dim(values, (seq_index ^ mask) * columns, columns, 1)

    return [block(0), exchange(block(2), 2), exchange(block(1), 1), exchange(block(3), 3)]


def body(
    tokens,
    norm_gain,
    query_weight,
    key_weight,
    value_weight,
    query_gain,
    key_gain,
    out_weight,
    ffn_gain,
    gate_weight,
    up_weight,
    down_weight,
    cotangent,
):
    bf16, f32 = jnp.bfloat16, jnp.float32
    size = lax.axis_size("fsdp")
    seq_index = lax.axis_index("seq")
    place = ring_place(lax.axis_index("fsdp"), size)
    own_rows, width = query_weight.shape
    head_part = query_gain.shape[0]
    head_width = head_part * size
    query_columns = width // 4
    key_columns = key_weight.shape[1] // 4
    ff_part = down_weight.shape[0]
    window = -(-ff_part // 64) * 16

    def columns_of(weight, count):
        return lax.dynamic_slice_in_dim(weight, seq_index * count, count, 1)

    def hidden_rows(weight):
        tall = jnp.pad(weight, ((0, 4 * window - ff_part), (0, 0)))
        return lax.dynamic_slice_in_dim(tall, seq_index * window, window, 0)

    gains = jnp.concatenate([norm_gain, ffn_gain, query_gain, key_gain])
    gain_count = gains.shape[0]
    qkv_columns = query_columns + 2 * key_columns
    gain_rows = jnp.pad(gains[None], ((0, 15), (0, qkv_columns - gain_count)))
    packed = jnp.concatenate(
        [
            jnp.concatenate(
                [
                    columns_of(query_weight, query_columns),
                    columns_of(key_weight, key_columns),
                    columns_of(value_weight, key_columns),
                ],
                axis=1,
            ),
            gain_rows,
        ],
        axis=0,
    )
    top = split_rows(packed.shape[0])
    owners = ring_owners(size, place)
    out_part = lax.all_gather(columns_of(out_weight, query_columns), "fsdp", axis=0, tiled=True)
    qkv_ring = GatherRing(packed[:top], packed[top:], size)
    for _ in range(size - 1):
        qkv_ring.step()
    started = qkv_ring.ahead[max(size - 3, 0)]
    ffn_ring = GatherRing(
        *pick_hidden(gate_weight, up_weight, seq_index, size, ff_part, window), size
    )
    down_all = lax.all_gather(
        after(hidden_rows(down_weight), started, out_part), "fsdp", axis=0, tiled=True
    )
    for step in range(1, size):
        ffn_ring.step(*{1: (started,), size - 1: (down_all,)}.get(step, ()))

    top_all = lay_out(qkv_ring.ahead, owners[0])
    bottom_all = lay_out(qkv_ring.behind, owners[1])
    gains_all = bottom_all[:, own_rows - top].astype(f32)
    first_gain = gains_all[:, :own_rows].reshape(-1)
    second_gain = gains_all[:, own_rows : 2 * own_rows].reshape(-1)
    q_gain_f = gains_all[:, 2 * own_rows : 2 * own_rows + head_part].reshape(-1)
    k_gain_f = gains_all[:, 2 * own_rows + head_part : 2 * (own_rows + head_part)].reshape(-1)
    qkv_all = jnp.concatenate([top_all, bottom_all[:, : own_rows - top]], axis=1).reshape(
        width, qkv_columns
    )

    inputs = tokens[0]
    tok_rows = inputs.shape[0]
    length = 4 * tok_rows
    input_blocks = gather_seq(inputs)
    inputs_all = jnp.concatenate(in_order(input_blocks, seq_index), axis=0).astype(f32)
    out_all = jnp.concatenate(
        in_order(gather_seq(out_part, input_blocks[1]), seq_index), axis=1
    )

    normed, norm_unit, norm_inverse = norm_forward(inputs_all, first_gain)
    normed_low = normed.astype(bf16)
    qkv_t = lax.dot_general(
        qkv_all, normed_low, (((0,), (1,)), ((), ())), preferred_element_type=f32
    )
    sizes = (query_columns // head_width, key_columns // head_width, head_width)
    cosine, sine = rope_rows(length, head_width)
    tables = (q_gain_f[:, None], k_gain_f[:, None], cosine, sine)
    mixed_heads, mixed_t, totals = attention_forward(qkv_t, *tables, sizes)
    mixed = jnp.concatenate(in_order(swap_rows(mixed_heads, seq_index), seq_index), axis=1)
    attended = jnp.dot(mixed, out_all, preferred_element_type=f32)
    middle = inputs.astype(f32) + attended
    normed_two, middle_unit, middle_inverse = norm_forward(middle, second_gain)
    normed_blocks = gather_seq(normed_two.astype(bf16))
    normed_two_all = jnp.concatenate(normed_blocks, axis=0)
    out_grad = cotangent[0]
    grad_blocks = gather_seq(out_grad, normed_blocks[1])
    out_grad_all = jnp.concatenate(grad_blocks, axis=0)
    mixed_all = jnp.concatenate(
        in_order(gather_seq(mixed_heads, grad_blocks[1]), seq_index), axis=1
    )

    slope, silu, hidden, gate_all, up_all = ffn_hidden(
        normed_two_all, ffn_ring.ahead, ffn_ring.behind, owners
    )
    down_weight_grad = transpose_dot(hidden, out_grad_all).astype(bf16)
    down_share = lax.psum_scatter(down_weight_grad, "fsdp", scatter_dimension=0, tiled=True)
    gate_grad, up_grad, *normed_partials = ffn_hidden_grad(
        after(out_grad_all, down_weight_grad), down_all, slope, silu, gate_all, up_all
    )
    normed_two_grad, half_sum = scatter_seq(*normed_partials)
    gate_weight_grad = transpose_dot(normed_two_all, gate_grad).astype(bf16)
    up_weight_grad = transpose_dot(normed_two_all, up_grad).astype(bf16)
    grad_ring = ScatterRing(
        gate_weight_grad.reshape(size, own_rows, size * window),
        up_weight_grad.reshape(size, own_rows, size * window),
        size,
        place,
    )
    grad_ring.step(half_sum)
    ffn_gain_grad = jnp.sum(normed_two_grad * middle_unit, axis=0)
    middle_grad = out_grad.astype(f32) + norm_backward(
        normed_two_grad, middle_unit, middle_inverse, second_gain
    )
    attended_low = middle_grad.astype(bf16)
    mixed_grad = dot_transposed(attended_low, out_all).astype(bf16)
    grad_ring.step(mixed_grad)
    mixed_grad_blocks = swap_columns(mixed_grad, seq_index)
    mixed_grad_heads = jnp.concatenate(in_order(mixed_grad_blocks, seq_index), axis=0)
    down_partial = jnp.dot(
        after(hidden, mixed_grad), down_all, preferred_element_type=f32
    )
    down_sum, _ = scatter_seq(down_partial[: length // 2], down_partial[length // 2 :])
    output = middle + down_sum
    attended_columns = jnp.concatenate(
        in_order(swap_columns(after(attended_low, *mixed_grad_blocks), seq_index), seq_index), axis=0
    )
    qkv_grad_t, head_gains = attention_backward(
        qkv_t, *tables, mixed_t, totals, mixed_grad_heads, sizes
    )
    out_weight_grad = transpose_dot(mixed_all, after(attended_columns, qkv_grad_t))
    out_share = lax.psum_scatter(
        after(out_weight_grad.astype(bf16), down_share), "fsdp", scatter_dimension=0, tiled=True
    )
    grad_ring.step(qkv_grad_t)
    head_gains = jnp.sum(head_gains, axis=1)
    query_gain_grad, key_gain_grad = head_gains[:head_width], head_gains[head_width:]
    qkv_weight_grad = lax.dot_general(
        normed_low, qkv_grad_t, (((0,), (1,)), ((), ())), preferred_element_type=f32
    )
    normed_partial = lax.dot_general(
        qkv_grad_t, qkv_all, (((0,), (1,)), ((), ())), preferred_element_type=f32
    )
    norm_gain_grad = jnp.sum(normed_partial * norm_unit, axis=0)
    partial_blocks = normed_partial.astype(bf16).reshape(4, tok_rows, width)

    def partial_pair(first, second):
        return jnp.concatenate(
            [
                lax.dynamic_index_in_dim(partial_blocks, seq_index ^ mask, 0, keepdims=False)
                for mask in (first, second)
            ],
            axis=0,
        )

    normed_grad, _ = scatter_seq(partial_pair(0, 2), partial_pair(1, 3))
    _, own_unit, own_inverse = norm_forward(inputs.astype(f32), first_gain)
    inputs_grad = middle_grad + norm_backward(normed_grad, own_unit, own_inverse, first_gain)

    gain_grads = jnp.concatenate(
        [
            norm_gain_grad.reshape(size, -1),
            ffn_gain_grad.reshape(size, -1),
            query_gain_grad.reshape(size, -1),
            key_gain_grad.reshape(size, -1),
        ],
        axis=1,
    )
    gain_blocks = jnp.pad(gain_grads[:, None], ((0, 0), (0, 15), (0, qkv_columns - gain_count)))
    qkv_blocks = qkv_weight_grad.reshape(size, own_rows, qkv_columns)
    last_ring = ScatterRing(
        qkv_blocks[:, :top],
        jnp.concatenate([qkv_blocks[:, top:], gain_blocks], axis=1),
        size,
        place,
    )
    shares = last_ring.step()
    while grad_ring.count < size - 1:
        extra = (down_share,) if grad_ring.count == size - 3 else ()
        held = (grad_ring.ahead, grad_ring.behind)
        gate_share, up_share = grad_ring.step(*shares, *extra)
        shares = last_ring.step(*held)
    while last_ring.count < size - 1:
        shares = last_ring.step()
    packed_share = jnp.concatenate(shares, axis=0)

    down_full = jnp.concatenate(in_order(gather_seq(down_share), seq_index), axis=0)[
        :ff_part
    ].astype(f32)

    def full_columns(share):
        return spread_hidden(share, *gather_pair(share), seq_index, size, ff_part, window)

    gate_full = full_columns(gate_share)
    up_full = full_columns(up_share)
    out_full = jnp.concatenate(in_order(gather_seq(out_share), seq_index), axis=1).astype(f32)
    packs = in_order(gather_seq(packed_share), seq_index)

    def unpack(first, count):
        return jnp.concatenate(
            [p[:own_rows, first : first + count] for p in packs], axis=1
        ).astype(f32)

    gain_sum = sum(p[own_rows, :gain_count].astype(f32) for p in packs)
    return (
        output[None].astype(bf16),
        inputs_grad[None].astype(bf16),
        gain_sum[:own_rows],
        unpack(0, query_columns),
        unpack(query_columns, key_columns),
        unpack(query_columns + key_columns, key_columns),
        gain_sum[2 * own_rows : 2 * own_rows + head_part],
        gain_sum[2 * own_rows + head_part :],
        out_full,
        gain_sum[own_rows : 2 * own_rows],
        gate_full,
        up_full,
        down_full,
    )


def solution(mesh):
    in_specs = (
        P("fsdp", "seq", None),
        P("fsdp"),
        P("fsdp", None),
        P("fsdp", None),
        P("fsdp", None),
        P("fsdp"),
        P("fsdp"),
        P("fsdp", None),
        P("fsdp"),
        P("fsdp", None),
        P("fsdp", None),
        P("fsdp", None),
        P("fsdp", "seq", None),
    )
    out_specs = (
        P("fsdp", "seq", None),
        P("fsdp", "seq", None),
        P("fsdp"),
        P("fsdp", None),
        P("fsdp", None),
        P("fsdp", None),
        P("fsdp"),
        P("fsdp"),
        P("fsdp", None),
        P("fsdp"),
        P("fsdp", None),
        P("fsdp", None),
        P("fsdp", None),
    )
    return jax.shard_map(body, mesh=mesh, in_specs=in_specs, out_specs=out_specs, check_vma=False)
```

```python
import functools
import math

import jax
import jax.numpy as jnp
import numpy as np
from jax import lax
from jax.experimental import pallas as pl
from jax.experimental.pallas import tpu as pltpu
from jax.sharding import PartitionSpec as P

norm_epsilon = 1e-05
TILE = 256
log2_e = math.log2(math.e)


def rope_rows(length, width):
    half_width = width // 2
    inverse = jnp.exp(
        jnp.arange(half_width, dtype=jnp.float32) * (-2.0 * math.log(1000000.0) / width)
    )
    angles = inverse[:, None] * jnp.arange(length, dtype=jnp.int32).astype(jnp.float32)[None, :]
    return jnp.cos(angles), jnp.sin(angles)


def head_norm(values):
    inverse = lax.rsqrt(jnp.mean(values * values, axis=0, keepdims=True) + norm_epsilon)
    return values * inverse, inverse


def head_turn(values, cosine, sine):
    half = values.shape[0] // 2
    first, second = values[:half], values[half:]
    return jnp.concatenate(
        [first * cosine - second * sine, second * cosine + first * sine], axis=0
    )


def head_turn_back(values, cosine, sine):
    half = values.shape[0] // 2
    first, second = values[:half], values[half:]
    return jnp.concatenate(
        [first * cosine + second * sine, second * cosine - first * sine], axis=0
    )


def fill_heads(qkv_ref, q_gain_ref, k_gain_ref, cos_ref, sin_ref, queries, keys, keys_t, values, values_t, sizes):
    heads, groups, width = sizes
    cosine, sine = cos_ref[...], sin_ref[...]

    @pl.loop(0, heads)
    def _(head):
        unit, _ = head_norm(qkv_ref[pl.ds(head * width, width), :])
        turned = head_turn(unit * q_gain_ref[...], cosine, sine)
        queries[head] = (turned * (width**-0.5 * log2_e)).astype(jnp.bfloat16)

    @pl.loop(0, groups)
    def _(group):
        unit, _ = head_norm(qkv_ref[pl.ds((heads + group) * width, width), :])
        turned = head_turn(unit * k_gain_ref[...], cosine, sine)
        keys[group] = turned.T.astype(jnp.bfloat16)
        if keys_t is not None:
            keys_t[group] = turned.astype(jnp.bfloat16)
        value = qkv_ref[pl.ds((heads + groups + group) * width, width), :]
        if values is not None:
            values[group] = value.T.astype(jnp.bfloat16)
        if values_t is not None:
            values_t[group] = value.astype(jnp.bfloat16)


def diagonal_mask():
    key_place = lax.broadcasted_iota(jnp.int32, (TILE, TILE), 0)
    query_place = lax.broadcasted_iota(jnp.int32, (TILE, TILE), 1)
    return key_place <= query_place


def causal_exp(scores, count):
    weights = jnp.exp2(scores)
    last = jnp.where(diagonal_mask(), weights[count - TILE :], 0.0)
    if count == TILE:
        return last
    return jnp.concatenate([weights[: count - TILE], last], axis=0)


def dot(left, right):
    return jnp.dot(left, right, preferred_element_type=jnp.float32)


def dot_nt(left, right):
    return lax.dot_general(
        left, right, (((1,), (1,)), ((), ())), preferred_element_type=jnp.float32
    )


def forward_kernel(sizes, qkv_ref, q_gain_ref, k_gain_ref, cos_ref, sin_ref, mixed_ref, mixed_t_ref, total_ref, queries, keys, values_t, mixed_f):
    heads, groups, width = sizes
    ratio = heads // groups
    length = qkv_ref.shape[1]
    fill_heads(qkv_ref, q_gain_ref, k_gain_ref, cos_ref, sin_ref, queries, keys, None, None, values_t, sizes)

    @pl.loop(0, heads)
    def _(head):
        group = head // ratio
        for tile in range(length // TILE):
            count = (tile + 1) * TILE
            columns = pl.ds(tile * TILE, TILE)
            scores = dot(keys[group, pl.ds(0, count), :], queries[head, :, columns])
            weights = causal_exp(scores, count)
            total = jnp.sum(weights, axis=0, keepdims=True)
            result = dot(values_t[group, :, pl.ds(0, count)], weights.astype(jnp.bfloat16))
            mixed_f[pl.ds(head * width, width), columns] = result * (1.0 / total)
            total_ref[pl.ds(head, 1), columns] = jnp.log2(total)

    for block in range(heads * width // 128):
        rows = mixed_f[pl.ds(block * 128, 128), :]
        mixed_t_ref[pl.ds(block * 128, 128), :] = rows.astype(jnp.bfloat16)
        mixed_ref[:, pl.ds(block * 128, 128)] = rows.T.astype(jnp.bfloat16)


def backward_kernel(sizes, qkv_ref, q_gain_ref, k_gain_ref, cos_ref, sin_ref, mixed_t_ref, total_ref, grad_ref, out_ref, gain_ref, queries, keys, keys_t, values, grads, key_sum, value_sum):
    heads, groups, width = sizes
    ratio = heads // groups
    length = qkv_ref.shape[1]
    fill_heads(qkv_ref, q_gain_ref, k_gain_ref, cos_ref, sin_ref, queries, keys, keys_t, values, None, sizes)
    for block in range(heads * width // 128):
        turned = grad_ref[:, pl.ds(block * 128, 128)].astype(jnp.float32).T
        grads[pl.ds(block * 128, 128), :] = turned.astype(jnp.bfloat16)
    key_sum[...] = jnp.zeros_like(key_sum)
    value_sum[...] = jnp.zeros_like(value_sum)
    gain_ref[...] = jnp.zeros_like(gain_ref)
    cosine, sine = cos_ref[...], sin_ref[...]

    def finish(grad_turned, rows, gain, first):
        grad = head_turn_back(grad_turned, cosine, sine)
        unit, inverse = head_norm(qkv_ref[rows, :])
        product = grad * unit
        part = product[:, :128]
        for lane in range(128, length, 128):
            part = part + product[:, lane : lane + 128]
        gain_ref[pl.ds(first, width), :] += part
        scaled = grad * gain
        before = inverse * (scaled - unit * jnp.mean(scaled * unit, axis=0, keepdims=True))
        out_ref[rows, :] = before.astype(jnp.bfloat16)

    @pl.loop(0, heads)
    def _(head):
        group = head // ratio
        rows = pl.ds(head * width, width)
        query_parts = []
        for tile in range(length // TILE):
            count = (tile + 1) * TILE
            columns = pl.ds(tile * TILE, TILE)
            query = queries[head, :, columns]
            grad = grads[rows, columns]
            scores = dot(keys[group, pl.ds(0, count), :], query) - total_ref[pl.ds(head, 1), columns]
            weights = causal_exp(scores, count)
            inner = jnp.sum(
                grad.astype(jnp.float32) * mixed_t_ref[rows, columns].astype(jnp.float32),
                axis=0,
                keepdims=True,
            )
            weight_grad = dot(values[group, pl.ds(0, count), :], grad)
            score_grad = (weights * (weight_grad - inner)).astype(jnp.bfloat16)
            query_parts.append(dot(keys_t[group, :, pl.ds(0, count)], score_grad))
            key_sum[group, pl.ds(0, count), :] += dot_nt(score_grad, query)
            value_sum[group, pl.ds(0, count), :] += dot_nt(weights.astype(jnp.bfloat16), grad)
        query_grad = jnp.concatenate(query_parts, axis=1) * width**-0.5
        finish(query_grad, rows, q_gain_ref[...], 0)

    for group in range(groups):
        key_grad = key_sum[group].T * (1.0 / log2_e)
        finish(key_grad, pl.ds((heads + group) * width, width), k_gain_ref[...], width)
        out_ref[pl.ds((heads + groups + group) * width, width), :] = value_sum[group].T.astype(
            jnp.bfloat16
        )


def attention_forward(qkv_t, q_gain, k_gain, cosine, sine, sizes):
    heads, groups, width = sizes
    length = qkv_t.shape[1]
    bf16, f32 = jnp.bfloat16, jnp.float32
    pairs = heads * length * length
    return pl.pallas_call(
        functools.partial(forward_kernel, sizes),
        out_shape=(
            jax.ShapeDtypeStruct((length, heads * width), bf16),
            jax.ShapeDtypeStruct((heads * width, length), bf16),
            jax.ShapeDtypeStruct((-(-heads // 8) * 8, length), f32),
        ),
        scratch_shapes=[
            pltpu.VMEM((heads, width, length), bf16),
            pltpu.VMEM((groups, length, width), bf16),
            pltpu.VMEM((groups, width, length), bf16),
            pltpu.VMEM((heads * width, length), f32),
        ],
        compiler_params=pltpu.CompilerParams(vmem_limit_bytes=32 * 2**20),
        cost_estimate=pl.CostEstimate(
            flops=8 * pairs * width, bytes_accessed=6 * 2**20, transcendentals=pairs
        ),
    )(qkv_t, q_gain, k_gain, cosine, sine)


def attention_backward(qkv_t, q_gain, k_gain, cosine, sine, mixed_t, total, mixed_grad, sizes):
    heads, groups, width = sizes
    length = qkv_t.shape[1]
    bf16, f32 = jnp.bfloat16, jnp.float32
    pairs = heads * length * length
    return pl.pallas_call(
        functools.partial(backward_kernel, sizes),
        out_shape=(
            jax.ShapeDtypeStruct(qkv_t.shape, bf16),
            jax.ShapeDtypeStruct((2 * width, 128), f32),
        ),
        scratch_shapes=[
            pltpu.VMEM((heads, width, length), bf16),
            pltpu.VMEM((groups, length, width), bf16),
            pltpu.VMEM((groups, width, length), bf16),
            pltpu.VMEM((groups, length, width), bf16),
            pltpu.VMEM((heads * width, length), bf16),
            pltpu.VMEM((groups, length, width), f32),
            pltpu.VMEM((groups, length, width), f32),
        ],
        compiler_params=pltpu.CompilerParams(vmem_limit_bytes=40 * 2**20),
        cost_estimate=pl.CostEstimate(
            flops=20 * pairs * width, bytes_accessed=8 * 2**20, transcendentals=pairs
        ),
    )(qkv_t, q_gain, k_gain, cosine, sine, mixed_t, total, mixed_grad)


def hidden_kernel(size, ids_ref, rows_ref, *refs):
    chunks, refs = refs[: 2 * size], refs[2 * size :]
    slope_ref, silu_ref, hidden_ref, gate_out, up_out, gate, up, in_sems, out_sems = refs
    step = pl.program_id(0)
    steps = pl.num_programs(0)
    rows = chunks[0].shape[0]

    @pl.when(step == 0)
    def _():
        @pl.loop(0, steps)
        def _(tile):
            columns = pl.ds(pl.multiple_of(tile * TILE, TILE), TILE)
            for which, target in ((0, gate), (1, up)):
                for index in range(size):
                    first = pl.multiple_of(ids_ref[which, index] * rows, 16)
                    pltpu.make_async_copy(
                        chunks[which * size + index].at[:, columns],
                        target.at[pl.ds(first, rows), columns],
                        in_sems.at[which, tile],
                    ).start()

    columns = pl.ds(pl.multiple_of(step * TILE, TILE), TILE)
    for which, target, result in ((0, gate, gate_out), (1, up, up_out)):
        part = target.at[:, columns]
        pltpu.make_async_copy(part, part, in_sems.at[which, step]).wait()
        pltpu.make_async_copy(part, result.at[:, columns], out_sems.at[which, step]).start()
    for first in range(0, rows_ref.shape[0], TILE):
        some = pl.ds(first, TILE)
        gate_act = dot(rows_ref[some, :], gate[:, columns])
        up_act = dot(rows_ref[some, :], up[:, columns])
        sigmoid = 0.5 + 0.5 * jnp.tanh(0.5 * gate_act)
        silu = gate_act * sigmoid
        hidden_ref[some, :] = (silu * up_act).astype(hidden_ref.dtype)
        silu_ref[some, :] = silu.astype(silu_ref.dtype)
        slope_ref[some, :] = (up_act * sigmoid * (1.0 + gate_act * (1.0 - sigmoid))).astype(
            slope_ref.dtype
        )

    @pl.when(step == steps - 1)
    def _():
        @pl.loop(0, steps)
        def _(tile):
            columns = pl.ds(pl.multiple_of(tile * TILE, TILE), TILE)
            for which, target, result in ((0, gate, gate_out), (1, up, up_out)):
                pltpu.make_async_copy(
                    target.at[:, columns], result.at[:, columns], out_sems.at[which, tile]
                ).wait()


def ffn_hidden(rows, gate_chunks, up_chunks, ids):
    size = len(gate_chunks)
    part, columns = gate_chunks[0].shape
    length, width = rows.shape
    bf16 = jnp.bfloat16
    tall = pl.BlockSpec((length, TILE), lambda i, ids: (0, i))
    act = jax.ShapeDtypeStruct((length, columns), bf16)
    weight = jax.ShapeDtypeStruct((width, columns), bf16)
    anywhere = pl.BlockSpec(memory_space=pl.ANY)
    return pl.pallas_call(
        functools.partial(hidden_kernel, size),
        grid_spec=pltpu.PrefetchScalarGridSpec(
            num_scalar_prefetch=1,
            grid=(columns // TILE,),
            in_specs=[pl.BlockSpec((length, width), lambda i, ids: (0, 0))] + [anywhere] * (2 * size),
            out_specs=[tall, tall, tall, anywhere, anywhere],
            scratch_shapes=[
                pltpu.VMEM((width, columns), bf16),
                pltpu.VMEM((width, columns), bf16),
                pltpu.SemaphoreType.DMA((2, columns // TILE)),
                pltpu.SemaphoreType.DMA((2, columns // TILE)),
            ],
        ),
        out_shape=(act, act, act, weight, weight),
        compiler_params=pltpu.CompilerParams(vmem_limit_bytes=40 * 2**20),
        cost_estimate=pl.CostEstimate(
            flops=4 * length * width * columns,
            bytes_accessed=36 * 2**20,
            transcendentals=length * columns,
        ),
    )(ids, rows, *gate_chunks, *up_chunks)


def hidden_grad_kernel(size, owners_ref, grad_ref, slope_ref, silu_ref, *refs):
    chunks, refs = refs[: 2 * size], refs[2 * size :]
    gate_out, up_out, down_out, down, in_sems, out_sem = refs
    step = pl.program_id(0)
    rows = chunks[0].shape[0]

    @pl.when(step == 0)
    def _():
        copies = []
        for which in range(2):
            for index in range(size):
                first = pl.multiple_of((2 * owners_ref[which, index] + which) * rows, 16)
                copies.append(
                    pltpu.make_async_copy(
                        chunks[which * size + index],
                        down.at[pl.ds(first, rows), :],
                        in_sems.at[which, index],
                    )
                )
        for copy in copies:
            copy.start()
        for copy in copies:
            copy.wait()
        pltpu.make_async_copy(down, down_out, out_sem).start()

    weight = down[pl.ds(pl.multiple_of(step * TILE, TILE), TILE), :]
    for first in range(0, grad_ref.shape[0], TILE):
        some = pl.ds(first, TILE)
        hidden_grad = dot_nt(grad_ref[some, :], weight)
        gate_out[some, :] = (hidden_grad * slope_ref[some, :].astype(jnp.float32)).astype(
            jnp.bfloat16
        )
        up_out[some, :] = (hidden_grad * silu_ref[some, :].astype(jnp.float32)).astype(
            jnp.bfloat16
        )

    @pl.when(step == pl.num_programs(0) - 1)
    def _():
        pltpu.make_async_copy(down, down_out, out_sem).wait()


def ffn_hidden_grad(out_grad, slope, silu, ahead, behind, owners):
    size = len(ahead)
    length, width = out_grad.shape
    columns = slope.shape[1]
    bf16 = jnp.bfloat16
    tall = pl.BlockSpec((length, TILE), lambda i, owners: (0, i))
    anywhere = pl.BlockSpec(memory_space=pl.ANY)
    act = jax.ShapeDtypeStruct((length, columns), bf16)
    weight = (2 * size * ahead[0].shape[0], width)
    return pl.pallas_call(
        functools.partial(hidden_grad_kernel, size),
        grid_spec=pltpu.PrefetchScalarGridSpec(
            num_scalar_prefetch=1,
            grid=(columns // TILE,),
            in_specs=[pl.BlockSpec((length, width), lambda i, owners: (0, 0)), tall, tall]
            + [anywhere] * (2 * size),
            out_specs=[tall, tall, anywhere],
            scratch_shapes=[
                pltpu.VMEM(weight, bf16),
                pltpu.SemaphoreType.DMA((2, size)),
                pltpu.SemaphoreType.DMA,
            ],
        ),
        out_shape=(act, act, jax.ShapeDtypeStruct(weight, bf16)),
        compiler_params=pltpu.CompilerParams(vmem_limit_bytes=32 * 2**20),
        cost_estimate=pl.CostEstimate(
            flops=2 * length * width * columns, bytes_accessed=28 * 2**20, transcendentals=0
        ),
    )(owners, out_grad, slope, silu, *ahead, *behind)


def rows_grad_kernel(gate_grad_ref, up_grad_ref, gate_ref, up_ref, own_ref, sent_ref):
    half = own_ref.shape[0]
    for first in range(0, 2 * half, half):
        some = pl.ds(first, half)
        total = dot_nt(gate_grad_ref[some, :], gate_ref[...]) + dot_nt(
            up_grad_ref[some, :], up_ref[...]
        )
        target = sent_ref if first else own_ref
        target[...] = total.astype(target.dtype)


def ffn_rows_grad(gate_grad, up_grad, gate, up):
    length, columns = gate_grad.shape
    width = gate.shape[0]
    whole = pl.BlockSpec((length, columns), lambda i: (0, 0))
    weight = pl.BlockSpec((TILE, columns), lambda i: (i, 0))
    half = pl.BlockSpec((length // 2, TILE), lambda i: (0, i))
    part = jax.ShapeDtypeStruct((length // 2, width), jnp.bfloat16)
    return pl.pallas_call(
        rows_grad_kernel,
        grid=(width // TILE,),
        in_specs=[whole, whole, weight, weight],
        out_specs=[half, half],
        out_shape=(part, part),
        compiler_params=pltpu.CompilerParams(vmem_limit_bytes=40 * 2**20),
        cost_estimate=pl.CostEstimate(
            flops=4 * length * width * columns, bytes_accessed=22 * 2**20, transcendentals=0
        ),
    )(gate_grad, up_grad, gate, up)


def lay_kernel(size, sizes, owners_ref, *refs):
    chunks, refs = refs[: 2 * size], refs[2 * size :]
    qkv_out, out_out, gains_out, sems = refs
    rows, top, qkv_columns, columns = sizes
    copies = []
    for which, count in ((0, top), (1, rows - top)):
        for index in range(size):
            chunk = chunks[which * size + index]
            owner = owners_ref[which, index]
            first = pl.multiple_of(owner * rows + which * top, 16)
            target = pl.ds(first, count)
            pairs = [
                (chunk.at[pl.ds(0, count), pl.ds(0, qkv_columns)], qkv_out.at[target, :]),
                (
                    chunk.at[pl.ds(0, count), pl.ds(qkv_columns, columns - qkv_columns)],
                    out_out.at[target, :],
                ),
            ]
            if which:
                pairs.append((chunk.at[pl.ds(count, 16), :], gains_out.at[owner]))
            for kind, (source, place) in enumerate(pairs):
                copies.append(pltpu.make_async_copy(source, place, sems.at[kind, which, index]))
    for copy in copies:
        copy.start()
    for copy in copies:
        copy.wait()


def lay_attention(ahead, behind, owners, rows, qkv_columns):
    size = len(ahead)
    top, columns = ahead[0].shape
    bf16 = jnp.bfloat16
    anywhere = pl.BlockSpec(memory_space=pl.ANY)
    return pl.pallas_call(
        functools.partial(lay_kernel, size, (rows, top, qkv_columns, columns)),
        grid_spec=pltpu.PrefetchScalarGridSpec(
            num_scalar_prefetch=1,
            grid=(1,),
            in_specs=[anywhere] * (2 * size),
            out_specs=[anywhere] * 3,
            scratch_shapes=[pltpu.SemaphoreType.DMA((3, 2, size))],
        ),
        out_shape=(
            jax.ShapeDtypeStruct((size * rows, qkv_columns), bf16),
            jax.ShapeDtypeStruct((size * rows, columns - qkv_columns), bf16),
            jax.ShapeDtypeStruct((size, 16, columns), bf16),
        ),
        cost_estimate=pl.CostEstimate(flops=0, bytes_accessed=7 * 2**20, transcendentals=0),
    )(owners, *ahead, *behind)


def add_kernel(owners_ref, came_ref, block_ref, out_ref):
    out_ref[...] = (came_ref[...].astype(jnp.float32) + block_ref[0].astype(jnp.float32)).astype(
        out_ref.dtype
    )


def copy_kernel(owners_ref, block_ref, out_ref):
    out_ref[...] = block_ref[0].astype(out_ref.dtype)


def with_own(came, blocks, owners, where, scale=1, offset=0):
    _, rows, columns = blocks.shape
    part = columns // 2
    flat = pl.BlockSpec((rows, part), lambda i, owners: (0, i))
    own = pl.BlockSpec(
        (1, rows, part), lambda i, owners: (owners[where[0], where[1]] * scale + offset, 0, i)
    )
    values = (blocks,) if came is None else (came, blocks)
    return pl.pallas_call(
        copy_kernel if came is None else add_kernel,
        grid_spec=pltpu.PrefetchScalarGridSpec(
            num_scalar_prefetch=1,
            grid=(2,),
            in_specs=[own] if came is None else [flat, own],
            out_specs=flat,
        ),
        out_shape=jax.ShapeDtypeStruct((rows, columns), jnp.bfloat16),
        cost_estimate=pl.CostEstimate(
            flops=rows * columns, bytes_accessed=6 * rows * columns, transcendentals=0
        ),
    )(owners, *values)


def pick_kernel(sizes, index_ref, gate_ref, up_ref, gate_out, up_out):
    size, part, window = sizes
    rows = gate_ref.shape[0]
    for source, target in ((gate_ref, gate_out), (up_ref, up_out)):
        for index in range(4):
            count = min(window, part - index * window)

            @pl.when(index_ref[0] == index)
            def _():
                parts = []
                for owner in range(size):
                    first = owner * part + index * window
                    low, high = first // 128 * 128, -(-(first + count) // 128) * 128
                    wide = source[:, low:high].astype(jnp.float32)
                    parts.append(wide[:, first - low : first - low + count])
                    if count < window:
                        parts.append(jnp.zeros((rows, window - count), jnp.float32))
                target[...] = jnp.concatenate(parts, axis=1).astype(target.dtype)


def pick_hidden(gate, up, seq_index, size, part, window):
    rows, columns = gate.shape
    block = 48 if rows % 48 == 0 else rows
    wide = pl.BlockSpec((block, columns), lambda i, index: (i, 0))
    narrow = pl.BlockSpec((block, size * window), lambda i, index: (i, 0))
    out = jax.ShapeDtypeStruct((rows, size * window), gate.dtype)
    return pl.pallas_call(
        functools.partial(pick_kernel, (size, part, window)),
        grid_spec=pltpu.PrefetchScalarGridSpec(
            num_scalar_prefetch=1,
            grid=(rows // block,),
            in_specs=[wide, wide],
            out_specs=[narrow, narrow],
        ),
        out_shape=(out, out),
        compiler_params=pltpu.CompilerParams(vmem_limit_bytes=32 * 2**20),
        cost_estimate=pl.CostEstimate(flops=0, bytes_accessed=8 * 2**20, transcendentals=0),
    )(jnp.reshape(seq_index, (1,)).astype(jnp.int32), gate, up)


def spread_kernel(sizes, index_ref, own_ref, other_ref, near_ref, far_ref, out_ref, parts):
    size, part, window = sizes
    me = index_ref[0]
    parts[me] = own_ref[...]
    parts[me ^ 2] = other_ref[...]
    parts[me ^ 1] = near_ref[...]
    parts[me ^ 3] = far_ref[...]
    pieces = []
    for owner in range(size):
        for index in range(4):
            count = min(window, part - index * window)
            first = owner * window
            low, high = first // 128 * 128, -(-(first + count) // 128) * 128
            wide = parts[index, :, low:high].astype(jnp.float32)
            pieces.append(wide[:, first - low : first - low + count])
    out_ref[...] = jnp.concatenate(pieces, axis=1)


def spread_hidden(pieces, seq_index, size, part, window):
    rows, columns = pieces[0].shape
    block = 48 if rows % 48 == 0 else rows
    narrow = pl.BlockSpec((block, columns), lambda i, index: (i, 0))
    return pl.pallas_call(
        functools.partial(spread_kernel, (size, part, window)),
        grid_spec=pltpu.PrefetchScalarGridSpec(
            num_scalar_prefetch=1,
            grid=(rows // block,),
            in_specs=[narrow] * 4,
            out_specs=pl.BlockSpec((block, size * part), lambda i, index: (i, 0)),
            scratch_shapes=[pltpu.VMEM((4, block, columns), pieces[0].dtype)],
        ),
        out_shape=jax.ShapeDtypeStruct((rows, size * part), jnp.float32),
        compiler_params=pltpu.CompilerParams(vmem_limit_bytes=32 * 2**20),
        cost_estimate=pl.CostEstimate(flops=0, bytes_accessed=8 * 2**20, transcendentals=0),
    )(jnp.reshape(seq_index, (1,)), *pieces)


def norm_forward(values, gain):
    inverse = lax.rsqrt(jnp.mean(values * values, axis=-1, keepdims=True) + norm_epsilon)
    unit = values * inverse
    return (unit * gain, unit, inverse)


def norm_backward(grad_in, unit, inverse, gain):
    scaled = grad_in * gain
    return inverse * (scaled - unit * jnp.mean(scaled * unit, axis=-1, keepdims=True))


def transpose_dot(left, right):
    return lax.dot_general(
        left, right, (((0,), (0,)), ((), ())), preferred_element_type=jnp.float32
    )


def dot_transposed(left, right):
    return lax.dot_general(
        left, right, (((1,), (1,)), ((), ())), preferred_element_type=jnp.float32
    )


def split_rows(rows):
    return (rows // 32) * 16


def ring_ids(size):
    return list(range(0, size, 2)) + [i for i in range(size - 1, 0, -1) if i % 2]


def ring_perms(size):
    ids = ring_ids(size)
    forward = [(ids[i], ids[(i + 1) % size]) for i in range(size)]
    return forward, [(b, a) for a, b in forward]


def ring_owners(size):
    ids = ring_ids(size)
    table = np.zeros((size, 4, size), np.int32)
    for place, device in enumerate(ids):
        for step in range(size):
            table[device, 0, step] = ids[(place - step) % size]
            table[device, 1, step] = ids[(place + step) % size]
            table[device, 2, step] = ids[(place - 1 - step) % size]
            table[device, 3, step] = ids[(place + 1 + step) % size]
    return lax.dynamic_index_in_dim(
        jnp.asarray(table), lax.axis_index("fsdp").astype(jnp.uint32), 0, keepdims=False
    )


def after(value, *needed):
    return lax.optimization_barrier((value, *needed))[0] if needed else value


class GatherRing:
    def __init__(self, ahead, behind, size):
        self.perms = ring_perms(size)
        self.ahead, self.behind = [ahead], [behind]

    def step(self, *needed):
        forward, backward = self.perms
        self.ahead.append(lax.ppermute(after(self.ahead[-1], *needed), "fsdp", forward))
        self.behind.append(lax.ppermute(after(self.behind[-1], *needed), "fsdp", backward))


class ScatterRing:
    def __init__(self, ahead_blocks, behind_blocks, size, owners):
        self.perms = ring_perms(size)
        self.owners, self.count = owners, 0
        self.blocks = (ahead_blocks, behind_blocks)
        self.ahead, self.behind = self.own(0), self.own(1)

    def own(self, way, came=None):
        blocks, *place = self.blocks[way]
        return with_own(came, blocks, self.owners, (2 + way, self.count), *place)

    def step(self, *needed):
        forward, backward = self.perms
        ahead = lax.ppermute(self.ahead, "fsdp", forward)
        behind = lax.ppermute(self.behind, "fsdp", backward)
        self.count += 1
        self.ahead = self.own(0, after(ahead, *needed))
        self.behind = self.own(1, after(behind, *needed))


def exchange(values, mask):
    return lax.ppermute(values, "seq", [(i, i ^ mask) for i in range(4)])


def gather_seq(block, *needed):
    block = after(block, *needed)
    other = exchange(block, 2)
    return [block, other, exchange(block, 1), exchange(other, 1)]


def in_order(pieces, seq_index):
    high, low = seq_index // 2, seq_index % 2

    def pick(first, second, flag):
        return jnp.where(flag == 0, first, second), jnp.where(flag == 0, second, first)

    mine = pick(pieces[0], pieces[1], high)
    theirs = pick(pieces[2], pieces[3], high)
    return [*pick(mine[0], theirs[0], low), *pick(mine[1], theirs[1], low)]


def scatter_seq(here, there):
    came = exchange(there.astype(jnp.bfloat16), 1).astype(jnp.float32)
    total = here.astype(jnp.float32) + came
    rows = total.shape[0] // 2
    sent = total[rows:].astype(jnp.bfloat16)
    return total[:rows] + exchange(sent, 2).astype(jnp.float32), sent


def swap_rows(values, seq_index):
    rows = values.shape[0] // 4

    def block(mask):
        return lax.dynamic_slice_in_dim(values, (seq_index ^ mask).astype(jnp.uint32) * rows, rows, 0)

    return [block(0), exchange(block(2), 2), exchange(block(1), 1), exchange(block(3), 3)]


def swap_columns(values, seq_index):
    columns = values.shape[1] // 4

    def block(mask):
        return lax.dynamic_slice_in_dim(values, (seq_index ^ mask).astype(jnp.uint32) * columns, columns, 1)

    return [block(0), exchange(block(2), 2), exchange(block(1), 1), exchange(block(3), 3)]


def body(
    tokens,
    norm_gain,
    query_weight,
    key_weight,
    value_weight,
    query_gain,
    key_gain,
    out_weight,
    ffn_gain,
    gate_weight,
    up_weight,
    down_weight,
    cotangent,
):
    bf16, f32 = jnp.bfloat16, jnp.float32
    size = lax.axis_size("fsdp")
    seq_index = lax.axis_index("seq")
    owners = ring_owners(size)
    own_rows, width = query_weight.shape
    head_part = query_gain.shape[0]
    head_width = head_part * size
    query_columns = width // 4
    key_columns = key_weight.shape[1] // 4
    ff_part = down_weight.shape[0]
    window = -(-ff_part // 64) * 16

    def columns_of(weight, count):
        return lax.dynamic_slice_in_dim(weight, seq_index.astype(jnp.uint32) * count, count, 1)

    def hidden_rows(weight):
        tall = jnp.pad(weight, ((0, 4 * window - ff_part), (0, 0)))
        return lax.dynamic_slice_in_dim(tall, seq_index.astype(jnp.uint32) * window, window, 0)

    gains = jnp.concatenate([norm_gain, ffn_gain, query_gain, key_gain])
    gain_count = gains.shape[0]
    qkv_columns = query_columns + 2 * key_columns
    packed_columns = qkv_columns + query_columns
    gain_rows = jnp.pad(gains[None], ((0, 15), (0, packed_columns - gain_count)))
    packed = jnp.concatenate(
        [
            columns_of(query_weight, query_columns),
            columns_of(key_weight, key_columns),
            columns_of(value_weight, key_columns),
            columns_of(out_weight, query_columns),
        ],
        axis=1,
    )
    top = split_rows(own_rows + 16)
    first_ring = GatherRing(
        packed[:top], jnp.concatenate([packed[top:], gain_rows], axis=0), size
    )
    for _ in range(size - 1):
        first_ring.step()
    started = first_ring.ahead[max(size - 3, 0)]
    ffn_ring = GatherRing(
        *pick_hidden(gate_weight, up_weight, seq_index, size, ff_part, window), size
    )
    down_rows = hidden_rows(down_weight)
    down_ring = GatherRing(down_rows[: window // 2], down_rows[window // 2 :], size)
    for step in range(1, size):
        ffn_ring.step(*((started,) if step == 1 else ()))
    for step in range(1, size):
        lag = min(step + 2, size - 1)
        down_ring.step(ffn_ring.ahead[lag], ffn_ring.behind[lag])

    qkv_all, out_part, gains_all = lay_attention(
        first_ring.ahead, first_ring.behind, owners, own_rows, qkv_columns
    )
    gains_all = gains_all[:, 0].astype(f32)
    first_gain = gains_all[:, :own_rows].reshape(-1)
    second_gain = gains_all[:, own_rows : 2 * own_rows].reshape(-1)
    q_gain_f = gains_all[:, 2 * own_rows : 2 * own_rows + head_part].reshape(-1)
    k_gain_f = gains_all[:, 2 * own_rows + head_part : 2 * (own_rows + head_part)].reshape(-1)

    inputs = tokens[0]
    tok_rows = inputs.shape[0]
    length = 4 * tok_rows
    input_blocks = gather_seq(inputs)
    inputs_all = jnp.concatenate(in_order(input_blocks, seq_index), axis=0).astype(f32)
    out_all = jnp.concatenate(
        in_order(gather_seq(out_part, input_blocks[1]), seq_index), axis=1
    )

    normed, norm_unit, norm_inverse = norm_forward(inputs_all, first_gain)
    normed_low = normed.astype(bf16)
    qkv_t = lax.dot_general(
        qkv_all, normed_low, (((0,), (1,)), ((), ())), preferred_element_type=f32
    )
    sizes = (query_columns // head_width, key_columns // head_width, head_width)
    cosine, sine = rope_rows(length, head_width)
    tables = (q_gain_f[:, None], k_gain_f[:, None], cosine, sine)
    mixed_heads, mixed_t, totals = attention_forward(qkv_t, *tables, sizes)
    mixed = jnp.concatenate(in_order(swap_rows(mixed_heads, seq_index), seq_index), axis=1)
    attended = jnp.dot(mixed, out_all, preferred_element_type=f32)
    middle = inputs.astype(f32) + attended
    normed_two, middle_unit, middle_inverse = norm_forward(middle, second_gain)
    normed_blocks = gather_seq(normed_two.astype(bf16))
    normed_two_all = jnp.concatenate(normed_blocks, axis=0)
    out_grad = cotangent[0]
    grad_blocks = gather_seq(out_grad, normed_blocks[1])
    out_grad_all = jnp.concatenate(grad_blocks, axis=0)
    mixed_all = jnp.concatenate(
        in_order(gather_seq(mixed_heads, grad_blocks[1]), seq_index), axis=1
    )

    slope, silu, hidden, gate_all, up_all = ffn_hidden(
        normed_two_all, ffn_ring.ahead, ffn_ring.behind, owners
    )
    down_weight_grad = transpose_dot(hidden, out_grad_all).astype(bf16)
    down_blocks = down_weight_grad.reshape(2 * size, window // 2, width)
    down_sums = ScatterRing((down_blocks, 2, 0), (down_blocks, 2, 1), size, owners)
    gate_grad, up_grad, down_all = ffn_hidden_grad(
        after(out_grad_all, down_weight_grad), slope, silu, down_ring.ahead, down_ring.behind, owners
    )
    down_sums.step(gate_grad)
    normed_partials = ffn_rows_grad(gate_grad, up_grad, gate_all, up_all)
    normed_two_grad, half_sum = scatter_seq(*normed_partials)
    down_sums.step(normed_partials[0])
    gate_weight_grad = transpose_dot(
        after(normed_two_all, normed_partials[0]), gate_grad
    ).astype(bf16)
    up_weight_grad = transpose_dot(
        after(normed_two_all, gate_weight_grad), up_grad
    ).astype(bf16)
    down_sums.step(up_weight_grad)
    ffn_sums = ScatterRing(
        (gate_weight_grad.reshape(size, own_rows, size * window),),
        (up_weight_grad.reshape(size, own_rows, size * window),),
        size,
        owners,
    )
    ffn_gain_grad = jnp.sum(normed_two_grad * middle_unit, axis=0)
    middle_grad = out_grad.astype(f32) + norm_backward(
        normed_two_grad, middle_unit, middle_inverse, second_gain
    )
    attended_low = middle_grad.astype(bf16)
    mixed_grad = dot_transposed(attended_low, out_all).astype(bf16)
    ffn_sums.step(mixed_grad)
    down_sums.step(mixed_grad)
    mixed_grad_blocks = swap_columns(mixed_grad, seq_index)
    mixed_grad_heads = jnp.concatenate(in_order(mixed_grad_blocks, seq_index), axis=0)
    down_partial = jnp.dot(
        after(hidden, mixed_grad), down_all, preferred_element_type=f32
    )
    down_sum, _ = scatter_seq(down_partial[: length // 2], down_partial[length // 2 :])
    output = middle + down_sum
    attended_columns = jnp.concatenate(
        in_order(swap_columns(after(attended_low, *mixed_grad_blocks), seq_index), seq_index), axis=0
    )
    qkv_grad_t, head_gains = attention_backward(
        qkv_t, *tables, mixed_t, totals, mixed_grad_heads, sizes
    )
    out_weight_grad = transpose_dot(mixed_all, after(attended_columns, qkv_grad_t))
    ffn_sums.step(qkv_grad_t)
    down_sums.step(qkv_grad_t)
    head_gains = jnp.sum(head_gains, axis=1)
    query_gain_grad, key_gain_grad = head_gains[:head_width], head_gains[head_width:]
    qkv_weight_grad = lax.dot_general(
        normed_low, qkv_grad_t, (((0,), (1,)), ((), ())), preferred_element_type=f32
    )
    normed_partial = lax.dot_general(
        qkv_grad_t, qkv_all, (((0,), (1,)), ((), ())), preferred_element_type=f32
    )
    norm_gain_grad = jnp.sum(normed_partial * norm_unit, axis=0)
    partial_blocks = normed_partial.astype(bf16).reshape(4, tok_rows, width)

    def partial_pair(first, second):
        return jnp.concatenate(
            [
                lax.dynamic_index_in_dim(partial_blocks, (seq_index ^ mask).astype(jnp.uint32), 0, keepdims=False)
                for mask in (first, second)
            ],
            axis=0,
        )

    normed_grad, _ = scatter_seq(partial_pair(0, 2), partial_pair(1, 3))
    _, own_unit, own_inverse = norm_forward(inputs.astype(f32), first_gain)
    inputs_grad = middle_grad + norm_backward(normed_grad, own_unit, own_inverse, first_gain)

    gain_grads = jnp.concatenate(
        [
            norm_gain_grad.reshape(size, -1),
            ffn_gain_grad.reshape(size, -1),
            query_gain_grad.reshape(size, -1),
            key_gain_grad.reshape(size, -1),
        ],
        axis=1,
    )
    gain_blocks = jnp.pad(
        gain_grads[:, None], ((0, 0), (0, 15), (0, packed_columns - gain_count))
    )
    packed_blocks = jnp.concatenate([qkv_weight_grad, out_weight_grad], axis=1).reshape(
        size, own_rows, packed_columns
    )
    top_blocks = packed_blocks[:, :top].astype(bf16)
    bottom_blocks = jnp.concatenate([packed_blocks[:, top:], gain_blocks], axis=1).astype(bf16)
    ffn_sums.step(top_blocks, bottom_blocks)
    down_sums.step(top_blocks, bottom_blocks)
    last_sums = ScatterRing((top_blocks,), (bottom_blocks,), size, owners)
    while ffn_sums.count < size - 1:
        ffn_sums.step()
        last_sums.step(ffn_sums.ahead, ffn_sums.behind)
        if down_sums.count < size - 1:
            down_sums.step()
    while last_sums.count < size - 1:
        last_sums.step()
    packed_share = jnp.concatenate([last_sums.ahead, last_sums.behind], axis=0)

    down_parts = [in_order(gather_seq(half), seq_index) for half in (down_sums.ahead, down_sums.behind)]
    down_full = jnp.concatenate(
        [half for pair in zip(*down_parts) for half in pair], axis=0
    )[:ff_part].astype(f32)

    gate_full, up_full = (
        spread_hidden(gather_seq(share), seq_index, size, ff_part, window)
        for share in (ffn_sums.ahead, ffn_sums.behind)
    )
    packs = in_order(gather_seq(packed_share), seq_index)

    def unpack(first, count):
        return jnp.concatenate(
            [p[:own_rows, first : first + count] for p in packs], axis=1
        ).astype(f32)

    gain_sum = sum(p[own_rows, :gain_count].astype(f32) for p in packs)
    return (
        output[None].astype(bf16),
        inputs_grad[None].astype(bf16),
        gain_sum[:own_rows],
        unpack(0, query_columns),
        unpack(query_columns, key_columns),
        unpack(query_columns + key_columns, key_columns),
        gain_sum[2 * own_rows : 2 * own_rows + head_part],
        gain_sum[2 * own_rows + head_part :],
        unpack(qkv_columns, query_columns),
        gain_sum[own_rows : 2 * own_rows],
        gate_full,
        up_full,
        down_full,
    )


def solution(mesh):
    in_specs = (
        P("fsdp", "seq", None),
        P("fsdp"),
        P("fsdp", None),
        P("fsdp", None),
        P("fsdp", None),
        P("fsdp"),
        P("fsdp"),
        P("fsdp", None),
        P("fsdp"),
        P("fsdp", None),
        P("fsdp", None),
        P("fsdp", None),
        P("fsdp", "seq", None),
    )
    out_specs = (
        P("fsdp", "seq", None),
        P("fsdp", "seq", None),
        P("fsdp"),
        P("fsdp", None),
        P("fsdp", None),
        P("fsdp", None),
        P("fsdp"),
        P("fsdp"),
        P("fsdp", None),
        P("fsdp"),
        P("fsdp", None),
        P("fsdp", None),
        P("fsdp", None),
    )
    return jax.shard_map(body, mesh=mesh, in_specs=in_specs, out_specs=out_specs, check_vma=False)
```

```python
import functools
import math

import jax
import jax.numpy as jnp
import numpy as np
from jax import lax
from jax.experimental import pallas as pl
from jax.experimental.pallas import tpu as pltpu
from jax.sharding import PartitionSpec as P

norm_epsilon = 1e-05
TILE = 256
log2_e = math.log2(math.e)


def rope_rows(length, width):
    half_width = width // 2
    inverse = jnp.exp(
        jnp.arange(half_width, dtype=jnp.float32) * (-2.0 * math.log(1000000.0) / width)
    )
    angles = inverse[:, None] * jnp.arange(length, dtype=jnp.int32).astype(jnp.float32)[None, :]
    return jnp.cos(angles), jnp.sin(angles)


def head_norm(values):
    inverse = lax.rsqrt(jnp.mean(values * values, axis=0, keepdims=True) + norm_epsilon)
    return values * inverse, inverse


def head_turn(values, cosine, sine):
    half = values.shape[0] // 2
    first, second = values[:half], values[half:]
    return jnp.concatenate(
        [first * cosine - second * sine, second * cosine + first * sine], axis=0
    )


def head_turn_back(values, cosine, sine):
    half = values.shape[0] // 2
    first, second = values[:half], values[half:]
    return jnp.concatenate(
        [first * cosine + second * sine, second * cosine - first * sine], axis=0
    )


def fill_heads(qkv_ref, q_gain_ref, k_gain_ref, cos_ref, sin_ref, queries, keys, keys_t, values, values_t, sizes):
    heads, groups, width = sizes
    cosine, sine = cos_ref[...], sin_ref[...]

    @pl.loop(0, heads)
    def _(head):
        unit, _ = head_norm(qkv_ref[pl.ds(head * width, width), :])
        turned = head_turn(unit * q_gain_ref[...], cosine, sine)
        queries[head] = (turned * (width**-0.5 * log2_e)).astype(jnp.bfloat16)

    @pl.loop(0, groups)
    def _(group):
        unit, _ = head_norm(qkv_ref[pl.ds((heads + group) * width, width), :])
        turned = head_turn(unit * k_gain_ref[...], cosine, sine)
        keys[group] = turned.T.astype(jnp.bfloat16)
        if keys_t is not None:
            keys_t[group] = turned.astype(jnp.bfloat16)
        value = qkv_ref[pl.ds((heads + groups + group) * width, width), :]
        if values is not None:
            values[group] = value.T.astype(jnp.bfloat16)
        if values_t is not None:
            values_t[group] = value.astype(jnp.bfloat16)


def diagonal_mask():
    key_place = lax.broadcasted_iota(jnp.int32, (TILE, TILE), 0)
    query_place = lax.broadcasted_iota(jnp.int32, (TILE, TILE), 1)
    return key_place <= query_place


def causal_exp(scores, count):
    weights = jnp.exp2(scores)
    last = jnp.where(diagonal_mask(), weights[count - TILE :], 0.0)
    if count == TILE:
        return last
    return jnp.concatenate([weights[: count - TILE], last], axis=0)


def dot(left, right):
    return jnp.dot(left, right, preferred_element_type=jnp.float32)


def dot_nt(left, right):
    return lax.dot_general(
        left, right, (((1,), (1,)), ((), ())), preferred_element_type=jnp.float32
    )


def forward_kernel(sizes, qkv_ref, q_gain_ref, k_gain_ref, cos_ref, sin_ref, mixed_ref, mixed_t_ref, total_ref, queries, keys, values_t, mixed_f):
    heads, groups, width = sizes
    ratio = heads // groups
    length = qkv_ref.shape[1]
    fill_heads(qkv_ref, q_gain_ref, k_gain_ref, cos_ref, sin_ref, queries, keys, None, None, values_t, sizes)

    @pl.loop(0, heads)
    def _(head):
        group = head // ratio
        for tile in range(length // TILE):
            count = (tile + 1) * TILE
            columns = pl.ds(tile * TILE, TILE)
            scores = dot(keys[group, pl.ds(0, count), :], queries[head, :, columns])
            weights = causal_exp(scores, count)
            total = jnp.sum(weights, axis=0, keepdims=True)
            result = dot(values_t[group, :, pl.ds(0, count)], weights.astype(jnp.bfloat16))
            mixed_f[pl.ds(head * width, width), columns] = result * (1.0 / total)
            total_ref[pl.ds(head, 1), columns] = jnp.log2(total)

    for block in range(heads * width // 128):
        rows = mixed_f[pl.ds(block * 128, 128), :]
        mixed_t_ref[pl.ds(block * 128, 128), :] = rows.astype(jnp.bfloat16)
        mixed_ref[:, pl.ds(block * 128, 128)] = rows.T.astype(jnp.bfloat16)


def backward_kernel(sizes, qkv_ref, q_gain_ref, k_gain_ref, cos_ref, sin_ref, mixed_t_ref, total_ref, grad_ref, out_ref, gain_ref, out_t, queries, keys, keys_t, values, grads, key_sum, value_sum):
    heads, groups, width = sizes
    ratio = heads // groups
    length = qkv_ref.shape[1]
    fill_heads(qkv_ref, q_gain_ref, k_gain_ref, cos_ref, sin_ref, queries, keys, keys_t, values, None, sizes)
    for block in range(heads * width // 128):
        turned = grad_ref[:, pl.ds(block * 128, 128)].astype(jnp.float32).T
        grads[pl.ds(block * 128, 128), :] = turned.astype(jnp.bfloat16)
    key_sum[...] = jnp.zeros_like(key_sum)
    value_sum[...] = jnp.zeros_like(value_sum)
    gain_ref[...] = jnp.zeros_like(gain_ref)
    cosine, sine = cos_ref[...], sin_ref[...]

    def finish(grad_turned, rows, gain, first):
        grad = head_turn_back(grad_turned, cosine, sine)
        unit, inverse = head_norm(qkv_ref[rows, :])
        product = grad * unit
        part = product[:, :128]
        for lane in range(128, length, 128):
            part = part + product[:, lane : lane + 128]
        gain_ref[pl.ds(first, width), :] += part
        scaled = grad * gain
        before = inverse * (scaled - unit * jnp.mean(scaled * unit, axis=0, keepdims=True))
        out_t[rows, :] = before

    @pl.loop(0, heads)
    def _(head):
        group = head // ratio
        rows = pl.ds(head * width, width)
        query_parts = []
        for tile in range(length // TILE):
            count = (tile + 1) * TILE
            columns = pl.ds(tile * TILE, TILE)
            query = queries[head, :, columns]
            grad = grads[rows, columns]
            scores = dot(keys[group, pl.ds(0, count), :], query) - total_ref[pl.ds(head, 1), columns]
            weights = causal_exp(scores, count)
            inner = jnp.sum(
                grad.astype(jnp.float32) * mixed_t_ref[rows, columns].astype(jnp.float32),
                axis=0,
                keepdims=True,
            )
            weight_grad = dot(values[group, pl.ds(0, count), :], grad)
            score_grad = (weights * (weight_grad - inner)).astype(jnp.bfloat16)
            query_parts.append(dot(keys_t[group, :, pl.ds(0, count)], score_grad))
            key_sum[group, pl.ds(0, count), :] += dot_nt(score_grad, query)
            value_sum[group, pl.ds(0, count), :] += dot_nt(weights.astype(jnp.bfloat16), grad)
        query_grad = jnp.concatenate(query_parts, axis=1) * width**-0.5
        finish(query_grad, rows, q_gain_ref[...], 0)

    for group in range(groups):
        key_grad = key_sum[group].T * (1.0 / log2_e)
        finish(key_grad, pl.ds((heads + group) * width, width), k_gain_ref[...], width)
        out_t[pl.ds((heads + groups + group) * width, width), :] = value_sum[group].T

    for block in range(out_t.shape[0] // 128):
        some = pl.ds(block * 128, 128)
        out_ref[:, some] = out_t[some, :].T.astype(jnp.bfloat16)


def attention_forward(qkv_t, q_gain, k_gain, cosine, sine, sizes):
    heads, groups, width = sizes
    length = qkv_t.shape[1]
    bf16, f32 = jnp.bfloat16, jnp.float32
    pairs = heads * length * length
    return pl.pallas_call(
        functools.partial(forward_kernel, sizes),
        out_shape=(
            jax.ShapeDtypeStruct((length, heads * width), bf16),
            jax.ShapeDtypeStruct((heads * width, length), bf16),
            jax.ShapeDtypeStruct((-(-heads // 8) * 8, length), f32),
        ),
        scratch_shapes=[
            pltpu.VMEM((heads, width, length), bf16),
            pltpu.VMEM((groups, length, width), bf16),
            pltpu.VMEM((groups, width, length), bf16),
            pltpu.VMEM((heads * width, length), f32),
        ],
        compiler_params=pltpu.CompilerParams(vmem_limit_bytes=32 * 2**20),
        cost_estimate=pl.CostEstimate(
            flops=8 * pairs * width, bytes_accessed=6 * 2**20, transcendentals=pairs
        ),
    )(qkv_t, q_gain, k_gain, cosine, sine)


def attention_backward(qkv_t, q_gain, k_gain, cosine, sine, mixed_t, total, mixed_grad, sizes):
    heads, groups, width = sizes
    length = qkv_t.shape[1]
    bf16, f32 = jnp.bfloat16, jnp.float32
    pairs = heads * length * length
    return pl.pallas_call(
        functools.partial(backward_kernel, sizes),
        out_shape=(
            jax.ShapeDtypeStruct(qkv_t.shape[::-1], bf16),
            jax.ShapeDtypeStruct((2 * width, 128), f32),
        ),
        scratch_shapes=[
            pltpu.VMEM(qkv_t.shape, f32),
            pltpu.VMEM((heads, width, length), bf16),
            pltpu.VMEM((groups, length, width), bf16),
            pltpu.VMEM((groups, width, length), bf16),
            pltpu.VMEM((groups, length, width), bf16),
            pltpu.VMEM((heads * width, length), bf16),
            pltpu.VMEM((groups, length, width), f32),
            pltpu.VMEM((groups, length, width), f32),
        ],
        compiler_params=pltpu.CompilerParams(vmem_limit_bytes=40 * 2**20),
        cost_estimate=pl.CostEstimate(
            flops=20 * pairs * width, bytes_accessed=8 * 2**20, transcendentals=pairs
        ),
    )(qkv_t, q_gain, k_gain, cosine, sine, mixed_t, total, mixed_grad)


def hidden_kernel(size, ids_ref, *refs):
    pieces, chunks, refs = refs[:4], refs[4 : 4 + 2 * size], refs[4 + 2 * size :]
    slope_ref, silu_ref, hidden_ref, gate_out, up_out, gate, up, in_sems, out_sems = refs
    step = pl.program_id(0)
    steps = pl.num_programs(0)
    rows = chunks[0].shape[0]

    @pl.when(step == 0)
    def _():
        @pl.loop(0, steps)
        def _(tile):
            columns = pl.ds(pl.multiple_of(tile * TILE, TILE), TILE)
            for which, target in ((0, gate), (1, up)):
                for index in range(size):
                    first = pl.multiple_of(ids_ref[which, index] * rows, 16)
                    pltpu.make_async_copy(
                        chunks[which * size + index].at[:, columns],
                        target.at[pl.ds(first, rows), columns],
                        in_sems.at[which, tile],
                    ).start()

    columns = pl.ds(pl.multiple_of(step * TILE, TILE), TILE)
    for which, target, result in ((0, gate, gate_out), (1, up, up_out)):
        part = target.at[:, columns]
        pltpu.make_async_copy(part, part, in_sems.at[which, step]).wait()
        pltpu.make_async_copy(part, result.at[:, columns], out_sems.at[which, step]).start()
    for index, piece in enumerate(pieces):
        some = pl.ds(index * piece.shape[0], piece.shape[0])
        gate_act = dot(piece[...], gate[:, columns])
        up_act = dot(piece[...], up[:, columns])
        sigmoid = 0.5 + 0.5 * jnp.tanh(0.5 * gate_act)
        silu = gate_act * sigmoid
        hidden_ref[some, :] = (silu * up_act).astype(hidden_ref.dtype)
        silu_ref[some, :] = silu.astype(silu_ref.dtype)
        slope_ref[some, :] = (up_act * sigmoid * (1.0 + gate_act * (1.0 - sigmoid))).astype(
            slope_ref.dtype
        )

    @pl.when(step == steps - 1)
    def _():
        @pl.loop(0, steps)
        def _(tile):
            columns = pl.ds(pl.multiple_of(tile * TILE, TILE), TILE)
            for which, target, result in ((0, gate, gate_out), (1, up, up_out)):
                pltpu.make_async_copy(
                    target.at[:, columns], result.at[:, columns], out_sems.at[which, tile]
                ).wait()


def ffn_hidden(pieces, gate_chunks, up_chunks, ids):
    size = len(gate_chunks)
    part, columns = gate_chunks[0].shape
    piece, width = pieces[0].shape
    length = 4 * piece
    bf16 = jnp.bfloat16
    tall = pl.BlockSpec((length, TILE), lambda i, ids: (0, i))
    act = jax.ShapeDtypeStruct((length, columns), bf16)
    weight = jax.ShapeDtypeStruct((width, columns), bf16)
    anywhere = pl.BlockSpec(memory_space=pl.ANY)
    return pl.pallas_call(
        functools.partial(hidden_kernel, size),
        grid_spec=pltpu.PrefetchScalarGridSpec(
            num_scalar_prefetch=1,
            grid=(columns // TILE,),
            in_specs=[pl.BlockSpec((piece, width), lambda i, ids: (0, 0))] * 4
            + [anywhere] * (2 * size),
            out_specs=[tall, tall, tall, anywhere, anywhere],
            scratch_shapes=[
                pltpu.VMEM((width, columns), bf16),
                pltpu.VMEM((width, columns), bf16),
                pltpu.SemaphoreType.DMA((2, columns // TILE)),
                pltpu.SemaphoreType.DMA((2, columns // TILE)),
            ],
        ),
        out_shape=(act, act, act, weight, weight),
        compiler_params=pltpu.CompilerParams(vmem_limit_bytes=56 * 2**20),
        cost_estimate=pl.CostEstimate(
            flops=4 * length * width * columns,
            bytes_accessed=36 * 2**20,
            transcendentals=length * columns,
        ),
    )(ids, *pieces, *gate_chunks, *up_chunks)


def hidden_grad_kernel(size, steps, owners_ref, *refs):
    pieces, refs = refs[:4], refs[4:]
    slope_ref, silu_ref, gate_ref, up_ref = refs[:4]
    chunks, refs = refs[4 : 4 + 2 * size], refs[4 + 2 * size :]
    gate_out, up_out, own_ref, other_ref, sent_ref, down_out = refs[:6]
    down, gate_grads, up_grads, in_sems, out_sem = refs[6:]
    step = pl.program_id(0)
    rows = chunks[0].shape[0]
    piece_rows = pieces[0].shape[0]

    @pl.when(step == 0)
    def _():
        copies = []
        for which in range(2):
            for index in range(size):
                first = pl.multiple_of((2 * owners_ref[which, index] + which) * rows, 16)
                copies.append(
                    pltpu.make_async_copy(
                        chunks[which * size + index],
                        down.at[pl.ds(first, rows), :],
                        in_sems.at[which, index],
                    )
                )
        for copy in copies:
            copy.start()
        for copy in copies:
            copy.wait()
        pltpu.make_async_copy(down, down_out, out_sem).start()

    @pl.when(step < steps)
    def _():
        columns = pl.ds(pl.multiple_of(step * TILE, TILE), TILE)
        weight = down[columns, :]
        for index, piece in enumerate(pieces):
            some = pl.ds(index * piece_rows, piece_rows)
            hidden_grad = dot_nt(piece[...], weight)
            gate_grad = (hidden_grad * slope_ref[some, :].astype(jnp.float32)).astype(jnp.bfloat16)
            up_grad = (hidden_grad * silu_ref[some, :].astype(jnp.float32)).astype(jnp.bfloat16)
            gate_out[some, :] = gate_grad
            up_out[some, :] = up_grad
            gate_grads[some, columns] = gate_grad
            up_grads[some, columns] = up_grad

    @pl.when(step >= steps)
    def _():
        targets = (
            own_ref,
            other_ref,
            sent_ref.at[pl.ds(0, piece_rows), :],
            sent_ref.at[pl.ds(piece_rows, piece_rows), :],
        )
        for index, target in enumerate(targets):
            some = pl.ds(index * piece_rows, piece_rows)
            total = dot_nt(gate_grads[some, :], gate_ref[...]) + dot_nt(
                up_grads[some, :], up_ref[...]
            )
            target[...] = total.astype(target.dtype)

    @pl.when(step == pl.num_programs(0) - 1)
    def _():
        pltpu.make_async_copy(down, down_out, out_sem).wait()


def ffn_hidden_grad(pieces, slope, silu, gate, up, ahead, behind, owners):
    size = len(ahead)
    piece, width = pieces[0].shape
    length, columns = slope.shape
    steps = columns // TILE
    bf16 = jnp.bfloat16
    tall = pl.BlockSpec((length, TILE), lambda i, owners: (0, jnp.minimum(i, steps - 1)))
    weight = pl.BlockSpec((TILE, columns), lambda i, owners: (jnp.maximum(i - steps, 0), 0))
    later = lambda i, owners: (0, jnp.maximum(i - steps, 0))
    anywhere = pl.BlockSpec(memory_space=pl.ANY)
    act = jax.ShapeDtypeStruct((length, columns), bf16)
    part = jax.ShapeDtypeStruct((piece, width), bf16)
    whole = (2 * size * ahead[0].shape[0], width)
    return pl.pallas_call(
        functools.partial(hidden_grad_kernel, size, steps),
        grid_spec=pltpu.PrefetchScalarGridSpec(
            num_scalar_prefetch=1,
            grid=(steps + width // TILE,),
            in_specs=[pl.BlockSpec((piece, width), lambda i, owners: (0, 0))] * 4
            + [tall, tall, weight, weight]
            + [anywhere] * (2 * size),
            out_specs=[
                tall,
                tall,
                pl.BlockSpec((piece, TILE), later),
                pl.BlockSpec((piece, TILE), later),
                pl.BlockSpec((2 * piece, TILE), later),
                anywhere,
            ],
            scratch_shapes=[
                pltpu.VMEM(whole, bf16),
                pltpu.VMEM((length, columns), bf16),
                pltpu.VMEM((length, columns), bf16),
                pltpu.SemaphoreType.DMA((2, size)),
                pltpu.SemaphoreType.DMA,
            ],
        ),
        out_shape=(
            act,
            act,
            part,
            part,
            jax.ShapeDtypeStruct((2 * piece, width), bf16),
            jax.ShapeDtypeStruct(whole, bf16),
        ),
        compiler_params=pltpu.CompilerParams(vmem_limit_bytes=56 * 2**20),
        cost_estimate=pl.CostEstimate(
            flops=6 * length * width * columns, bytes_accessed=45 * 2**20, transcendentals=0
        ),
    )(owners, *pieces, slope, silu, gate, up, *ahead, *behind)


def lay_kernel(size, sizes, owners_ref, *refs):
    chunks, refs = refs[: 2 * size], refs[2 * size :]
    qkv_out, out_out, gains_out, sems = refs
    rows, top, qkv_columns, columns = sizes
    copies = []
    for which, count in ((0, top), (1, rows - top)):
        for index in range(size):
            chunk = chunks[which * size + index]
            owner = owners_ref[which, index]
            first = pl.multiple_of(owner * rows + which * top, 16)
            target = pl.ds(first, count)
            pairs = [
                (chunk.at[pl.ds(0, count), pl.ds(0, qkv_columns)], qkv_out.at[target, :]),
                (
                    chunk.at[pl.ds(0, count), pl.ds(qkv_columns, columns - qkv_columns)],
                    out_out.at[target, :],
                ),
            ]
            if which:
                pairs.append((chunk.at[pl.ds(count, 16), :], gains_out.at[owner]))
            for kind, (source, place) in enumerate(pairs):
                copies.append(pltpu.make_async_copy(source, place, sems.at[kind, which, index]))
    for copy in copies:
        copy.start()
    for copy in copies:
        copy.wait()


def lay_attention(ahead, behind, owners, rows, qkv_columns):
    size = len(ahead)
    top, columns = ahead[0].shape
    bf16 = jnp.bfloat16
    anywhere = pl.BlockSpec(memory_space=pl.ANY)
    return pl.pallas_call(
        functools.partial(lay_kernel, size, (rows, top, qkv_columns, columns)),
        grid_spec=pltpu.PrefetchScalarGridSpec(
            num_scalar_prefetch=1,
            grid=(1,),
            in_specs=[anywhere] * (2 * size),
            out_specs=[pl.BlockSpec(memory_space=pltpu.VMEM)] * 3,
            scratch_shapes=[pltpu.SemaphoreType.DMA((3, 2, size))],
        ),
        out_shape=(
            jax.ShapeDtypeStruct((size * rows, qkv_columns), bf16),
            jax.ShapeDtypeStruct((size * rows, columns - qkv_columns), bf16),
            jax.ShapeDtypeStruct((size, 16, columns), bf16),
        ),
        cost_estimate=pl.CostEstimate(flops=0, bytes_accessed=7 * 2**20, transcendentals=0),
    )(owners, *ahead, *behind)


def pick_kernel(sizes, index_ref, gate_ref, up_ref, gate_out, up_out):
    size, part, window = sizes
    rows = gate_ref.shape[0]
    for source, target in ((gate_ref, gate_out), (up_ref, up_out)):
        for index in range(4):
            count = min(window, part - index * window)

            @pl.when(index_ref[0] == index)
            def _():
                parts = []
                for owner in range(size):
                    first = owner * part + index * window
                    low, high = first // 128 * 128, -(-(first + count) // 128) * 128
                    wide = source[:, low:high].astype(jnp.float32)
                    parts.append(wide[:, first - low : first - low + count])
                    if count < window:
                        parts.append(jnp.zeros((rows, window - count), jnp.float32))
                target[...] = jnp.concatenate(parts, axis=1).astype(target.dtype)


def pick_hidden(gate, up, seq_index, size, part, window):
    rows, columns = gate.shape
    block = 48 if rows % 48 == 0 else rows
    wide = pl.BlockSpec((block, columns), lambda i, index: (i, 0))
    narrow = pl.BlockSpec((block, size * window), lambda i, index: (i, 0))
    out = jax.ShapeDtypeStruct((rows, size * window), gate.dtype)
    return pl.pallas_call(
        functools.partial(pick_kernel, (size, part, window)),
        grid_spec=pltpu.PrefetchScalarGridSpec(
            num_scalar_prefetch=1,
            grid=(rows // block,),
            in_specs=[wide, wide],
            out_specs=[narrow, narrow],
        ),
        out_shape=(out, out),
        compiler_params=pltpu.CompilerParams(vmem_limit_bytes=32 * 2**20),
        cost_estimate=pl.CostEstimate(flops=0, bytes_accessed=8 * 2**20, transcendentals=0),
    )(jnp.reshape(seq_index, (1,)).astype(jnp.int32), gate, up)


def spread_kernel(sizes, index_ref, own_ref, other_ref, near_ref, far_ref, out_ref, parts):
    size, part, window = sizes
    me = index_ref[0]
    parts[me] = own_ref[...]
    parts[me ^ 2] = other_ref[...]
    parts[me ^ 1] = near_ref[...]
    parts[me ^ 3] = far_ref[...]
    pieces = []
    for owner in range(size):
        for index in range(4):
            count = min(window, part - index * window)
            first = owner * window
            low, high = first // 128 * 128, -(-(first + count) // 128) * 128
            wide = parts[index, :, low:high].astype(jnp.float32)
            pieces.append(wide[:, first - low : first - low + count])
    out_ref[...] = jnp.concatenate(pieces, axis=1)


def spread_hidden(pieces, seq_index, size, part, window):
    rows, columns = pieces[0].shape
    block = 48 if rows % 48 == 0 else rows
    narrow = pl.BlockSpec((block, columns), lambda i, index: (i, 0))
    return pl.pallas_call(
        functools.partial(spread_kernel, (size, part, window)),
        grid_spec=pltpu.PrefetchScalarGridSpec(
            num_scalar_prefetch=1,
            grid=(rows // block,),
            in_specs=[narrow] * 4,
            out_specs=pl.BlockSpec((block, size * part), lambda i, index: (i, 0)),
            scratch_shapes=[pltpu.VMEM((4, block, columns), pieces[0].dtype)],
        ),
        out_shape=jax.ShapeDtypeStruct((rows, size * part), jnp.float32),
        compiler_params=pltpu.CompilerParams(vmem_limit_bytes=32 * 2**20),
        cost_estimate=pl.CostEstimate(flops=0, bytes_accessed=8 * 2**20, transcendentals=0),
    )(jnp.reshape(seq_index, (1,)), *pieces)


def norm_forward(values, gain):
    inverse = lax.rsqrt(jnp.mean(values * values, axis=-1, keepdims=True) + norm_epsilon)
    unit = values * inverse
    return (unit * gain, unit, inverse)


def norm_backward(grad_in, unit, inverse, gain):
    scaled = grad_in * gain
    return inverse * (scaled - unit * jnp.mean(scaled * unit, axis=-1, keepdims=True))


def transpose_dot(left, right):
    return lax.dot_general(
        left, right, (((0,), (0,)), ((), ())), preferred_element_type=jnp.float32
    )


def dot_transposed(left, right):
    return lax.dot_general(
        left, right, (((1,), (1,)), ((), ())), preferred_element_type=jnp.float32
    )


def split_rows(rows):
    return (rows // 32) * 16


def ring_ids(size):
    return list(range(0, size, 2)) + [i for i in range(size - 1, 0, -1) if i % 2]


def ring_perms(size):
    ids = ring_ids(size)
    forward = [(ids[i], ids[(i + 1) % size]) for i in range(size)]
    return forward, [(b, a) for a, b in forward]


def ring_owners(size):
    ids = ring_ids(size)
    table = np.zeros((size, 4, size), np.int32)
    for place, device in enumerate(ids):
        for step in range(size):
            table[device, 0, step] = ids[(place - step) % size]
            table[device, 1, step] = ids[(place + step) % size]
            table[device, 2, step] = ids[(place - 1 - step) % size]
            table[device, 3, step] = ids[(place + 1 + step) % size]
    return lax.dynamic_index_in_dim(
        jnp.asarray(table), lax.axis_index("fsdp").astype(jnp.uint32), 0, keepdims=False
    )


def after(value, *needed):
    return lax.optimization_barrier((value, *needed))[0] if needed else value


class GatherRing:
    def __init__(self, ahead, behind, size):
        self.perms = ring_perms(size)
        self.ahead, self.behind = [ahead], [behind]

    def step(self, *needed):
        forward, backward = self.perms
        self.ahead.append(lax.ppermute(after(self.ahead[-1], *needed), "fsdp", forward))
        self.behind.append(lax.ppermute(after(self.behind[-1], *needed), "fsdp", backward))


class ScatterRing:
    def __init__(self, way, blocks, size, owners):
        self.perm = ring_perms(size)[way]
        self.owners = lax.squeeze(lax.slice_in_dim(owners, 2 + way, 3 + way), (0,)).astype(
            jnp.uint32
        )
        self.blocks, self.count = blocks, 0
        self.sum = self.own().astype(jnp.bfloat16)

    def own(self):
        owner = lax.squeeze(lax.slice_in_dim(self.owners, self.count, self.count + 1), (0,))
        zero = jnp.uint32(0)
        shape = (1, *self.blocks.shape[1:])
        return lax.dynamic_slice(self.blocks, (owner, zero, zero), shape)[0].astype(jnp.float32)

    def step(self, *needed):
        came = after(lax.ppermute(self.sum, "fsdp", self.perm), *needed)
        self.count += 1
        self.sum = (came.astype(jnp.float32) + self.own()).astype(jnp.bfloat16)
        return self.sum


def exchange(values, mask):
    return lax.ppermute(values, "seq", [(i, i ^ mask) for i in range(4)])


def gather_seq(block, *needed):
    block = after(block, *needed)
    other = exchange(block, 2)
    return [block, other, exchange(block, 1), exchange(other, 1)]


def in_order(pieces, seq_index):
    high, low = seq_index // 2, seq_index % 2

    def pick(first, second, flag):
        return jnp.where(flag == 0, first, second), jnp.where(flag == 0, second, first)

    mine = pick(pieces[0], pieces[1], high)
    theirs = pick(pieces[2], pieces[3], high)
    return [*pick(mine[0], theirs[0], low), *pick(mine[1], theirs[1], low)]


def scatter_seq(own, other, there):
    rows = own.shape[0]
    came = exchange(there, 1).astype(jnp.float32)
    sent = (other.astype(jnp.float32) + came[rows:]).astype(jnp.bfloat16)
    near = own.astype(jnp.float32) + came[:rows]
    return near + exchange(sent, 2).astype(jnp.float32), sent


def swap_rows(values, seq_index):
    rows = values.shape[0] // 4

    def block(mask):
        return lax.dynamic_slice_in_dim(values, (seq_index ^ mask).astype(jnp.uint32) * rows, rows, 0)

    return [block(0), exchange(block(2), 2), exchange(block(1), 1), exchange(block(3), 3)]


def swap_columns(values, seq_index):
    columns = values.shape[1] // 4

    def block(mask):
        return lax.dynamic_slice_in_dim(values, (seq_index ^ mask).astype(jnp.uint32) * columns, columns, 1)

    return [block(0), exchange(block(2), 2), exchange(block(1), 1), exchange(block(3), 3)]


def body(
    tokens,
    norm_gain,
    query_weight,
    key_weight,
    value_weight,
    query_gain,
    key_gain,
    out_weight,
    ffn_gain,
    gate_weight,
    up_weight,
    down_weight,
    cotangent,
):
    bf16, f32 = jnp.bfloat16, jnp.float32
    size = lax.axis_size("fsdp")
    seq_index = lax.axis_index("seq")
    owners = ring_owners(size)
    own_rows, width = query_weight.shape
    head_part = query_gain.shape[0]
    head_width = head_part * size
    query_columns = width // 4
    key_columns = key_weight.shape[1] // 4
    ff_part = down_weight.shape[0]
    window = -(-ff_part // 64) * 16

    def columns_of(weight, count):
        return lax.dynamic_slice_in_dim(weight, seq_index.astype(jnp.uint32) * count, count, 1)

    def hidden_rows(weight):
        tall = jnp.pad(weight, ((0, 4 * window - ff_part), (0, 0)))
        return lax.dynamic_slice_in_dim(tall, seq_index.astype(jnp.uint32) * window, window, 0)

    gains = jnp.concatenate([norm_gain, ffn_gain, query_gain, key_gain])
    gain_count = gains.shape[0]
    qkv_columns = query_columns + 2 * key_columns
    packed_columns = qkv_columns + query_columns
    gain_rows = jnp.pad(gains[None], ((0, 15), (0, packed_columns - gain_count)))
    packed = jnp.concatenate(
        [
            columns_of(query_weight, query_columns),
            columns_of(key_weight, key_columns),
            columns_of(value_weight, key_columns),
            columns_of(out_weight, query_columns),
        ],
        axis=1,
    )
    top = split_rows(own_rows + 16)
    first_ring = GatherRing(
        packed[:top], jnp.concatenate([packed[top:], gain_rows], axis=0), size
    )
    for _ in range(size - 1):
        first_ring.step()
    started = first_ring.ahead[max(size - 3, 0)]
    ffn_ring = GatherRing(
        *pick_hidden(gate_weight, up_weight, seq_index, size, ff_part, window), size
    )
    down_rows = hidden_rows(down_weight)
    down_ring = GatherRing(down_rows[: window // 2], down_rows[window // 2 :], size)
    for step in range(1, size):
        ffn_ring.step(*((started,) if step == 1 else ()))
    for step in range(1, size):
        lag = min(step + 2, size - 1)
        down_ring.step(ffn_ring.ahead[lag], ffn_ring.behind[lag])

    qkv_all, out_part, gains_all = lay_attention(
        first_ring.ahead, first_ring.behind, owners, own_rows, qkv_columns
    )
    gains_all = gains_all[:, 0].astype(f32)
    first_gain = gains_all[:, :own_rows].reshape(-1)
    second_gain = gains_all[:, own_rows : 2 * own_rows].reshape(-1)
    q_gain_f = gains_all[:, 2 * own_rows : 2 * own_rows + head_part].reshape(-1)
    k_gain_f = gains_all[:, 2 * own_rows + head_part : 2 * (own_rows + head_part)].reshape(-1)

    inputs = tokens[0]
    tok_rows = inputs.shape[0]
    length = 4 * tok_rows
    input_blocks = gather_seq(inputs)
    inputs_all = jnp.concatenate(in_order(input_blocks, seq_index), axis=0).astype(f32)
    out_all = jnp.concatenate(
        in_order(gather_seq(out_part, input_blocks[1]), seq_index), axis=1
    )

    normed, norm_unit, norm_inverse = norm_forward(inputs_all, first_gain)
    normed_low = normed.astype(bf16)
    qkv_t = lax.dot_general(
        qkv_all, normed_low, (((0,), (1,)), ((), ())), preferred_element_type=f32
    )
    sizes = (query_columns // head_width, key_columns // head_width, head_width)
    cosine, sine = rope_rows(length, head_width)
    tables = (q_gain_f[:, None], k_gain_f[:, None], cosine, sine)
    mixed_heads, mixed_t, totals = attention_forward(qkv_t, *tables, sizes)
    mixed = jnp.concatenate(in_order(swap_rows(mixed_heads, seq_index), seq_index), axis=1)
    attended = jnp.dot(mixed, out_all, preferred_element_type=f32)
    middle = inputs.astype(f32) + attended
    normed_two, middle_unit, middle_inverse = norm_forward(middle, second_gain)
    normed_blocks = gather_seq(normed_two.astype(bf16))
    normed_two_all = jnp.concatenate(normed_blocks, axis=0)
    out_grad = cotangent[0]
    grad_blocks = gather_seq(out_grad, normed_blocks[1])
    out_grad_all = jnp.concatenate(grad_blocks, axis=0)
    mixed_all = jnp.concatenate(
        in_order(gather_seq(mixed_heads, grad_blocks[1]), seq_index), axis=1
    )

    slope, silu, hidden, gate_all, up_all = ffn_hidden(
        normed_blocks, ffn_ring.ahead, ffn_ring.behind, owners
    )
    down_weight_grad = transpose_dot(hidden, out_grad_all).astype(bf16)
    down_sums = ScatterRing(0, down_weight_grad.reshape(size, window, width), size, owners)
    gate_grad, up_grad, *normed_parts, down_all = ffn_hidden_grad(
        [after(block, down_sums.sum) for block in grad_blocks],
        slope,
        silu,
        gate_all,
        up_all,
        down_ring.ahead,
        down_ring.behind,
        owners,
    )
    down_sums.step(gate_grad)
    normed_two_grad, half_sum = scatter_seq(*normed_parts)
    gate_weight_grad = transpose_dot(
        after(normed_two_all, down_sums.sum), gate_grad
    ).astype(bf16)
    gate_sums = ScatterRing(
        0, gate_weight_grad.reshape(size, own_rows, size * window), size, owners
    )
    up_weight_grad = transpose_dot(after(normed_two_all, gate_sums.sum), up_grad).astype(bf16)
    up_sums = ScatterRing(1, up_weight_grad.reshape(size, own_rows, size * window), size, owners)
    down_sums.step(up_sums.sum)
    ffn_gain_grad = jnp.sum(normed_two_grad * middle_unit, axis=0)
    middle_grad = out_grad.astype(f32) + norm_backward(
        normed_two_grad, middle_unit, middle_inverse, second_gain
    )
    attended_low = middle_grad.astype(bf16)
    mixed_grad = dot_transposed(attended_low, out_all).astype(bf16)
    gate_sums.step(mixed_grad)
    up_sums.step(mixed_grad)
    down_sums.step(mixed_grad)
    mixed_grad_blocks = swap_columns(mixed_grad, seq_index)
    mixed_grad_heads = jnp.concatenate(in_order(mixed_grad_blocks, seq_index), axis=0)
    attended_columns = jnp.concatenate(
        in_order(swap_columns(after(attended_low, *mixed_grad_blocks), seq_index), seq_index), axis=0
    )
    qkv_grad, head_gains = attention_backward(
        qkv_t, *tables, mixed_t, totals, mixed_grad_heads, sizes
    )
    out_weight_grad = transpose_dot(mixed_all, after(attended_columns, qkv_grad))
    gate_sums.step(qkv_grad)
    up_sums.step(qkv_grad)
    down_sums.step(qkv_grad)
    head_gains = jnp.sum(head_gains, axis=1)
    query_gain_grad, key_gain_grad = head_gains[:head_width], head_gains[head_width:]
    qkv_weight_grad = transpose_dot(normed_low, qkv_grad)
    normed_partial = dot_transposed(qkv_grad, qkv_all)
    norm_gain_grad = jnp.sum(normed_partial * norm_unit, axis=0)
    partial_blocks = normed_partial.astype(bf16).reshape(4, tok_rows, width)

    def partial_of(mask):
        index = (seq_index ^ mask).astype(jnp.uint32)
        return lax.dynamic_index_in_dim(partial_blocks, index, 0, keepdims=False)

    normed_grad, _ = scatter_seq(
        partial_of(0),
        partial_of(2),
        jnp.concatenate([partial_of(1), partial_of(3)], axis=0),
    )
    _, own_unit, own_inverse = norm_forward(inputs.astype(f32), first_gain)
    inputs_grad = middle_grad + norm_backward(normed_grad, own_unit, own_inverse, first_gain)

    gain_grads = jnp.concatenate(
        [
            norm_gain_grad.reshape(size, -1),
            ffn_gain_grad.reshape(size, -1),
            query_gain_grad.reshape(size, -1),
            key_gain_grad.reshape(size, -1),
        ],
        axis=1,
    )
    gain_blocks = jnp.pad(
        gain_grads[:, None], ((0, 0), (0, 15), (0, packed_columns - gain_count))
    )
    packed_blocks = jnp.concatenate(
        [
            jnp.concatenate([qkv_weight_grad, out_weight_grad], axis=1).reshape(
                size, own_rows, packed_columns
            ),
            gain_blocks,
        ],
        axis=1,
    ).astype(bf16)
    gate_sums.step(packed_blocks)
    up_sums.step(packed_blocks)
    last_sums = ScatterRing(1, packed_blocks, size, owners)
    while gate_sums.count < size - 1:
        if down_sums.count < size - 1:
            down_sums.step(gate_sums.sum)
        gate_sums.step()
        up_sums.step()
        last_sums.step(gate_sums.sum, up_sums.sum)
        if gate_sums.count == size - 3:
            late = gate_sums.sum
    while down_sums.count < size - 1:
        down_sums.step()
    while last_sums.count < size - 1:
        last_sums.step()
    packed_share = last_sums.sum

    down_partial = jnp.dot(
        after(hidden, late, up_sums.sum), down_all, preferred_element_type=f32
    ).astype(bf16)
    down_sum, _ = scatter_seq(
        down_partial[:tok_rows], down_partial[tok_rows : 2 * tok_rows], down_partial[2 * tok_rows :]
    )
    output = middle + down_sum
    down_full = jnp.concatenate(in_order(gather_seq(down_sums.sum), seq_index), axis=0)[
        :ff_part
    ].astype(f32)
    gate_full, up_full = (
        spread_hidden(gather_seq(share), seq_index, size, ff_part, window)
        for share in (gate_sums.sum, up_sums.sum)
    )
    packs = in_order(gather_seq(packed_share), seq_index)

    def unpack(first, count):
        return jnp.concatenate(
            [p[:own_rows, first : first + count] for p in packs], axis=1
        ).astype(f32)

    gain_sum = sum(p[own_rows, :gain_count].astype(f32) for p in packs)
    return (
        output[None].astype(bf16),
        inputs_grad[None].astype(bf16),
        gain_sum[:own_rows],
        unpack(0, query_columns),
        unpack(query_columns, key_columns),
        unpack(query_columns + key_columns, key_columns),
        gain_sum[2 * own_rows : 2 * own_rows + head_part],
        gain_sum[2 * own_rows + head_part :],
        unpack(qkv_columns, query_columns),
        gain_sum[own_rows : 2 * own_rows],
        gate_full,
        up_full,
        down_full,
    )


def solution(mesh):
    in_specs = (
        P("fsdp", "seq", None),
        P("fsdp"),
        P("fsdp", None),
        P("fsdp", None),
        P("fsdp", None),
        P("fsdp"),
        P("fsdp"),
        P("fsdp", None),
        P("fsdp"),
        P("fsdp", None),
        P("fsdp", None),
        P("fsdp", None),
        P("fsdp", "seq", None),
    )
    out_specs = (
        P("fsdp", "seq", None),
        P("fsdp", "seq", None),
        P("fsdp"),
        P("fsdp", None),
        P("fsdp", None),
        P("fsdp", None),
        P("fsdp"),
        P("fsdp"),
        P("fsdp", None),
        P("fsdp"),
        P("fsdp", None),
        P("fsdp", None),
        P("fsdp", None),
    )
    return jax.shard_map(body, mesh=mesh, in_specs=in_specs, out_specs=out_specs, check_vma=False)
```

```python
import functools
import math

import jax
import jax.numpy as jnp
import numpy as np
from jax import lax
from jax.experimental import pallas as pl
from jax.experimental.layout import Layout, with_layout_constraint
from jax.experimental.pallas import tpu as pltpu
from jax.sharding import PartitionSpec as P

norm_epsilon = 1e-05
TILE = 256
log2_e = math.log2(math.e)


def rope_rows(length, width):
    half_width = width // 2
    inverse = jnp.exp(
        jnp.arange(half_width, dtype=jnp.float32) * (-2.0 * math.log(1000000.0) / width)
    )
    angles = inverse[:, None] * jnp.arange(length, dtype=jnp.int32).astype(jnp.float32)[None, :]
    return jnp.cos(angles), jnp.sin(angles)


def head_norm(values):
    inverse = lax.rsqrt(jnp.mean(values * values, axis=0, keepdims=True) + norm_epsilon)
    return values * inverse, inverse


def head_turn(values, cosine, sine):
    half = values.shape[0] // 2
    first, second = values[:half], values[half:]
    return jnp.concatenate(
        [first * cosine - second * sine, second * cosine + first * sine], axis=0
    )


def head_turn_back(values, cosine, sine):
    half = values.shape[0] // 2
    first, second = values[:half], values[half:]
    return jnp.concatenate(
        [first * cosine + second * sine, second * cosine - first * sine], axis=0
    )


def fill_heads(qkv_ref, q_gain_ref, k_gain_ref, cos_ref, sin_ref, queries, keys, keys_t, values, values_t, sizes):
    heads, groups, width = sizes
    cosine, sine = cos_ref[...], sin_ref[...]

    @pl.loop(0, heads)
    def _(head):
        unit, _ = head_norm(qkv_ref[pl.ds(head * width, width), :])
        turned = head_turn(unit * q_gain_ref[...], cosine, sine)
        queries[head] = (turned * (width**-0.5 * log2_e)).astype(jnp.bfloat16)

    @pl.loop(0, groups)
    def _(group):
        unit, _ = head_norm(qkv_ref[pl.ds((heads + group) * width, width), :])
        turned = head_turn(unit * k_gain_ref[...], cosine, sine)
        keys[group] = turned.T.astype(jnp.bfloat16)
        if keys_t is not None:
            keys_t[group] = turned.astype(jnp.bfloat16)
        value = qkv_ref[pl.ds((heads + groups + group) * width, width), :]
        if values is not None:
            values[group] = value.T.astype(jnp.bfloat16)
        if values_t is not None:
            values_t[group] = value.astype(jnp.bfloat16)


def diagonal_mask():
    key_place = lax.broadcasted_iota(jnp.int32, (TILE, TILE), 0)
    query_place = lax.broadcasted_iota(jnp.int32, (TILE, TILE), 1)
    return key_place <= query_place


def causal_exp(scores, count):
    weights = jnp.exp2(scores)
    last = jnp.where(diagonal_mask(), weights[count - TILE :], 0.0)
    if count == TILE:
        return last
    return jnp.concatenate([weights[: count - TILE], last], axis=0)


def dot(left, right):
    return jnp.dot(left, right, preferred_element_type=jnp.float32)


def dot_nt(left, right):
    return lax.dot_general(
        left, right, (((1,), (1,)), ((), ())), preferred_element_type=jnp.float32
    )


def forward_kernel(sizes, qkv_ref, q_gain_ref, k_gain_ref, cos_ref, sin_ref, mixed_ref, mixed_t_ref, total_ref, queries, keys, values_t, mixed_f):
    heads, groups, width = sizes
    ratio = heads // groups
    length = qkv_ref.shape[1]
    fill_heads(qkv_ref, q_gain_ref, k_gain_ref, cos_ref, sin_ref, queries, keys, None, None, values_t, sizes)

    @pl.loop(0, heads)
    def _(head):
        group = head // ratio
        for tile in range(length // TILE):
            count = (tile + 1) * TILE
            columns = pl.ds(tile * TILE, TILE)
            scores = dot(keys[group, pl.ds(0, count), :], queries[head, :, columns])
            weights = causal_exp(scores, count)
            total = jnp.sum(weights, axis=0, keepdims=True)
            result = dot(values_t[group, :, pl.ds(0, count)], weights.astype(jnp.bfloat16))
            mixed_f[pl.ds(head * width, width), columns] = result * (1.0 / total)
            total_ref[pl.ds(head, 1), columns] = jnp.log2(total)

    for block in range(heads * width // 128):
        rows = mixed_f[pl.ds(block * 128, 128), :]
        mixed_t_ref[pl.ds(block * 128, 128), :] = rows.astype(jnp.bfloat16)
        mixed_ref[:, pl.ds(block * 128, 128)] = rows.T.astype(jnp.bfloat16)


def backward_kernel(sizes, qkv_ref, q_gain_ref, k_gain_ref, cos_ref, sin_ref, mixed_t_ref, total_ref, grad_ref, out_ref, gain_ref, out_t, queries, keys, keys_t, values, grads, key_sum, value_sum):
    heads, groups, width = sizes
    ratio = heads // groups
    length = qkv_ref.shape[1]
    fill_heads(qkv_ref, q_gain_ref, k_gain_ref, cos_ref, sin_ref, queries, keys, keys_t, values, None, sizes)
    for block in range(heads * width // 128):
        turned = grad_ref[:, pl.ds(block * 128, 128)].astype(jnp.float32).T
        grads[pl.ds(block * 128, 128), :] = turned.astype(jnp.bfloat16)
    key_sum[...] = jnp.zeros_like(key_sum)
    value_sum[...] = jnp.zeros_like(value_sum)
    gain_ref[...] = jnp.zeros_like(gain_ref)
    cosine, sine = cos_ref[...], sin_ref[...]

    def finish(grad_turned, rows, gain, first):
        grad = head_turn_back(grad_turned, cosine, sine)
        unit, inverse = head_norm(qkv_ref[rows, :])
        product = grad * unit
        part = product[:, :128]
        for lane in range(128, length, 128):
            part = part + product[:, lane : lane + 128]
        gain_ref[pl.ds(first, width), :] += part
        scaled = grad * gain
        before = inverse * (scaled - unit * jnp.mean(scaled * unit, axis=0, keepdims=True))
        out_t[rows, :] = before

    @pl.loop(0, heads)
    def _(head):
        group = head // ratio
        rows = pl.ds(head * width, width)
        query_parts = []
        for tile in range(length // TILE):
            count = (tile + 1) * TILE
            columns = pl.ds(tile * TILE, TILE)
            query = queries[head, :, columns]
            grad = grads[rows, columns]
            scores = dot(keys[group, pl.ds(0, count), :], query) - total_ref[pl.ds(head, 1), columns]
            weights = causal_exp(scores, count)
            inner = jnp.sum(
                grad.astype(jnp.float32) * mixed_t_ref[rows, columns].astype(jnp.float32),
                axis=0,
                keepdims=True,
            )
            weight_grad = dot(values[group, pl.ds(0, count), :], grad)
            score_grad = (weights * (weight_grad - inner)).astype(jnp.bfloat16)
            query_parts.append(dot(keys_t[group, :, pl.ds(0, count)], score_grad))
            key_sum[group, pl.ds(0, count), :] += dot_nt(score_grad, query)
            value_sum[group, pl.ds(0, count), :] += dot_nt(weights.astype(jnp.bfloat16), grad)
        query_grad = jnp.concatenate(query_parts, axis=1) * width**-0.5
        finish(query_grad, rows, q_gain_ref[...], 0)

    for group in range(groups):
        key_grad = key_sum[group].T * (1.0 / log2_e)
        finish(key_grad, pl.ds((heads + group) * width, width), k_gain_ref[...], width)
        out_t[pl.ds((heads + groups + group) * width, width), :] = value_sum[group].T

    for block in range(out_t.shape[0] // 128):
        some = pl.ds(block * 128, 128)
        out_ref[:, some] = out_t[some, :].T.astype(jnp.bfloat16)


def attention_forward(qkv_t, q_gain, k_gain, cosine, sine, sizes):
    heads, groups, width = sizes
    length = qkv_t.shape[1]
    bf16, f32 = jnp.bfloat16, jnp.float32
    pairs = heads * length * length
    return pl.pallas_call(
        functools.partial(forward_kernel, sizes),
        out_shape=(
            jax.ShapeDtypeStruct((length, heads * width), bf16),
            jax.ShapeDtypeStruct((heads * width, length), bf16),
            jax.ShapeDtypeStruct((-(-heads // 8) * 8, length), f32),
        ),
        scratch_shapes=[
            pltpu.VMEM((heads, width, length), bf16),
            pltpu.VMEM((groups, length, width), bf16),
            pltpu.VMEM((groups, width, length), bf16),
            pltpu.VMEM((heads * width, length), f32),
        ],
        compiler_params=pltpu.CompilerParams(vmem_limit_bytes=32 * 2**20),
        cost_estimate=pl.CostEstimate(
            flops=8 * pairs * width, bytes_accessed=6 * 2**20, transcendentals=pairs
        ),
    )(qkv_t, q_gain, k_gain, cosine, sine)


def attention_backward(qkv_t, q_gain, k_gain, cosine, sine, mixed_t, total, mixed_grad, sizes):
    heads, groups, width = sizes
    length = qkv_t.shape[1]
    bf16, f32 = jnp.bfloat16, jnp.float32
    pairs = heads * length * length
    return pl.pallas_call(
        functools.partial(backward_kernel, sizes),
        out_shape=(
            jax.ShapeDtypeStruct(qkv_t.shape[::-1], bf16),
            jax.ShapeDtypeStruct((2 * width, 128), f32),
        ),
        scratch_shapes=[
            pltpu.VMEM(qkv_t.shape, f32),
            pltpu.VMEM((heads, width, length), bf16),
            pltpu.VMEM((groups, length, width), bf16),
            pltpu.VMEM((groups, width, length), bf16),
            pltpu.VMEM((groups, length, width), bf16),
            pltpu.VMEM((heads * width, length), bf16),
            pltpu.VMEM((groups, length, width), f32),
            pltpu.VMEM((groups, length, width), f32),
        ],
        compiler_params=pltpu.CompilerParams(vmem_limit_bytes=40 * 2**20),
        cost_estimate=pl.CostEstimate(
            flops=20 * pairs * width, bytes_accessed=8 * 2**20, transcendentals=pairs
        ),
    )(qkv_t, q_gain, k_gain, cosine, sine, mixed_t, total, mixed_grad)


def hidden_kernel(size, ids_ref, *refs):
    pieces, chunks, refs = refs[:4], refs[4 : 4 + 2 * size], refs[4 + 2 * size :]
    slope_ref, silu_ref, hidden_ref, gate_out, up_out, tokens, gate, up, *sems = refs
    row_sems, in_sems, out_sems = sems
    step = pl.program_id(0)
    steps = pl.num_programs(0)
    rows = chunks[0].shape[0]
    piece = pieces[0].shape[0]

    @pl.when(step == 0)
    def _():
        copies = [
            pltpu.make_async_copy(
                source, tokens.at[pl.ds(index * piece, piece), :], row_sems.at[index]
            )
            for index, source in enumerate(pieces)
        ]
        for copy in copies:
            copy.start()

        @pl.loop(0, steps)
        def _(tile):
            columns = pl.ds(pl.multiple_of(tile * TILE, TILE), TILE)
            for which, target in ((0, gate), (1, up)):
                for index in range(size):
                    first = pl.multiple_of(ids_ref[which, index] * rows, 16)
                    pltpu.make_async_copy(
                        chunks[which * size + index].at[:, columns],
                        target.at[pl.ds(first, rows), columns],
                        in_sems.at[which, tile],
                    ).start()

        for copy in copies:
            copy.wait()

    columns = pl.ds(pl.multiple_of(step * TILE, TILE), TILE)
    for which, target, result in ((0, gate, gate_out), (1, up, up_out)):
        part = target.at[:, columns]
        pltpu.make_async_copy(part, part, in_sems.at[which, step]).wait()
        pltpu.make_async_copy(part, result.at[:, columns], out_sems.at[which, step]).start()
    for half in range(2):
        some = pl.ds(half * 2 * piece, 2 * piece)
        gate_act = dot(tokens[some, :], gate[:, columns])
        up_act = dot(tokens[some, :], up[:, columns])
        sigmoid = 0.5 + 0.5 * jnp.tanh(0.5 * gate_act)
        silu = gate_act * sigmoid
        hidden_ref[some, :] = (silu * up_act).astype(hidden_ref.dtype)
        silu_ref[some, :] = silu.astype(silu_ref.dtype)
        slope_ref[some, :] = (up_act * sigmoid * (1.0 + gate_act * (1.0 - sigmoid))).astype(
            slope_ref.dtype
        )

    @pl.when(step == steps - 1)
    def _():
        @pl.loop(0, steps)
        def _(tile):
            columns = pl.ds(pl.multiple_of(tile * TILE, TILE), TILE)
            for which, target, result in ((0, gate, gate_out), (1, up, up_out)):
                pltpu.make_async_copy(
                    target.at[:, columns], result.at[:, columns], out_sems.at[which, tile]
                ).wait()


def ffn_hidden(pieces, gate_chunks, up_chunks, ids):
    size = len(gate_chunks)
    part, columns = gate_chunks[0].shape
    piece, width = pieces[0].shape
    length = 4 * piece
    bf16 = jnp.bfloat16
    tall = pl.BlockSpec((length, TILE), lambda i, ids: (0, i))
    act = jax.ShapeDtypeStruct((length, columns), bf16)
    weight = jax.ShapeDtypeStruct((width, columns), bf16)
    anywhere = pl.BlockSpec(memory_space=pl.ANY)
    return pl.pallas_call(
        functools.partial(hidden_kernel, size),
        grid_spec=pltpu.PrefetchScalarGridSpec(
            num_scalar_prefetch=1,
            grid=(columns // TILE,),
            in_specs=[anywhere] * (4 + 2 * size),
            out_specs=[tall, tall, tall, anywhere, anywhere],
            scratch_shapes=[
                pltpu.VMEM((length, width), bf16),
                pltpu.VMEM((width, columns), bf16),
                pltpu.VMEM((width, columns), bf16),
                pltpu.SemaphoreType.DMA((4,)),
                pltpu.SemaphoreType.DMA((2, columns // TILE)),
                pltpu.SemaphoreType.DMA((2, columns // TILE)),
            ],
        ),
        out_shape=(act, act, act, weight, weight),
        compiler_params=pltpu.CompilerParams(vmem_limit_bytes=56 * 2**20),
        cost_estimate=pl.CostEstimate(
            flops=4 * length * width * columns,
            bytes_accessed=36 * 2**20,
            transcendentals=length * columns,
        ),
    )(ids, *pieces, *gate_chunks, *up_chunks)


def hidden_grad_kernel(size, steps, owners_ref, *refs):
    grad_ref, slope_ref, silu_ref, gate_ref, up_ref = refs[:5]
    chunks, refs = refs[5 : 5 + 2 * size], refs[5 + 2 * size :]
    gate_out, up_out, own_ref, other_ref, sent_ref, down_out = refs[:6]
    down, gate_grads, up_grads, in_sems, out_sem = refs[6:]
    step = pl.program_id(0)
    rows = chunks[0].shape[0]
    piece = own_ref.shape[0]

    @pl.when(step == 0)
    def _():
        copies = []
        for which in range(2):
            for index in range(size):
                first = pl.multiple_of((2 * owners_ref[which, index] + which) * rows, 16)
                copies.append(
                    pltpu.make_async_copy(
                        chunks[which * size + index],
                        down.at[pl.ds(first, rows), :],
                        in_sems.at[which, index],
                    )
                )
        for copy in copies:
            copy.start()
        for copy in copies:
            copy.wait()
        pltpu.make_async_copy(down, down_out, out_sem).start()

    @pl.when(step < steps)
    def _():
        columns = pl.ds(pl.multiple_of(step * TILE, TILE), TILE)
        weight = down[columns, :]
        for half in range(2):
            some = pl.ds(half * 2 * piece, 2 * piece)
            hidden_grad = dot_nt(grad_ref[some, :], weight)
            gate_grad = (hidden_grad * slope_ref[some, :].astype(jnp.float32)).astype(jnp.bfloat16)
            up_grad = (hidden_grad * silu_ref[some, :].astype(jnp.float32)).astype(jnp.bfloat16)
            gate_out[some, :] = gate_grad
            up_out[some, :] = up_grad
            gate_grads[some, columns] = gate_grad
            up_grads[some, columns] = up_grad

    @pl.when(step >= steps)
    def _():
        total = dot_nt(gate_grads[...], gate_ref[...]) + dot_nt(up_grads[...], up_ref[...])
        total = total.astype(jnp.bfloat16)
        own_ref[...] = total[:piece]
        other_ref[...] = total[piece : 2 * piece]
        sent_ref[...] = total[2 * piece :]

    @pl.when(step == pl.num_programs(0) - 1)
    def _():
        pltpu.make_async_copy(down, down_out, out_sem).wait()


def ffn_hidden_grad(out_grad, slope, silu, gate, up, ahead, behind, owners):
    size = len(ahead)
    length, width = out_grad.shape
    piece = length // 4
    columns = slope.shape[1]
    steps = columns // TILE
    bf16 = jnp.bfloat16
    tall = pl.BlockSpec((length, TILE), lambda i, owners: (0, jnp.minimum(i, steps - 1)))
    weight = pl.BlockSpec((TILE, columns), lambda i, owners: (jnp.maximum(i - steps, 0), 0))
    later = lambda i, owners: (0, jnp.maximum(i - steps, 0))
    anywhere = pl.BlockSpec(memory_space=pl.ANY)
    act = jax.ShapeDtypeStruct((length, columns), bf16)
    part = jax.ShapeDtypeStruct((piece, width), bf16)
    whole = (2 * size * ahead[0].shape[0], width)
    return pl.pallas_call(
        functools.partial(hidden_grad_kernel, size, steps),
        grid_spec=pltpu.PrefetchScalarGridSpec(
            num_scalar_prefetch=1,
            grid=(steps + width // TILE,),
            in_specs=[pl.BlockSpec((length, width), lambda i, owners: (0, 0))]
            + [tall, tall, weight, weight]
            + [anywhere] * (2 * size),
            out_specs=[
                tall,
                tall,
                pl.BlockSpec((piece, TILE), later),
                pl.BlockSpec((piece, TILE), later),
                pl.BlockSpec((2 * piece, TILE), later),
                anywhere,
            ],
            scratch_shapes=[
                pltpu.VMEM(whole, bf16),
                pltpu.VMEM((length, columns), bf16),
                pltpu.VMEM((length, columns), bf16),
                pltpu.SemaphoreType.DMA((2, size)),
                pltpu.SemaphoreType.DMA,
            ],
        ),
        out_shape=(
            act,
            act,
            part,
            part,
            jax.ShapeDtypeStruct((2 * piece, width), bf16),
            jax.ShapeDtypeStruct(whole, bf16),
        ),
        compiler_params=pltpu.CompilerParams(vmem_limit_bytes=56 * 2**20),
        cost_estimate=pl.CostEstimate(
            flops=6 * length * width * columns, bytes_accessed=45 * 2**20, transcendentals=0
        ),
    )(owners, out_grad, slope, silu, gate, up, *ahead, *behind)


def lay_kernel(size, sizes, owners_ref, *refs):
    chunks, refs = refs[: 2 * size], refs[2 * size :]
    qkv_out, out_out, gains_out, sems = refs
    rows, top, qkv_columns, columns = sizes
    copies = []
    for which, count in ((0, top), (1, rows - top)):
        for index in range(size):
            chunk = chunks[which * size + index]
            owner = owners_ref[which, index]
            first = pl.multiple_of(owner * rows + which * top, 16)
            target = pl.ds(first, count)
            pairs = [
                (chunk.at[pl.ds(0, count), pl.ds(0, qkv_columns)], qkv_out.at[target, :]),
                (
                    chunk.at[pl.ds(0, count), pl.ds(qkv_columns, columns - qkv_columns)],
                    out_out.at[target, :],
                ),
            ]
            if which:
                pairs.append((chunk.at[pl.ds(count, 16), :], gains_out.at[owner]))
            for kind, (source, place) in enumerate(pairs):
                copies.append(pltpu.make_async_copy(source, place, sems.at[kind, which, index]))
    for copy in copies:
        copy.start()
    for copy in copies:
        copy.wait()


def lay_attention(ahead, behind, owners, rows, qkv_columns):
    size = len(ahead)
    top, columns = ahead[0].shape
    bf16 = jnp.bfloat16
    anywhere = pl.BlockSpec(memory_space=pl.ANY)
    return pl.pallas_call(
        functools.partial(lay_kernel, size, (rows, top, qkv_columns, columns)),
        grid_spec=pltpu.PrefetchScalarGridSpec(
            num_scalar_prefetch=1,
            grid=(1,),
            in_specs=[anywhere] * (2 * size),
            out_specs=[pl.BlockSpec(memory_space=pltpu.VMEM)] * 3,
            scratch_shapes=[pltpu.SemaphoreType.DMA((3, 2, size))],
        ),
        out_shape=(
            jax.ShapeDtypeStruct((size * rows, qkv_columns), bf16),
            jax.ShapeDtypeStruct((size * rows, columns - qkv_columns), bf16),
            jax.ShapeDtypeStruct((size, 16, columns), bf16),
        ),
        cost_estimate=pl.CostEstimate(flops=0, bytes_accessed=7 * 2**20, transcendentals=0),
    )(owners, *ahead, *behind)


def pick_kernel(sizes, index_ref, gate_ref, up_ref, gate_out, up_out):
    size, part, window = sizes
    rows = gate_ref.shape[0]
    for source, target in ((gate_ref, gate_out), (up_ref, up_out)):
        for index in range(4):
            count = min(window, part - index * window)

            @pl.when(index_ref[0] == index)
            def _():
                parts = []
                for owner in range(size):
                    first = owner * part + index * window
                    low, high = first // 128 * 128, -(-(first + count) // 128) * 128
                    wide = source[:, low:high].astype(jnp.float32)
                    parts.append(wide[:, first - low : first - low + count])
                    if count < window:
                        parts.append(jnp.zeros((rows, window - count), jnp.float32))
                target[...] = jnp.concatenate(parts, axis=1).astype(target.dtype)


def pick_hidden(gate, up, seq_index, size, part, window):
    rows, columns = gate.shape
    block = 48 if rows % 48 == 0 else rows
    wide = pl.BlockSpec((block, columns), lambda i, index: (i, 0))
    narrow = pl.BlockSpec((block, size * window), lambda i, index: (i, 0))
    out = jax.ShapeDtypeStruct((rows, size * window), gate.dtype)
    return pl.pallas_call(
        functools.partial(pick_kernel, (size, part, window)),
        grid_spec=pltpu.PrefetchScalarGridSpec(
            num_scalar_prefetch=1,
            grid=(rows // block,),
            in_specs=[wide, wide],
            out_specs=[narrow, narrow],
        ),
        out_shape=(out, out),
        compiler_params=pltpu.CompilerParams(vmem_limit_bytes=32 * 2**20),
        cost_estimate=pl.CostEstimate(flops=0, bytes_accessed=8 * 2**20, transcendentals=0),
    )(jnp.reshape(seq_index, (1,)).astype(jnp.int32), gate, up)


def spread_kernel(sizes, index_ref, own_ref, other_ref, near_ref, far_ref, out_ref, parts):
    size, part, window = sizes
    me = index_ref[0]
    parts[me] = own_ref[...]
    parts[me ^ 2] = other_ref[...]
    parts[me ^ 1] = near_ref[...]
    parts[me ^ 3] = far_ref[...]
    pieces = []
    for owner in range(size):
        for index in range(4):
            count = min(window, part - index * window)
            first = owner * window
            low, high = first // 128 * 128, -(-(first + count) // 128) * 128
            wide = parts[index, :, low:high].astype(jnp.float32)
            pieces.append(wide[:, first - low : first - low + count])
    out_ref[...] = jnp.concatenate(pieces, axis=1)


def spread_hidden(pieces, which, seq_index, size, part, window):
    _, rows, columns = pieces[0].shape
    block = 48 if rows % 48 == 0 else rows
    narrow = pl.BlockSpec((None, block, columns), lambda i, index: (which, i, 0))
    return pl.pallas_call(
        functools.partial(spread_kernel, (size, part, window)),
        grid_spec=pltpu.PrefetchScalarGridSpec(
            num_scalar_prefetch=1,
            grid=(rows // block,),
            in_specs=[narrow] * 4,
            out_specs=pl.BlockSpec((block, size * part), lambda i, index: (i, 0)),
            scratch_shapes=[pltpu.VMEM((4, block, columns), pieces[0].dtype)],
        ),
        out_shape=jax.ShapeDtypeStruct((rows, size * part), jnp.float32),
        compiler_params=pltpu.CompilerParams(vmem_limit_bytes=32 * 2**20),
        cost_estimate=pl.CostEstimate(flops=0, bytes_accessed=64 * 2**20, transcendentals=0),
    )(jnp.reshape(seq_index, (1,)), *pieces)


def norm_forward(values, gain):
    inverse = lax.rsqrt(jnp.mean(values * values, axis=-1, keepdims=True) + norm_epsilon)
    unit = values * inverse
    return (unit * gain, unit, inverse)


def norm_backward(grad_in, unit, inverse, gain):
    scaled = grad_in * gain
    return inverse * (scaled - unit * jnp.mean(scaled * unit, axis=-1, keepdims=True))


def transpose_dot(left, right):
    return lax.dot_general(
        left, right, (((0,), (0,)), ((), ())), preferred_element_type=jnp.float32
    )


def by_rows(values):
    return with_layout_constraint(values, Layout(major_to_minor=(0, 1)))


def dot_transposed(left, right):
    return lax.dot_general(
        left, right, (((1,), (1,)), ((), ())), preferred_element_type=jnp.float32
    )


def split_rows(rows):
    return (rows // 32) * 16


def ring_ids(size):
    return list(range(0, size, 2)) + [i for i in range(size - 1, 0, -1) if i % 2]


def ring_perms(size):
    ids = ring_ids(size)
    forward = [(ids[i], ids[(i + 1) % size]) for i in range(size)]
    return forward, [(b, a) for a, b in forward]


def ring_owners(size):
    ids = ring_ids(size)
    table = np.zeros((size, 4, size), np.int32)
    for place, device in enumerate(ids):
        for step in range(size):
            table[device, 0, step] = ids[(place - step) % size]
            table[device, 1, step] = ids[(place + step) % size]
            table[device, 2, step] = ids[(place - 1 - step) % size]
            table[device, 3, step] = ids[(place + 1 + step) % size]
    return lax.dynamic_index_in_dim(
        jnp.asarray(table), lax.axis_index("fsdp").astype(jnp.uint32), 0, keepdims=False
    )


def after(value, *needed):
    return lax.optimization_barrier((value, *needed))[0] if needed else value


class GatherRing:
    def __init__(self, ahead, behind, size):
        self.perms = ring_perms(size)
        self.ahead, self.behind = [ahead], [behind]

    def step(self, *needed):
        forward, backward = self.perms
        self.ahead.append(lax.ppermute(after(self.ahead[-1], *needed), "fsdp", forward))
        self.behind.append(lax.ppermute(after(self.behind[-1], *needed), "fsdp", backward))


class ScatterRing:
    def __init__(self, way, blocks, size, owners):
        self.perm = ring_perms(size)[way]
        self.owners = lax.squeeze(lax.slice_in_dim(owners, 2 + way, 3 + way), (0,)).astype(
            jnp.uint32
        )
        self.blocks, self.count = blocks, 0
        self.sum = self.own().astype(jnp.bfloat16)

    def own(self):
        owner = lax.squeeze(lax.slice_in_dim(self.owners, self.count, self.count + 1), (0,))
        zero = jnp.uint32(0)
        shape = (1, *self.blocks.shape[1:])
        return lax.dynamic_slice(self.blocks, (owner, zero, zero), shape)[0].astype(jnp.float32)

    def step(self, *needed):
        came = after(lax.ppermute(self.sum, "fsdp", self.perm), *needed)
        self.count += 1
        self.sum = (came.astype(jnp.float32) + self.own()).astype(jnp.bfloat16)
        return self.sum


def exchange(values, mask):
    return lax.ppermute(values, "seq", [(i, i ^ mask) for i in range(4)])


def gather_seq(block, *needed):
    block = after(block, *needed)
    other = exchange(block, 2)
    return [block, other, exchange(block, 1), exchange(other, 1)]


def in_order(pieces, seq_index):
    high, low = seq_index // 2, seq_index % 2

    def pick(first, second, flag):
        return jnp.where(flag == 0, first, second), jnp.where(flag == 0, second, first)

    mine = pick(pieces[0], pieces[1], high)
    theirs = pick(pieces[2], pieces[3], high)
    return [*pick(mine[0], theirs[0], low), *pick(mine[1], theirs[1], low)]


def scatter_seq(own, other, there):
    rows = own.shape[0]
    came = exchange(there, 1).astype(jnp.float32)
    sent = (other.astype(jnp.float32) + came[rows:]).astype(jnp.bfloat16)
    near = own.astype(jnp.float32) + came[:rows]
    return near + exchange(sent, 2).astype(jnp.float32), sent


def swap_rows(values, seq_index):
    rows = values.shape[0] // 4

    def block(mask):
        return lax.dynamic_slice_in_dim(values, (seq_index ^ mask).astype(jnp.uint32) * rows, rows, 0)

    return [block(0), exchange(block(2), 2), exchange(block(1), 1), exchange(block(3), 3)]


def swap_columns(values, seq_index):
    columns = values.shape[1] // 4

    def block(mask):
        return lax.dynamic_slice_in_dim(values, (seq_index ^ mask).astype(jnp.uint32) * columns, columns, 1)

    return [block(0), exchange(block(2), 2), exchange(block(1), 1), exchange(block(3), 3)]


def body(
    tokens,
    norm_gain,
    query_weight,
    key_weight,
    value_weight,
    query_gain,
    key_gain,
    out_weight,
    ffn_gain,
    gate_weight,
    up_weight,
    down_weight,
    cotangent,
):
    bf16, f32 = jnp.bfloat16, jnp.float32
    size = lax.axis_size("fsdp")
    seq_index = lax.axis_index("seq")
    owners = ring_owners(size)
    own_rows, width = query_weight.shape
    head_part = query_gain.shape[0]
    head_width = head_part * size
    query_columns = width // 4
    key_columns = key_weight.shape[1] // 4
    ff_part = down_weight.shape[0]
    window = -(-ff_part // 64) * 16

    def columns_of(weight, count):
        return lax.dynamic_slice_in_dim(weight, seq_index.astype(jnp.uint32) * count, count, 1)

    def hidden_rows(weight):
        tall = jnp.pad(weight, ((0, 4 * window - ff_part), (0, 0)))
        return lax.dynamic_slice_in_dim(tall, seq_index.astype(jnp.uint32) * window, window, 0)

    gains = jnp.concatenate([norm_gain, ffn_gain, query_gain, key_gain])
    gain_count = gains.shape[0]
    qkv_columns = query_columns + 2 * key_columns
    packed_columns = qkv_columns + query_columns
    gain_rows = jnp.pad(gains[None], ((0, 15), (0, packed_columns - gain_count)))
    packed = jnp.concatenate(
        [
            columns_of(query_weight, query_columns),
            columns_of(key_weight, key_columns),
            columns_of(value_weight, key_columns),
            columns_of(out_weight, query_columns),
        ],
        axis=1,
    )
    top = split_rows(own_rows + 16)
    first_ring = GatherRing(
        packed[:top], jnp.concatenate([packed[top:], gain_rows], axis=0), size
    )
    for _ in range(size - 1):
        first_ring.step()
    started = first_ring.ahead[2]
    ffn_ring = GatherRing(
        *pick_hidden(gate_weight, up_weight, seq_index, size, ff_part, window), size
    )
    down_rows = hidden_rows(down_weight)
    down_ring = GatherRing(down_rows[: window // 2], down_rows[window // 2 :], size)
    for step in range(1, size):
        ffn_ring.step(*((started,) if step == 1 else ()))
    for step in range(1, size):
        lag = min(step + 3, size - 1)
        down_ring.step(ffn_ring.ahead[lag], ffn_ring.behind[lag])

    qkv_all, out_part, gains_all = lay_attention(
        first_ring.ahead, first_ring.behind, owners, own_rows, qkv_columns
    )
    gains_all = gains_all[:, 0].astype(f32)
    first_gain = gains_all[:, :own_rows].reshape(-1)
    second_gain = gains_all[:, own_rows : 2 * own_rows].reshape(-1)
    q_gain_f = gains_all[:, 2 * own_rows : 2 * own_rows + head_part].reshape(-1)
    k_gain_f = gains_all[:, 2 * own_rows + head_part : 2 * (own_rows + head_part)].reshape(-1)

    inputs = tokens[0]
    tok_rows = inputs.shape[0]
    length = 4 * tok_rows
    input_blocks = gather_seq(inputs)
    inputs_all = jnp.concatenate(in_order(input_blocks, seq_index), axis=0).astype(f32)
    out_all = jnp.concatenate(
        in_order(gather_seq(out_part, input_blocks[1]), seq_index), axis=1
    )

    normed, norm_unit, norm_inverse = norm_forward(inputs_all, first_gain)
    normed_low = normed.astype(bf16)
    qkv_t = lax.dot_general(
        qkv_all, normed_low, (((0,), (1,)), ((), ())), preferred_element_type=f32
    )
    sizes = (query_columns // head_width, key_columns // head_width, head_width)
    cosine, sine = rope_rows(length, head_width)
    tables = (q_gain_f[:, None], k_gain_f[:, None], cosine, sine)
    mixed_heads, mixed_t, totals = attention_forward(qkv_t, *tables, sizes)
    mixed = jnp.concatenate(in_order(swap_rows(mixed_heads, seq_index), seq_index), axis=1)
    attended = jnp.dot(mixed, out_all, preferred_element_type=f32)
    middle = inputs.astype(f32) + attended
    normed_two, middle_unit, middle_inverse = norm_forward(middle, second_gain)
    normed_blocks = gather_seq(normed_two.astype(bf16))
    normed_two_all = jnp.concatenate(normed_blocks, axis=0)
    out_grad = cotangent[0]
    grad_blocks = gather_seq(out_grad, normed_blocks[1])
    out_grad_all = jnp.concatenate(grad_blocks, axis=0)
    mixed_all = jnp.concatenate(
        in_order(gather_seq(mixed_heads, grad_blocks[1]), seq_index), axis=1
    )

    slope, silu, hidden, gate_all, up_all = ffn_hidden(
        normed_blocks, ffn_ring.ahead, ffn_ring.behind, owners
    )
    gate_grad, up_grad, *normed_parts, down_all = ffn_hidden_grad(
        out_grad_all,
        slope,
        silu,
        gate_all,
        up_all,
        down_ring.ahead,
        down_ring.behind,
        owners,
    )
    normed_two_grad, half_sum = scatter_seq(*normed_parts)
    down_weight_grad = transpose_dot(after(hidden, normed_parts[2]), out_grad_all).astype(bf16)
    down_share = lax.psum_scatter(down_weight_grad, "fsdp", scatter_dimension=0, tiled=True)
    gate_weight_grad = transpose_dot(
        after(normed_two_all, half_sum, down_weight_grad), gate_grad
    ).astype(bf16)
    gate_sums = ScatterRing(
        0, gate_weight_grad.reshape(size, own_rows, size * window), size, owners
    )
    up_weight_grad = transpose_dot(after(normed_two_all, gate_sums.sum), up_grad).astype(bf16)
    up_sums = ScatterRing(1, up_weight_grad.reshape(size, own_rows, size * window), size, owners)
    ffn_gain_grad = jnp.sum(normed_two_grad * middle_unit, axis=0)
    middle_grad = out_grad.astype(f32) + norm_backward(
        normed_two_grad, middle_unit, middle_inverse, second_gain
    )
    attended_low = middle_grad.astype(bf16)
    mixed_grad = dot_transposed(attended_low, out_all).astype(bf16)
    mixed_grad_blocks = swap_columns(mixed_grad, seq_index)
    mixed_grad_heads = jnp.concatenate(in_order(mixed_grad_blocks, seq_index), axis=0)
    qkv_grad, head_gains = attention_backward(
        qkv_t, *tables, mixed_t, totals, mixed_grad_heads, sizes
    )
    attended_blocks = [
        after(block, qkv_grad)
        for block in swap_columns(after(attended_low, mixed_grad), seq_index)
    ]
    attended_columns = jnp.concatenate(in_order(attended_blocks, seq_index), axis=0)
    out_weight_grad = by_rows(transpose_dot(mixed_all, attended_columns).astype(bf16))
    gate_sums.step(qkv_grad)
    up_sums.step(qkv_grad)
    head_gains = jnp.sum(head_gains, axis=1)
    query_gain_grad, key_gain_grad = head_gains[:head_width], head_gains[head_width:]
    qkv_weight_grad = by_rows(transpose_dot(normed_low, qkv_grad).astype(bf16))
    normed_partial = dot_transposed(qkv_grad, qkv_all)
    norm_gain_grad = jnp.sum(normed_partial * norm_unit, axis=0)
    partial_blocks = normed_partial.astype(bf16).reshape(4, tok_rows, width)

    def partial_of(mask):
        index = (seq_index ^ mask).astype(jnp.uint32)
        return lax.dynamic_index_in_dim(partial_blocks, index, 0, keepdims=False)

    normed_grad, normed_sent = scatter_seq(
        partial_of(0),
        partial_of(2),
        jnp.concatenate([partial_of(1), partial_of(3)], axis=0),
    )
    _, own_unit, own_inverse = norm_forward(inputs.astype(f32), first_gain)
    inputs_grad = middle_grad + norm_backward(normed_grad, own_unit, own_inverse, first_gain)

    gain_grads = jnp.concatenate(
        [
            norm_gain_grad.reshape(size, -1),
            ffn_gain_grad.reshape(size, -1),
            query_gain_grad.reshape(size, -1),
            key_gain_grad.reshape(size, -1),
        ],
        axis=1,
    )
    gain_blocks = jnp.pad(
        gain_grads[:, None], ((0, 0), (0, 15), (0, packed_columns - gain_count))
    )
    packed_blocks = jnp.concatenate([qkv_weight_grad, out_weight_grad], axis=1).reshape(
        size, own_rows, packed_columns
    )
    top_blocks = packed_blocks[:, :top]
    bottom_blocks = jnp.concatenate([packed_blocks[:, top:], gain_blocks.astype(bf16)], axis=1)
    gate_sums.step(top_blocks, bottom_blocks)
    up_sums.step(top_blocks, bottom_blocks)
    last_sums = (
        ScatterRing(0, top_blocks, size, owners),
        ScatterRing(1, bottom_blocks, size, owners),
    )
    down_partial = jnp.dot(
        after(hidden, gate_sums.sum), down_all, preferred_element_type=f32
    ).astype(bf16)
    down_sum, down_sent = scatter_seq(
        down_partial[:tok_rows],
        down_partial[tok_rows : 2 * tok_rows],
        down_partial[2 * tok_rows :],
    )
    done = size - 1
    down_pieces = gather_seq(down_share)
    while gate_sums.count < done:
        left = done - gate_sums.count
        needed = {
            4: (down_share, normed_sent),
            3: (down_sent,),
            2: (normed_grad, down_pieces[1]),
            1: (down_sum,),
        }.get(left, ())
        gate_sums.step(*needed)
        up_sums.step(*needed)
        for way in last_sums:
            for _ in range(2 if left in (1, 2, 4) else 1):
                if way.count < done:
                    way.step(*((gate_sums.sum, up_sums.sum) if left > 1 else (down_sum,)))
    for way in last_sums:
        while way.count < done:
            way.step()
    packed_share = jnp.concatenate([way.sum for way in last_sums], axis=0)
    ffn_blocks = gather_seq(jnp.stack([gate_sums.sum, up_sums.sum]))
    output = middle + down_sum
    down_full = jnp.concatenate(in_order(down_pieces, seq_index), axis=0)[
        :ff_part
    ].astype(f32)
    gate_full, up_full = (
        spread_hidden(ffn_blocks, which, seq_index, size, ff_part, window) for which in range(2)
    )
    packs = in_order(gather_seq(packed_share), seq_index)

    def unpack(first, count):
        return jnp.concatenate(
            [p[:own_rows, first : first + count] for p in packs], axis=1
        ).astype(f32)

    gain_sum = sum(p[own_rows, :gain_count].astype(f32) for p in packs)
    return (
        output[None].astype(bf16),
        inputs_grad[None].astype(bf16),
        gain_sum[:own_rows],
        unpack(0, query_columns),
        unpack(query_columns, key_columns),
        unpack(query_columns + key_columns, key_columns),
        gain_sum[2 * own_rows : 2 * own_rows + head_part],
        gain_sum[2 * own_rows + head_part :],
        unpack(qkv_columns, query_columns),
        gain_sum[own_rows : 2 * own_rows],
        gate_full,
        up_full,
        down_full,
    )


def solution(mesh):
    in_specs = (
        P("fsdp", "seq", None),
        P("fsdp"),
        P("fsdp", None),
        P("fsdp", None),
        P("fsdp", None),
        P("fsdp"),
        P("fsdp"),
        P("fsdp", None),
        P("fsdp"),
        P("fsdp", None),
        P("fsdp", None),
        P("fsdp", None),
        P("fsdp", "seq", None),
    )
    out_specs = (
        P("fsdp", "seq", None),
        P("fsdp", "seq", None),
        P("fsdp"),
        P("fsdp", None),
        P("fsdp", None),
        P("fsdp", None),
        P("fsdp"),
        P("fsdp"),
        P("fsdp", None),
        P("fsdp"),
        P("fsdp", None),
        P("fsdp", None),
        P("fsdp", None),
    )
    return jax.shard_map(body, mesh=mesh, in_specs=in_specs, out_specs=out_specs, check_vma=False)
```

```python
import functools
import math

import jax
import jax.numpy as jnp
import numpy as np
from jax import lax
from jax.experimental import pallas as pl
from jax.experimental.layout import Layout, with_layout_constraint
from jax.experimental.pallas import tpu as pltpu
from jax.sharding import PartitionSpec as P

norm_epsilon = 1e-05
TILE = 256
log2_e = math.log2(math.e)


def rope_rows(length, width):
    half_width = width // 2
    inverse = jnp.exp(
        jnp.arange(half_width, dtype=jnp.float32) * (-2.0 * math.log(1000000.0) / width)
    )
    angles = inverse[:, None] * jnp.arange(length, dtype=jnp.int32).astype(jnp.float32)[None, :]
    return jnp.cos(angles), jnp.sin(angles)


def head_norm(values):
    inverse = lax.rsqrt(jnp.mean(values * values, axis=0, keepdims=True) + norm_epsilon)
    return values * inverse, inverse


def head_turn(values, cosine, sine):
    half = values.shape[0] // 2
    first, second = values[:half], values[half:]
    return jnp.concatenate(
        [first * cosine - second * sine, second * cosine + first * sine], axis=0
    )


def head_turn_back(values, cosine, sine):
    half = values.shape[0] // 2
    first, second = values[:half], values[half:]
    return jnp.concatenate(
        [first * cosine + second * sine, second * cosine - first * sine], axis=0
    )


def fill_heads(qkv_ref, q_gain_ref, k_gain_ref, cos_ref, sin_ref, queries, keys, keys_t, values, values_t, sizes):
    heads, groups, width = sizes
    cosine, sine = cos_ref[...], sin_ref[...]

    @pl.loop(0, heads)
    def _(head):
        unit, _ = head_norm(qkv_ref[pl.ds(head * width, width), :])
        turned = head_turn(unit * q_gain_ref[...], cosine, sine)
        queries[head] = (turned * (width**-0.5 * log2_e)).astype(jnp.bfloat16)

    @pl.loop(0, groups)
    def _(group):
        unit, _ = head_norm(qkv_ref[pl.ds((heads + group) * width, width), :])
        turned = head_turn(unit * k_gain_ref[...], cosine, sine)
        keys[group] = turned.T.astype(jnp.bfloat16)
        if keys_t is not None:
            keys_t[group] = turned.astype(jnp.bfloat16)
        value = qkv_ref[pl.ds((heads + groups + group) * width, width), :]
        if values is not None:
            values[group] = value.T.astype(jnp.bfloat16)
        if values_t is not None:
            values_t[group] = value.astype(jnp.bfloat16)


def diagonal_mask():
    key_place = lax.broadcasted_iota(jnp.int32, (TILE, TILE), 0)
    query_place = lax.broadcasted_iota(jnp.int32, (TILE, TILE), 1)
    return key_place <= query_place


def causal_exp(scores, count):
    weights = jnp.exp2(scores)
    last = jnp.where(diagonal_mask(), weights[count - TILE :], 0.0)
    if count == TILE:
        return last
    return jnp.concatenate([weights[: count - TILE], last], axis=0)


def dot(left, right):
    return jnp.dot(left, right, preferred_element_type=jnp.float32)


def dot_nt(left, right):
    return lax.dot_general(
        left, right, (((1,), (1,)), ((), ())), preferred_element_type=jnp.float32
    )


def forward_kernel(sizes, qkv_ref, q_gain_ref, k_gain_ref, cos_ref, sin_ref, mixed_ref, mixed_t_ref, total_ref, queries, keys, values_t, mixed_f):
    heads, groups, width = sizes
    ratio = heads // groups
    length = qkv_ref.shape[1]
    fill_heads(qkv_ref, q_gain_ref, k_gain_ref, cos_ref, sin_ref, queries, keys, None, None, values_t, sizes)

    @pl.loop(0, heads)
    def _(head):
        group = head // ratio
        for tile in range(length // TILE):
            count = (tile + 1) * TILE
            columns = pl.ds(tile * TILE, TILE)
            scores = dot(keys[group, pl.ds(0, count), :], queries[head, :, columns])
            weights = causal_exp(scores, count)
            total = jnp.sum(weights, axis=0, keepdims=True)
            result = dot(values_t[group, :, pl.ds(0, count)], weights.astype(jnp.bfloat16))
            mixed_f[pl.ds(head * width, width), columns] = result * (1.0 / total)
            total_ref[pl.ds(head, 1), columns] = jnp.log2(total)

    for block in range(heads * width // 128):
        rows = mixed_f[pl.ds(block * 128, 128), :]
        mixed_t_ref[pl.ds(block * 128, 128), :] = rows.astype(jnp.bfloat16)
        mixed_ref[:, pl.ds(block * 128, 128)] = rows.T.astype(jnp.bfloat16)


def backward_kernel(sizes, qkv_ref, q_gain_ref, k_gain_ref, cos_ref, sin_ref, mixed_t_ref, total_ref, grad_ref, out_ref, gain_ref, out_t, queries, keys, keys_t, values, grads, key_sum, value_sum):
    heads, groups, width = sizes
    ratio = heads // groups
    length = qkv_ref.shape[1]
    fill_heads(qkv_ref, q_gain_ref, k_gain_ref, cos_ref, sin_ref, queries, keys, keys_t, values, None, sizes)
    for block in range(heads * width // 128):
        turned = grad_ref[:, pl.ds(block * 128, 128)].astype(jnp.float32).T
        grads[pl.ds(block * 128, 128), :] = turned.astype(jnp.bfloat16)
    key_sum[...] = jnp.zeros_like(key_sum)
    value_sum[...] = jnp.zeros_like(value_sum)
    gain_ref[...] = jnp.zeros_like(gain_ref)
    cosine, sine = cos_ref[...], sin_ref[...]

    def finish(grad_turned, rows, gain, first):
        grad = head_turn_back(grad_turned, cosine, sine)
        unit, inverse = head_norm(qkv_ref[rows, :])
        product = grad * unit
        part = product[:, :128]
        for lane in range(128, length, 128):
            part = part + product[:, lane : lane + 128]
        gain_ref[pl.ds(first, width), :] += part
        scaled = grad * gain
        before = inverse * (scaled - unit * jnp.mean(scaled * unit, axis=0, keepdims=True))
        out_t[rows, :] = before

    @pl.loop(0, heads)
    def _(head):
        group = head // ratio
        rows = pl.ds(head * width, width)
        query_parts = []
        for tile in range(length // TILE):
            count = (tile + 1) * TILE
            columns = pl.ds(tile * TILE, TILE)
            query = queries[head, :, columns]
            grad = grads[rows, columns]
            scores = dot(keys[group, pl.ds(0, count), :], query) - total_ref[pl.ds(head, 1), columns]
            weights = causal_exp(scores, count)
            inner = jnp.sum(
                grad.astype(jnp.float32) * mixed_t_ref[rows, columns].astype(jnp.float32),
                axis=0,
                keepdims=True,
            )
            weight_grad = dot(values[group, pl.ds(0, count), :], grad)
            score_grad = (weights * (weight_grad - inner)).astype(jnp.bfloat16)
            query_parts.append(dot(keys_t[group, :, pl.ds(0, count)], score_grad))
            key_sum[group, pl.ds(0, count), :] += dot_nt(score_grad, query)
            value_sum[group, pl.ds(0, count), :] += dot_nt(weights.astype(jnp.bfloat16), grad)
        query_grad = jnp.concatenate(query_parts, axis=1) * width**-0.5
        finish(query_grad, rows, q_gain_ref[...], 0)

    for group in range(groups):
        key_grad = key_sum[group].T * (1.0 / log2_e)
        finish(key_grad, pl.ds((heads + group) * width, width), k_gain_ref[...], width)
        out_t[pl.ds((heads + groups + group) * width, width), :] = value_sum[group].T

    for block in range(out_t.shape[0] // 128):
        some = pl.ds(block * 128, 128)
        out_ref[:, some] = out_t[some, :].T.astype(jnp.bfloat16)


def attention_forward(qkv_t, q_gain, k_gain, cosine, sine, sizes):
    heads, groups, width = sizes
    length = qkv_t.shape[1]
    bf16, f32 = jnp.bfloat16, jnp.float32
    pairs = heads * length * length
    return pl.pallas_call(
        functools.partial(forward_kernel, sizes),
        out_shape=(
            jax.ShapeDtypeStruct((length, heads * width), bf16),
            jax.ShapeDtypeStruct((heads * width, length), bf16),
            jax.ShapeDtypeStruct((-(-heads // 8) * 8, length), f32),
        ),
        scratch_shapes=[
            pltpu.VMEM((heads, width, length), bf16),
            pltpu.VMEM((groups, length, width), bf16),
            pltpu.VMEM((groups, width, length), bf16),
            pltpu.VMEM((heads * width, length), f32),
        ],
        compiler_params=pltpu.CompilerParams(vmem_limit_bytes=32 * 2**20),
        cost_estimate=pl.CostEstimate(
            flops=8 * pairs * width, bytes_accessed=6 * 2**20, transcendentals=pairs
        ),
    )(qkv_t, q_gain, k_gain, cosine, sine)


def attention_backward(qkv_t, q_gain, k_gain, cosine, sine, mixed_t, total, mixed_grad, sizes):
    heads, groups, width = sizes
    length = qkv_t.shape[1]
    bf16, f32 = jnp.bfloat16, jnp.float32
    pairs = heads * length * length
    return pl.pallas_call(
        functools.partial(backward_kernel, sizes),
        out_shape=(
            jax.ShapeDtypeStruct(qkv_t.shape[::-1], bf16),
            jax.ShapeDtypeStruct((2 * width, 128), f32),
        ),
        scratch_shapes=[
            pltpu.VMEM(qkv_t.shape, f32),
            pltpu.VMEM((heads, width, length), bf16),
            pltpu.VMEM((groups, length, width), bf16),
            pltpu.VMEM((groups, width, length), bf16),
            pltpu.VMEM((groups, length, width), bf16),
            pltpu.VMEM((heads * width, length), bf16),
            pltpu.VMEM((groups, length, width), f32),
            pltpu.VMEM((groups, length, width), f32),
        ],
        compiler_params=pltpu.CompilerParams(vmem_limit_bytes=40 * 2**20),
        cost_estimate=pl.CostEstimate(flops=0, bytes_accessed=2**20, transcendentals=0),
    )(qkv_t, q_gain, k_gain, cosine, sine, mixed_t, total, mixed_grad)


def hidden_kernel(size, ids_ref, *refs):
    pieces, chunks, refs = refs[:4], refs[4 : 4 + 2 * size], refs[4 + 2 * size :]
    slope_ref, silu_ref, hidden_ref, gate_out, up_out, tokens, gate, up, *sems = refs
    row_sems, in_sems, out_sems = sems
    step = pl.program_id(0)
    steps = pl.num_programs(0)
    rows = chunks[0].shape[0]
    piece = pieces[0].shape[0]

    @pl.when(step == 0)
    def _():
        copies = [
            pltpu.make_async_copy(
                source, tokens.at[pl.ds(index * piece, piece), :], row_sems.at[index]
            )
            for index, source in enumerate(pieces)
        ]
        for copy in copies:
            copy.start()

        @pl.loop(0, steps)
        def _(tile):
            columns = pl.ds(pl.multiple_of(tile * TILE, TILE), TILE)
            for which, target in ((0, gate), (1, up)):
                for index in range(size):
                    first = pl.multiple_of(ids_ref[which, index] * rows, 16)
                    pltpu.make_async_copy(
                        chunks[which * size + index].at[:, columns],
                        target.at[pl.ds(first, rows), columns],
                        in_sems.at[which, tile],
                    ).start()

        for copy in copies:
            copy.wait()

    columns = pl.ds(pl.multiple_of(step * TILE, TILE), TILE)
    for which, target, result in ((0, gate, gate_out), (1, up, up_out)):
        part = target.at[:, columns]
        pltpu.make_async_copy(part, part, in_sems.at[which, step]).wait()
        pltpu.make_async_copy(part, result.at[:, columns], out_sems.at[which, step]).start()
    for half in range(2):
        some = pl.ds(half * 2 * piece, 2 * piece)
        gate_act = dot(tokens[some, :], gate[:, columns])
        up_act = dot(tokens[some, :], up[:, columns])
        sigmoid = 0.5 + 0.5 * jnp.tanh(0.5 * gate_act)
        silu = gate_act * sigmoid
        hidden_ref[some, :] = (silu * up_act).astype(hidden_ref.dtype)
        silu_ref[some, :] = silu.astype(silu_ref.dtype)
        slope_ref[some, :] = (up_act * sigmoid * (1.0 + gate_act * (1.0 - sigmoid))).astype(
            slope_ref.dtype
        )

    @pl.when(step == steps - 1)
    def _():
        @pl.loop(0, steps)
        def _(tile):
            columns = pl.ds(pl.multiple_of(tile * TILE, TILE), TILE)
            for which, target, result in ((0, gate, gate_out), (1, up, up_out)):
                pltpu.make_async_copy(
                    target.at[:, columns], result.at[:, columns], out_sems.at[which, tile]
                ).wait()


def ffn_hidden(pieces, gate_chunks, up_chunks, ids):
    size = len(gate_chunks)
    part, columns = gate_chunks[0].shape
    piece, width = pieces[0].shape
    length = 4 * piece
    bf16 = jnp.bfloat16
    tall = pl.BlockSpec((length, TILE), lambda i, ids: (0, i))
    act = jax.ShapeDtypeStruct((length, columns), bf16)
    weight = jax.ShapeDtypeStruct((width, columns), bf16)
    anywhere = pl.BlockSpec(memory_space=pl.ANY)
    return pl.pallas_call(
        functools.partial(hidden_kernel, size),
        grid_spec=pltpu.PrefetchScalarGridSpec(
            num_scalar_prefetch=1,
            grid=(columns // TILE,),
            in_specs=[anywhere] * (4 + 2 * size),
            out_specs=[tall, tall, tall, anywhere, anywhere],
            scratch_shapes=[
                pltpu.VMEM((length, width), bf16),
                pltpu.VMEM((width, columns), bf16),
                pltpu.VMEM((width, columns), bf16),
                pltpu.SemaphoreType.DMA((4,)),
                pltpu.SemaphoreType.DMA((2, columns // TILE)),
                pltpu.SemaphoreType.DMA((2, columns // TILE)),
            ],
        ),
        out_shape=(act, act, act, weight, weight),
        compiler_params=pltpu.CompilerParams(vmem_limit_bytes=56 * 2**20),
        cost_estimate=pl.CostEstimate(
            flops=4 * length * width * columns,
            bytes_accessed=36 * 2**20,
            transcendentals=length * columns,
        ),
    )(ids, *pieces, *gate_chunks, *up_chunks)


def hidden_grad_kernel(size, owners_ref, grad_ref, slope_ref, silu_ref, *refs):
    chunks, refs = refs[: 2 * size], refs[2 * size :]
    gate_out, up_out, down_out, down, in_sems, out_sem = refs
    step = pl.program_id(0)
    rows = chunks[0].shape[0]

    @pl.when(step == 0)
    def _():
        copies = []
        for which in range(2):
            for index in range(size):
                first = pl.multiple_of((2 * owners_ref[which, index] + which) * rows, 16)
                copies.append(
                    pltpu.make_async_copy(
                        chunks[which * size + index],
                        down.at[pl.ds(first, rows), :],
                        in_sems.at[which, index],
                    )
                )
        for copy in copies:
            copy.start()
        for copy in copies:
            copy.wait()
        pltpu.make_async_copy(down, down_out, out_sem).start()

    weight = down[pl.ds(pl.multiple_of(step * TILE, TILE), TILE), :]
    hidden_grad = dot_nt(grad_ref[...], weight)
    gate_out[...] = (hidden_grad * slope_ref[...].astype(jnp.float32)).astype(jnp.bfloat16)
    up_out[...] = (hidden_grad * silu_ref[...].astype(jnp.float32)).astype(jnp.bfloat16)

    @pl.when(step == pl.num_programs(0) - 1)
    def _():
        pltpu.make_async_copy(down, down_out, out_sem).wait()


def ffn_hidden_grad(out_grad, slope, silu, ahead, behind, owners):
    size = len(ahead)
    length, width = out_grad.shape
    columns = slope.shape[1]
    bf16 = jnp.bfloat16
    tall = pl.BlockSpec((length, TILE), lambda i, owners: (0, i))
    anywhere = pl.BlockSpec(memory_space=pl.ANY)
    act = jax.ShapeDtypeStruct((length, columns), bf16)
    weight = (2 * size * ahead[0].shape[0], width)
    return pl.pallas_call(
        functools.partial(hidden_grad_kernel, size),
        grid_spec=pltpu.PrefetchScalarGridSpec(
            num_scalar_prefetch=1,
            grid=(columns // TILE,),
            in_specs=[pl.BlockSpec((length, width), lambda i, owners: (0, 0)), tall, tall]
            + [anywhere] * (2 * size),
            out_specs=[tall, tall, anywhere],
            scratch_shapes=[
                pltpu.VMEM(weight, bf16),
                pltpu.SemaphoreType.DMA((2, size)),
                pltpu.SemaphoreType.DMA,
            ],
        ),
        out_shape=(act, act, jax.ShapeDtypeStruct(weight, bf16)),
        compiler_params=pltpu.CompilerParams(vmem_limit_bytes=56 * 2**20),
        cost_estimate=pl.CostEstimate(flops=0, bytes_accessed=2**20, transcendentals=0),
    )(owners, out_grad, slope, silu, *ahead, *behind)


def rows_grad_kernel(gate_grad_ref, up_grad_ref, gate_ref, up_ref, own_ref, other_ref, sent_ref):
    piece = own_ref.shape[0]
    total = dot_nt(gate_grad_ref[...], gate_ref[...]) + dot_nt(up_grad_ref[...], up_ref[...])
    total = total.astype(jnp.bfloat16)
    own_ref[...] = total[:piece]
    other_ref[...] = total[piece : 2 * piece]
    sent_ref[...] = total[2 * piece :]


def ffn_rows_grad(gate_grad, up_grad, gate, up):
    length, columns = gate_grad.shape
    width = gate.shape[0]
    piece = length // 4
    bf16 = jnp.bfloat16
    whole = pl.BlockSpec((length, columns), lambda i: (0, 0))
    weight = pl.BlockSpec((TILE, columns), lambda i: (i, 0))
    part = pl.BlockSpec((piece, TILE), lambda i: (0, i))
    return pl.pallas_call(
        rows_grad_kernel,
        grid=(width // TILE,),
        in_specs=[whole, whole, weight, weight],
        out_specs=[part, part, pl.BlockSpec((2 * piece, TILE), lambda i: (0, i))],
        out_shape=(
            jax.ShapeDtypeStruct((piece, width), bf16),
            jax.ShapeDtypeStruct((piece, width), bf16),
            jax.ShapeDtypeStruct((2 * piece, width), bf16),
        ),
        compiler_params=pltpu.CompilerParams(vmem_limit_bytes=56 * 2**20),
        cost_estimate=pl.CostEstimate(flops=0, bytes_accessed=2**20, transcendentals=0),
    )(gate_grad, up_grad, gate, up)


def lay_kernel(size, sizes, owners_ref, *refs):
    chunks, refs = refs[: 2 * size], refs[2 * size :]
    qkv_out, out_out, gains_out, sems = refs
    rows, top, qkv_columns, columns = sizes
    copies = []
    for which, count in ((0, top), (1, rows - top)):
        for index in range(size):
            chunk = chunks[which * size + index]
            owner = owners_ref[which, index]
            first = pl.multiple_of(owner * rows + which * top, 16)
            target = pl.ds(first, count)
            pairs = [
                (chunk.at[pl.ds(0, count), pl.ds(0, qkv_columns)], qkv_out.at[target, :]),
                (
                    chunk.at[pl.ds(0, count), pl.ds(qkv_columns, columns - qkv_columns)],
                    out_out.at[target, :],
                ),
            ]
            if which:
                pairs.append((chunk.at[pl.ds(count, 16), :], gains_out.at[owner]))
            for kind, (source, place) in enumerate(pairs):
                copies.append(pltpu.make_async_copy(source, place, sems.at[kind, which, index]))
    for copy in copies:
        copy.start()
    for copy in copies:
        copy.wait()


def lay_attention(ahead, behind, owners, rows, qkv_columns):
    size = len(ahead)
    top, columns = ahead[0].shape
    bf16 = jnp.bfloat16
    anywhere = pl.BlockSpec(memory_space=pl.ANY)
    return pl.pallas_call(
        functools.partial(lay_kernel, size, (rows, top, qkv_columns, columns)),
        grid_spec=pltpu.PrefetchScalarGridSpec(
            num_scalar_prefetch=1,
            grid=(1,),
            in_specs=[anywhere] * (2 * size),
            out_specs=[pl.BlockSpec(memory_space=pltpu.VMEM)] * 3,
            scratch_shapes=[pltpu.SemaphoreType.DMA((3, 2, size))],
        ),
        out_shape=(
            jax.ShapeDtypeStruct((size * rows, qkv_columns), bf16),
            jax.ShapeDtypeStruct((size * rows, columns - qkv_columns), bf16),
            jax.ShapeDtypeStruct((size, 16, columns), bf16),
        ),
        cost_estimate=pl.CostEstimate(flops=0, bytes_accessed=7 * 2**20, transcendentals=0),
    )(owners, *ahead, *behind)


def pick_kernel(sizes, index_ref, gate_ref, up_ref, gate_out, up_out):
    size, part, window = sizes
    rows = gate_ref.shape[0]
    for source, target in ((gate_ref, gate_out), (up_ref, up_out)):
        for index in range(4):
            count = min(window, part - index * window)

            @pl.when(index_ref[0] == index)
            def _():
                parts = []
                for owner in range(size):
                    first = owner * part + index * window
                    low, high = first // 128 * 128, -(-(first + count) // 128) * 128
                    wide = source[:, low:high].astype(jnp.float32)
                    parts.append(wide[:, first - low : first - low + count])
                    if count < window:
                        parts.append(jnp.zeros((rows, window - count), jnp.float32))
                target[...] = jnp.concatenate(parts, axis=1).astype(target.dtype)


def pick_hidden(gate, up, seq_index, size, part, window):
    rows, columns = gate.shape
    block = 48 if rows % 48 == 0 else rows
    wide = pl.BlockSpec((block, columns), lambda i, index: (i, 0))
    narrow = pl.BlockSpec((block, size * window), lambda i, index: (i, 0))
    out = jax.ShapeDtypeStruct((rows, size * window), gate.dtype)
    return pl.pallas_call(
        functools.partial(pick_kernel, (size, part, window)),
        grid_spec=pltpu.PrefetchScalarGridSpec(
            num_scalar_prefetch=1,
            grid=(rows // block,),
            in_specs=[wide, wide],
            out_specs=[narrow, narrow],
        ),
        out_shape=(out, out),
        compiler_params=pltpu.CompilerParams(vmem_limit_bytes=32 * 2**20),
        cost_estimate=pl.CostEstimate(flops=0, bytes_accessed=8 * 2**20, transcendentals=0),
    )(jnp.reshape(seq_index, (1,)).astype(jnp.int32), gate, up)


def spread_kernel(sizes, index_ref, own_ref, other_ref, near_ref, far_ref, out_ref, parts):
    size, part, window = sizes
    me = index_ref[0]
    parts[me] = own_ref[...]
    parts[me ^ 2] = other_ref[...]
    parts[me ^ 1] = near_ref[...]
    parts[me ^ 3] = far_ref[...]
    pieces = []
    for owner in range(size):
        for index in range(4):
            count = min(window, part - index * window)
            first = owner * window
            low, high = first // 128 * 128, -(-(first + count) // 128) * 128
            wide = parts[index, :, low:high].astype(jnp.float32)
            pieces.append(wide[:, first - low : first - low + count])
    out_ref[...] = jnp.concatenate(pieces, axis=1)


def spread_hidden(pieces, which, seq_index, size, part, window):
    _, rows, columns = pieces[0].shape
    block = 48 if rows % 48 == 0 else rows
    narrow = pl.BlockSpec((None, block, columns), lambda i, index: (which, i, 0))
    return pl.pallas_call(
        functools.partial(spread_kernel, (size, part, window)),
        grid_spec=pltpu.PrefetchScalarGridSpec(
            num_scalar_prefetch=1,
            grid=(rows // block,),
            in_specs=[narrow] * 4,
            out_specs=pl.BlockSpec((block, size * part), lambda i, index: (i, 0)),
            scratch_shapes=[pltpu.VMEM((4, block, columns), pieces[0].dtype)],
        ),
        out_shape=jax.ShapeDtypeStruct((rows, size * part), jnp.float32),
        compiler_params=pltpu.CompilerParams(vmem_limit_bytes=32 * 2**20),
        cost_estimate=pl.CostEstimate(flops=0, bytes_accessed=64 * 2**20, transcendentals=0),
    )(jnp.reshape(seq_index, (1,)), *pieces)


def norm_forward(values, gain):
    inverse = lax.rsqrt(jnp.mean(values * values, axis=-1, keepdims=True) + norm_epsilon)
    unit = values * inverse
    return (unit * gain, unit, inverse)


def norm_backward(grad_in, unit, inverse, gain):
    scaled = grad_in * gain
    return inverse * (scaled - unit * jnp.mean(scaled * unit, axis=-1, keepdims=True))


def transpose_dot(left, right):
    return lax.dot_general(
        left, right, (((0,), (0,)), ((), ())), preferred_element_type=jnp.float32
    )


def by_rows(values):
    return with_layout_constraint(values, Layout(major_to_minor=(0, 1)))


def dot_transposed(left, right):
    return lax.dot_general(
        left, right, (((1,), (1,)), ((), ())), preferred_element_type=jnp.float32
    )


def split_rows(rows):
    return (rows // 32) * 16


def ring_ids(size):
    return list(range(0, size, 2)) + [i for i in range(size - 1, 0, -1) if i % 2]


def ring_perms(size):
    ids = ring_ids(size)
    forward = [(ids[i], ids[(i + 1) % size]) for i in range(size)]
    return forward, [(b, a) for a, b in forward]


def ring_owners(size):
    ids = ring_ids(size)
    table = np.zeros((size, 4, size), np.int32)
    for place, device in enumerate(ids):
        for step in range(size):
            table[device, 0, step] = ids[(place - step) % size]
            table[device, 1, step] = ids[(place + step) % size]
            table[device, 2, step] = ids[(place - 1 - step) % size]
            table[device, 3, step] = ids[(place + 1 + step) % size]
    return lax.dynamic_index_in_dim(
        jnp.asarray(table), lax.axis_index("fsdp").astype(jnp.uint32), 0, keepdims=False
    )


def after(value, *needed):
    return lax.optimization_barrier((value, *needed))[0] if needed else value


class GatherRing:
    def __init__(self, ahead, behind, size):
        self.perms = ring_perms(size)
        self.ahead, self.behind = [ahead], [behind]

    def step(self, *needed):
        forward, backward = self.perms
        self.ahead.append(lax.ppermute(after(self.ahead[-1], *needed), "fsdp", forward))
        self.behind.append(lax.ppermute(after(self.behind[-1], *needed), "fsdp", backward))


class ScatterRing:
    def __init__(self, way, blocks, size, owners):
        self.perm = ring_perms(size)[way]
        self.owners = lax.squeeze(lax.slice_in_dim(owners, 2 + way, 3 + way), (0,)).astype(
            jnp.uint32
        )
        self.blocks, self.count = blocks, 0
        self.sum = self.own().astype(jnp.bfloat16)

    def own(self):
        owner = lax.squeeze(lax.slice_in_dim(self.owners, self.count, self.count + 1), (0,))
        zero = jnp.uint32(0)
        shape = (1, *self.blocks.shape[1:])
        return lax.dynamic_slice(self.blocks, (owner, zero, zero), shape)[0].astype(jnp.float32)

    def step(self, *needed):
        came = after(lax.ppermute(self.sum, "fsdp", self.perm), *needed)
        self.count += 1
        self.sum = (came.astype(jnp.float32) + self.own()).astype(jnp.bfloat16)
        return self.sum


def exchange(values, mask):
    return lax.ppermute(values, "seq", [(i, i ^ mask) for i in range(4)])


def gather_seq(block, *needed):
    block = after(block, *needed)
    other = exchange(block, 2)
    return [block, other, exchange(block, 1), exchange(other, 1)]


def in_order(pieces, seq_index):
    high, low = seq_index // 2, seq_index % 2

    def pick(first, second, flag):
        return jnp.where(flag == 0, first, second), jnp.where(flag == 0, second, first)

    mine = pick(pieces[0], pieces[1], high)
    theirs = pick(pieces[2], pieces[3], high)
    return [*pick(mine[0], theirs[0], low), *pick(mine[1], theirs[1], low)]


def scatter_seq(own, other, there):
    rows = own.shape[0]
    came = exchange(there, 1).astype(jnp.float32)
    sent = (other.astype(jnp.float32) + came[rows:]).astype(jnp.bfloat16)
    near = own.astype(jnp.float32) + came[:rows]
    return near + exchange(sent, 2).astype(jnp.float32), sent


def swap(blocks):
    return lax.all_to_all(blocks, "seq", split_axis=0, concat_axis=0, tiled=True)


def side_by_side(blocks):
    return blocks.transpose(1, 0, 2).reshape(blocks.shape[1], -1)


def apart(values):
    return values.reshape(values.shape[0], 4, -1).transpose(1, 0, 2)


def body(
    tokens,
    norm_gain,
    query_weight,
    key_weight,
    value_weight,
    query_gain,
    key_gain,
    out_weight,
    ffn_gain,
    gate_weight,
    up_weight,
    down_weight,
    cotangent,
):
    bf16, f32 = jnp.bfloat16, jnp.float32
    size = lax.axis_size("fsdp")
    seq_index = lax.axis_index("seq")
    owners = ring_owners(size)
    own_rows, width = query_weight.shape
    head_part = query_gain.shape[0]
    head_width = head_part * size
    query_columns = width // 4
    key_columns = key_weight.shape[1] // 4
    ff_part = down_weight.shape[0]
    window = -(-ff_part // 64) * 16

    def columns_of(weight, count):
        return lax.dynamic_slice_in_dim(weight, seq_index.astype(jnp.uint32) * count, count, 1)

    def hidden_rows(weight):
        tall = jnp.pad(weight, ((0, 4 * window - ff_part), (0, 0)))
        return lax.dynamic_slice_in_dim(tall, seq_index.astype(jnp.uint32) * window, window, 0)

    gains = jnp.concatenate([norm_gain, ffn_gain, query_gain, key_gain])
    gain_count = gains.shape[0]
    qkv_columns = query_columns + 2 * key_columns
    packed_columns = qkv_columns + query_columns
    gain_rows = jnp.pad(gains[None], ((0, 15), (0, packed_columns - gain_count)))
    packed = jnp.concatenate(
        [
            columns_of(query_weight, query_columns),
            columns_of(key_weight, key_columns),
            columns_of(value_weight, key_columns),
            columns_of(out_weight, query_columns),
        ],
        axis=1,
    )
    top = split_rows(own_rows + 16)
    first_ring = GatherRing(
        packed[:top], jnp.concatenate([packed[top:], gain_rows], axis=0), size
    )
    for _ in range(size - 1):
        first_ring.step()
    ffn_ring = GatherRing(
        *pick_hidden(gate_weight, up_weight, seq_index, size, ff_part, window), size
    )
    down_rows = hidden_rows(down_weight)
    down_ring = GatherRing(down_rows[: window // 2], down_rows[window // 2 :], size)
    for step in range(1, size):
        ffn_ring.step()
    for step in range(1, size):
        lag = min(step + 1, size - 1)
        down_ring.step(ffn_ring.ahead[lag], ffn_ring.behind[lag])

    qkv_all, out_part, gains_all = lay_attention(
        first_ring.ahead, first_ring.behind, owners, own_rows, qkv_columns
    )
    gains_all = gains_all[:, 0].astype(f32)
    first_gain = gains_all[:, :own_rows].reshape(-1)
    second_gain = gains_all[:, own_rows : 2 * own_rows].reshape(-1)
    q_gain_f = gains_all[:, 2 * own_rows : 2 * own_rows + head_part].reshape(-1)
    k_gain_f = gains_all[:, 2 * own_rows + head_part : 2 * (own_rows + head_part)].reshape(-1)

    inputs = tokens[0]
    tok_rows = inputs.shape[0]
    length = 4 * tok_rows
    input_blocks = gather_seq(inputs)
    inputs_all = jnp.concatenate(in_order(input_blocks, seq_index), axis=0).astype(f32)
    out_grad = cotangent[0]
    grad_blocks = gather_seq(out_grad, input_blocks[1])
    out_grad_all = jnp.concatenate(grad_blocks, axis=0)
    out_all = jnp.concatenate(
        in_order(gather_seq(out_part, input_blocks[1]), seq_index), axis=1
    )

    normed, norm_unit, norm_inverse = norm_forward(inputs_all, first_gain)
    normed_low = normed.astype(bf16)
    qkv_t = lax.dot_general(
        qkv_all, normed_low, (((0,), (1,)), ((), ())), preferred_element_type=f32
    )
    sizes = (query_columns // head_width, key_columns // head_width, head_width)
    cosine, sine = rope_rows(length, head_width)
    tables = (q_gain_f[:, None], k_gain_f[:, None], cosine, sine)
    mixed_heads, mixed_t, totals = attention_forward(qkv_t, *tables, sizes)
    mixed = side_by_side(swap(mixed_heads.reshape(4, tok_rows, query_columns)))
    attended = jnp.dot(mixed, out_all, preferred_element_type=f32)
    middle = inputs.astype(f32) + attended
    normed_two, middle_unit, middle_inverse = norm_forward(middle, second_gain)
    normed_blocks = gather_seq(normed_two.astype(bf16))
    normed_two_all = jnp.concatenate(normed_blocks, axis=0)
    mixed_all = jnp.concatenate(
        in_order(gather_seq(mixed_heads, normed_blocks[1]), seq_index), axis=1
    )

    slope, silu, hidden, gate_all, up_all = ffn_hidden(
        normed_blocks, ffn_ring.ahead, ffn_ring.behind, owners
    )
    down_weight_grad = transpose_dot(hidden, out_grad_all).astype(bf16)
    down_blocks = down_weight_grad.reshape(size, window, width)
    down_sums = (ScatterRing(0, down_blocks, size, owners),)
    gate_grad, up_grad, down_all = ffn_hidden_grad(
        after(out_grad_all, *(way.sum for way in down_sums)),
        slope,
        silu,
        down_ring.ahead,
        down_ring.behind,
        owners,
    )
    gate_weight_grad = transpose_dot(normed_two_all, gate_grad).astype(bf16)
    gate_sums = ScatterRing(
        0, gate_weight_grad.reshape(size, own_rows, size * window), size, owners
    )
    up_weight_grad = transpose_dot(after(normed_two_all, gate_sums.sum), up_grad).astype(bf16)
    up_sums = ScatterRing(1, up_weight_grad.reshape(size, own_rows, size * window), size, owners)
    ffn_sums = (gate_sums, up_sums)
    normed_parts = ffn_rows_grad(after(gate_grad, up_sums.sum), up_grad, gate_all, up_all)
    normed_two_grad, half_sum = scatter_seq(*normed_parts)

    def advance(rings, *needed):
        for way in rings:
            if way.count < size - 1:
                way.step(*needed)

    advance(down_sums, gate_grad)
    advance(ffn_sums, normed_parts[0])
    advance(down_sums, normed_parts[0])
    advance(ffn_sums, half_sum)
    advance(down_sums, half_sum)
    ffn_gain_grad = jnp.sum(normed_two_grad * middle_unit, axis=0)
    middle_grad = out_grad.astype(f32) + norm_backward(
        normed_two_grad, middle_unit, middle_inverse, second_gain
    )
    attended_low = middle_grad.astype(bf16)
    mixed_grad = dot_transposed(attended_low, out_all).astype(bf16)
    advance(ffn_sums, mixed_grad)
    advance(down_sums, mixed_grad)
    mixed_grad_heads = swap(apart(mixed_grad)).reshape(length, query_columns)
    qkv_grad, head_gains = attention_backward(
        qkv_t, *tables, mixed_t, totals, mixed_grad_heads, sizes
    )
    attended_columns = after(
        swap(apart(after(attended_low, mixed_grad_heads))), qkv_grad
    ).reshape(length, query_columns)
    out_weight_grad = by_rows(transpose_dot(mixed_all, attended_columns).astype(bf16))
    advance(ffn_sums, qkv_grad)
    advance(down_sums, qkv_grad)
    qkv_grad = after(qkv_grad, gate_sums.sum, up_sums.sum)
    head_gains = jnp.sum(head_gains, axis=1)
    query_gain_grad, key_gain_grad = head_gains[:head_width], head_gains[head_width:]
    qkv_weight_grad = by_rows(transpose_dot(normed_low, qkv_grad).astype(bf16))
    normed_partial = dot_transposed(qkv_grad, qkv_all)
    norm_gain_grad = jnp.sum(normed_partial * norm_unit, axis=0)
    partial_blocks = normed_partial.astype(bf16).reshape(4, tok_rows, width)

    def partial_of(mask):
        index = (seq_index ^ mask).astype(jnp.uint32)
        return lax.dynamic_index_in_dim(partial_blocks, index, 0, keepdims=False)

    normed_grad, normed_sent = scatter_seq(
        partial_of(0),
        partial_of(2),
        jnp.concatenate([partial_of(1), partial_of(3)], axis=0),
    )
    _, own_unit, own_inverse = norm_forward(inputs.astype(f32), first_gain)
    inputs_grad = middle_grad + norm_backward(normed_grad, own_unit, own_inverse, first_gain)

    gain_grads = jnp.concatenate(
        [
            norm_gain_grad.reshape(size, -1),
            ffn_gain_grad.reshape(size, -1),
            query_gain_grad.reshape(size, -1),
            key_gain_grad.reshape(size, -1),
        ],
        axis=1,
    )
    gain_blocks = jnp.pad(
        gain_grads[:, None], ((0, 0), (0, 15), (0, packed_columns - gain_count))
    )
    packed_blocks = jnp.concatenate([qkv_weight_grad, out_weight_grad], axis=1).reshape(
        size, own_rows, packed_columns
    )
    packed_blocks = jnp.concatenate([packed_blocks, gain_blocks.astype(bf16)], axis=1)
    advance(ffn_sums, packed_blocks)
    advance(down_sums, packed_blocks)
    last_sums = (ScatterRing(1, packed_blocks, size, owners),)
    down_partial = jnp.dot(
        after(hidden, gate_sums.sum), down_all, preferred_element_type=f32
    ).astype(bf16)
    down_sum, down_sent = scatter_seq(
        down_partial[:tok_rows],
        down_partial[tok_rows : 2 * tok_rows],
        down_partial[2 * tok_rows :],
    )
    needed = (normed_sent,)
    while gate_sums.count < size - 1:
        advance(ffn_sums, *needed)
        advance(down_sums, *needed)
        advance(last_sums, gate_sums.sum, up_sums.sum)
        advance(last_sums, gate_sums.sum, up_sums.sum)
        needed = (down_sent,)
    advance(down_sums)
    both = jnp.stack([gate_sums.sum, up_sums.sum])
    while last_sums[0].count < size - 1:
        advance(last_sums, both)
    down_share = down_sums[0].sum
    down_pieces = gather_seq(down_share)
    packed_share = last_sums[0].sum
    ffn_blocks = gather_seq(both)
    output = middle + down_sum
    down_full = jnp.concatenate(in_order(down_pieces, seq_index), axis=0)[
        :ff_part
    ].astype(f32)
    gate_full, up_full = (
        spread_hidden(ffn_blocks, which, seq_index, size, ff_part, window) for which in range(2)
    )
    packs = in_order(gather_seq(packed_share), seq_index)

    def unpack(first, count):
        return jnp.concatenate(
            [p[:own_rows, first : first + count] for p in packs], axis=1
        ).astype(f32)

    gain_sum = sum(p[own_rows, :gain_count].astype(f32) for p in packs)
    return (
        output[None].astype(bf16),
        inputs_grad[None].astype(bf16),
        gain_sum[:own_rows],
        unpack(0, query_columns),
        unpack(query_columns, key_columns),
        unpack(query_columns + key_columns, key_columns),
        gain_sum[2 * own_rows : 2 * own_rows + head_part],
        gain_sum[2 * own_rows + head_part :],
        unpack(qkv_columns, query_columns),
        gain_sum[own_rows : 2 * own_rows],
        gate_full,
        up_full,
        down_full,
    )


def solution(mesh):
    in_specs = (
        P("fsdp", "seq", None),
        P("fsdp"),
        P("fsdp", None),
        P("fsdp", None),
        P("fsdp", None),
        P("fsdp"),
        P("fsdp"),
        P("fsdp", None),
        P("fsdp"),
        P("fsdp", None),
        P("fsdp", None),
        P("fsdp", None),
        P("fsdp", "seq", None),
    )
    out_specs = (
        P("fsdp", "seq", None),
        P("fsdp", "seq", None),
        P("fsdp"),
        P("fsdp", None),
        P("fsdp", None),
        P("fsdp", None),
        P("fsdp"),
        P("fsdp"),
        P("fsdp", None),
        P("fsdp"),
        P("fsdp", None),
        P("fsdp", None),
        P("fsdp", None),
    )
    return jax.shard_map(body, mesh=mesh, in_specs=in_specs, out_specs=out_specs, check_vma=False)
```

```python
import functools
import math

import jax
import jax.numpy as jnp
import numpy as np
from jax import lax
from jax.experimental import pallas as pl
from jax.experimental.layout import Layout, with_layout_constraint
from jax.experimental.pallas import tpu as pltpu
from jax.sharding import PartitionSpec as P

norm_epsilon = 1e-05
TILE = 256
log2_e = math.log2(math.e)


def rope_rows(length, width):
    half_width = width // 2
    inverse = jnp.exp(
        jnp.arange(half_width, dtype=jnp.float32) * (-2.0 * math.log(1000000.0) / width)
    )
    angles = inverse[:, None] * jnp.arange(length, dtype=jnp.int32).astype(jnp.float32)[None, :]
    return jnp.cos(angles), jnp.sin(angles)


def head_norm(values):
    inverse = lax.rsqrt(jnp.mean(values * values, axis=0, keepdims=True) + norm_epsilon)
    return values * inverse, inverse


def head_turn(values, cosine, sine):
    half = values.shape[0] // 2
    first, second = values[:half], values[half:]
    return jnp.concatenate(
        [first * cosine - second * sine, second * cosine + first * sine], axis=0
    )


def head_turn_back(values, cosine, sine):
    half = values.shape[0] // 2
    first, second = values[:half], values[half:]
    return jnp.concatenate(
        [first * cosine + second * sine, second * cosine - first * sine], axis=0
    )


def fill_heads(qkv_ref, q_gain_ref, k_gain_ref, cos_ref, sin_ref, queries, keys, keys_t, values, values_t, sizes):
    heads, groups, width = sizes
    cosine, sine = cos_ref[...], sin_ref[...]

    @pl.loop(0, heads)
    def _(head):
        unit, _ = head_norm(qkv_ref[pl.ds(head * width, width), :])
        turned = head_turn(unit * q_gain_ref[...], cosine, sine)
        queries[head] = (turned * (width**-0.5 * log2_e)).astype(jnp.bfloat16)

    @pl.loop(0, groups)
    def _(group):
        unit, _ = head_norm(qkv_ref[pl.ds((heads + group) * width, width), :])
        turned = head_turn(unit * k_gain_ref[...], cosine, sine)
        keys[group] = turned.T.astype(jnp.bfloat16)
        if keys_t is not None:
            keys_t[group] = turned.astype(jnp.bfloat16)
        value = qkv_ref[pl.ds((heads + groups + group) * width, width), :]
        if values is not None:
            values[group] = value.T.astype(jnp.bfloat16)
        if values_t is not None:
            values_t[group] = value.astype(jnp.bfloat16)


def diagonal_mask():
    key_place = lax.broadcasted_iota(jnp.int32, (TILE, TILE), 0)
    query_place = lax.broadcasted_iota(jnp.int32, (TILE, TILE), 1)
    return key_place <= query_place


def causal_exp(scores, count):
    weights = jnp.exp2(scores)
    last = jnp.where(diagonal_mask(), weights[count - TILE :], 0.0)
    if count == TILE:
        return last
    return jnp.concatenate([weights[: count - TILE], last], axis=0)


def dot(left, right):
    return jnp.dot(left, right, preferred_element_type=jnp.float32)


def dot_nt(left, right):
    return lax.dot_general(
        left, right, (((1,), (1,)), ((), ())), preferred_element_type=jnp.float32
    )


def forward_kernel(sizes, qkv_ref, q_gain_ref, k_gain_ref, cos_ref, sin_ref, mixed_ref, mixed_t_ref, total_ref, queries, keys, values_t, mixed_f):
    heads, groups, width = sizes
    ratio = heads // groups
    length = qkv_ref.shape[1]
    fill_heads(qkv_ref, q_gain_ref, k_gain_ref, cos_ref, sin_ref, queries, keys, None, None, values_t, sizes)

    @pl.loop(0, heads)
    def _(head):
        group = head // ratio
        for tile in range(length // TILE):
            count = (tile + 1) * TILE
            columns = pl.ds(tile * TILE, TILE)
            scores = dot(keys[group, pl.ds(0, count), :], queries[head, :, columns])
            weights = causal_exp(scores, count)
            total = jnp.sum(weights, axis=0, keepdims=True)
            result = dot(values_t[group, :, pl.ds(0, count)], weights.astype(jnp.bfloat16))
            mixed_f[pl.ds(head * width, width), columns] = result * (1.0 / total)
            total_ref[pl.ds(head, 1), columns] = jnp.log2(total)

    for block in range(heads * width // 128):
        rows = mixed_f[pl.ds(block * 128, 128), :]
        mixed_t_ref[pl.ds(block * 128, 128), :] = rows.astype(jnp.bfloat16)
        mixed_ref[:, pl.ds(block * 128, 128)] = rows.T.astype(jnp.bfloat16)


def backward_kernel(sizes, qkv_ref, q_gain_ref, k_gain_ref, cos_ref, sin_ref, mixed_t_ref, total_ref, grad_ref, out_ref, gain_ref, out_t, queries, keys, keys_t, values, grads, key_sum, value_sum):
    heads, groups, width = sizes
    ratio = heads // groups
    length = qkv_ref.shape[1]
    fill_heads(qkv_ref, q_gain_ref, k_gain_ref, cos_ref, sin_ref, queries, keys, keys_t, values, None, sizes)
    for block in range(heads * width // 128):
        turned = grad_ref[:, pl.ds(block * 128, 128)].astype(jnp.float32).T
        grads[pl.ds(block * 128, 128), :] = turned.astype(jnp.bfloat16)
    key_sum[...] = jnp.zeros_like(key_sum)
    value_sum[...] = jnp.zeros_like(value_sum)
    gain_ref[...] = jnp.zeros_like(gain_ref)
    cosine, sine = cos_ref[...], sin_ref[...]

    def finish(grad_turned, rows, gain, first):
        grad = head_turn_back(grad_turned, cosine, sine)
        unit, inverse = head_norm(qkv_ref[rows, :])
        product = grad * unit
        part = product[:, :128]
        for lane in range(128, length, 128):
            part = part + product[:, lane : lane + 128]
        gain_ref[pl.ds(first, width), :] += part
        scaled = grad * gain
        before = inverse * (scaled - unit * jnp.mean(scaled * unit, axis=0, keepdims=True))
        out_t[rows, :] = before

    @pl.loop(0, heads)
    def _(head):
        group = head // ratio
        rows = pl.ds(head * width, width)
        query_parts = []
        for tile in range(length // TILE):
            count = (tile + 1) * TILE
            columns = pl.ds(tile * TILE, TILE)
            query = queries[head, :, columns]
            grad = grads[rows, columns]
            scores = dot(keys[group, pl.ds(0, count), :], query) - total_ref[pl.ds(head, 1), columns]
            weights = causal_exp(scores, count)
            inner = jnp.sum(
                grad.astype(jnp.float32) * mixed_t_ref[rows, columns].astype(jnp.float32),
                axis=0,
                keepdims=True,
            )
            weight_grad = dot(values[group, pl.ds(0, count), :], grad)
            score_grad = (weights * (weight_grad - inner)).astype(jnp.bfloat16)
            query_parts.append(dot(keys_t[group, :, pl.ds(0, count)], score_grad))
            key_sum[group, pl.ds(0, count), :] += dot_nt(score_grad, query)
            value_sum[group, pl.ds(0, count), :] += dot_nt(weights.astype(jnp.bfloat16), grad)
        query_grad = jnp.concatenate(query_parts, axis=1) * width**-0.5
        finish(query_grad, rows, q_gain_ref[...], 0)

    for group in range(groups):
        key_grad = key_sum[group].T * (1.0 / log2_e)
        finish(key_grad, pl.ds((heads + group) * width, width), k_gain_ref[...], width)
        out_t[pl.ds((heads + groups + group) * width, width), :] = value_sum[group].T

    for block in range(out_t.shape[0] // 128):
        some = pl.ds(block * 128, 128)
        out_ref[:, some] = out_t[some, :].T.astype(jnp.bfloat16)


def attention_forward(qkv_t, q_gain, k_gain, cosine, sine, sizes):
    heads, groups, width = sizes
    length = qkv_t.shape[1]
    bf16, f32 = jnp.bfloat16, jnp.float32
    pairs = heads * length * length
    return pl.pallas_call(
        functools.partial(forward_kernel, sizes),
        out_shape=(
            jax.ShapeDtypeStruct((length, heads * width), bf16),
            jax.ShapeDtypeStruct((heads * width, length), bf16),
            jax.ShapeDtypeStruct((-(-heads // 8) * 8, length), f32),
        ),
        scratch_shapes=[
            pltpu.VMEM((heads, width, length), bf16),
            pltpu.VMEM((groups, length, width), bf16),
            pltpu.VMEM((groups, width, length), bf16),
            pltpu.VMEM((heads * width, length), f32),
        ],
        compiler_params=pltpu.CompilerParams(vmem_limit_bytes=32 * 2**20),
        cost_estimate=pl.CostEstimate(
            flops=8 * pairs * width, bytes_accessed=6 * 2**20, transcendentals=pairs
        ),
    )(qkv_t, q_gain, k_gain, cosine, sine)


def attention_backward(qkv_t, q_gain, k_gain, cosine, sine, mixed_t, total, mixed_grad, sizes):
    heads, groups, width = sizes
    length = qkv_t.shape[1]
    bf16, f32 = jnp.bfloat16, jnp.float32
    pairs = heads * length * length
    return pl.pallas_call(
        functools.partial(backward_kernel, sizes),
        out_shape=(
            jax.ShapeDtypeStruct(qkv_t.shape[::-1], bf16),
            jax.ShapeDtypeStruct((2 * width, 128), f32),
        ),
        scratch_shapes=[
            pltpu.VMEM(qkv_t.shape, f32),
            pltpu.VMEM((heads, width, length), bf16),
            pltpu.VMEM((groups, length, width), bf16),
            pltpu.VMEM((groups, width, length), bf16),
            pltpu.VMEM((groups, length, width), bf16),
            pltpu.VMEM((heads * width, length), bf16),
            pltpu.VMEM((groups, length, width), f32),
            pltpu.VMEM((groups, length, width), f32),
        ],
        compiler_params=pltpu.CompilerParams(vmem_limit_bytes=40 * 2**20),
        cost_estimate=pl.CostEstimate(flops=0, bytes_accessed=2**20, transcendentals=0),
    )(qkv_t, q_gain, k_gain, cosine, sine, mixed_t, total, mixed_grad)


def hidden_kernel(size, ids_ref, *refs):
    pieces, chunks, refs = refs[:4], refs[4 : 4 + 2 * size], refs[4 + 2 * size :]
    slope_ref, silu_ref, hidden_ref, gate_out, up_out, tokens, gate, up, *sems = refs
    row_sems, in_sems, out_sems = sems
    step = pl.program_id(0)
    steps = pl.num_programs(0)
    rows = chunks[0].shape[0]
    piece = pieces[0].shape[0]

    @pl.when(step == 0)
    def _():
        copies = [
            pltpu.make_async_copy(
                source, tokens.at[pl.ds(index * piece, piece), :], row_sems.at[index]
            )
            for index, source in enumerate(pieces)
        ]
        for copy in copies:
            copy.start()

        @pl.loop(0, steps)
        def _(tile):
            columns = pl.ds(pl.multiple_of(tile * TILE, TILE), TILE)
            for which, target in ((0, gate), (1, up)):
                for index in range(size):
                    first = pl.multiple_of(ids_ref[which, index] * rows, 16)
                    pltpu.make_async_copy(
                        chunks[which * size + index].at[:, columns],
                        target.at[pl.ds(first, rows), columns],
                        in_sems.at[which, tile],
                    ).start()

        for copy in copies:
            copy.wait()

    columns = pl.ds(pl.multiple_of(step * TILE, TILE), TILE)
    for which, target, result in ((0, gate, gate_out), (1, up, up_out)):
        part = target.at[:, columns]
        pltpu.make_async_copy(part, part, in_sems.at[which, step]).wait()
        pltpu.make_async_copy(part, result.at[:, columns], out_sems.at[which, step]).start()
    for half in range(2):
        some = pl.ds(half * 2 * piece, 2 * piece)
        gate_act = dot(tokens[some, :], gate[:, columns])
        up_act = dot(tokens[some, :], up[:, columns])
        sigmoid = 0.5 + 0.5 * jnp.tanh(0.5 * gate_act)
        silu = gate_act * sigmoid
        hidden_ref[some, :] = (silu * up_act).astype(hidden_ref.dtype)
        silu_ref[some, :] = silu.astype(silu_ref.dtype)
        slope_ref[some, :] = (up_act * sigmoid * (1.0 + gate_act * (1.0 - sigmoid))).astype(
            slope_ref.dtype
        )

    @pl.when(step == steps - 1)
    def _():
        @pl.loop(0, steps)
        def _(tile):
            columns = pl.ds(pl.multiple_of(tile * TILE, TILE), TILE)
            for which, target, result in ((0, gate, gate_out), (1, up, up_out)):
                pltpu.make_async_copy(
                    target.at[:, columns], result.at[:, columns], out_sems.at[which, tile]
                ).wait()


def ffn_hidden(pieces, gate_chunks, up_chunks, ids):
    size = len(gate_chunks)
    part, columns = gate_chunks[0].shape
    piece, width = pieces[0].shape
    length = 4 * piece
    bf16 = jnp.bfloat16
    tall = pl.BlockSpec((length, TILE), lambda i, ids: (0, i))
    act = jax.ShapeDtypeStruct((length, columns), bf16)
    weight = jax.ShapeDtypeStruct((width, columns), bf16)
    anywhere = pl.BlockSpec(memory_space=pl.ANY)
    return pl.pallas_call(
        functools.partial(hidden_kernel, size),
        grid_spec=pltpu.PrefetchScalarGridSpec(
            num_scalar_prefetch=1,
            grid=(columns // TILE,),
            in_specs=[anywhere] * (4 + 2 * size),
            out_specs=[tall, tall, tall, anywhere, anywhere],
            scratch_shapes=[
                pltpu.VMEM((length, width), bf16),
                pltpu.VMEM((width, columns), bf16),
                pltpu.VMEM((width, columns), bf16),
                pltpu.SemaphoreType.DMA((4,)),
                pltpu.SemaphoreType.DMA((2, columns // TILE)),
                pltpu.SemaphoreType.DMA((2, columns // TILE)),
            ],
        ),
        out_shape=(act, act, act, weight, weight),
        compiler_params=pltpu.CompilerParams(vmem_limit_bytes=56 * 2**20),
        cost_estimate=pl.CostEstimate(
            flops=4 * length * width * columns,
            bytes_accessed=36 * 2**20,
            transcendentals=length * columns,
        ),
    )(ids, *pieces, *gate_chunks, *up_chunks)


def hidden_grad_kernel(size, owners_ref, grad_ref, slope_ref, silu_ref, *refs):
    chunks, refs = refs[: 2 * size], refs[2 * size :]
    gate_out, up_out, down_out, down, in_sems, out_sem = refs
    step = pl.program_id(0)
    rows = chunks[0].shape[0]

    @pl.when(step == 0)
    def _():
        copies = []
        for which in range(2):
            for index in range(size):
                first = pl.multiple_of((2 * owners_ref[which, index] + which) * rows, 16)
                copies.append(
                    pltpu.make_async_copy(
                        chunks[which * size + index],
                        down.at[pl.ds(first, rows), :],
                        in_sems.at[which, index],
                    )
                )
        for copy in copies:
            copy.start()
        for copy in copies:
            copy.wait()
        pltpu.make_async_copy(down, down_out, out_sem).start()

    weight = down[pl.ds(pl.multiple_of(step * TILE, TILE), TILE), :]
    hidden_grad = dot_nt(grad_ref[...], weight)
    gate_out[...] = (hidden_grad * slope_ref[...].astype(jnp.float32)).astype(jnp.bfloat16)
    up_out[...] = (hidden_grad * silu_ref[...].astype(jnp.float32)).astype(jnp.bfloat16)

    @pl.when(step == pl.num_programs(0) - 1)
    def _():
        pltpu.make_async_copy(down, down_out, out_sem).wait()


def ffn_hidden_grad(out_grad, slope, silu, ahead, behind, owners):
    size = len(ahead)
    length, width = out_grad.shape
    columns = slope.shape[1]
    bf16 = jnp.bfloat16
    tall = pl.BlockSpec((length, TILE), lambda i, owners: (0, i))
    anywhere = pl.BlockSpec(memory_space=pl.ANY)
    act = jax.ShapeDtypeStruct((length, columns), bf16)
    weight = (2 * size * ahead[0].shape[0], width)
    return pl.pallas_call(
        functools.partial(hidden_grad_kernel, size),
        grid_spec=pltpu.PrefetchScalarGridSpec(
            num_scalar_prefetch=1,
            grid=(columns // TILE,),
            in_specs=[pl.BlockSpec((length, width), lambda i, owners: (0, 0)), tall, tall]
            + [anywhere] * (2 * size),
            out_specs=[tall, tall, anywhere],
            scratch_shapes=[
                pltpu.VMEM(weight, bf16),
                pltpu.SemaphoreType.DMA((2, size)),
                pltpu.SemaphoreType.DMA,
            ],
        ),
        out_shape=(act, act, jax.ShapeDtypeStruct(weight, bf16)),
        compiler_params=pltpu.CompilerParams(vmem_limit_bytes=56 * 2**20),
        cost_estimate=pl.CostEstimate(flops=0, bytes_accessed=2**20, transcendentals=0),
    )(owners, out_grad, slope, silu, *ahead, *behind)


def rows_grad_kernel(gate_grad_ref, up_grad_ref, gate_ref, up_ref, own_ref, other_ref, sent_ref):
    piece = own_ref.shape[0]
    total = dot_nt(gate_grad_ref[...], gate_ref[...]) + dot_nt(up_grad_ref[...], up_ref[...])
    total = total.astype(jnp.bfloat16)
    own_ref[...] = total[:piece]
    other_ref[...] = total[piece : 2 * piece]
    sent_ref[...] = total[2 * piece :]


def ffn_rows_grad(gate_grad, up_grad, gate, up):
    length, columns = gate_grad.shape
    width = gate.shape[0]
    piece = length // 4
    bf16 = jnp.bfloat16
    whole = pl.BlockSpec((length, columns), lambda i: (0, 0))
    weight = pl.BlockSpec((TILE, columns), lambda i: (i, 0))
    part = pl.BlockSpec((piece, TILE), lambda i: (0, i))
    return pl.pallas_call(
        rows_grad_kernel,
        grid=(width // TILE,),
        in_specs=[whole, whole, weight, weight],
        out_specs=[part, part, pl.BlockSpec((2 * piece, TILE), lambda i: (0, i))],
        out_shape=(
            jax.ShapeDtypeStruct((piece, width), bf16),
            jax.ShapeDtypeStruct((piece, width), bf16),
            jax.ShapeDtypeStruct((2 * piece, width), bf16),
        ),
        compiler_params=pltpu.CompilerParams(vmem_limit_bytes=56 * 2**20),
        cost_estimate=pl.CostEstimate(flops=0, bytes_accessed=2**20, transcendentals=0),
    )(gate_grad, up_grad, gate, up)


def lay_kernel(size, sizes, owners_ref, *refs):
    chunks, refs = refs[: 2 * size], refs[2 * size :]
    qkv_out, out_out, gains_out, sems = refs
    rows, top, qkv_columns, columns = sizes
    copies = []
    for which, count in ((0, top), (1, rows - top)):
        for index in range(size):
            chunk = chunks[which * size + index]
            owner = owners_ref[which, index]
            first = pl.multiple_of(owner * rows + which * top, 16)
            target = pl.ds(first, count)
            pairs = [
                (chunk.at[pl.ds(0, count), pl.ds(0, qkv_columns)], qkv_out.at[target, :]),
                (
                    chunk.at[pl.ds(0, count), pl.ds(qkv_columns, columns - qkv_columns)],
                    out_out.at[target, :],
                ),
            ]
            if which:
                pairs.append((chunk.at[pl.ds(count, 16), :], gains_out.at[owner]))
            for kind, (source, place) in enumerate(pairs):
                copies.append(pltpu.make_async_copy(source, place, sems.at[kind, which, index]))
    for copy in copies:
        copy.start()
    for copy in copies:
        copy.wait()


def lay_attention(ahead, behind, owners, rows, qkv_columns):
    size = len(ahead)
    top, columns = ahead[0].shape
    bf16 = jnp.bfloat16
    anywhere = pl.BlockSpec(memory_space=pl.ANY)
    return pl.pallas_call(
        functools.partial(lay_kernel, size, (rows, top, qkv_columns, columns)),
        grid_spec=pltpu.PrefetchScalarGridSpec(
            num_scalar_prefetch=1,
            grid=(1,),
            in_specs=[anywhere] * (2 * size),
            out_specs=[pl.BlockSpec(memory_space=pltpu.VMEM)] * 3,
            scratch_shapes=[pltpu.SemaphoreType.DMA((3, 2, size))],
        ),
        out_shape=(
            jax.ShapeDtypeStruct((size * rows, qkv_columns), bf16),
            jax.ShapeDtypeStruct((size * rows, columns - qkv_columns), bf16),
            jax.ShapeDtypeStruct((size, 16, columns), bf16),
        ),
        cost_estimate=pl.CostEstimate(flops=0, bytes_accessed=7 * 2**20, transcendentals=0),
    )(owners, *ahead, *behind)


def pick_kernel(sizes, index_ref, gate_ref, up_ref, gate_out, up_out):
    size, part, window = sizes
    rows = gate_ref.shape[0]
    for source, target in ((gate_ref, gate_out), (up_ref, up_out)):
        for index in range(4):
            count = min(window, part - index * window)

            @pl.when(index_ref[0] == index)
            def _():
                parts = []
                for owner in range(size):
                    first = owner * part + index * window
                    low, high = first // 128 * 128, -(-(first + count) // 128) * 128
                    wide = source[:, low:high].astype(jnp.float32)
                    parts.append(wide[:, first - low : first - low + count])
                    if count < window:
                        parts.append(jnp.zeros((rows, window - count), jnp.float32))
                target[...] = jnp.concatenate(parts, axis=1).astype(target.dtype)


def pick_hidden(gate, up, seq_index, size, part, window):
    rows, columns = gate.shape
    block = 48 if rows % 48 == 0 else rows
    wide = pl.BlockSpec((block, columns), lambda i, index: (i, 0))
    narrow = pl.BlockSpec((block, size * window), lambda i, index: (i, 0))
    out = jax.ShapeDtypeStruct((rows, size * window), gate.dtype)
    return pl.pallas_call(
        functools.partial(pick_kernel, (size, part, window)),
        grid_spec=pltpu.PrefetchScalarGridSpec(
            num_scalar_prefetch=1,
            grid=(rows // block,),
            in_specs=[wide, wide],
            out_specs=[narrow, narrow],
        ),
        out_shape=(out, out),
        compiler_params=pltpu.CompilerParams(vmem_limit_bytes=32 * 2**20),
        cost_estimate=pl.CostEstimate(flops=0, bytes_accessed=8 * 2**20, transcendentals=0),
    )(jnp.reshape(seq_index, (1,)).astype(jnp.int32), gate, up)


def spread_kernel(sizes, index_ref, own_ref, other_ref, near_ref, far_ref, out_ref, parts):
    size, part, window = sizes
    me = index_ref[0]
    parts[me] = own_ref[...]
    parts[me ^ 2] = other_ref[...]
    parts[me ^ 1] = near_ref[...]
    parts[me ^ 3] = far_ref[...]
    pieces = []
    for owner in range(size):
        for index in range(4):
            count = min(window, part - index * window)
            first = owner * window
            low, high = first // 128 * 128, -(-(first + count) // 128) * 128
            wide = parts[index, :, low:high].astype(jnp.float32)
            pieces.append(wide[:, first - low : first - low + count])
    out_ref[...] = jnp.concatenate(pieces, axis=1)


def spread_hidden(pieces, which, seq_index, size, part, window):
    _, rows, columns = pieces[0].shape
    block = 48 if rows % 48 == 0 else rows
    narrow = pl.BlockSpec((None, block, columns), lambda i, index: (which, i, 0))
    return pl.pallas_call(
        functools.partial(spread_kernel, (size, part, window)),
        grid_spec=pltpu.PrefetchScalarGridSpec(
            num_scalar_prefetch=1,
            grid=(rows // block,),
            in_specs=[narrow] * 4,
            out_specs=pl.BlockSpec((block, size * part), lambda i, index: (i, 0)),
            scratch_shapes=[pltpu.VMEM((4, block, columns), pieces[0].dtype)],
        ),
        out_shape=jax.ShapeDtypeStruct((rows, size * part), jnp.float32),
        compiler_params=pltpu.CompilerParams(vmem_limit_bytes=32 * 2**20),
        cost_estimate=pl.CostEstimate(flops=0, bytes_accessed=64 * 2**20, transcendentals=0),
    )(jnp.reshape(seq_index, (1,)), *pieces)


def norm_forward(values, gain):
    inverse = lax.rsqrt(jnp.mean(values * values, axis=-1, keepdims=True) + norm_epsilon)
    unit = values * inverse
    return (unit * gain, unit, inverse)


def norm_backward(grad_in, unit, inverse, gain):
    scaled = grad_in * gain
    return inverse * (scaled - unit * jnp.mean(scaled * unit, axis=-1, keepdims=True))


def transpose_dot(left, right):
    return lax.dot_general(
        left, right, (((0,), (0,)), ((), ())), preferred_element_type=jnp.float32
    )


def by_rows(values):
    return with_layout_constraint(values, Layout(major_to_minor=(0, 1)))


def dot_transposed(left, right):
    return lax.dot_general(
        left, right, (((1,), (1,)), ((), ())), preferred_element_type=jnp.float32
    )


def split_rows(rows):
    return (rows // 32) * 16


def ring_ids(size):
    return list(range(0, size, 2)) + [i for i in range(size - 1, 0, -1) if i % 2]


def ring_perms(size):
    ids = ring_ids(size)
    forward = [(ids[i], ids[(i + 1) % size]) for i in range(size)]
    return forward, [(b, a) for a, b in forward]


def ring_owners(size):
    ids = ring_ids(size)
    table = np.zeros((size, 4, size), np.int32)
    for place, device in enumerate(ids):
        for step in range(size):
            table[device, 0, step] = ids[(place - step) % size]
            table[device, 1, step] = ids[(place + step) % size]
            table[device, 2, step] = ids[(place - 1 - step) % size]
            table[device, 3, step] = ids[(place + 1 + step) % size]
    return lax.dynamic_index_in_dim(
        jnp.asarray(table), lax.axis_index("fsdp").astype(jnp.uint32), 0, keepdims=False
    )


def after(value, *needed):
    return lax.optimization_barrier((value, *needed))[0] if needed else value


class GatherRing:
    def __init__(self, ahead, behind, size):
        self.perms = ring_perms(size)
        self.ahead, self.behind = [ahead], [behind]

    def step(self, *needed):
        forward, backward = self.perms
        self.ahead.append(after(lax.ppermute(self.ahead[-1], "fsdp", forward), *needed))
        self.behind.append(after(lax.ppermute(self.behind[-1], "fsdp", backward), *needed))


class ScatterRing:
    def __init__(self, way, blocks, size, owners, rows=None):
        self.perm = ring_perms(size)[way]
        self.owners = lax.squeeze(lax.slice_in_dim(owners, 2 + way, 3 + way), (0,)).astype(
            jnp.uint32
        )
        self.blocks, self.count = blocks, 0
        self.first, self.last = rows or (0, blocks.shape[1])
        self.sum = self.own().astype(jnp.bfloat16)

    def own(self):
        owner = lax.squeeze(lax.slice_in_dim(self.owners, self.count, self.count + 1), (0,))
        zero = jnp.uint32(0)
        shape = (1, self.last - self.first, self.blocks.shape[2])
        start = (owner, jnp.uint32(self.first), zero)
        return lax.dynamic_slice(self.blocks, start, shape)[0].astype(jnp.float32)

    def step(self, *needed):
        came = after(lax.ppermute(self.sum, "fsdp", self.perm), *needed)
        self.count += 1
        self.sum = (came.astype(jnp.float32) + self.own()).astype(jnp.bfloat16)
        return self.sum


def exchange(values, mask):
    return lax.ppermute(values, "seq", [(i, i ^ mask) for i in range(4)])


def gather_seq(block, *needed):
    block = after(block, *needed)
    other = exchange(block, 2)
    return [block, other, exchange(block, 1), exchange(other, 1)]


def in_order(pieces, seq_index):
    high, low = seq_index // 2, seq_index % 2

    def pick(first, second, flag):
        return jnp.where(flag == 0, first, second), jnp.where(flag == 0, second, first)

    mine = pick(pieces[0], pieces[1], high)
    theirs = pick(pieces[2], pieces[3], high)
    return [*pick(mine[0], theirs[0], low), *pick(mine[1], theirs[1], low)]


def scatter_seq(own, other, there):
    rows = own.shape[0]
    came = exchange(there, 1).astype(jnp.float32)
    sent = (other.astype(jnp.float32) + came[rows:]).astype(jnp.bfloat16)
    near = own.astype(jnp.float32) + came[:rows]
    return near + exchange(sent, 2).astype(jnp.float32), sent


def swap(blocks):
    return lax.all_to_all(blocks, "seq", split_axis=0, concat_axis=0, tiled=True)


def side_by_side(blocks):
    return blocks.transpose(1, 0, 2).reshape(blocks.shape[1], -1)


def apart(values):
    return values.reshape(values.shape[0], 4, -1).transpose(1, 0, 2)


def body(
    tokens,
    norm_gain,
    query_weight,
    key_weight,
    value_weight,
    query_gain,
    key_gain,
    out_weight,
    ffn_gain,
    gate_weight,
    up_weight,
    down_weight,
    cotangent,
):
    bf16, f32 = jnp.bfloat16, jnp.float32
    size = lax.axis_size("fsdp")
    seq_index = lax.axis_index("seq")
    owners = ring_owners(size)
    own_rows, width = query_weight.shape
    head_part = query_gain.shape[0]
    head_width = head_part * size
    query_columns = width // 4
    key_columns = key_weight.shape[1] // 4
    ff_part = down_weight.shape[0]
    window = -(-ff_part // 64) * 16

    def columns_of(weight, count):
        return lax.dynamic_slice_in_dim(weight, seq_index.astype(jnp.uint32) * count, count, 1)

    def hidden_rows(weight):
        tall = jnp.pad(weight, ((0, 4 * window - ff_part), (0, 0)))
        return lax.dynamic_slice_in_dim(tall, seq_index.astype(jnp.uint32) * window, window, 0)

    gains = jnp.concatenate([norm_gain, ffn_gain, query_gain, key_gain])
    gain_count = gains.shape[0]
    qkv_columns = query_columns + 2 * key_columns
    packed_columns = qkv_columns + query_columns
    gain_rows = jnp.pad(gains[None], ((0, 15), (0, packed_columns - gain_count)))
    packed = jnp.concatenate(
        [
            columns_of(query_weight, query_columns),
            columns_of(key_weight, key_columns),
            columns_of(value_weight, key_columns),
            columns_of(out_weight, query_columns),
        ],
        axis=1,
    )
    top = split_rows(own_rows + 16)
    first_ring = GatherRing(
        packed[:top], jnp.concatenate([packed[top:], gain_rows], axis=0), size
    )
    for _ in range(size - 1):
        first_ring.step()
    ffn_ring = GatherRing(
        *pick_hidden(gate_weight, up_weight, seq_index, size, ff_part, window), size
    )
    down_rows = hidden_rows(down_weight)
    lag = 2

    def advance(rings, *needed):
        for way in rings:
            if way.count < size - 1:
                way.step(*needed)

    def gather(count, *needed):
        for _ in range(count):
            if len(ffn_ring.ahead) > lag + 1 and len(rings[0].ahead) < size:
                rings[0].step(*needed)
            if len(ffn_ring.ahead) < size:
                ffn_ring.step(*needed)
                if len(ffn_ring.ahead) == lag + 2:
                    start = after(down_rows, ffn_ring.ahead[-1], ffn_ring.behind[-1])
                    rings.append(GatherRing(start[: window // 2], start[window // 2 :], size))

    rings = []
    gather(2)

    qkv_all, out_part, gains_all = lay_attention(
        first_ring.ahead, first_ring.behind, owners, own_rows, qkv_columns
    )
    gains_all = gains_all[:, 0].astype(f32)
    first_gain = gains_all[:, :own_rows].reshape(-1)
    second_gain = gains_all[:, own_rows : 2 * own_rows].reshape(-1)
    q_gain_f = gains_all[:, 2 * own_rows : 2 * own_rows + head_part].reshape(-1)
    k_gain_f = gains_all[:, 2 * own_rows + head_part : 2 * (own_rows + head_part)].reshape(-1)

    inputs = tokens[0]
    tok_rows = inputs.shape[0]
    length = 4 * tok_rows
    input_blocks = gather_seq(inputs)
    inputs_all = jnp.concatenate(in_order(input_blocks, seq_index), axis=0).astype(f32)
    out_grad = cotangent[0]
    grad_blocks = gather_seq(out_grad, input_blocks[1])
    out_grad_all = jnp.concatenate(grad_blocks, axis=0)


    out_other = exchange(after(out_part, input_blocks[1]), 2)
    normed, norm_unit, norm_inverse = norm_forward(inputs_all, first_gain)
    normed_low = after(normed.astype(bf16), grad_blocks[1])
    qkv_t = lax.dot_general(
        qkv_all, normed_low, (((0,), (1,)), ((), ())), preferred_element_type=f32
    )
    gather(1, qkv_t)
    sizes = (query_columns // head_width, key_columns // head_width, head_width)
    cosine, sine = rope_rows(length, head_width)
    tables = (q_gain_f[:, None], k_gain_f[:, None], cosine, sine)
    mixed_heads, mixed_t, totals = attention_forward(qkv_t, *tables, sizes)
    gather(1, mixed_heads)
    mixed = side_by_side(swap(mixed_heads.reshape(4, tok_rows, query_columns)))
    out_other = after(out_other, mixed_heads)
    out_blocks = [out_part, out_other, exchange(out_part, 1), exchange(out_other, 1)]
    out_all = jnp.concatenate(in_order(out_blocks, seq_index), axis=1)
    attended = jnp.dot(mixed, out_all, preferred_element_type=f32)
    middle = inputs.astype(f32) + attended
    normed_two, middle_unit, middle_inverse = norm_forward(middle, second_gain)
    normed_two_low = normed_two.astype(bf16)
    gather(1, normed_two_low)
    normed_blocks = gather_seq(normed_two_low)
    gather(size - len(ffn_ring.ahead) + 1, normed_blocks[1])
    normed_two_all = jnp.concatenate(normed_blocks, axis=0)
    mixed_all = jnp.concatenate(
        in_order(gather_seq(mixed_heads, normed_blocks[1]), seq_index), axis=1
    )

    slope, silu, hidden, gate_all, up_all = ffn_hidden(
        normed_blocks, ffn_ring.ahead, ffn_ring.behind, owners
    )
    down_ring = rings[0]
    while len(down_ring.ahead) < size:
        down_ring.step(hidden)
    down_weight_grad = transpose_dot(hidden, out_grad_all).astype(bf16)
    down_blocks = down_weight_grad.reshape(size, window, width)
    down_sums = (
        ScatterRing(0, down_blocks, size, owners, (0, window // 2)),
        ScatterRing(1, down_blocks, size, owners, (window // 2, window)),
    )
    gate_grad, up_grad, down_all = ffn_hidden_grad(
        after(out_grad_all, *(way.sum for way in down_sums)),
        slope,
        silu,
        down_ring.ahead,
        down_ring.behind,
        owners,
    )
    advance(down_sums, gate_grad)
    gate_weight_grad = transpose_dot(
        after(normed_two_all, *(way.sum for way in down_sums)), gate_grad
    ).astype(bf16)
    gate_sums = ScatterRing(
        0, gate_weight_grad.reshape(size, own_rows, size * window), size, owners
    )
    up_weight_grad = transpose_dot(after(normed_two_all, gate_sums.sum), up_grad).astype(bf16)
    up_sums = ScatterRing(1, up_weight_grad.reshape(size, own_rows, size * window), size, owners)
    ffn_sums = (gate_sums, up_sums)
    advance(down_sums, up_sums.sum)
    normed_parts = ffn_rows_grad(
        after(gate_grad, *(way.sum for way in down_sums)), up_grad, gate_all, up_all
    )
    normed_two_grad, half_sum = scatter_seq(*normed_parts)
    advance(ffn_sums, normed_parts[0])
    advance(down_sums, normed_parts[0])
    advance(ffn_sums, half_sum)
    advance(down_sums, half_sum)
    ffn_gain_grad = jnp.sum(normed_two_grad * middle_unit, axis=0)
    middle_grad = out_grad.astype(f32) + norm_backward(
        normed_two_grad, middle_unit, middle_inverse, second_gain
    )
    attended_low = middle_grad.astype(bf16)
    mixed_grad = dot_transposed(attended_low, out_all).astype(bf16)
    advance(ffn_sums, mixed_grad)
    advance(down_sums, mixed_grad)
    mixed_grad_heads = swap(apart(mixed_grad)).reshape(length, query_columns)
    qkv_grad, head_gains = attention_backward(
        qkv_t, *tables, mixed_t, totals, mixed_grad_heads, sizes
    )
    attended_columns = after(
        swap(apart(after(attended_low, mixed_grad_heads))), qkv_grad
    ).reshape(length, query_columns)
    out_weight_grad = by_rows(transpose_dot(mixed_all, attended_columns).astype(bf16))
    advance(ffn_sums, qkv_grad)
    advance(down_sums, qkv_grad)
    qkv_grad = after(qkv_grad, gate_sums.sum, up_sums.sum)
    head_gains = jnp.sum(head_gains, axis=1)
    query_gain_grad, key_gain_grad = head_gains[:head_width], head_gains[head_width:]
    qkv_weight_grad = by_rows(transpose_dot(normed_low, qkv_grad).astype(bf16))
    normed_partial = dot_transposed(qkv_grad, qkv_all)
    norm_gain_grad = jnp.sum(normed_partial * norm_unit, axis=0)
    partial_blocks = normed_partial.astype(bf16).reshape(4, tok_rows, width)

    def partial_of(mask):
        index = (seq_index ^ mask).astype(jnp.uint32)
        return lax.dynamic_index_in_dim(partial_blocks, index, 0, keepdims=False)

    normed_grad, normed_sent = scatter_seq(
        partial_of(0),
        partial_of(2),
        jnp.concatenate([partial_of(1), partial_of(3)], axis=0),
    )
    _, own_unit, own_inverse = norm_forward(inputs.astype(f32), first_gain)
    inputs_grad = middle_grad + norm_backward(normed_grad, own_unit, own_inverse, first_gain)

    gain_grads = jnp.concatenate(
        [
            norm_gain_grad.reshape(size, -1),
            ffn_gain_grad.reshape(size, -1),
            query_gain_grad.reshape(size, -1),
            key_gain_grad.reshape(size, -1),
        ],
        axis=1,
    )
    gain_blocks = jnp.pad(
        gain_grads[:, None], ((0, 0), (0, 15), (0, packed_columns - gain_count))
    )
    packed_blocks = jnp.concatenate([qkv_weight_grad, out_weight_grad], axis=1).reshape(
        size, own_rows, packed_columns
    )
    packed_blocks = jnp.concatenate([packed_blocks, gain_blocks.astype(bf16)], axis=1)
    last_sums = (
        ScatterRing(0, packed_blocks, size, owners, (0, top)),
        ScatterRing(1, packed_blocks, size, owners, (top, own_rows + 16)),
    )
    advance(ffn_sums, *(way.sum for way in last_sums))
    advance(down_sums, *(way.sum for way in last_sums))
    advance(last_sums)
    advance(last_sums)
    down_share = jnp.concatenate([way.sum for way in down_sums], axis=0)
    down_pieces = gather_seq(down_share)
    down_partial = jnp.dot(
        after(hidden, gate_sums.sum), down_all, preferred_element_type=f32
    ).astype(bf16)
    down_sum, down_sent = scatter_seq(
        down_partial[:tok_rows],
        down_partial[tok_rows : 2 * tok_rows],
        down_partial[2 * tok_rows :],
    )
    rest = [(down_sum, down_pieces[1]), (normed_grad, down_sent)]
    while gate_sums.count < size - 1:
        advance(last_sums, gate_sums.sum, up_sums.sum)
        advance(ffn_sums, *(rest.pop() if rest else ()))
        advance(last_sums, gate_sums.sum, up_sums.sum)
    both = jnp.stack([gate_sums.sum, up_sums.sum])
    ffn_blocks = gather_seq(both)
    while last_sums[0].count < size - 1:
        advance(last_sums, ffn_blocks[1])
    packed_share = jnp.concatenate([way.sum for way in last_sums], axis=0)
    output = middle + down_sum
    down_full = jnp.concatenate(in_order(down_pieces, seq_index), axis=0)[
        :ff_part
    ].astype(f32)
    gate_full, up_full = (
        spread_hidden(ffn_blocks, which, seq_index, size, ff_part, window) for which in range(2)
    )
    packs = in_order(gather_seq(packed_share), seq_index)

    def unpack(first, count):
        return jnp.concatenate(
            [p[:own_rows, first : first + count] for p in packs], axis=1
        ).astype(f32)

    gain_sum = sum(p[own_rows, :gain_count].astype(f32) for p in packs)
    return (
        output[None].astype(bf16),
        inputs_grad[None].astype(bf16),
        gain_sum[:own_rows],
        unpack(0, query_columns),
        unpack(query_columns, key_columns),
        unpack(query_columns + key_columns, key_columns),
        gain_sum[2 * own_rows : 2 * own_rows + head_part],
        gain_sum[2 * own_rows + head_part :],
        unpack(qkv_columns, query_columns),
        gain_sum[own_rows : 2 * own_rows],
        gate_full,
        up_full,
        down_full,
    )


def solution(mesh):
    in_specs = (
        P("fsdp", "seq", None),
        P("fsdp"),
        P("fsdp", None),
        P("fsdp", None),
        P("fsdp", None),
        P("fsdp"),
        P("fsdp"),
        P("fsdp", None),
        P("fsdp"),
        P("fsdp", None),
        P("fsdp", None),
        P("fsdp", None),
        P("fsdp", "seq", None),
    )
    out_specs = (
        P("fsdp", "seq", None),
        P("fsdp", "seq", None),
        P("fsdp"),
        P("fsdp", None),
        P("fsdp", None),
        P("fsdp", None),
        P("fsdp"),
        P("fsdp"),
        P("fsdp", None),
        P("fsdp"),
        P("fsdp", None),
        P("fsdp", None),
        P("fsdp", None),
    )
    return jax.shard_map(body, mesh=mesh, in_specs=in_specs, out_specs=out_specs, check_vma=False)
```

```python
import functools
import math

import jax
import jax.numpy as jnp
import numpy as np
from jax import lax
from jax.experimental import pallas as pl
from jax.experimental.layout import Layout, with_layout_constraint
from jax.experimental.pallas import tpu as pltpu
from jax.sharding import PartitionSpec as P

norm_epsilon = 1e-05
TILE = 256
log2_e = math.log2(math.e)


def rope_rows(length, width):
    half_width = width // 2
    inverse = jnp.exp(
        jnp.arange(half_width, dtype=jnp.float32) * (-2.0 * math.log(1000000.0) / width)
    )
    angles = inverse[:, None] * jnp.arange(length, dtype=jnp.int32).astype(jnp.float32)[None, :]
    return jnp.cos(angles), jnp.sin(angles)


def head_norm(values):
    inverse = lax.rsqrt(jnp.mean(values * values, axis=0, keepdims=True) + norm_epsilon)
    return values * inverse, inverse


def head_turn(values, cosine, sine):
    half = values.shape[0] // 2
    first, second = values[:half], values[half:]
    return jnp.concatenate(
        [first * cosine - second * sine, second * cosine + first * sine], axis=0
    )


def head_turn_back(values, cosine, sine):
    half = values.shape[0] // 2
    first, second = values[:half], values[half:]
    return jnp.concatenate(
        [first * cosine + second * sine, second * cosine - first * sine], axis=0
    )


def fill_heads(qkv_ref, q_gain_ref, k_gain_ref, cos_ref, sin_ref, queries, keys, keys_t, values, values_t, sizes):
    heads, groups, width = sizes
    cosine, sine = cos_ref[...], sin_ref[...]

    @pl.loop(0, heads)
    def _(head):
        unit, _ = head_norm(qkv_ref[pl.ds(head * width, width), :])
        turned = head_turn(unit * q_gain_ref[...], cosine, sine)
        queries[head] = (turned * (width**-0.5 * log2_e)).astype(jnp.bfloat16)

    @pl.loop(0, groups)
    def _(group):
        unit, _ = head_norm(qkv_ref[pl.ds((heads + group) * width, width), :])
        turned = head_turn(unit * k_gain_ref[...], cosine, sine)
        keys[group] = turned.T.astype(jnp.bfloat16)
        if keys_t is not None:
            keys_t[group] = turned.astype(jnp.bfloat16)
        value = qkv_ref[pl.ds((heads + groups + group) * width, width), :]
        if values is not None:
            values[group] = value.T.astype(jnp.bfloat16)
        if values_t is not None:
            values_t[group] = value.astype(jnp.bfloat16)


def diagonal_mask():
    key_place = lax.broadcasted_iota(jnp.int32, (TILE, TILE), 0)
    query_place = lax.broadcasted_iota(jnp.int32, (TILE, TILE), 1)
    return key_place <= query_place


def causal_exp(scores, count):
    weights = jnp.exp2(scores)
    last = jnp.where(diagonal_mask(), weights[count - TILE :], 0.0)
    if count == TILE:
        return last
    return jnp.concatenate([weights[: count - TILE], last], axis=0)


def dot(left, right):
    return jnp.dot(left, right, preferred_element_type=jnp.float32)


def dot_nt(left, right):
    return lax.dot_general(
        left, right, (((1,), (1,)), ((), ())), preferred_element_type=jnp.float32
    )


def forward_kernel(sizes, qkv_ref, q_gain_ref, k_gain_ref, cos_ref, sin_ref, mixed_ref, mixed_t_ref, total_ref, queries, keys, values_t, mixed_f):
    heads, groups, width = sizes
    ratio = heads // groups
    length = qkv_ref.shape[1]
    fill_heads(qkv_ref, q_gain_ref, k_gain_ref, cos_ref, sin_ref, queries, keys, None, None, values_t, sizes)

    @pl.loop(0, heads)
    def _(head):
        group = head // ratio
        for tile in range(length // TILE):
            count = (tile + 1) * TILE
            columns = pl.ds(tile * TILE, TILE)
            scores = dot(keys[group, pl.ds(0, count), :], queries[head, :, columns])
            weights = causal_exp(scores, count)
            total = jnp.sum(weights, axis=0, keepdims=True)
            result = dot(values_t[group, :, pl.ds(0, count)], weights.astype(jnp.bfloat16))
            mixed_f[pl.ds(head * width, width), columns] = result * (1.0 / total)
            total_ref[pl.ds(head, 1), columns] = jnp.log2(total)

    for block in range(heads * width // 128):
        rows = mixed_f[pl.ds(block * 128, 128), :]
        mixed_t_ref[pl.ds(block * 128, 128), :] = rows.astype(jnp.bfloat16)
        mixed_ref[:, pl.ds(block * 128, 128)] = rows.T.astype(jnp.bfloat16)


def backward_kernel(sizes, qkv_ref, q_gain_ref, k_gain_ref, cos_ref, sin_ref, mixed_t_ref, total_ref, grad_ref, out_ref, gain_ref, out_t, queries, keys, keys_t, values, grads, key_sum, value_sum):
    heads, groups, width = sizes
    ratio = heads // groups
    length = qkv_ref.shape[1]
    fill_heads(qkv_ref, q_gain_ref, k_gain_ref, cos_ref, sin_ref, queries, keys, keys_t, values, None, sizes)
    for block in range(heads * width // 128):
        turned = grad_ref[:, pl.ds(block * 128, 128)].astype(jnp.float32).T
        grads[pl.ds(block * 128, 128), :] = turned.astype(jnp.bfloat16)
    key_sum[...] = jnp.zeros_like(key_sum)
    value_sum[...] = jnp.zeros_like(value_sum)
    gain_ref[...] = jnp.zeros_like(gain_ref)
    cosine, sine = cos_ref[...], sin_ref[...]

    def finish(grad_turned, rows, gain, first):
        grad = head_turn_back(grad_turned, cosine, sine)
        unit, inverse = head_norm(qkv_ref[rows, :])
        product = grad * unit
        part = product[:, :128]
        for lane in range(128, length, 128):
            part = part + product[:, lane : lane + 128]
        gain_ref[pl.ds(first, width), :] += part
        scaled = grad * gain
        before = inverse * (scaled - unit * jnp.mean(scaled * unit, axis=0, keepdims=True))
        out_t[rows, :] = before

    @pl.loop(0, heads)
    def _(head):
        group = head // ratio
        rows = pl.ds(head * width, width)
        query_parts = []
        for tile in range(length // TILE):
            count = (tile + 1) * TILE
            columns = pl.ds(tile * TILE, TILE)
            query = queries[head, :, columns]
            grad = grads[rows, columns]
            scores = dot(keys[group, pl.ds(0, count), :], query) - total_ref[pl.ds(head, 1), columns]
            weights = causal_exp(scores, count)
            inner = jnp.sum(
                grad.astype(jnp.float32) * mixed_t_ref[rows, columns].astype(jnp.float32),
                axis=0,
                keepdims=True,
            )
            weight_grad = dot(values[group, pl.ds(0, count), :], grad)
            score_grad = (weights * (weight_grad - inner)).astype(jnp.bfloat16)
            query_parts.append(dot(keys_t[group, :, pl.ds(0, count)], score_grad))
            key_sum[group, pl.ds(0, count), :] += dot_nt(score_grad, query)
            value_sum[group, pl.ds(0, count), :] += dot_nt(weights.astype(jnp.bfloat16), grad)
        query_grad = jnp.concatenate(query_parts, axis=1) * width**-0.5
        finish(query_grad, rows, q_gain_ref[...], 0)

    for group in range(groups):
        key_grad = key_sum[group].T * (1.0 / log2_e)
        finish(key_grad, pl.ds((heads + group) * width, width), k_gain_ref[...], width)
        out_t[pl.ds((heads + groups + group) * width, width), :] = value_sum[group].T

    for block in range(out_t.shape[0] // 128):
        some = pl.ds(block * 128, 128)
        out_ref[:, some] = out_t[some, :].T.astype(jnp.bfloat16)


def attention_forward(qkv_t, q_gain, k_gain, cosine, sine, sizes):
    heads, groups, width = sizes
    length = qkv_t.shape[1]
    bf16, f32 = jnp.bfloat16, jnp.float32
    pairs = heads * length * length
    return pl.pallas_call(
        functools.partial(forward_kernel, sizes),
        out_shape=(
            jax.ShapeDtypeStruct((length, heads * width), bf16),
            jax.ShapeDtypeStruct((heads * width, length), bf16),
            jax.ShapeDtypeStruct((-(-heads // 8) * 8, length), f32),
        ),
        scratch_shapes=[
            pltpu.VMEM((heads, width, length), bf16),
            pltpu.VMEM((groups, length, width), bf16),
            pltpu.VMEM((groups, width, length), bf16),
            pltpu.VMEM((heads * width, length), f32),
        ],
        compiler_params=pltpu.CompilerParams(vmem_limit_bytes=32 * 2**20),
        cost_estimate=pl.CostEstimate(
            flops=8 * pairs * width, bytes_accessed=6 * 2**20, transcendentals=pairs
        ),
    )(qkv_t, q_gain, k_gain, cosine, sine)


def attention_backward(qkv_t, q_gain, k_gain, cosine, sine, mixed_t, total, mixed_grad, sizes):
    heads, groups, width = sizes
    length = qkv_t.shape[1]
    bf16, f32 = jnp.bfloat16, jnp.float32
    pairs = heads * length * length
    return pl.pallas_call(
        functools.partial(backward_kernel, sizes),
        out_shape=(
            jax.ShapeDtypeStruct(qkv_t.shape[::-1], bf16),
            jax.ShapeDtypeStruct((2 * width, 128), f32),
        ),
        scratch_shapes=[
            pltpu.VMEM(qkv_t.shape, f32),
            pltpu.VMEM((heads, width, length), bf16),
            pltpu.VMEM((groups, length, width), bf16),
            pltpu.VMEM((groups, width, length), bf16),
            pltpu.VMEM((groups, length, width), bf16),
            pltpu.VMEM((heads * width, length), bf16),
            pltpu.VMEM((groups, length, width), f32),
            pltpu.VMEM((groups, length, width), f32),
        ],
        compiler_params=pltpu.CompilerParams(vmem_limit_bytes=40 * 2**20),
        cost_estimate=pl.CostEstimate(flops=0, bytes_accessed=2**20, transcendentals=0),
    )(qkv_t, q_gain, k_gain, cosine, sine, mixed_t, total, mixed_grad)


def hidden_kernel(size, ids_ref, *refs):
    pieces, chunks, refs = refs[:4], refs[4 : 4 + 2 * size], refs[4 + 2 * size :]
    slope_ref, silu_ref, hidden_ref, gate_out, up_out, tokens, gate, up, *sems = refs
    row_sems, in_sems, out_sems = sems
    step = pl.program_id(0)
    steps = pl.num_programs(0)
    rows = chunks[0].shape[0]
    piece = pieces[0].shape[0]

    @pl.when(step == 0)
    def _():
        copies = [
            pltpu.make_async_copy(
                source, tokens.at[pl.ds(index * piece, piece), :], row_sems.at[index]
            )
            for index, source in enumerate(pieces)
        ]
        for copy in copies:
            copy.start()

        @pl.loop(0, steps)
        def _(tile):
            columns = pl.ds(pl.multiple_of(tile * TILE, TILE), TILE)
            for which, target in ((0, gate), (1, up)):
                for index in range(size):
                    first = pl.multiple_of(ids_ref[which, index] * rows, 16)
                    pltpu.make_async_copy(
                        chunks[which * size + index].at[:, columns],
                        target.at[pl.ds(first, rows), columns],
                        in_sems.at[which, tile],
                    ).start()

        for copy in copies:
            copy.wait()

    columns = pl.ds(pl.multiple_of(step * TILE, TILE), TILE)
    for which, target, result in ((0, gate, gate_out), (1, up, up_out)):
        part = target.at[:, columns]
        pltpu.make_async_copy(part, part, in_sems.at[which, step]).wait()
        pltpu.make_async_copy(part, result.at[:, columns], out_sems.at[which, step]).start()
    for half in range(2):
        some = pl.ds(half * 2 * piece, 2 * piece)
        gate_act = dot(tokens[some, :], gate[:, columns])
        up_act = dot(tokens[some, :], up[:, columns])
        sigmoid = 0.5 + 0.5 * jnp.tanh(0.5 * gate_act)
        silu = gate_act * sigmoid
        hidden_ref[some, :] = (silu * up_act).astype(hidden_ref.dtype)
        silu_ref[some, :] = silu.astype(silu_ref.dtype)
        slope_ref[some, :] = (up_act * sigmoid * (1.0 + gate_act * (1.0 - sigmoid))).astype(
            slope_ref.dtype
        )

    @pl.when(step == steps - 1)
    def _():
        @pl.loop(0, steps)
        def _(tile):
            columns = pl.ds(pl.multiple_of(tile * TILE, TILE), TILE)
            for which, target, result in ((0, gate, gate_out), (1, up, up_out)):
                pltpu.make_async_copy(
                    target.at[:, columns], result.at[:, columns], out_sems.at[which, tile]
                ).wait()


def ffn_hidden(pieces, gate_chunks, up_chunks, ids):
    size = len(gate_chunks)
    part, columns = gate_chunks[0].shape
    piece, width = pieces[0].shape
    length = 4 * piece
    bf16 = jnp.bfloat16
    tall = pl.BlockSpec((length, TILE), lambda i, ids: (0, i))
    act = jax.ShapeDtypeStruct((length, columns), bf16)
    weight = jax.ShapeDtypeStruct((width, columns), bf16)
    anywhere = pl.BlockSpec(memory_space=pl.ANY)
    return pl.pallas_call(
        functools.partial(hidden_kernel, size),
        grid_spec=pltpu.PrefetchScalarGridSpec(
            num_scalar_prefetch=1,
            grid=(columns // TILE,),
            in_specs=[anywhere] * (4 + 2 * size),
            out_specs=[tall, tall, tall, anywhere, anywhere],
            scratch_shapes=[
                pltpu.VMEM((length, width), bf16),
                pltpu.VMEM((width, columns), bf16),
                pltpu.VMEM((width, columns), bf16),
                pltpu.SemaphoreType.DMA((4,)),
                pltpu.SemaphoreType.DMA((2, columns // TILE)),
                pltpu.SemaphoreType.DMA((2, columns // TILE)),
            ],
        ),
        out_shape=(act, act, act, weight, weight),
        compiler_params=pltpu.CompilerParams(vmem_limit_bytes=56 * 2**20),
        cost_estimate=pl.CostEstimate(
            flops=4 * length * width * columns,
            bytes_accessed=36 * 2**20,
            transcendentals=length * columns,
        ),
    )(ids, *pieces, *gate_chunks, *up_chunks)


def hidden_grad_kernel(size, owners_ref, grad_ref, slope_ref, silu_ref, *refs):
    chunks, refs = refs[: 2 * size], refs[2 * size :]
    gate_out, up_out, down_out, down, in_sems, out_sem = refs
    step = pl.program_id(0)
    rows = chunks[0].shape[0]

    @pl.when(step == 0)
    def _():
        copies = []
        for which in range(2):
            for index in range(size):
                first = pl.multiple_of((2 * owners_ref[which, index] + which) * rows, 16)
                copies.append(
                    pltpu.make_async_copy(
                        chunks[which * size + index],
                        down.at[pl.ds(first, rows), :],
                        in_sems.at[which, index],
                    )
                )
        for copy in copies:
            copy.start()
        for copy in copies:
            copy.wait()
        pltpu.make_async_copy(down, down_out, out_sem).start()

    weight = down[pl.ds(pl.multiple_of(step * TILE, TILE), TILE), :]
    hidden_grad = dot_nt(grad_ref[...], weight)
    gate_out[...] = (hidden_grad * slope_ref[...].astype(jnp.float32)).astype(jnp.bfloat16)
    up_out[...] = (hidden_grad * silu_ref[...].astype(jnp.float32)).astype(jnp.bfloat16)

    @pl.when(step == pl.num_programs(0) - 1)
    def _():
        pltpu.make_async_copy(down, down_out, out_sem).wait()


def ffn_hidden_grad(out_grad, slope, silu, ahead, behind, owners):
    size = len(ahead)
    length, width = out_grad.shape
    columns = slope.shape[1]
    bf16 = jnp.bfloat16
    tall = pl.BlockSpec((length, TILE), lambda i, owners: (0, i))
    anywhere = pl.BlockSpec(memory_space=pl.ANY)
    act = jax.ShapeDtypeStruct((length, columns), bf16)
    weight = (2 * size * ahead[0].shape[0], width)
    return pl.pallas_call(
        functools.partial(hidden_grad_kernel, size),
        grid_spec=pltpu.PrefetchScalarGridSpec(
            num_scalar_prefetch=1,
            grid=(columns // TILE,),
            in_specs=[pl.BlockSpec((length, width), lambda i, owners: (0, 0)), tall, tall]
            + [anywhere] * (2 * size),
            out_specs=[tall, tall, anywhere],
            scratch_shapes=[
                pltpu.VMEM(weight, bf16),
                pltpu.SemaphoreType.DMA((2, size)),
                pltpu.SemaphoreType.DMA,
            ],
        ),
        out_shape=(act, act, jax.ShapeDtypeStruct(weight, bf16)),
        compiler_params=pltpu.CompilerParams(vmem_limit_bytes=56 * 2**20),
        cost_estimate=pl.CostEstimate(flops=0, bytes_accessed=2**20, transcendentals=0),
    )(owners, out_grad, slope, silu, *ahead, *behind)


def rows_grad_kernel(gate_grad_ref, up_grad_ref, gate_ref, up_ref, own_ref, other_ref, sent_ref):
    piece = own_ref.shape[0]
    total = dot_nt(gate_grad_ref[...], gate_ref[...]) + dot_nt(up_grad_ref[...], up_ref[...])
    total = total.astype(jnp.bfloat16)
    own_ref[...] = total[:piece]
    other_ref[...] = total[piece : 2 * piece]
    sent_ref[...] = total[2 * piece :]


def ffn_rows_grad(gate_grad, up_grad, gate, up):
    length, columns = gate_grad.shape
    width = gate.shape[0]
    piece = length // 4
    bf16 = jnp.bfloat16
    whole = pl.BlockSpec((length, columns), lambda i: (0, 0))
    weight = pl.BlockSpec((TILE, columns), lambda i: (i, 0))
    part = pl.BlockSpec((piece, TILE), lambda i: (0, i))
    return pl.pallas_call(
        rows_grad_kernel,
        grid=(width // TILE,),
        in_specs=[whole, whole, weight, weight],
        out_specs=[part, part, pl.BlockSpec((2 * piece, TILE), lambda i: (0, i))],
        out_shape=(
            jax.ShapeDtypeStruct((piece, width), bf16),
            jax.ShapeDtypeStruct((piece, width), bf16),
            jax.ShapeDtypeStruct((2 * piece, width), bf16),
        ),
        compiler_params=pltpu.CompilerParams(vmem_limit_bytes=56 * 2**20),
        cost_estimate=pl.CostEstimate(flops=0, bytes_accessed=2**20, transcendentals=0),
    )(gate_grad, up_grad, gate, up)


def lay_kernel(size, sizes, owners_ref, *refs):
    chunks, refs = refs[: 2 * size], refs[2 * size :]
    qkv_out, out_out, gains_out, sems = refs
    rows, top, qkv_columns, columns = sizes
    copies = []
    for which, count in ((0, top), (1, rows - top)):
        for index in range(size):
            chunk = chunks[which * size + index]
            owner = owners_ref[which, index]
            first = pl.multiple_of(owner * rows + which * top, 16)
            target = pl.ds(first, count)
            pairs = [
                (chunk.at[pl.ds(0, count), pl.ds(0, qkv_columns)], qkv_out.at[target, :]),
                (
                    chunk.at[pl.ds(0, count), pl.ds(qkv_columns, columns - qkv_columns)],
                    out_out.at[target, :],
                ),
            ]
            if which:
                pairs.append((chunk.at[pl.ds(count, 16), :], gains_out.at[owner]))
            for kind, (source, place) in enumerate(pairs):
                copies.append(pltpu.make_async_copy(source, place, sems.at[kind, which, index]))
    for copy in copies:
        copy.start()
    for copy in copies:
        copy.wait()


def lay_attention(ahead, behind, owners, rows, qkv_columns):
    size = len(ahead)
    top, columns = ahead[0].shape
    bf16 = jnp.bfloat16
    anywhere = pl.BlockSpec(memory_space=pl.ANY)
    return pl.pallas_call(
        functools.partial(lay_kernel, size, (rows, top, qkv_columns, columns)),
        grid_spec=pltpu.PrefetchScalarGridSpec(
            num_scalar_prefetch=1,
            grid=(1,),
            in_specs=[anywhere] * (2 * size),
            out_specs=[pl.BlockSpec(memory_space=pltpu.VMEM)] * 3,
            scratch_shapes=[pltpu.SemaphoreType.DMA((3, 2, size))],
        ),
        out_shape=(
            jax.ShapeDtypeStruct((size * rows, qkv_columns), bf16),
            jax.ShapeDtypeStruct((size * rows, columns - qkv_columns), bf16),
            jax.ShapeDtypeStruct((size, 16, columns), bf16),
        ),
        cost_estimate=pl.CostEstimate(flops=0, bytes_accessed=7 * 2**20, transcendentals=0),
    )(owners, *ahead, *behind)


def pick_kernel(sizes, index_ref, gate_ref, up_ref, gate_out, up_out):
    size, part, window = sizes
    rows = gate_ref.shape[0]
    for source, target in ((gate_ref, gate_out), (up_ref, up_out)):
        for index in range(4):
            count = min(window, part - index * window)

            @pl.when(index_ref[0] == index)
            def _():
                parts = []
                for owner in range(size):
                    first = owner * part + index * window
                    low, high = first // 128 * 128, -(-(first + count) // 128) * 128
                    wide = source[:, low:high].astype(jnp.float32)
                    parts.append(wide[:, first - low : first - low + count])
                    if count < window:
                        parts.append(jnp.zeros((rows, window - count), jnp.float32))
                target[...] = jnp.concatenate(parts, axis=1).astype(target.dtype)


def pick_hidden(gate, up, seq_index, size, part, window):
    rows, columns = gate.shape
    block = 48 if rows % 48 == 0 else rows
    wide = pl.BlockSpec((block, columns), lambda i, index: (i, 0))
    narrow = pl.BlockSpec((block, size * window), lambda i, index: (i, 0))
    out = jax.ShapeDtypeStruct((rows, size * window), gate.dtype)
    return pl.pallas_call(
        functools.partial(pick_kernel, (size, part, window)),
        grid_spec=pltpu.PrefetchScalarGridSpec(
            num_scalar_prefetch=1,
            grid=(rows // block,),
            in_specs=[wide, wide],
            out_specs=[narrow, narrow],
        ),
        out_shape=(out, out),
        compiler_params=pltpu.CompilerParams(vmem_limit_bytes=32 * 2**20),
        cost_estimate=pl.CostEstimate(flops=0, bytes_accessed=8 * 2**20, transcendentals=0),
    )(jnp.reshape(seq_index, (1,)).astype(jnp.int32), gate, up)


def spread_kernel(sizes, index_ref, own_ref, other_ref, near_ref, far_ref, out_ref, parts):
    size, part, window = sizes
    me = index_ref[0]
    parts[me] = own_ref[...]
    parts[me ^ 2] = other_ref[...]
    parts[me ^ 1] = near_ref[...]
    parts[me ^ 3] = far_ref[...]
    pieces = []
    for owner in range(size):
        for index in range(4):
            count = min(window, part - index * window)
            first = owner * window
            low, high = first // 128 * 128, -(-(first + count) // 128) * 128
            wide = parts[index, :, low:high].astype(jnp.float32)
            pieces.append(wide[:, first - low : first - low + count])
    out_ref[...] = jnp.concatenate(pieces, axis=1)


def spread_hidden(pieces, which, seq_index, size, part, window):
    _, rows, columns = pieces[0].shape
    block = 48 if rows % 48 == 0 else rows
    narrow = pl.BlockSpec((None, block, columns), lambda i, index: (which, i, 0))
    return pl.pallas_call(
        functools.partial(spread_kernel, (size, part, window)),
        grid_spec=pltpu.PrefetchScalarGridSpec(
            num_scalar_prefetch=1,
            grid=(rows // block,),
            in_specs=[narrow] * 4,
            out_specs=pl.BlockSpec((block, size * part), lambda i, index: (i, 0)),
            scratch_shapes=[pltpu.VMEM((4, block, columns), pieces[0].dtype)],
        ),
        out_shape=jax.ShapeDtypeStruct((rows, size * part), jnp.float32),
        compiler_params=pltpu.CompilerParams(vmem_limit_bytes=32 * 2**20),
        cost_estimate=pl.CostEstimate(flops=0, bytes_accessed=64 * 2**20, transcendentals=0),
    )(jnp.reshape(seq_index, (1,)), *pieces)


def norm_forward(values, gain):
    inverse = lax.rsqrt(jnp.mean(values * values, axis=-1, keepdims=True) + norm_epsilon)
    unit = values * inverse
    return (unit * gain, unit, inverse)


def norm_backward(grad_in, unit, inverse, gain):
    scaled = grad_in * gain
    return inverse * (scaled - unit * jnp.mean(scaled * unit, axis=-1, keepdims=True))


def transpose_dot(left, right):
    return lax.dot_general(
        left, right, (((0,), (0,)), ((), ())), preferred_element_type=jnp.float32
    )


def by_rows(values):
    return with_layout_constraint(values, Layout(major_to_minor=(0, 1)))


def dot_transposed(left, right):
    return lax.dot_general(
        left, right, (((1,), (1,)), ((), ())), preferred_element_type=jnp.float32
    )


def split_rows(rows):
    return (rows // 32) * 16


def ring_ids(size):
    return list(range(0, size, 2)) + [i for i in range(size - 1, 0, -1) if i % 2]


def ring_perms(size):
    ids = ring_ids(size)
    forward = [(ids[i], ids[(i + 1) % size]) for i in range(size)]
    return forward, [(b, a) for a, b in forward]


def ring_owners(size):
    ids = ring_ids(size)
    table = np.zeros((size, 4, size), np.int32)
    for place, device in enumerate(ids):
        for step in range(size):
            table[device, 0, step] = ids[(place - step) % size]
            table[device, 1, step] = ids[(place + step) % size]
            table[device, 2, step] = ids[(place - 1 - step) % size]
            table[device, 3, step] = ids[(place + 1 + step) % size]
    return lax.dynamic_index_in_dim(
        jnp.asarray(table), lax.axis_index("fsdp").astype(jnp.uint32), 0, keepdims=False
    )


def after(value, *needed):
    return lax.optimization_barrier((value, *needed))[0] if needed else value


class GatherRing:
    def __init__(self, ahead, behind, size):
        self.perms = ring_perms(size)
        self.ahead, self.behind = [ahead], [behind]

    def step(self, first=(), last=()):
        forward, backward = self.perms
        ahead = lax.ppermute(after(self.ahead[-1], *first), "fsdp", forward)
        behind = lax.ppermute(after(self.behind[-1], *first), "fsdp", backward)
        self.ahead.append(after(ahead, *last))
        self.behind.append(after(behind, *last))


class ScatterRing:
    def __init__(self, way, blocks, size, owners, rows=None):
        self.perm = ring_perms(size)[way]
        self.owners = lax.squeeze(lax.slice_in_dim(owners, 2 + way, 3 + way), (0,)).astype(
            jnp.uint32
        )
        self.blocks, self.count = blocks, 0
        self.first, self.last = rows or (0, blocks.shape[1])
        self.sum = self.own().astype(jnp.bfloat16)

    def own(self):
        owner = lax.squeeze(lax.slice_in_dim(self.owners, self.count, self.count + 1), (0,))
        zero = jnp.uint32(0)
        shape = (1, self.last - self.first, self.blocks.shape[2])
        start = (owner, jnp.uint32(self.first), zero)
        return lax.dynamic_slice(self.blocks, start, shape)[0].astype(jnp.float32)

    def step(self, *needed):
        came = after(lax.ppermute(self.sum, "fsdp", self.perm), *needed)
        self.count += 1
        self.sum = (came.astype(jnp.float32) + self.own()).astype(jnp.bfloat16)
        return self.sum


def exchange(values, mask):
    return lax.ppermute(values, "seq", [(i, i ^ mask) for i in range(4)])


def gather_seq(block, *needed):
    block = after(block, *needed)
    other = exchange(block, 2)
    return [block, other, exchange(block, 1), exchange(other, 1)]


def in_order(pieces, seq_index):
    high, low = seq_index // 2, seq_index % 2

    def pick(first, second, flag):
        return jnp.where(flag == 0, first, second), jnp.where(flag == 0, second, first)

    mine = pick(pieces[0], pieces[1], high)
    theirs = pick(pieces[2], pieces[3], high)
    return [*pick(mine[0], theirs[0], low), *pick(mine[1], theirs[1], low)]


def scatter_seq(own, other, there):
    rows = own.shape[0]
    came = exchange(there, 1).astype(jnp.float32)
    sent = (other.astype(jnp.float32) + came[rows:]).astype(jnp.bfloat16)
    near = own.astype(jnp.float32) + came[:rows]
    return near + exchange(sent, 2).astype(jnp.float32), sent


def swap(blocks):
    return lax.all_to_all(blocks, "seq", split_axis=0, concat_axis=0, tiled=True)


def side_by_side(blocks):
    return blocks.transpose(1, 0, 2).reshape(blocks.shape[1], -1)


def apart(values):
    return values.reshape(values.shape[0], 4, -1).transpose(1, 0, 2)


def body(
    tokens,
    norm_gain,
    query_weight,
    key_weight,
    value_weight,
    query_gain,
    key_gain,
    out_weight,
    ffn_gain,
    gate_weight,
    up_weight,
    down_weight,
    cotangent,
):
    bf16, f32 = jnp.bfloat16, jnp.float32
    size = lax.axis_size("fsdp")
    seq_index = lax.axis_index("seq")
    owners = ring_owners(size)
    own_rows, width = query_weight.shape
    head_part = query_gain.shape[0]
    head_width = head_part * size
    query_columns = width // 4
    key_columns = key_weight.shape[1] // 4
    ff_part = down_weight.shape[0]
    window = -(-ff_part // 64) * 16

    def columns_of(weight, count):
        return lax.dynamic_slice_in_dim(weight, seq_index.astype(jnp.uint32) * count, count, 1)

    def hidden_rows(weight):
        tall = jnp.pad(weight, ((0, 4 * window - ff_part), (0, 0)))
        return lax.dynamic_slice_in_dim(tall, seq_index.astype(jnp.uint32) * window, window, 0)

    gains = jnp.concatenate([norm_gain, ffn_gain, query_gain, key_gain])
    gain_count = gains.shape[0]
    qkv_columns = query_columns + 2 * key_columns
    packed_columns = qkv_columns + query_columns
    gain_rows = jnp.pad(gains[None], ((0, 15), (0, packed_columns - gain_count)))
    packed = jnp.concatenate(
        [
            columns_of(query_weight, query_columns),
            columns_of(key_weight, key_columns),
            columns_of(value_weight, key_columns),
            columns_of(out_weight, query_columns),
        ],
        axis=1,
    )
    top = split_rows(own_rows + 16)
    first_ring = GatherRing(
        packed[:top], jnp.concatenate([packed[top:], gain_rows], axis=0), size
    )
    for _ in range(size - 1):
        first_ring.step()
    ffn_ring = GatherRing(
        *pick_hidden(gate_weight, up_weight, seq_index, size, ff_part, window), size
    )
    down_rows = hidden_rows(down_weight)
    def advance(rings, *needed):
        for way in rings:
            if way.count < size - 1:
                way.step(*needed)

    for step in range(1, size):
        ffn_ring.step((first_ring.ahead[2],) if step == 1 else ())
    down_ring = GatherRing(down_rows[: window // 2], down_rows[window // 2 :], size)
    for step in range(1, size - 2):
        lag = min(step + 2, size - 1)
        down_ring.step((ffn_ring.ahead[lag], ffn_ring.behind[lag]))

    qkv_all, out_part, gains_all = lay_attention(
        first_ring.ahead, first_ring.behind, owners, own_rows, qkv_columns
    )
    gains_all = gains_all[:, 0].astype(f32)
    first_gain = gains_all[:, :own_rows].reshape(-1)
    second_gain = gains_all[:, own_rows : 2 * own_rows].reshape(-1)
    q_gain_f = gains_all[:, 2 * own_rows : 2 * own_rows + head_part].reshape(-1)
    k_gain_f = gains_all[:, 2 * own_rows + head_part : 2 * (own_rows + head_part)].reshape(-1)

    inputs = tokens[0]
    tok_rows = inputs.shape[0]
    length = 4 * tok_rows
    input_blocks = gather_seq(inputs)
    inputs_all = jnp.concatenate(in_order(input_blocks, seq_index), axis=0).astype(f32)
    out_grad = cotangent[0]
    grad_blocks = gather_seq(out_grad, input_blocks[1])
    out_grad_all = jnp.concatenate(grad_blocks, axis=0)


    out_other = exchange(after(out_part, input_blocks[1]), 2)
    normed, norm_unit, norm_inverse = norm_forward(inputs_all, first_gain)
    normed_low = after(normed.astype(bf16), grad_blocks[1])
    qkv_t = lax.dot_general(
        qkv_all, normed_low, (((0,), (1,)), ((), ())), preferred_element_type=f32
    )
    sizes = (query_columns // head_width, key_columns // head_width, head_width)
    cosine, sine = rope_rows(length, head_width)
    tables = (q_gain_f[:, None], k_gain_f[:, None], cosine, sine)
    mixed_heads, mixed_t, totals = attention_forward(qkv_t, *tables, sizes)
    mixed = side_by_side(swap(mixed_heads.reshape(4, tok_rows, query_columns)))
    out_other = after(out_other, mixed_heads)
    out_blocks = [out_part, out_other, exchange(out_part, 1), exchange(out_other, 1)]
    out_all = jnp.concatenate(in_order(out_blocks, seq_index), axis=1)
    attended = jnp.dot(mixed, out_all, preferred_element_type=f32)
    middle = inputs.astype(f32) + attended
    normed_two, middle_unit, middle_inverse = norm_forward(middle, second_gain)
    normed_two_low = normed_two.astype(bf16)
    normed_blocks = gather_seq(normed_two_low)
    normed_two_all = jnp.concatenate(normed_blocks, axis=0)
    mixed_all = jnp.concatenate(
        in_order(gather_seq(mixed_heads, normed_blocks[1]), seq_index), axis=1
    )

    slope, silu, hidden, gate_all, up_all = ffn_hidden(
        normed_blocks, ffn_ring.ahead, ffn_ring.behind, owners
    )
    while len(down_ring.ahead) < size:
        down_ring.step((), (hidden,))
    down_weight_grad = transpose_dot(hidden, out_grad_all).astype(bf16)
    down_blocks = down_weight_grad.reshape(size, window, width)
    down_sums = (
        ScatterRing(0, down_blocks, size, owners, (0, window // 2)),
        ScatterRing(1, down_blocks, size, owners, (window // 2, window)),
    )
    gate_grad, up_grad, down_all = ffn_hidden_grad(
        after(out_grad_all, *(way.sum for way in down_sums)),
        slope,
        silu,
        down_ring.ahead,
        down_ring.behind,
        owners,
    )
    advance(down_sums, gate_grad)
    gate_weight_grad = transpose_dot(
        after(normed_two_all, *(way.sum for way in down_sums)), gate_grad
    ).astype(bf16)
    gate_sums = ScatterRing(
        0, gate_weight_grad.reshape(size, own_rows, size * window), size, owners
    )
    up_weight_grad = transpose_dot(after(normed_two_all, gate_sums.sum), up_grad).astype(bf16)
    up_sums = ScatterRing(1, up_weight_grad.reshape(size, own_rows, size * window), size, owners)
    ffn_sums = (gate_sums, up_sums)
    advance(down_sums, up_sums.sum)
    normed_parts = ffn_rows_grad(
        after(gate_grad, *(way.sum for way in down_sums)), up_grad, gate_all, up_all
    )
    normed_two_grad, half_sum = scatter_seq(*normed_parts)
    advance(ffn_sums, normed_parts[0])
    advance(down_sums, normed_parts[0])
    advance(ffn_sums, half_sum)
    advance(down_sums, half_sum)
    ffn_gain_grad = jnp.sum(normed_two_grad * middle_unit, axis=0)
    middle_grad = out_grad.astype(f32) + norm_backward(
        normed_two_grad, middle_unit, middle_inverse, second_gain
    )
    attended_low = middle_grad.astype(bf16)
    mixed_grad = dot_transposed(attended_low, out_all).astype(bf16)
    advance(ffn_sums, mixed_grad)
    advance(down_sums, mixed_grad)
    mixed_grad_heads = swap(apart(mixed_grad)).reshape(length, query_columns)
    qkv_grad, head_gains = attention_backward(
        qkv_t, *tables, mixed_t, totals, mixed_grad_heads, sizes
    )
    attended_columns = after(
        swap(apart(after(attended_low, mixed_grad_heads))), qkv_grad
    ).reshape(length, query_columns)
    out_weight_grad = by_rows(transpose_dot(mixed_all, attended_columns).astype(bf16))
    advance(ffn_sums, qkv_grad)
    advance(down_sums, qkv_grad)
    qkv_grad = after(qkv_grad, gate_sums.sum, up_sums.sum)
    head_gains = jnp.sum(head_gains, axis=1)
    query_gain_grad, key_gain_grad = head_gains[:head_width], head_gains[head_width:]
    qkv_weight_grad = by_rows(transpose_dot(normed_low, qkv_grad).astype(bf16))
    normed_partial = dot_transposed(qkv_grad, qkv_all)
    norm_gain_grad = jnp.sum(normed_partial * norm_unit, axis=0)
    partial_blocks = normed_partial.astype(bf16).reshape(4, tok_rows, width)

    def partial_of(mask):
        index = (seq_index ^ mask).astype(jnp.uint32)
        return lax.dynamic_index_in_dim(partial_blocks, index, 0, keepdims=False)

    normed_grad, normed_sent = scatter_seq(
        partial_of(0),
        partial_of(2),
        jnp.concatenate([partial_of(1), partial_of(3)], axis=0),
    )
    _, own_unit, own_inverse = norm_forward(inputs.astype(f32), first_gain)
    inputs_grad = middle_grad + norm_backward(normed_grad, own_unit, own_inverse, first_gain)

    gain_grads = jnp.concatenate(
        [
            norm_gain_grad.reshape(size, -1),
            ffn_gain_grad.reshape(size, -1),
            query_gain_grad.reshape(size, -1),
            key_gain_grad.reshape(size, -1),
        ],
        axis=1,
    )
    gain_blocks = jnp.pad(
        gain_grads[:, None], ((0, 0), (0, 15), (0, packed_columns - gain_count))
    )
    packed_blocks = jnp.concatenate([qkv_weight_grad, out_weight_grad], axis=1).reshape(
        size, own_rows, packed_columns
    )
    packed_blocks = jnp.concatenate([packed_blocks, gain_blocks.astype(bf16)], axis=1)
    last_sums = (
        ScatterRing(0, packed_blocks, size, owners, (0, top)),
        ScatterRing(1, packed_blocks, size, owners, (top, own_rows + 16)),
    )
    advance(ffn_sums, *(way.sum for way in last_sums))
    advance(down_sums, *(way.sum for way in last_sums))
    down_share = jnp.concatenate([way.sum for way in down_sums], axis=0)
    down_pieces = gather_seq(down_share)
    down_partial = jnp.dot(
        after(hidden, gate_sums.sum), down_all, preferred_element_type=f32
    ).astype(bf16)
    down_sum, down_sent = scatter_seq(
        down_partial[:tok_rows],
        down_partial[tok_rows : 2 * tok_rows],
        down_partial[2 * tok_rows :],
    )
    rest = [(down_sum, down_pieces[1]), (normed_grad, down_sent)]
    while gate_sums.count < size - 1:
        advance(ffn_sums, *(rest.pop() if rest else ()))
        advance(last_sums, gate_sums.sum, up_sums.sum)
        advance(last_sums, gate_sums.sum, up_sums.sum)
    both = jnp.stack([gate_sums.sum, up_sums.sum])
    ffn_blocks = gather_seq(both)
    while last_sums[0].count < size - 1:
        advance(last_sums, *((ffn_blocks[1],) if last_sums[0].count == size - 2 else (both,)))
    packed_share = jnp.concatenate([way.sum for way in last_sums], axis=0)
    output = middle + down_sum
    down_full = jnp.concatenate(in_order(down_pieces, seq_index), axis=0)[
        :ff_part
    ].astype(f32)
    gate_full, up_full = (
        spread_hidden(ffn_blocks, which, seq_index, size, ff_part, window) for which in range(2)
    )
    packs = in_order(gather_seq(packed_share), seq_index)

    def unpack(first, count):
        return jnp.concatenate(
            [p[:own_rows, first : first + count] for p in packs], axis=1
        ).astype(f32)

    gain_sum = sum(p[own_rows, :gain_count].astype(f32) for p in packs)
    return (
        output[None].astype(bf16),
        inputs_grad[None].astype(bf16),
        gain_sum[:own_rows],
        unpack(0, query_columns),
        unpack(query_columns, key_columns),
        unpack(query_columns + key_columns, key_columns),
        gain_sum[2 * own_rows : 2 * own_rows + head_part],
        gain_sum[2 * own_rows + head_part :],
        unpack(qkv_columns, query_columns),
        gain_sum[own_rows : 2 * own_rows],
        gate_full,
        up_full,
        down_full,
    )


def solution(mesh):
    in_specs = (
        P("fsdp", "seq", None),
        P("fsdp"),
        P("fsdp", None),
        P("fsdp", None),
        P("fsdp", None),
        P("fsdp"),
        P("fsdp"),
        P("fsdp", None),
        P("fsdp"),
        P("fsdp", None),
        P("fsdp", None),
        P("fsdp", None),
        P("fsdp", "seq", None),
    )
    out_specs = (
        P("fsdp", "seq", None),
        P("fsdp", "seq", None),
        P("fsdp"),
        P("fsdp", None),
        P("fsdp", None),
        P("fsdp", None),
        P("fsdp"),
        P("fsdp"),
        P("fsdp", None),
        P("fsdp"),
        P("fsdp", None),
        P("fsdp", None),
        P("fsdp", None),
    )
    return jax.shard_map(body, mesh=mesh, in_specs=in_specs, out_specs=out_specs, check_vma=False)
```

```python
import functools
import math

import jax
import jax.numpy as jnp
import numpy as np
from jax import lax
from jax.experimental import pallas as pl
from jax.experimental.layout import Layout, with_layout_constraint
from jax.experimental.pallas import tpu as pltpu
from jax.sharding import PartitionSpec as P

norm_epsilon = 1e-05
TILE = 256
log2_e = math.log2(math.e)


def rope_rows(length, width):
    half_width = width // 2
    inverse = jnp.exp(
        jnp.arange(half_width, dtype=jnp.float32) * (-2.0 * math.log(1000000.0) / width)
    )
    angles = inverse[:, None] * jnp.arange(length, dtype=jnp.int32).astype(jnp.float32)[None, :]
    return jnp.cos(angles), jnp.sin(angles)


def head_norm(values):
    inverse = lax.rsqrt(jnp.mean(values * values, axis=0, keepdims=True) + norm_epsilon)
    return values * inverse, inverse


def head_turn(values, cosine, sine):
    half = values.shape[0] // 2
    first, second = values[:half], values[half:]
    return jnp.concatenate(
        [first * cosine - second * sine, second * cosine + first * sine], axis=0
    )


def head_turn_back(values, cosine, sine):
    half = values.shape[0] // 2
    first, second = values[:half], values[half:]
    return jnp.concatenate(
        [first * cosine + second * sine, second * cosine - first * sine], axis=0
    )


def fill_heads(qkv_ref, q_gain_ref, k_gain_ref, cos_ref, sin_ref, queries, keys, keys_t, values, values_t, sizes):
    heads, groups, width = sizes
    cosine, sine = cos_ref[...], sin_ref[...]

    @pl.loop(0, heads)
    def _(head):
        unit, _ = head_norm(qkv_ref[pl.ds(head * width, width), :])
        turned = head_turn(unit * q_gain_ref[...], cosine, sine)
        queries[head] = (turned * (width**-0.5 * log2_e)).astype(jnp.bfloat16)

    @pl.loop(0, groups)
    def _(group):
        unit, _ = head_norm(qkv_ref[pl.ds((heads + group) * width, width), :])
        turned = head_turn(unit * k_gain_ref[...], cosine, sine)
        keys[group] = turned.T.astype(jnp.bfloat16)
        if keys_t is not None:
            keys_t[group] = turned.astype(jnp.bfloat16)
        value = qkv_ref[pl.ds((heads + groups + group) * width, width), :]
        if values is not None:
            values[group] = value.T.astype(jnp.bfloat16)
        if values_t is not None:
            values_t[group] = value.astype(jnp.bfloat16)


def diagonal_mask():
    key_place = lax.broadcasted_iota(jnp.int32, (TILE, TILE), 0)
    query_place = lax.broadcasted_iota(jnp.int32, (TILE, TILE), 1)
    return key_place <= query_place


def causal_exp(scores, count):
    weights = jnp.exp2(scores)
    last = jnp.where(diagonal_mask(), weights[count - TILE :], 0.0)
    if count == TILE:
        return last
    return jnp.concatenate([weights[: count - TILE], last], axis=0)


def dot(left, right):
    return jnp.dot(left, right, preferred_element_type=jnp.float32)


def dot_nt(left, right):
    return lax.dot_general(
        left, right, (((1,), (1,)), ((), ())), preferred_element_type=jnp.float32
    )


def forward_kernel(sizes, qkv_ref, q_gain_ref, k_gain_ref, cos_ref, sin_ref, mixed_ref, mixed_t_ref, total_ref, queries, keys, values_t, mixed_f):
    heads, groups, width = sizes
    ratio = heads // groups
    length = qkv_ref.shape[1]
    fill_heads(qkv_ref, q_gain_ref, k_gain_ref, cos_ref, sin_ref, queries, keys, None, None, values_t, sizes)

    @pl.loop(0, heads)
    def _(head):
        group = head // ratio
        for tile in range(length // TILE):
            count = (tile + 1) * TILE
            columns = pl.ds(tile * TILE, TILE)
            scores = dot(keys[group, pl.ds(0, count), :], queries[head, :, columns])
            weights = causal_exp(scores, count)
            total = jnp.sum(weights, axis=0, keepdims=True)
            result = dot(values_t[group, :, pl.ds(0, count)], weights.astype(jnp.bfloat16))
            mixed_f[pl.ds(head * width, width), columns] = result * (1.0 / total)
            total_ref[pl.ds(head, 1), columns] = jnp.log2(total)

    for block in range(heads * width // 128):
        rows = mixed_f[pl.ds(block * 128, 128), :]
        mixed_t_ref[pl.ds(block * 128, 128), :] = rows.astype(jnp.bfloat16)
        mixed_ref[:, pl.ds(block * 128, 128)] = rows.T.astype(jnp.bfloat16)


def backward_kernel(sizes, qkv_ref, q_gain_ref, k_gain_ref, cos_ref, sin_ref, mixed_t_ref, total_ref, grad_ref, out_ref, gain_ref, out_t, queries, keys, keys_t, values, grads, key_sum, value_sum):
    heads, groups, width = sizes
    ratio = heads // groups
    length = qkv_ref.shape[1]
    fill_heads(qkv_ref, q_gain_ref, k_gain_ref, cos_ref, sin_ref, queries, keys, keys_t, values, None, sizes)
    for block in range(heads * width // 128):
        turned = grad_ref[:, pl.ds(block * 128, 128)].astype(jnp.float32).T
        grads[pl.ds(block * 128, 128), :] = turned.astype(jnp.bfloat16)
    key_sum[...] = jnp.zeros_like(key_sum)
    value_sum[...] = jnp.zeros_like(value_sum)
    gain_ref[...] = jnp.zeros_like(gain_ref)
    cosine, sine = cos_ref[...], sin_ref[...]

    def finish(grad_turned, rows, gain, first):
        grad = head_turn_back(grad_turned, cosine, sine)
        unit, inverse = head_norm(qkv_ref[rows, :])
        product = grad * unit
        part = product[:, :128]
        for lane in range(128, length, 128):
            part = part + product[:, lane : lane + 128]
        gain_ref[pl.ds(first, width), :] += part
        scaled = grad * gain
        before = inverse * (scaled - unit * jnp.mean(scaled * unit, axis=0, keepdims=True))
        out_t[rows, :] = before

    @pl.loop(0, heads)
    def _(head):
        group = head // ratio
        rows = pl.ds(head * width, width)
        query_parts = []
        for tile in range(length // TILE):
            count = (tile + 1) * TILE
            columns = pl.ds(tile * TILE, TILE)
            query = queries[head, :, columns]
            grad = grads[rows, columns]
            scores = dot(keys[group, pl.ds(0, count), :], query) - total_ref[pl.ds(head, 1), columns]
            weights = causal_exp(scores, count)
            inner = jnp.sum(
                grad.astype(jnp.float32) * mixed_t_ref[rows, columns].astype(jnp.float32),
                axis=0,
                keepdims=True,
            )
            weight_grad = dot(values[group, pl.ds(0, count), :], grad)
            score_grad = (weights * (weight_grad - inner)).astype(jnp.bfloat16)
            query_parts.append(dot(keys_t[group, :, pl.ds(0, count)], score_grad))
            key_sum[group, pl.ds(0, count), :] += dot_nt(score_grad, query)
            value_sum[group, pl.ds(0, count), :] += dot_nt(weights.astype(jnp.bfloat16), grad)
        query_grad = jnp.concatenate(query_parts, axis=1) * width**-0.5
        finish(query_grad, rows, q_gain_ref[...], 0)

    for group in range(groups):
        key_grad = key_sum[group].T * (1.0 / log2_e)
        finish(key_grad, pl.ds((heads + group) * width, width), k_gain_ref[...], width)
        out_t[pl.ds((heads + groups + group) * width, width), :] = value_sum[group].T

    for block in range(out_t.shape[0] // 128):
        some = pl.ds(block * 128, 128)
        out_ref[:, some] = out_t[some, :].T.astype(jnp.bfloat16)


def attention_forward(qkv_t, q_gain, k_gain, cosine, sine, sizes):
    heads, groups, width = sizes
    length = qkv_t.shape[1]
    bf16, f32 = jnp.bfloat16, jnp.float32
    pairs = heads * length * length
    return pl.pallas_call(
        functools.partial(forward_kernel, sizes),
        out_shape=(
            jax.ShapeDtypeStruct((length, heads * width), bf16),
            jax.ShapeDtypeStruct((heads * width, length), bf16),
            jax.ShapeDtypeStruct((-(-heads // 8) * 8, length), f32),
        ),
        scratch_shapes=[
            pltpu.VMEM((heads, width, length), bf16),
            pltpu.VMEM((groups, length, width), bf16),
            pltpu.VMEM((groups, width, length), bf16),
            pltpu.VMEM((heads * width, length), f32),
        ],
        compiler_params=pltpu.CompilerParams(vmem_limit_bytes=32 * 2**20),
        cost_estimate=pl.CostEstimate(
            flops=8 * pairs * width, bytes_accessed=6 * 2**20, transcendentals=pairs
        ),
    )(qkv_t, q_gain, k_gain, cosine, sine)


def attention_backward(qkv_t, q_gain, k_gain, cosine, sine, mixed_t, total, mixed_grad, sizes):
    heads, groups, width = sizes
    length = qkv_t.shape[1]
    bf16, f32 = jnp.bfloat16, jnp.float32
    pairs = heads * length * length
    return pl.pallas_call(
        functools.partial(backward_kernel, sizes),
        out_shape=(
            jax.ShapeDtypeStruct(qkv_t.shape[::-1], bf16),
            jax.ShapeDtypeStruct((2 * width, 128), f32),
        ),
        scratch_shapes=[
            pltpu.VMEM(qkv_t.shape, f32),
            pltpu.VMEM((heads, width, length), bf16),
            pltpu.VMEM((groups, length, width), bf16),
            pltpu.VMEM((groups, width, length), bf16),
            pltpu.VMEM((groups, length, width), bf16),
            pltpu.VMEM((heads * width, length), bf16),
            pltpu.VMEM((groups, length, width), f32),
            pltpu.VMEM((groups, length, width), f32),
        ],
        compiler_params=pltpu.CompilerParams(vmem_limit_bytes=40 * 2**20),
        cost_estimate=pl.CostEstimate(flops=0, bytes_accessed=2**20, transcendentals=0),
    )(qkv_t, q_gain, k_gain, cosine, sine, mixed_t, total, mixed_grad)


def hidden_kernel(size, ids_ref, *refs):
    pieces, chunks, refs = refs[:4], refs[4 : 4 + 2 * size], refs[4 + 2 * size :]
    slope_ref, silu_ref, hidden_ref, gate_out, up_out, tokens, gate, up, *sems = refs
    row_sems, in_sems, out_sems = sems
    step = pl.program_id(0)
    steps = pl.num_programs(0)
    rows = chunks[0].shape[0]
    piece = pieces[0].shape[0]

    @pl.when(step == 0)
    def _():
        copies = [
            pltpu.make_async_copy(
                source, tokens.at[pl.ds(index * piece, piece), :], row_sems.at[index]
            )
            for index, source in enumerate(pieces)
        ]
        for copy in copies:
            copy.start()

        @pl.loop(0, steps)
        def _(tile):
            columns = pl.ds(pl.multiple_of(tile * TILE, TILE), TILE)
            for which, target in ((0, gate), (1, up)):
                for index in range(size):
                    first = pl.multiple_of(ids_ref[which, index] * rows, 16)
                    pltpu.make_async_copy(
                        chunks[which * size + index].at[:, columns],
                        target.at[pl.ds(first, rows), columns],
                        in_sems.at[which, tile],
                    ).start()

        for copy in copies:
            copy.wait()

    columns = pl.ds(pl.multiple_of(step * TILE, TILE), TILE)
    for which, target, result in ((0, gate, gate_out), (1, up, up_out)):
        part = target.at[:, columns]
        pltpu.make_async_copy(part, part, in_sems.at[which, step]).wait()
        pltpu.make_async_copy(part, result.at[:, columns], out_sems.at[which, step]).start()
    for half in range(2):
        some = pl.ds(half * 2 * piece, 2 * piece)
        gate_act = dot(tokens[some, :], gate[:, columns])
        up_act = dot(tokens[some, :], up[:, columns])
        sigmoid = 0.5 + 0.5 * jnp.tanh(0.5 * gate_act)
        silu = gate_act * sigmoid
        hidden_ref[some, :] = (silu * up_act).astype(hidden_ref.dtype)
        silu_ref[some, :] = silu.astype(silu_ref.dtype)
        slope_ref[some, :] = (up_act * sigmoid * (1.0 + gate_act * (1.0 - sigmoid))).astype(
            slope_ref.dtype
        )

    @pl.when(step == steps - 1)
    def _():
        @pl.loop(0, steps)
        def _(tile):
            columns = pl.ds(pl.multiple_of(tile * TILE, TILE), TILE)
            for which, target, result in ((0, gate, gate_out), (1, up, up_out)):
                pltpu.make_async_copy(
                    target.at[:, columns], result.at[:, columns], out_sems.at[which, tile]
                ).wait()


def ffn_hidden(pieces, gate_chunks, up_chunks, ids):
    size = len(gate_chunks)
    part, columns = gate_chunks[0].shape
    piece, width = pieces[0].shape
    length = 4 * piece
    bf16 = jnp.bfloat16
    tall = pl.BlockSpec((length, TILE), lambda i, ids: (0, i))
    act = jax.ShapeDtypeStruct((length, columns), bf16)
    weight = jax.ShapeDtypeStruct((width, columns), bf16)
    anywhere = pl.BlockSpec(memory_space=pl.ANY)
    return pl.pallas_call(
        functools.partial(hidden_kernel, size),
        grid_spec=pltpu.PrefetchScalarGridSpec(
            num_scalar_prefetch=1,
            grid=(columns // TILE,),
            in_specs=[anywhere] * (4 + 2 * size),
            out_specs=[tall, tall, tall, anywhere, anywhere],
            scratch_shapes=[
                pltpu.VMEM((length, width), bf16),
                pltpu.VMEM((width, columns), bf16),
                pltpu.VMEM((width, columns), bf16),
                pltpu.SemaphoreType.DMA((4,)),
                pltpu.SemaphoreType.DMA((2, columns // TILE)),
                pltpu.SemaphoreType.DMA((2, columns // TILE)),
            ],
        ),
        out_shape=(act, act, act, weight, weight),
        compiler_params=pltpu.CompilerParams(vmem_limit_bytes=56 * 2**20),
        cost_estimate=pl.CostEstimate(
            flops=4 * length * width * columns,
            bytes_accessed=36 * 2**20,
            transcendentals=length * columns,
        ),
    )(ids, *pieces, *gate_chunks, *up_chunks)


def hidden_grad_kernel(size, owners_ref, grad_ref, rows_t_ref, slope_ref, silu_ref, *refs):
    chunks, refs = refs[: 2 * size], refs[2 * size :]
    gate_out, up_out, gate_sum, up_sum, down_out, down, in_sems, out_sem = refs
    step = pl.program_id(0)
    rows = chunks[0].shape[0]

    @pl.when(step == 0)
    def _():
        copies = []
        for which in range(2):
            for index in range(size):
                first = pl.multiple_of((2 * owners_ref[which, index] + which) * rows, 16)
                copies.append(
                    pltpu.make_async_copy(
                        chunks[which * size + index],
                        down.at[pl.ds(first, rows), :],
                        in_sems.at[which, index],
                    )
                )
        for copy in copies:
            copy.start()
        for copy in copies:
            copy.wait()
        pltpu.make_async_copy(down, down_out, out_sem).start()

    weight = down[pl.ds(pl.multiple_of(step * TILE, TILE), TILE), :]
    hidden_grad = dot_nt(grad_ref[...], weight)
    gate_grad = (hidden_grad * slope_ref[...].astype(jnp.float32)).astype(jnp.bfloat16)
    up_grad = (hidden_grad * silu_ref[...].astype(jnp.float32)).astype(jnp.bfloat16)
    gate_out[...] = gate_grad
    up_out[...] = up_grad
    gate_sum[...] = dot(rows_t_ref[...], gate_grad).astype(gate_sum.dtype)
    up_sum[...] = dot(rows_t_ref[...], up_grad).astype(up_sum.dtype)

    @pl.when(step == pl.num_programs(0) - 1)
    def _():
        pltpu.make_async_copy(down, down_out, out_sem).wait()


def ffn_hidden_grad(out_grad, rows_t, slope, silu, ahead, behind, owners):
    size = len(ahead)
    length, width = out_grad.shape
    columns = slope.shape[1]
    bf16 = jnp.bfloat16
    tall = pl.BlockSpec((length, TILE), lambda i, owners: (0, i))
    wide = pl.BlockSpec((width, TILE), lambda i, owners: (0, i))
    anywhere = pl.BlockSpec(memory_space=pl.ANY)
    act = jax.ShapeDtypeStruct((length, columns), bf16)
    weight = (2 * size * ahead[0].shape[0], width)
    return pl.pallas_call(
        functools.partial(hidden_grad_kernel, size),
        grid_spec=pltpu.PrefetchScalarGridSpec(
            num_scalar_prefetch=1,
            grid=(columns // TILE,),
            in_specs=[
                pl.BlockSpec((length, width), lambda i, owners: (0, 0)),
                pl.BlockSpec((width, length), lambda i, owners: (0, 0)),
                tall,
                tall,
            ]
            + [anywhere] * (2 * size),
            out_specs=[tall, tall, wide, wide, anywhere],
            scratch_shapes=[
                pltpu.VMEM(weight, bf16),
                pltpu.SemaphoreType.DMA((2, size)),
                pltpu.SemaphoreType.DMA,
            ],
        ),
        out_shape=(
            act,
            act,
            jax.ShapeDtypeStruct((width, columns), bf16),
            jax.ShapeDtypeStruct((width, columns), bf16),
            jax.ShapeDtypeStruct(weight, bf16),
        ),
        compiler_params=pltpu.CompilerParams(vmem_limit_bytes=56 * 2**20),
        cost_estimate=pl.CostEstimate(flops=0, bytes_accessed=2**20, transcendentals=0),
    )(owners, out_grad, rows_t, slope, silu, *ahead, *behind)


def rows_grad_kernel(gate_grad_ref, up_grad_ref, gate_ref, up_ref, own_ref, other_ref, sent_ref):
    piece = own_ref.shape[0]
    total = dot_nt(gate_grad_ref[...], gate_ref[...]) + dot_nt(up_grad_ref[...], up_ref[...])
    total = total.astype(jnp.bfloat16)
    own_ref[...] = total[:piece]
    other_ref[...] = total[piece : 2 * piece]
    sent_ref[...] = total[2 * piece :]


def ffn_rows_grad(gate_grad, up_grad, gate, up):
    length, columns = gate_grad.shape
    width = gate.shape[0]
    piece = length // 4
    bf16 = jnp.bfloat16
    whole = pl.BlockSpec((length, columns), lambda i: (0, 0))
    weight = pl.BlockSpec((TILE, columns), lambda i: (i, 0))
    part = pl.BlockSpec((piece, TILE), lambda i: (0, i))
    return pl.pallas_call(
        rows_grad_kernel,
        grid=(width // TILE,),
        in_specs=[whole, whole, weight, weight],
        out_specs=[part, part, pl.BlockSpec((2 * piece, TILE), lambda i: (0, i))],
        out_shape=(
            jax.ShapeDtypeStruct((piece, width), bf16),
            jax.ShapeDtypeStruct((piece, width), bf16),
            jax.ShapeDtypeStruct((2 * piece, width), bf16),
        ),
        compiler_params=pltpu.CompilerParams(vmem_limit_bytes=56 * 2**20),
        cost_estimate=pl.CostEstimate(flops=0, bytes_accessed=2**20, transcendentals=0),
    )(gate_grad, up_grad, gate, up)


def lay_kernel(size, sizes, owners_ref, *refs):
    chunks, refs = refs[: 2 * size], refs[2 * size :]
    qkv_out, out_out, gains_out, sems = refs
    rows, top, qkv_columns, columns = sizes
    copies = []
    for which, count in ((0, top), (1, rows - top)):
        for index in range(size):
            chunk = chunks[which * size + index]
            owner = owners_ref[which, index]
            first = pl.multiple_of(owner * rows + which * top, 16)
            target = pl.ds(first, count)
            pairs = [
                (chunk.at[pl.ds(0, count), pl.ds(0, qkv_columns)], qkv_out.at[target, :]),
                (
                    chunk.at[pl.ds(0, count), pl.ds(qkv_columns, columns - qkv_columns)],
                    out_out.at[target, :],
                ),
            ]
            if which:
                pairs.append((chunk.at[pl.ds(count, 16), :], gains_out.at[owner]))
            for kind, (source, place) in enumerate(pairs):
                copies.append(pltpu.make_async_copy(source, place, sems.at[kind, which, index]))
    for copy in copies:
        copy.start()
    for copy in copies:
        copy.wait()


def lay_attention(ahead, behind, owners, rows, qkv_columns):
    size = len(ahead)
    top, columns = ahead[0].shape
    bf16 = jnp.bfloat16
    anywhere = pl.BlockSpec(memory_space=pl.ANY)
    return pl.pallas_call(
        functools.partial(lay_kernel, size, (rows, top, qkv_columns, columns)),
        grid_spec=pltpu.PrefetchScalarGridSpec(
            num_scalar_prefetch=1,
            grid=(1,),
            in_specs=[anywhere] * (2 * size),
            out_specs=[pl.BlockSpec(memory_space=pltpu.VMEM)] * 3,
            scratch_shapes=[pltpu.SemaphoreType.DMA((3, 2, size))],
        ),
        out_shape=(
            jax.ShapeDtypeStruct((size * rows, qkv_columns), bf16),
            jax.ShapeDtypeStruct((size * rows, columns - qkv_columns), bf16),
            jax.ShapeDtypeStruct((size, 16, columns), bf16),
        ),
        cost_estimate=pl.CostEstimate(flops=0, bytes_accessed=7 * 2**20, transcendentals=0),
    )(owners, *ahead, *behind)


def pick_kernel(sizes, index_ref, gate_ref, up_ref, gate_out, up_out):
    size, part, window = sizes
    rows = gate_ref.shape[0]
    for source, target in ((gate_ref, gate_out), (up_ref, up_out)):
        for index in range(4):
            count = min(window, part - index * window)

            @pl.when(index_ref[0] == index)
            def _():
                parts = []
                for owner in range(size):
                    first = owner * part + index * window
                    low, high = first // 128 * 128, -(-(first + count) // 128) * 128
                    wide = source[:, low:high].astype(jnp.float32)
                    parts.append(wide[:, first - low : first - low + count])
                    if count < window:
                        parts.append(jnp.zeros((rows, window - count), jnp.float32))
                target[...] = jnp.concatenate(parts, axis=1).astype(target.dtype)


def pick_hidden(gate, up, seq_index, size, part, window):
    rows, columns = gate.shape
    block = 48 if rows % 48 == 0 else rows
    wide = pl.BlockSpec((block, columns), lambda i, index: (i, 0))
    narrow = pl.BlockSpec((block, size * window), lambda i, index: (i, 0))
    out = jax.ShapeDtypeStruct((rows, size * window), gate.dtype)
    return pl.pallas_call(
        functools.partial(pick_kernel, (size, part, window)),
        grid_spec=pltpu.PrefetchScalarGridSpec(
            num_scalar_prefetch=1,
            grid=(rows // block,),
            in_specs=[wide, wide],
            out_specs=[narrow, narrow],
        ),
        out_shape=(out, out),
        compiler_params=pltpu.CompilerParams(vmem_limit_bytes=32 * 2**20),
        cost_estimate=pl.CostEstimate(flops=0, bytes_accessed=8 * 2**20, transcendentals=0),
    )(jnp.reshape(seq_index, (1,)).astype(jnp.int32), gate, up)


def spread_kernel(sizes, index_ref, own_ref, other_ref, near_ref, far_ref, out_ref, parts):
    size, part, window = sizes
    me = index_ref[0]
    parts[me] = own_ref[...]
    parts[me ^ 2] = other_ref[...]
    parts[me ^ 1] = near_ref[...]
    parts[me ^ 3] = far_ref[...]
    pieces = []
    for owner in range(size):
        for index in range(4):
            count = min(window, part - index * window)
            first = owner * window
            low, high = first // 128 * 128, -(-(first + count) // 128) * 128
            wide = parts[index, :, low:high].astype(jnp.float32)
            pieces.append(wide[:, first - low : first - low + count])
    out_ref[...] = jnp.concatenate(pieces, axis=1)


def spread_hidden(pieces, which, seq_index, size, part, window):
    _, rows, columns = pieces[0].shape
    block = 48 if rows % 48 == 0 else rows
    narrow = pl.BlockSpec((None, block, columns), lambda i, index: (which, i, 0))
    return pl.pallas_call(
        functools.partial(spread_kernel, (size, part, window)),
        grid_spec=pltpu.PrefetchScalarGridSpec(
            num_scalar_prefetch=1,
            grid=(rows // block,),
            in_specs=[narrow] * 4,
            out_specs=pl.BlockSpec((block, size * part), lambda i, index: (i, 0)),
            scratch_shapes=[pltpu.VMEM((4, block, columns), pieces[0].dtype)],
        ),
        out_shape=jax.ShapeDtypeStruct((rows, size * part), jnp.float32),
        compiler_params=pltpu.CompilerParams(vmem_limit_bytes=32 * 2**20),
        cost_estimate=pl.CostEstimate(flops=0, bytes_accessed=64 * 2**20, transcendentals=0),
    )(jnp.reshape(seq_index, (1,)), *pieces)


def norm_forward(values, gain):
    inverse = lax.rsqrt(jnp.mean(values * values, axis=-1, keepdims=True) + norm_epsilon)
    unit = values * inverse
    return (unit * gain, unit, inverse)


def norm_backward(grad_in, unit, inverse, gain):
    scaled = grad_in * gain
    return inverse * (scaled - unit * jnp.mean(scaled * unit, axis=-1, keepdims=True))


def transpose_dot(left, right):
    return lax.dot_general(
        left, right, (((0,), (0,)), ((), ())), preferred_element_type=jnp.float32
    )


def by_rows(values):
    return with_layout_constraint(values, Layout(major_to_minor=(0, 1)))


def dot_transposed(left, right):
    return lax.dot_general(
        left, right, (((1,), (1,)), ((), ())), preferred_element_type=jnp.float32
    )


def split_rows(rows):
    return (rows // 32) * 16


def ring_ids(size):
    return list(range(0, size, 2)) + [i for i in range(size - 1, 0, -1) if i % 2]


def ring_perms(size):
    ids = ring_ids(size)
    forward = [(ids[i], ids[(i + 1) % size]) for i in range(size)]
    return forward, [(b, a) for a, b in forward]


def ring_owners(size):
    ids = ring_ids(size)
    table = np.zeros((size, 4, size), np.int32)
    for place, device in enumerate(ids):
        for step in range(size):
            table[device, 0, step] = ids[(place - step) % size]
            table[device, 1, step] = ids[(place + step) % size]
            table[device, 2, step] = ids[(place - 1 - step) % size]
            table[device, 3, step] = ids[(place + 1 + step) % size]
    return lax.dynamic_index_in_dim(
        jnp.asarray(table), lax.axis_index("fsdp").astype(jnp.uint32), 0, keepdims=False
    )


def after(value, *needed):
    return lax.optimization_barrier((value, *needed))[0] if needed else value


class GatherRing:
    def __init__(self, ahead, behind, size):
        self.perms = ring_perms(size)
        self.ahead, self.behind = [ahead], [behind]

    def step(self, first=(), last=()):
        forward, backward = self.perms
        ahead = lax.ppermute(after(self.ahead[-1], *first), "fsdp", forward)
        behind = lax.ppermute(after(self.behind[-1], *first), "fsdp", backward)
        self.ahead.append(after(ahead, *last))
        self.behind.append(after(behind, *last))


class ScatterRing:
    def __init__(self, way, blocks, size, owners, rows=None):
        self.perm = ring_perms(size)[way]
        self.owners = lax.squeeze(lax.slice_in_dim(owners, 2 + way, 3 + way), (0,)).astype(
            jnp.uint32
        )
        self.blocks, self.count = blocks, 0
        self.first, self.last = rows or (0, blocks.shape[1])
        self.sum = self.own().astype(jnp.bfloat16)

    def own(self):
        owner = lax.squeeze(lax.slice_in_dim(self.owners, self.count, self.count + 1), (0,))
        zero = jnp.uint32(0)
        shape = (1, self.last - self.first, self.blocks.shape[2])
        start = (owner, jnp.uint32(self.first), zero)
        return lax.dynamic_slice(self.blocks, start, shape)[0].astype(jnp.float32)

    def step(self, *needed):
        came = after(lax.ppermute(self.sum, "fsdp", self.perm), *needed)
        self.count += 1
        self.sum = (came.astype(jnp.float32) + self.own()).astype(jnp.bfloat16)
        return self.sum


def exchange(values, mask):
    return lax.ppermute(values, "seq", [(i, i ^ mask) for i in range(4)])


def gather_seq(block, *needed):
    block = after(block, *needed)
    other = exchange(block, 2)
    return [block, other, exchange(block, 1), exchange(other, 1)]


def in_order(pieces, seq_index):
    high, low = seq_index // 2, seq_index % 2

    def pick(first, second, flag):
        return jnp.where(flag == 0, first, second), jnp.where(flag == 0, second, first)

    mine = pick(pieces[0], pieces[1], high)
    theirs = pick(pieces[2], pieces[3], high)
    return [*pick(mine[0], theirs[0], low), *pick(mine[1], theirs[1], low)]


def scatter_seq(own, other, there):
    rows = own.shape[0]
    came = exchange(there, 1).astype(jnp.float32)
    sent = (other.astype(jnp.float32) + came[rows:]).astype(jnp.bfloat16)
    near = own.astype(jnp.float32) + came[:rows]
    return near + exchange(sent, 2).astype(jnp.float32), sent


def swap(blocks):
    return lax.all_to_all(blocks, "seq", split_axis=0, concat_axis=0, tiled=True)


def side_by_side(blocks):
    return blocks.transpose(1, 0, 2).reshape(blocks.shape[1], -1)


def apart(values):
    return values.reshape(values.shape[0], 4, -1).transpose(1, 0, 2)


def body(
    tokens,
    norm_gain,
    query_weight,
    key_weight,
    value_weight,
    query_gain,
    key_gain,
    out_weight,
    ffn_gain,
    gate_weight,
    up_weight,
    down_weight,
    cotangent,
):
    bf16, f32 = jnp.bfloat16, jnp.float32
    size = lax.axis_size("fsdp")
    seq_index = lax.axis_index("seq")
    owners = ring_owners(size)
    own_rows, width = query_weight.shape
    head_part = query_gain.shape[0]
    head_width = head_part * size
    query_columns = width // 4
    key_columns = key_weight.shape[1] // 4
    ff_part = down_weight.shape[0]
    window = -(-ff_part // 64) * 16

    def columns_of(weight, count):
        return lax.dynamic_slice_in_dim(weight, seq_index.astype(jnp.uint32) * count, count, 1)

    def hidden_rows(weight):
        tall = jnp.pad(weight, ((0, 4 * window - ff_part), (0, 0)))
        return lax.dynamic_slice_in_dim(tall, seq_index.astype(jnp.uint32) * window, window, 0)

    gains = jnp.concatenate([norm_gain, ffn_gain, query_gain, key_gain])
    gain_count = gains.shape[0]
    qkv_columns = query_columns + 2 * key_columns
    packed_columns = qkv_columns + query_columns
    gain_rows = jnp.pad(gains[None], ((0, 15), (0, packed_columns - gain_count)))
    packed = jnp.concatenate(
        [
            columns_of(query_weight, query_columns),
            columns_of(key_weight, key_columns),
            columns_of(value_weight, key_columns),
            columns_of(out_weight, query_columns),
        ],
        axis=1,
    )
    top = split_rows(own_rows + 16)
    first_ring = GatherRing(
        packed[:top], jnp.concatenate([packed[top:], gain_rows], axis=0), size
    )
    for _ in range(size - 1):
        first_ring.step()
    ffn_ring = GatherRing(
        *pick_hidden(gate_weight, up_weight, seq_index, size, ff_part, window), size
    )
    down_rows = hidden_rows(down_weight)
    def advance(rings, *needed):
        for way in rings:
            if way.count < size - 1:
                way.step(*needed)

    for step in range(1, size):
        ffn_ring.step((first_ring.ahead[2],) if step == 1 else ())
    down_ring = GatherRing(down_rows[: window // 2], down_rows[window // 2 :], size)

    def gather_down(count, first=(), last=()):
        for _ in range(count):
            lag = min(len(down_ring.ahead) + 2, size - 1)
            down_ring.step((ffn_ring.ahead[lag], ffn_ring.behind[lag], *first), last)


    qkv_all, out_part, gains_all = lay_attention(
        first_ring.ahead, first_ring.behind, owners, own_rows, qkv_columns
    )
    gains_all = gains_all[:, 0].astype(f32)
    first_gain = gains_all[:, :own_rows].reshape(-1)
    second_gain = gains_all[:, own_rows : 2 * own_rows].reshape(-1)
    q_gain_f = gains_all[:, 2 * own_rows : 2 * own_rows + head_part].reshape(-1)
    k_gain_f = gains_all[:, 2 * own_rows + head_part : 2 * (own_rows + head_part)].reshape(-1)

    inputs = tokens[0]
    tok_rows = inputs.shape[0]
    length = 4 * tok_rows
    input_blocks = gather_seq(inputs)
    inputs_all = jnp.concatenate(in_order(input_blocks, seq_index), axis=0).astype(f32)
    out_grad = cotangent[0]
    grad_blocks = gather_seq(out_grad, input_blocks[1])
    out_grad_all = jnp.concatenate(grad_blocks, axis=0)


    out_other = exchange(after(out_part, input_blocks[1]), 2)
    normed, norm_unit, norm_inverse = norm_forward(inputs_all, first_gain)
    normed_low = after(normed.astype(bf16), grad_blocks[1])
    qkv_t = lax.dot_general(
        qkv_all, normed_low, (((0,), (1,)), ((), ())), preferred_element_type=f32
    )
    sizes = (query_columns // head_width, key_columns // head_width, head_width)
    cosine, sine = rope_rows(length, head_width)
    tables = (q_gain_f[:, None], k_gain_f[:, None], cosine, sine)
    mixed_heads, mixed_t, totals = attention_forward(qkv_t, *tables, sizes)
    mixed = side_by_side(swap(mixed_heads.reshape(4, tok_rows, query_columns)))
    out_other = after(out_other, mixed_heads)
    out_blocks = [out_part, out_other, exchange(out_part, 1), exchange(out_other, 1)]
    out_all = jnp.concatenate(in_order(out_blocks, seq_index), axis=1)
    attended = jnp.dot(mixed, out_all, preferred_element_type=f32)
    middle = inputs.astype(f32) + attended
    normed_two, middle_unit, middle_inverse = norm_forward(middle, second_gain)
    normed_two_low = normed_two.astype(bf16)
    normed_blocks = gather_seq(normed_two_low)
    gather_down(1, (mixed,), (normed_two_low,))
    gather_down(1)
    gather_down(size - 5)
    mixed_all = jnp.concatenate(
        in_order(gather_seq(mixed_heads, normed_blocks[1]), seq_index), axis=1
    )

    slope, silu, hidden, gate_all, up_all = ffn_hidden(
        normed_blocks, ffn_ring.ahead, ffn_ring.behind, owners
    )
    while len(down_ring.ahead) < size:
        down_ring.step((), (hidden,))
    down_weight_grad = transpose_dot(hidden, out_grad_all).astype(bf16)
    down_blocks = down_weight_grad.reshape(size, window, width)
    down_sums = (
        ScatterRing(0, down_blocks, size, owners, (0, window // 2)),
        ScatterRing(1, down_blocks, size, owners, (window // 2, window)),
    )
    gate_grad, up_grad, gate_weight_grad, up_weight_grad, down_all = ffn_hidden_grad(
        after(out_grad_all, *(way.sum for way in down_sums)),
        jnp.concatenate(normed_blocks, axis=0).T,
        slope,
        silu,
        down_ring.ahead,
        down_ring.behind,
        owners,
    )
    advance(down_sums, gate_grad)
    gate_sums = ScatterRing(
        0, gate_weight_grad.reshape(size, own_rows, size * window), size, owners
    )
    up_sums = ScatterRing(1, up_weight_grad.reshape(size, own_rows, size * window), size, owners)
    ffn_sums = (gate_sums, up_sums)
    normed_parts = ffn_rows_grad(
        after(gate_grad, *(way.sum for way in (*down_sums, *ffn_sums))), up_grad, gate_all, up_all
    )
    normed_two_grad, half_sum = scatter_seq(*normed_parts)
    advance(ffn_sums, normed_parts[0])
    advance(down_sums, normed_parts[0])
    advance(ffn_sums, half_sum)
    advance(down_sums, half_sum)
    advance(down_sums, half_sum)
    ffn_gain_grad = jnp.sum(normed_two_grad * middle_unit, axis=0)
    middle_grad = out_grad.astype(f32) + norm_backward(
        normed_two_grad, middle_unit, middle_inverse, second_gain
    )
    attended_low = middle_grad.astype(bf16)
    mixed_grad = dot_transposed(attended_low, out_all).astype(bf16)
    advance(ffn_sums, mixed_grad)
    advance(down_sums, mixed_grad)
    mixed_grad_heads = swap(apart(mixed_grad)).reshape(length, query_columns)
    qkv_grad, head_gains = attention_backward(
        qkv_t, *tables, mixed_t, totals, mixed_grad_heads, sizes
    )
    attended_columns = after(
        swap(apart(after(attended_low, mixed_grad_heads))), qkv_grad
    ).reshape(length, query_columns)
    out_weight_grad = by_rows(transpose_dot(mixed_all, attended_columns).astype(bf16))
    advance(ffn_sums, qkv_grad)
    advance(down_sums, qkv_grad)
    qkv_grad = after(qkv_grad, gate_sums.sum, up_sums.sum)
    head_gains = jnp.sum(head_gains, axis=1)
    query_gain_grad, key_gain_grad = head_gains[:head_width], head_gains[head_width:]
    qkv_weight_grad = by_rows(transpose_dot(normed_low, qkv_grad).astype(bf16))
    normed_partial = dot_transposed(qkv_grad, qkv_all)
    norm_gain_grad = jnp.sum(normed_partial * norm_unit, axis=0)
    partial_blocks = normed_partial.astype(bf16).reshape(4, tok_rows, width)

    def partial_of(mask):
        index = (seq_index ^ mask).astype(jnp.uint32)
        return lax.dynamic_index_in_dim(partial_blocks, index, 0, keepdims=False)

    normed_grad, normed_sent = scatter_seq(
        partial_of(0),
        partial_of(2),
        jnp.concatenate([partial_of(1), partial_of(3)], axis=0),
    )
    _, own_unit, own_inverse = norm_forward(inputs.astype(f32), first_gain)
    inputs_grad = middle_grad + norm_backward(normed_grad, own_unit, own_inverse, first_gain)

    gain_grads = jnp.concatenate(
        [
            norm_gain_grad.reshape(size, -1),
            ffn_gain_grad.reshape(size, -1),
            query_gain_grad.reshape(size, -1),
            key_gain_grad.reshape(size, -1),
        ],
        axis=1,
    )
    gain_blocks = jnp.pad(
        gain_grads[:, None], ((0, 0), (0, 15), (0, packed_columns - gain_count))
    )
    packed_blocks = jnp.concatenate([qkv_weight_grad, out_weight_grad], axis=1).reshape(
        size, own_rows, packed_columns
    )
    packed_blocks = jnp.concatenate([packed_blocks, gain_blocks.astype(bf16)], axis=1)
    last_sums = (
        ScatterRing(0, packed_blocks, size, owners, (0, top)),
        ScatterRing(1, packed_blocks, size, owners, (top, own_rows + 16)),
    )
    advance(ffn_sums, *(way.sum for way in last_sums))
    advance(down_sums, *(way.sum for way in last_sums))
    down_share = jnp.concatenate([way.sum for way in down_sums], axis=0)
    down_pieces = gather_seq(down_share)
    down_partial = jnp.dot(
        after(hidden, gate_sums.sum), down_all, preferred_element_type=f32
    ).astype(bf16)
    down_sum, down_sent = scatter_seq(
        down_partial[:tok_rows],
        down_partial[tok_rows : 2 * tok_rows],
        down_partial[2 * tok_rows :],
    )
    advance(last_sums, gate_sums.sum, up_sums.sum)
    advance(last_sums, down_sent)
    rest = [(down_sum, down_pieces[1]), (normed_grad, down_sent)]
    while gate_sums.count < size - 1:
        advance(ffn_sums, *(rest.pop() if rest else ()))
        if gate_sums.count < size - 1:
            advance(last_sums, gate_sums.sum, up_sums.sum)
            advance(last_sums, gate_sums.sum, up_sums.sum)
    both = jnp.stack([gate_sums.sum, up_sums.sum])
    ffn_blocks = gather_seq(both)
    while last_sums[0].count < size - 1:
        advance(last_sums, *((ffn_blocks[1],) if last_sums[0].count == size - 2 else (both,)))
    packed_share = jnp.concatenate([way.sum for way in last_sums], axis=0)
    output = middle + down_sum
    down_full = jnp.concatenate(in_order(down_pieces, seq_index), axis=0)[
        :ff_part
    ].astype(f32)
    gate_full, up_full = (
        spread_hidden(ffn_blocks, which, seq_index, size, ff_part, window) for which in range(2)
    )
    packs = in_order(gather_seq(packed_share), seq_index)

    def unpack(first, count):
        return jnp.concatenate(
            [p[:own_rows, first : first + count] for p in packs], axis=1
        ).astype(f32)

    gain_sum = sum(p[own_rows, :gain_count].astype(f32) for p in packs)
    return (
        output[None].astype(bf16),
        inputs_grad[None].astype(bf16),
        gain_sum[:own_rows],
        unpack(0, query_columns),
        unpack(query_columns, key_columns),
        unpack(query_columns + key_columns, key_columns),
        gain_sum[2 * own_rows : 2 * own_rows + head_part],
        gain_sum[2 * own_rows + head_part :],
        unpack(qkv_columns, query_columns),
        gain_sum[own_rows : 2 * own_rows],
        gate_full,
        up_full,
        down_full,
    )


def solution(mesh):
    in_specs = (
        P("fsdp", "seq", None),
        P("fsdp"),
        P("fsdp", None),
        P("fsdp", None),
        P("fsdp", None),
        P("fsdp"),
        P("fsdp"),
        P("fsdp", None),
        P("fsdp"),
        P("fsdp", None),
        P("fsdp", None),
        P("fsdp", None),
        P("fsdp", "seq", None),
    )
    out_specs = (
        P("fsdp", "seq", None),
        P("fsdp", "seq", None),
        P("fsdp"),
        P("fsdp", None),
        P("fsdp", None),
        P("fsdp", None),
        P("fsdp"),
        P("fsdp"),
        P("fsdp", None),
        P("fsdp"),
        P("fsdp", None),
        P("fsdp", None),
        P("fsdp", None),
    )
    return jax.shard_map(body, mesh=mesh, in_specs=in_specs, out_specs=out_specs, check_vma=False)
```

```python
import functools
import math

import jax
import jax.numpy as jnp
import numpy as np
from jax import lax
from jax.experimental import pallas as pl
from jax.experimental.layout import Layout, with_layout_constraint
from jax.experimental.pallas import tpu as pltpu
from jax.sharding import PartitionSpec as P

norm_epsilon = 1e-05
TILE = 256
log2_e = math.log2(math.e)


def rope_rows(length, width):
    half_width = width // 2
    inverse = jnp.exp(
        jnp.arange(half_width, dtype=jnp.float32) * (-2.0 * math.log(1000000.0) / width)
    )
    angles = inverse[:, None] * jnp.arange(length, dtype=jnp.int32).astype(jnp.float32)[None, :]
    return jnp.cos(angles), jnp.sin(angles)


def head_norm(values):
    inverse = lax.rsqrt(jnp.mean(values * values, axis=0, keepdims=True) + norm_epsilon)
    return values * inverse, inverse


def head_turn(values, cosine, sine):
    half = values.shape[0] // 2
    first, second = values[:half], values[half:]
    return jnp.concatenate(
        [first * cosine - second * sine, second * cosine + first * sine], axis=0
    )


def head_turn_back(values, cosine, sine):
    half = values.shape[0] // 2
    first, second = values[:half], values[half:]
    return jnp.concatenate(
        [first * cosine + second * sine, second * cosine - first * sine], axis=0
    )


def fill_heads(qkv_ref, q_gain_ref, k_gain_ref, cos_ref, sin_ref, queries, keys, keys_t, values, values_t, sizes):
    heads, groups, width = sizes
    cosine, sine = cos_ref[...], sin_ref[...]

    @pl.loop(0, heads)
    def _(head):
        unit, _ = head_norm(qkv_ref[pl.ds(head * width, width), :])
        turned = head_turn(unit * q_gain_ref[...], cosine, sine)
        queries[head] = (turned * (width**-0.5 * log2_e)).astype(jnp.bfloat16)

    @pl.loop(0, groups)
    def _(group):
        unit, _ = head_norm(qkv_ref[pl.ds((heads + group) * width, width), :])
        turned = head_turn(unit * k_gain_ref[...], cosine, sine)
        keys[group] = turned.T.astype(jnp.bfloat16)
        if keys_t is not None:
            keys_t[group] = turned.astype(jnp.bfloat16)
        value = qkv_ref[pl.ds((heads + groups + group) * width, width), :]
        if values is not None:
            values[group] = value.T.astype(jnp.bfloat16)
        if values_t is not None:
            values_t[group] = value.astype(jnp.bfloat16)


def diagonal_mask():
    key_place = lax.broadcasted_iota(jnp.int32, (TILE, TILE), 0)
    query_place = lax.broadcasted_iota(jnp.int32, (TILE, TILE), 1)
    return key_place <= query_place


def causal_exp(scores, count):
    weights = jnp.exp2(scores)
    last = jnp.where(diagonal_mask(), weights[count - TILE :], 0.0)
    if count == TILE:
        return last
    return jnp.concatenate([weights[: count - TILE], last], axis=0)


def dot(left, right):
    return jnp.dot(left, right, preferred_element_type=jnp.float32)


def dot_nt(left, right):
    return lax.dot_general(
        left, right, (((1,), (1,)), ((), ())), preferred_element_type=jnp.float32
    )


def forward_kernel(sizes, qkv_ref, q_gain_ref, k_gain_ref, cos_ref, sin_ref, mixed_ref, mixed_t_ref, total_ref, queries, keys, values_t, mixed_f):
    heads, groups, width = sizes
    ratio = heads // groups
    length = qkv_ref.shape[1]
    fill_heads(qkv_ref, q_gain_ref, k_gain_ref, cos_ref, sin_ref, queries, keys, None, None, values_t, sizes)

    @pl.loop(0, heads)
    def _(head):
        group = head // ratio
        for tile in range(length // TILE):
            count = (tile + 1) * TILE
            columns = pl.ds(tile * TILE, TILE)
            scores = dot(keys[group, pl.ds(0, count), :], queries[head, :, columns])
            weights = causal_exp(scores, count)
            total = jnp.sum(weights, axis=0, keepdims=True)
            result = dot(values_t[group, :, pl.ds(0, count)], weights.astype(jnp.bfloat16))
            mixed_f[pl.ds(head * width, width), columns] = result * (1.0 / total)
            total_ref[pl.ds(head, 1), columns] = jnp.log2(total)

    for block in range(heads * width // 128):
        rows = mixed_f[pl.ds(block * 128, 128), :]
        mixed_t_ref[pl.ds(block * 128, 128), :] = rows.astype(jnp.bfloat16)
        mixed_ref[:, pl.ds(block * 128, 128)] = rows.T.astype(jnp.bfloat16)


def backward_kernel(sizes, qkv_ref, q_gain_ref, k_gain_ref, cos_ref, sin_ref, mixed_t_ref, total_ref, grad_ref, out_ref, gain_ref, out_t, queries, keys, keys_t, values, grads, key_sum, value_sum):
    heads, groups, width = sizes
    ratio = heads // groups
    length = qkv_ref.shape[1]
    fill_heads(qkv_ref, q_gain_ref, k_gain_ref, cos_ref, sin_ref, queries, keys, keys_t, values, None, sizes)
    for block in range(heads * width // 128):
        turned = grad_ref[:, pl.ds(block * 128, 128)].astype(jnp.float32).T
        grads[pl.ds(block * 128, 128), :] = turned.astype(jnp.bfloat16)
    key_sum[...] = jnp.zeros_like(key_sum)
    value_sum[...] = jnp.zeros_like(value_sum)
    gain_ref[...] = jnp.zeros_like(gain_ref)
    cosine, sine = cos_ref[...], sin_ref[...]

    def finish(grad_turned, rows, gain, first):
        grad = head_turn_back(grad_turned, cosine, sine)
        unit, inverse = head_norm(qkv_ref[rows, :])
        product = grad * unit
        part = product[:, :128]
        for lane in range(128, length, 128):
            part = part + product[:, lane : lane + 128]
        gain_ref[pl.ds(first, width), :] += part
        scaled = grad * gain
        before = inverse * (scaled - unit * jnp.mean(scaled * unit, axis=0, keepdims=True))
        out_t[rows, :] = before

    @pl.loop(0, heads)
    def _(head):
        group = head // ratio
        rows = pl.ds(head * width, width)
        query_parts = []
        for tile in range(length // TILE):
            count = (tile + 1) * TILE
            columns = pl.ds(tile * TILE, TILE)
            query = queries[head, :, columns]
            grad = grads[rows, columns]
            scores = dot(keys[group, pl.ds(0, count), :], query) - total_ref[pl.ds(head, 1), columns]
            weights = causal_exp(scores, count)
            inner = jnp.sum(
                grad.astype(jnp.float32) * mixed_t_ref[rows, columns].astype(jnp.float32),
                axis=0,
                keepdims=True,
            )
            weight_grad = dot(values[group, pl.ds(0, count), :], grad)
            score_grad = (weights * (weight_grad - inner)).astype(jnp.bfloat16)
            query_parts.append(dot(keys_t[group, :, pl.ds(0, count)], score_grad))
            key_sum[group, pl.ds(0, count), :] += dot_nt(score_grad, query)
            value_sum[group, pl.ds(0, count), :] += dot_nt(weights.astype(jnp.bfloat16), grad)
        query_grad = jnp.concatenate(query_parts, axis=1) * width**-0.5
        finish(query_grad, rows, q_gain_ref[...], 0)

    for group in range(groups):
        key_grad = key_sum[group].T * (1.0 / log2_e)
        finish(key_grad, pl.ds((heads + group) * width, width), k_gain_ref[...], width)
        out_t[pl.ds((heads + groups + group) * width, width), :] = value_sum[group].T

    for block in range(out_t.shape[0] // 128):
        some = pl.ds(block * 128, 128)
        out_ref[:, some] = out_t[some, :].T.astype(jnp.bfloat16)


def attention_forward(qkv_t, q_gain, k_gain, cosine, sine, sizes):
    heads, groups, width = sizes
    length = qkv_t.shape[1]
    bf16, f32 = jnp.bfloat16, jnp.float32
    pairs = heads * length * length
    return pl.pallas_call(
        functools.partial(forward_kernel, sizes),
        out_shape=(
            jax.ShapeDtypeStruct((length, heads * width), bf16),
            jax.ShapeDtypeStruct((heads * width, length), bf16),
            jax.ShapeDtypeStruct((-(-heads // 8) * 8, length), f32),
        ),
        scratch_shapes=[
            pltpu.VMEM((heads, width, length), bf16),
            pltpu.VMEM((groups, length, width), bf16),
            pltpu.VMEM((groups, width, length), bf16),
            pltpu.VMEM((heads * width, length), f32),
        ],
        compiler_params=pltpu.CompilerParams(vmem_limit_bytes=32 * 2**20),
        cost_estimate=pl.CostEstimate(
            flops=8 * pairs * width, bytes_accessed=6 * 2**20, transcendentals=pairs
        ),
    )(qkv_t, q_gain, k_gain, cosine, sine)


def attention_backward(qkv_t, q_gain, k_gain, cosine, sine, mixed_t, total, mixed_grad, sizes):
    heads, groups, width = sizes
    length = qkv_t.shape[1]
    bf16, f32 = jnp.bfloat16, jnp.float32
    pairs = heads * length * length
    return pl.pallas_call(
        functools.partial(backward_kernel, sizes),
        out_shape=(
            jax.ShapeDtypeStruct(qkv_t.shape[::-1], bf16),
            jax.ShapeDtypeStruct((2 * width, 128), f32),
        ),
        scratch_shapes=[
            pltpu.VMEM(qkv_t.shape, f32),
            pltpu.VMEM((heads, width, length), bf16),
            pltpu.VMEM((groups, length, width), bf16),
            pltpu.VMEM((groups, width, length), bf16),
            pltpu.VMEM((groups, length, width), bf16),
            pltpu.VMEM((heads * width, length), bf16),
            pltpu.VMEM((groups, length, width), f32),
            pltpu.VMEM((groups, length, width), f32),
        ],
        compiler_params=pltpu.CompilerParams(vmem_limit_bytes=40 * 2**20),
        cost_estimate=pl.CostEstimate(flops=0, bytes_accessed=2**20, transcendentals=0),
    )(qkv_t, q_gain, k_gain, cosine, sine, mixed_t, total, mixed_grad)


def hidden_kernel(size, ids_ref, *refs):
    pieces, chunks, refs = refs[:4], refs[4 : 4 + 2 * size], refs[4 + 2 * size :]
    slope_ref, silu_ref, hidden_ref, gate_out, up_out, tokens, gate, up, *sems = refs
    row_sems, in_sems, out_sems = sems
    step = pl.program_id(0)
    steps = pl.num_programs(0)
    rows = chunks[0].shape[0]
    piece = pieces[0].shape[0]

    @pl.when(step == 0)
    def _():
        copies = [
            pltpu.make_async_copy(
                source, tokens.at[pl.ds(index * piece, piece), :], row_sems.at[index]
            )
            for index, source in enumerate(pieces)
        ]
        for copy in copies:
            copy.start()

        @pl.loop(0, steps)
        def _(tile):
            columns = pl.ds(pl.multiple_of(tile * TILE, TILE), TILE)
            for which, target in ((0, gate), (1, up)):
                for index in range(size):
                    first = pl.multiple_of(ids_ref[which, index] * rows, 16)
                    pltpu.make_async_copy(
                        chunks[which * size + index].at[:, columns],
                        target.at[pl.ds(first, rows), columns],
                        in_sems.at[which, tile],
                    ).start()

        for copy in copies:
            copy.wait()

    columns = pl.ds(pl.multiple_of(step * TILE, TILE), TILE)
    for which, target, result in ((0, gate, gate_out), (1, up, up_out)):
        part = target.at[:, columns]
        pltpu.make_async_copy(part, part, in_sems.at[which, step]).wait()
        pltpu.make_async_copy(part, result.at[:, columns], out_sems.at[which, step]).start()
    for half in range(2):
        some = pl.ds(half * 2 * piece, 2 * piece)
        gate_act = dot(tokens[some, :], gate[:, columns])
        up_act = dot(tokens[some, :], up[:, columns])
        sigmoid = 0.5 + 0.5 * jnp.tanh(0.5 * gate_act)
        silu = gate_act * sigmoid
        hidden_ref[some, :] = (silu * up_act).astype(hidden_ref.dtype)
        silu_ref[some, :] = silu.astype(silu_ref.dtype)
        slope_ref[some, :] = (up_act * sigmoid * (1.0 + gate_act * (1.0 - sigmoid))).astype(
            slope_ref.dtype
        )

    @pl.when(step == steps - 1)
    def _():
        @pl.loop(0, steps)
        def _(tile):
            columns = pl.ds(pl.multiple_of(tile * TILE, TILE), TILE)
            for which, target, result in ((0, gate, gate_out), (1, up, up_out)):
                pltpu.make_async_copy(
                    target.at[:, columns], result.at[:, columns], out_sems.at[which, tile]
                ).wait()


def ffn_hidden(pieces, gate_chunks, up_chunks, ids):
    size = len(gate_chunks)
    part, columns = gate_chunks[0].shape
    piece, width = pieces[0].shape
    length = 4 * piece
    bf16 = jnp.bfloat16
    tall = pl.BlockSpec((length, TILE), lambda i, ids: (0, i))
    act = jax.ShapeDtypeStruct((length, columns), bf16)
    weight = jax.ShapeDtypeStruct((width, columns), bf16)
    anywhere = pl.BlockSpec(memory_space=pl.ANY)
    return pl.pallas_call(
        functools.partial(hidden_kernel, size),
        grid_spec=pltpu.PrefetchScalarGridSpec(
            num_scalar_prefetch=1,
            grid=(columns // TILE,),
            in_specs=[anywhere] * (4 + 2 * size),
            out_specs=[tall, tall, tall, anywhere, anywhere],
            scratch_shapes=[
                pltpu.VMEM((length, width), bf16),
                pltpu.VMEM((width, columns), bf16),
                pltpu.VMEM((width, columns), bf16),
                pltpu.SemaphoreType.DMA((4,)),
                pltpu.SemaphoreType.DMA((2, columns // TILE)),
                pltpu.SemaphoreType.DMA((2, columns // TILE)),
            ],
        ),
        out_shape=(act, act, act, weight, weight),
        compiler_params=pltpu.CompilerParams(vmem_limit_bytes=56 * 2**20),
        cost_estimate=pl.CostEstimate(
            flops=4 * length * width * columns,
            bytes_accessed=36 * 2**20,
            transcendentals=length * columns,
        ),
    )(ids, *pieces, *gate_chunks, *up_chunks)


def hidden_grad_kernel(size, owners_ref, grad_ref, slope_ref, silu_ref, *refs):
    chunks, refs = refs[: 2 * size], refs[2 * size :]
    gate_out, up_out, down_out, down, in_sems, out_sem = refs
    step = pl.program_id(0)
    rows = chunks[0].shape[0]

    @pl.when(step == 0)
    def _():
        copies = []
        for which in range(2):
            for index in range(size):
                first = pl.multiple_of((2 * owners_ref[which, index] + which) * rows, 16)
                copies.append(
                    pltpu.make_async_copy(
                        chunks[which * size + index],
                        down.at[pl.ds(first, rows), :],
                        in_sems.at[which, index],
                    )
                )
        for copy in copies:
            copy.start()
        for copy in copies:
            copy.wait()
        pltpu.make_async_copy(down, down_out, out_sem).start()

    weight = down[pl.ds(pl.multiple_of(step * TILE, TILE), TILE), :]
    hidden_grad = dot_nt(grad_ref[...], weight)
    gate_out[...] = (hidden_grad * slope_ref[...].astype(jnp.float32)).astype(jnp.bfloat16)
    up_out[...] = (hidden_grad * silu_ref[...].astype(jnp.float32)).astype(jnp.bfloat16)

    @pl.when(step == pl.num_programs(0) - 1)
    def _():
        pltpu.make_async_copy(down, down_out, out_sem).wait()


def ffn_hidden_grad(out_grad, slope, silu, ahead, behind, owners):
    size = len(ahead)
    length, width = out_grad.shape
    columns = slope.shape[1]
    bf16 = jnp.bfloat16
    tall = pl.BlockSpec((length, TILE), lambda i, owners: (0, i))
    anywhere = pl.BlockSpec(memory_space=pl.ANY)
    act = jax.ShapeDtypeStruct((length, columns), bf16)
    weight = (2 * size * ahead[0].shape[0], width)
    return pl.pallas_call(
        functools.partial(hidden_grad_kernel, size),
        grid_spec=pltpu.PrefetchScalarGridSpec(
            num_scalar_prefetch=1,
            grid=(columns // TILE,),
            in_specs=[pl.BlockSpec((length, width), lambda i, owners: (0, 0)), tall, tall]
            + [anywhere] * (2 * size),
            out_specs=[tall, tall, anywhere],
            scratch_shapes=[
                pltpu.VMEM(weight, bf16),
                pltpu.SemaphoreType.DMA((2, size)),
                pltpu.SemaphoreType.DMA,
            ],
        ),
        out_shape=(act, act, jax.ShapeDtypeStruct(weight, bf16)),
        compiler_params=pltpu.CompilerParams(vmem_limit_bytes=56 * 2**20),
        cost_estimate=pl.CostEstimate(flops=0, bytes_accessed=2**20, transcendentals=0),
    )(owners, out_grad, slope, silu, *ahead, *behind)


def rows_grad_kernel(gate_grad_ref, up_grad_ref, gate_ref, up_ref, own_ref, other_ref, sent_ref):
    piece = own_ref.shape[0]
    total = dot_nt(gate_grad_ref[...], gate_ref[...]) + dot_nt(up_grad_ref[...], up_ref[...])
    total = total.astype(jnp.bfloat16)
    own_ref[...] = total[:piece]
    other_ref[...] = total[piece : 2 * piece]
    sent_ref[...] = total[2 * piece :]


def ffn_rows_grad(gate_grad, up_grad, gate, up):
    length, columns = gate_grad.shape
    width = gate.shape[0]
    piece = length // 4
    bf16 = jnp.bfloat16
    whole = pl.BlockSpec((length, columns), lambda i: (0, 0))
    weight = pl.BlockSpec((TILE, columns), lambda i: (i, 0))
    part = pl.BlockSpec((piece, TILE), lambda i: (0, i))
    return pl.pallas_call(
        rows_grad_kernel,
        grid=(width // TILE,),
        in_specs=[whole, whole, weight, weight],
        out_specs=[part, part, pl.BlockSpec((2 * piece, TILE), lambda i: (0, i))],
        out_shape=(
            jax.ShapeDtypeStruct((piece, width), bf16),
            jax.ShapeDtypeStruct((piece, width), bf16),
            jax.ShapeDtypeStruct((2 * piece, width), bf16),
        ),
        compiler_params=pltpu.CompilerParams(vmem_limit_bytes=56 * 2**20),
        cost_estimate=pl.CostEstimate(flops=0, bytes_accessed=2**20, transcendentals=0),
    )(gate_grad, up_grad, gate, up)


def lay_kernel(size, sizes, owners_ref, *refs):
    chunks, refs = refs[: 2 * size], refs[2 * size :]
    qkv_out, out_out, gains_out, sems = refs
    rows, top, qkv_columns, columns = sizes
    copies = []
    for which, count in ((0, top), (1, rows - top)):
        for index in range(size):
            chunk = chunks[which * size + index]
            owner = owners_ref[which, index]
            first = pl.multiple_of(owner * rows + which * top, 16)
            target = pl.ds(first, count)
            pairs = [
                (chunk.at[pl.ds(0, count), pl.ds(0, qkv_columns)], qkv_out.at[target, :]),
                (
                    chunk.at[pl.ds(0, count), pl.ds(qkv_columns, columns - qkv_columns)],
                    out_out.at[target, :],
                ),
            ]
            if which:
                pairs.append((chunk.at[pl.ds(count, 16), :], gains_out.at[owner]))
            for kind, (source, place) in enumerate(pairs):
                copies.append(pltpu.make_async_copy(source, place, sems.at[kind, which, index]))
    for copy in copies:
        copy.start()
    for copy in copies:
        copy.wait()


def lay_attention(ahead, behind, owners, rows, qkv_columns):
    size = len(ahead)
    top, columns = ahead[0].shape
    bf16 = jnp.bfloat16
    anywhere = pl.BlockSpec(memory_space=pl.ANY)
    return pl.pallas_call(
        functools.partial(lay_kernel, size, (rows, top, qkv_columns, columns)),
        grid_spec=pltpu.PrefetchScalarGridSpec(
            num_scalar_prefetch=1,
            grid=(1,),
            in_specs=[anywhere] * (2 * size),
            out_specs=[pl.BlockSpec(memory_space=pltpu.VMEM)] * 3,
            scratch_shapes=[pltpu.SemaphoreType.DMA((3, 2, size))],
        ),
        out_shape=(
            jax.ShapeDtypeStruct((size * rows, qkv_columns), bf16),
            jax.ShapeDtypeStruct((size * rows, columns - qkv_columns), bf16),
            jax.ShapeDtypeStruct((size, 16, columns), bf16),
        ),
        cost_estimate=pl.CostEstimate(flops=0, bytes_accessed=7 * 2**20, transcendentals=0),
    )(owners, *ahead, *behind)


def pick_kernel(sizes, index_ref, gate_ref, up_ref, gate_out, up_out):
    size, part, window = sizes
    rows = gate_ref.shape[0]
    for source, target in ((gate_ref, gate_out), (up_ref, up_out)):
        for index in range(4):
            count = min(window, part - index * window)

            @pl.when(index_ref[0] == index)
            def _():
                parts = []
                for owner in range(size):
                    first = owner * part + index * window
                    low, high = first // 128 * 128, -(-(first + count) // 128) * 128
                    wide = source[:, low:high].astype(jnp.float32)
                    parts.append(wide[:, first - low : first - low + count])
                    if count < window:
                        parts.append(jnp.zeros((rows, window - count), jnp.float32))
                target[...] = jnp.concatenate(parts, axis=1).astype(target.dtype)


def pick_hidden(gate, up, seq_index, size, part, window):
    rows, columns = gate.shape
    block = 48 if rows % 48 == 0 else rows
    wide = pl.BlockSpec((block, columns), lambda i, index: (i, 0))
    narrow = pl.BlockSpec((block, size * window), lambda i, index: (i, 0))
    out = jax.ShapeDtypeStruct((rows, size * window), gate.dtype)
    return pl.pallas_call(
        functools.partial(pick_kernel, (size, part, window)),
        grid_spec=pltpu.PrefetchScalarGridSpec(
            num_scalar_prefetch=1,
            grid=(rows // block,),
            in_specs=[wide, wide],
            out_specs=[narrow, narrow],
        ),
        out_shape=(out, out),
        compiler_params=pltpu.CompilerParams(vmem_limit_bytes=32 * 2**20),
        cost_estimate=pl.CostEstimate(flops=0, bytes_accessed=8 * 2**20, transcendentals=0),
    )(jnp.reshape(seq_index, (1,)).astype(jnp.int32), gate, up)


def spread_kernel(sizes, index_ref, own_ref, other_ref, near_ref, far_ref, out_ref, parts):
    size, part, window = sizes
    me = index_ref[0]
    parts[me] = own_ref[...]
    parts[me ^ 2] = other_ref[...]
    parts[me ^ 1] = near_ref[...]
    parts[me ^ 3] = far_ref[...]
    pieces = []
    for owner in range(size):
        for index in range(4):
            count = min(window, part - index * window)
            first = owner * window
            low, high = first // 128 * 128, -(-(first + count) // 128) * 128
            wide = parts[index, :, low:high].astype(jnp.float32)
            pieces.append(wide[:, first - low : first - low + count])
    out_ref[...] = jnp.concatenate(pieces, axis=1)


def spread_hidden(pieces, which, seq_index, size, part, window):
    _, rows, columns = pieces[0].shape
    block = 48 if rows % 48 == 0 else rows
    narrow = pl.BlockSpec((None, block, columns), lambda i, index: (which, i, 0))
    return pl.pallas_call(
        functools.partial(spread_kernel, (size, part, window)),
        grid_spec=pltpu.PrefetchScalarGridSpec(
            num_scalar_prefetch=1,
            grid=(rows // block,),
            in_specs=[narrow] * 4,
            out_specs=pl.BlockSpec((block, size * part), lambda i, index: (i, 0)),
            scratch_shapes=[pltpu.VMEM((4, block, columns), pieces[0].dtype)],
        ),
        out_shape=jax.ShapeDtypeStruct((rows, size * part), jnp.float32),
        compiler_params=pltpu.CompilerParams(vmem_limit_bytes=32 * 2**20),
        cost_estimate=pl.CostEstimate(flops=0, bytes_accessed=64 * 2**20, transcendentals=0),
    )(jnp.reshape(seq_index, (1,)), *pieces)


def norm_forward(values, gain):
    inverse = lax.rsqrt(jnp.mean(values * values, axis=-1, keepdims=True) + norm_epsilon)
    unit = values * inverse
    return (unit * gain, unit, inverse)


def norm_backward(grad_in, unit, inverse, gain):
    scaled = grad_in * gain
    return inverse * (scaled - unit * jnp.mean(scaled * unit, axis=-1, keepdims=True))


def transpose_dot(left, right):
    return lax.dot_general(
        left, right, (((0,), (0,)), ((), ())), preferred_element_type=jnp.float32
    )


def by_rows(values):
    return with_layout_constraint(values, Layout(major_to_minor=(0, 1)))


def dot_transposed(left, right):
    return lax.dot_general(
        left, right, (((1,), (1,)), ((), ())), preferred_element_type=jnp.float32
    )


def split_rows(rows):
    return (rows // 32) * 16


def ring_ids(size):
    return list(range(0, size, 2)) + [i for i in range(size - 1, 0, -1) if i % 2]


def ring_perms(size):
    ids = ring_ids(size)
    forward = [(ids[i], ids[(i + 1) % size]) for i in range(size)]
    return forward, [(b, a) for a, b in forward]


def ring_owners(size):
    ids = ring_ids(size)
    table = np.zeros((size, 4, size), np.int32)
    for place, device in enumerate(ids):
        for step in range(size):
            table[device, 0, step] = ids[(place - step) % size]
            table[device, 1, step] = ids[(place + step) % size]
            table[device, 2, step] = ids[(place - 1 - step) % size]
            table[device, 3, step] = ids[(place + 1 + step) % size]
    return lax.dynamic_index_in_dim(
        jnp.asarray(table), lax.axis_index("fsdp").astype(jnp.uint32), 0, keepdims=False
    )


def after(value, *needed):
    return lax.optimization_barrier((value, *needed))[0] if needed else value


class GatherRing:
    def __init__(self, ahead, behind, size):
        self.perms = ring_perms(size)
        self.ahead, self.behind = [ahead], [behind]

    def step(self, first=(), last=()):
        forward, backward = self.perms
        ahead = lax.ppermute(after(self.ahead[-1], *first), "fsdp", forward)
        behind = lax.ppermute(after(self.behind[-1], *first), "fsdp", backward)
        self.ahead.append(after(ahead, *last))
        self.behind.append(after(behind, *last))


class ScatterRing:
    def __init__(self, way, blocks, size, owners, rows=None):
        self.perm = ring_perms(size)[way]
        self.owners = lax.squeeze(lax.slice_in_dim(owners, 2 + way, 3 + way), (0,)).astype(
            jnp.uint32
        )
        self.blocks, self.count = blocks, 0
        self.first, self.last = rows or (0, blocks.shape[1])
        self.sum = self.own().astype(jnp.bfloat16)

    def own(self):
        owner = lax.squeeze(lax.slice_in_dim(self.owners, self.count, self.count + 1), (0,))
        zero = jnp.uint32(0)
        shape = (1, self.last - self.first, self.blocks.shape[2])
        start = (owner, jnp.uint32(self.first), zero)
        return lax.dynamic_slice(self.blocks, start, shape)[0].astype(jnp.float32)

    def step(self, *needed):
        came = after(lax.ppermute(self.sum, "fsdp", self.perm), *needed)
        self.count += 1
        self.sum = (came.astype(jnp.float32) + self.own()).astype(jnp.bfloat16)
        return self.sum


def exchange(values, mask):
    return lax.ppermute(values, "seq", [(i, i ^ mask) for i in range(4)])


def gather_seq(block, *needed):
    block = after(block, *needed)
    other = exchange(block, 2)
    return [block, other, exchange(block, 1), exchange(other, 1)]


def in_order(pieces, seq_index):
    high, low = seq_index // 2, seq_index % 2

    def pick(first, second, flag):
        return jnp.where(flag == 0, first, second), jnp.where(flag == 0, second, first)

    mine = pick(pieces[0], pieces[1], high)
    theirs = pick(pieces[2], pieces[3], high)
    return [*pick(mine[0], theirs[0], low), *pick(mine[1], theirs[1], low)]


def scatter_seq(own, other, there):
    rows = own.shape[0]
    came = exchange(there, 1).astype(jnp.float32)
    sent = (other.astype(jnp.float32) + came[rows:]).astype(jnp.bfloat16)
    near = own.astype(jnp.float32) + came[:rows]
    return near + exchange(sent, 2).astype(jnp.float32), sent


def swap(blocks):
    return lax.all_to_all(blocks, "seq", split_axis=0, concat_axis=0, tiled=True)


def side_by_side(blocks):
    return blocks.transpose(1, 0, 2).reshape(blocks.shape[1], -1)


def apart(values):
    return values.reshape(values.shape[0], 4, -1).transpose(1, 0, 2)


def body(
    tokens,
    norm_gain,
    query_weight,
    key_weight,
    value_weight,
    query_gain,
    key_gain,
    out_weight,
    ffn_gain,
    gate_weight,
    up_weight,
    down_weight,
    cotangent,
):
    bf16, f32 = jnp.bfloat16, jnp.float32
    size = lax.axis_size("fsdp")
    seq_index = lax.axis_index("seq")
    owners = ring_owners(size)
    own_rows, width = query_weight.shape
    head_part = query_gain.shape[0]
    head_width = head_part * size
    query_columns = width // 4
    key_columns = key_weight.shape[1] // 4
    ff_part = down_weight.shape[0]
    window = -(-ff_part // 64) * 16

    def columns_of(weight, count):
        return lax.dynamic_slice_in_dim(weight, seq_index.astype(jnp.uint32) * count, count, 1)

    def hidden_rows(weight):
        tall = jnp.pad(weight, ((0, 4 * window - ff_part), (0, 0)))
        return lax.dynamic_slice_in_dim(tall, seq_index.astype(jnp.uint32) * window, window, 0)

    gains = jnp.concatenate([norm_gain, ffn_gain, query_gain, key_gain])
    gain_count = gains.shape[0]
    qkv_columns = query_columns + 2 * key_columns
    packed_columns = qkv_columns + query_columns
    gain_rows = jnp.pad(gains[None], ((0, 15), (0, packed_columns - gain_count)))
    packed = jnp.concatenate(
        [
            columns_of(query_weight, query_columns),
            columns_of(key_weight, key_columns),
            columns_of(value_weight, key_columns),
            columns_of(out_weight, query_columns),
        ],
        axis=1,
    )
    top = split_rows(own_rows + 16)
    first_ring = GatherRing(
        packed[:top], jnp.concatenate([packed[top:], gain_rows], axis=0), size
    )
    for _ in range(size - 1):
        first_ring.step()
    ffn_ring = GatherRing(
        *pick_hidden(gate_weight, up_weight, seq_index, size, ff_part, window), size
    )
    down_rows = hidden_rows(down_weight)
    def advance(rings, *needed):
        for way in rings:
            if way.count < size - 1:
                way.step(*needed)

    for step in range(1, size):
        ffn_ring.step((first_ring.ahead[2],) if step == 1 else ())
    down_ring = GatherRing(down_rows[: window // 2], down_rows[window // 2 :], size)
    for step in range(1, size - 2):
        lag = min(step + 2, size - 1)
        down_ring.step((ffn_ring.ahead[lag], ffn_ring.behind[lag]))

    qkv_all, out_part, gains_all = lay_attention(
        first_ring.ahead, first_ring.behind, owners, own_rows, qkv_columns
    )
    gains_all = gains_all[:, 0].astype(f32)
    first_gain = gains_all[:, :own_rows].reshape(-1)
    second_gain = gains_all[:, own_rows : 2 * own_rows].reshape(-1)
    q_gain_f = gains_all[:, 2 * own_rows : 2 * own_rows + head_part].reshape(-1)
    k_gain_f = gains_all[:, 2 * own_rows + head_part : 2 * (own_rows + head_part)].reshape(-1)

    inputs = tokens[0]
    tok_rows = inputs.shape[0]
    length = 4 * tok_rows
    input_blocks = gather_seq(inputs)
    inputs_all = jnp.concatenate(in_order(input_blocks, seq_index), axis=0).astype(f32)
    out_grad = cotangent[0]
    grad_blocks = gather_seq(out_grad, input_blocks[1])
    out_grad_all = jnp.concatenate(grad_blocks, axis=0)


    out_other = exchange(after(out_part, input_blocks[1]), 2)
    normed, _, _ = norm_forward(inputs_all, first_gain)
    normed_low = after(normed.astype(bf16), grad_blocks[1])
    qkv_t = lax.dot_general(
        qkv_all, normed_low, (((0,), (1,)), ((), ())), preferred_element_type=f32
    )
    sizes = (query_columns // head_width, key_columns // head_width, head_width)
    cosine, sine = rope_rows(length, head_width)
    tables = (q_gain_f[:, None], k_gain_f[:, None], cosine, sine)
    mixed_heads, mixed_t, totals = attention_forward(qkv_t, *tables, sizes)
    mixed = side_by_side(swap(mixed_heads.reshape(4, tok_rows, query_columns)))
    out_other = after(out_other, mixed_heads)
    out_blocks = [out_part, out_other, exchange(out_part, 1), exchange(out_other, 1)]
    out_all = jnp.concatenate(in_order(out_blocks, seq_index), axis=1)
    attended = jnp.dot(mixed, out_all, preferred_element_type=f32)
    middle = inputs.astype(f32) + attended
    normed_two, middle_unit, middle_inverse = norm_forward(middle, second_gain)
    normed_two_low = normed_two.astype(bf16)
    normed_blocks = gather_seq(normed_two_low)
    normed_two_all = jnp.concatenate(normed_blocks, axis=0)
    mixed_all = jnp.concatenate(
        in_order(gather_seq(mixed_heads, normed_blocks[1]), seq_index), axis=1
    )

    slope, silu, hidden, gate_all, up_all = ffn_hidden(
        [after(normed_blocks[0], down_ring.ahead[-1], down_ring.behind[-1]), *normed_blocks[1:]],
        ffn_ring.ahead,
        ffn_ring.behind,
        owners,
    )
    down_ring.step((), (hidden,))
    hidden = after(hidden, down_ring.ahead[-1], down_ring.behind[-1])
    down_ring.step()
    down_weight_grad = transpose_dot(hidden, out_grad_all).astype(bf16)
    down_blocks = down_weight_grad.reshape(size, window, width)
    down_sums = (ScatterRing(0, down_blocks, size, owners),)
    gate_grad, up_grad, down_all = ffn_hidden_grad(
        after(out_grad_all, *(way.sum for way in down_sums)),
        slope,
        silu,
        down_ring.ahead,
        down_ring.behind,
        owners,
    )
    advance(down_sums, gate_grad)
    gate_weight_grad = transpose_dot(
        after(normed_two_all, *(way.sum for way in down_sums)), gate_grad
    ).astype(bf16)
    gate_sums = ScatterRing(
        0, gate_weight_grad.reshape(size, own_rows, size * window), size, owners
    )
    up_weight_grad = transpose_dot(after(normed_two_all, gate_sums.sum), up_grad).astype(bf16)
    up_sums = ScatterRing(1, up_weight_grad.reshape(size, own_rows, size * window), size, owners)
    ffn_sums = (gate_sums, up_sums)
    normed_parts = ffn_rows_grad(after(gate_grad, up_sums.sum), up_grad, gate_all, up_all)
    normed_two_grad, half_sum = scatter_seq(*normed_parts)
    advance(ffn_sums, normed_parts[0])
    advance(ffn_sums, half_sum)
    ffn_gain_grad = jnp.sum(normed_two_grad * middle_unit, axis=0)
    middle_grad = out_grad.astype(f32) + norm_backward(
        normed_two_grad, middle_unit, middle_inverse, second_gain
    )
    attended_low = middle_grad.astype(bf16)
    mixed_grad = dot_transposed(attended_low, out_all).astype(bf16)
    advance(ffn_sums, mixed_grad)
    mixed_grad_heads = after(swap(apart(mixed_grad)), gate_sums.sum, up_sums.sum).reshape(
        length, query_columns
    )
    qkv_grad, head_gains = attention_backward(
        qkv_t, *tables, mixed_t, totals, mixed_grad_heads, sizes
    )
    attended_columns = after(
        swap(apart(after(attended_low, mixed_grad_heads))), qkv_grad
    ).reshape(length, query_columns)
    out_weight_grad = by_rows(transpose_dot(mixed_all, attended_columns).astype(bf16))
    advance(ffn_sums, qkv_grad)
    advance(down_sums, qkv_grad)
    qkv_grad = after(qkv_grad, gate_sums.sum, up_sums.sum)
    head_gains = jnp.sum(head_gains, axis=1)
    query_gain_grad, key_gain_grad = head_gains[:head_width], head_gains[head_width:]
    qkv_weight_grad = transpose_dot(normed_low, qkv_grad)
    norm_gain_grad = jnp.sum(qkv_weight_grad * qkv_all.astype(f32), axis=1) / first_gain
    qkv_weight_grad = by_rows(qkv_weight_grad.astype(bf16))
    normed_partial = dot_transposed(qkv_grad, qkv_all)
    partial_blocks = normed_partial.astype(bf16).reshape(4, tok_rows, width)

    def partial_of(mask):
        index = (seq_index ^ mask).astype(jnp.uint32)
        return lax.dynamic_index_in_dim(partial_blocks, index, 0, keepdims=False)

    normed_grad, normed_sent = scatter_seq(
        partial_of(0),
        partial_of(2),
        jnp.concatenate([partial_of(1), partial_of(3)], axis=0),
    )
    _, own_unit, own_inverse = norm_forward(inputs.astype(f32), first_gain)
    inputs_grad = middle_grad + norm_backward(normed_grad, own_unit, own_inverse, first_gain)

    gain_grads = jnp.concatenate(
        [
            norm_gain_grad.reshape(size, -1),
            ffn_gain_grad.reshape(size, -1),
            query_gain_grad.reshape(size, -1),
            key_gain_grad.reshape(size, -1),
        ],
        axis=1,
    )
    gain_blocks = jnp.pad(
        gain_grads[:, None], ((0, 0), (0, 15), (0, packed_columns - gain_count))
    )
    packed_blocks = jnp.concatenate([qkv_weight_grad, out_weight_grad], axis=1).reshape(
        size, own_rows, packed_columns
    )
    packed_blocks = jnp.concatenate([packed_blocks, gain_blocks.astype(bf16)], axis=1)
    last_sums = (ScatterRing(1, packed_blocks, size, owners),)
    advance(ffn_sums, last_sums[0].sum)
    down_partial = jnp.dot(
        after(hidden, gate_sums.sum), down_all, preferred_element_type=f32
    ).astype(bf16)
    down_sum, down_sent = scatter_seq(
        down_partial[:tok_rows],
        down_partial[tok_rows : 2 * tok_rows],
        down_partial[2 * tok_rows :],
    )
    advance(last_sums, gate_sums.sum, up_sums.sum)
    advance(down_sums, gate_sums.sum, up_sums.sum)
    while gate_sums.count < size - 1:
        advance(ffn_sums, normed_sent)
    both = jnp.stack([gate_sums.sum, up_sums.sum])
    ffn_blocks = gather_seq(both)
    pins = [(both, down_sent), (both, down_sent), (ffn_blocks[1], normed_grad), (down_sum,)]
    while last_sums[0].count < size - 1 or down_sums[0].count < size - 1:
        needed = pins.pop(0) if pins else ()
        advance(last_sums, *needed)
        advance(down_sums, *needed)
    down_pieces = gather_seq(down_sums[0].sum)
    packed_share = last_sums[0].sum
    output = middle + down_sum
    down_full = jnp.concatenate(in_order(down_pieces, seq_index), axis=0)[
        :ff_part
    ].astype(f32)
    gate_full, up_full = (
        spread_hidden(ffn_blocks, which, seq_index, size, ff_part, window) for which in range(2)
    )
    packs = in_order(gather_seq(packed_share), seq_index)

    def unpack(first, count):
        return jnp.concatenate(
            [p[:own_rows, first : first + count] for p in packs], axis=1
        ).astype(f32)

    gain_sum = sum(p[own_rows, :gain_count].astype(f32) for p in packs)
    return (
        output[None].astype(bf16),
        inputs_grad[None].astype(bf16),
        gain_sum[:own_rows],
        unpack(0, query_columns),
        unpack(query_columns, key_columns),
        unpack(query_columns + key_columns, key_columns),
        gain_sum[2 * own_rows : 2 * own_rows + head_part],
        gain_sum[2 * own_rows + head_part :],
        unpack(qkv_columns, query_columns),
        gain_sum[own_rows : 2 * own_rows],
        gate_full,
        up_full,
        down_full,
    )


def solution(mesh):
    in_specs = (
        P("fsdp", "seq", None),
        P("fsdp"),
        P("fsdp", None),
        P("fsdp", None),
        P("fsdp", None),
        P("fsdp"),
        P("fsdp"),
        P("fsdp", None),
        P("fsdp"),
        P("fsdp", None),
        P("fsdp", None),
        P("fsdp", None),
        P("fsdp", "seq", None),
    )
    out_specs = (
        P("fsdp", "seq", None),
        P("fsdp", "seq", None),
        P("fsdp"),
        P("fsdp", None),
        P("fsdp", None),
        P("fsdp", None),
        P("fsdp"),
        P("fsdp"),
        P("fsdp", None),
        P("fsdp"),
        P("fsdp", None),
        P("fsdp", None),
        P("fsdp", None),
    )
    return jax.shard_map(body, mesh=mesh, in_specs=in_specs, out_specs=out_specs, check_vma=False)
```

```python
import functools
import math

import jax
import jax.numpy as jnp
import numpy as np
from jax import lax
from jax.experimental import pallas as pl
from jax.experimental.layout import Layout, with_layout_constraint
from jax.experimental.pallas import tpu as pltpu
from jax.sharding import PartitionSpec as P

norm_epsilon = 1e-05
TILE = 256
log2_e = math.log2(math.e)


def rope_rows(length, width):
    half_width = width // 2
    inverse = jnp.exp(
        jnp.arange(half_width, dtype=jnp.float32) * (-2.0 * math.log(1000000.0) / width)
    )
    angles = inverse[:, None] * jnp.arange(length, dtype=jnp.int32).astype(jnp.float32)[None, :]
    return jnp.cos(angles), jnp.sin(angles)


def head_norm(values):
    inverse = lax.rsqrt(jnp.mean(values * values, axis=0, keepdims=True) + norm_epsilon)
    return values * inverse, inverse


def head_turn(values, cosine, sine):
    half = values.shape[0] // 2
    first, second = values[:half], values[half:]
    return jnp.concatenate(
        [first * cosine - second * sine, second * cosine + first * sine], axis=0
    )


def head_turn_back(values, cosine, sine):
    half = values.shape[0] // 2
    first, second = values[:half], values[half:]
    return jnp.concatenate(
        [first * cosine + second * sine, second * cosine - first * sine], axis=0
    )


def fill_heads(qkv_ref, q_gain_ref, k_gain_ref, cos_ref, sin_ref, queries, keys, keys_t, values, values_t, sizes):
    heads, groups, width = sizes
    cosine, sine = cos_ref[...], sin_ref[...]

    @pl.loop(0, heads)
    def _(head):
        unit, _ = head_norm(qkv_ref[pl.ds(head * width, width), :])
        turned = head_turn(unit * q_gain_ref[...], cosine, sine)
        queries[head] = (turned * (width**-0.5 * log2_e)).astype(jnp.bfloat16)

    @pl.loop(0, groups)
    def _(group):
        unit, _ = head_norm(qkv_ref[pl.ds((heads + group) * width, width), :])
        turned = head_turn(unit * k_gain_ref[...], cosine, sine)
        keys[group] = turned.T.astype(jnp.bfloat16)
        if keys_t is not None:
            keys_t[group] = turned.astype(jnp.bfloat16)
        value = qkv_ref[pl.ds((heads + groups + group) * width, width), :]
        if values is not None:
            values[group] = value.T.astype(jnp.bfloat16)
        if values_t is not None:
            values_t[group] = value.astype(jnp.bfloat16)


def diagonal_mask():
    key_place = lax.broadcasted_iota(jnp.int32, (TILE, TILE), 0)
    query_place = lax.broadcasted_iota(jnp.int32, (TILE, TILE), 1)
    return key_place <= query_place


def causal_exp(scores, count):
    weights = jnp.exp2(scores)
    last = jnp.where(diagonal_mask(), weights[count - TILE :], 0.0)
    if count == TILE:
        return last
    return jnp.concatenate([weights[: count - TILE], last], axis=0)


def dot(left, right):
    return jnp.dot(left, right, preferred_element_type=jnp.float32)


def dot_nt(left, right):
    return lax.dot_general(
        left, right, (((1,), (1,)), ((), ())), preferred_element_type=jnp.float32
    )


def forward_kernel(sizes, qkv_ref, q_gain_ref, k_gain_ref, cos_ref, sin_ref, mixed_ref, mixed_t_ref, total_ref, queries, keys, values_t, mixed_f):
    heads, groups, width = sizes
    ratio = heads // groups
    length = qkv_ref.shape[1]
    fill_heads(qkv_ref, q_gain_ref, k_gain_ref, cos_ref, sin_ref, queries, keys, None, None, values_t, sizes)

    @pl.loop(0, heads)
    def _(head):
        group = head // ratio
        for tile in range(length // TILE):
            count = (tile + 1) * TILE
            columns = pl.ds(tile * TILE, TILE)
            scores = dot(keys[group, pl.ds(0, count), :], queries[head, :, columns])
            weights = causal_exp(scores, count)
            total = jnp.sum(weights, axis=0, keepdims=True)
            result = dot(values_t[group, :, pl.ds(0, count)], weights.astype(jnp.bfloat16))
            mixed_f[pl.ds(head * width, width), columns] = result * (1.0 / total)
            total_ref[pl.ds(head, 1), columns] = jnp.log2(total)

    for block in range(heads * width // 128):
        rows = mixed_f[pl.ds(block * 128, 128), :]
        mixed_t_ref[pl.ds(block * 128, 128), :] = rows.astype(jnp.bfloat16)
        mixed_ref[:, pl.ds(block * 128, 128)] = rows.T.astype(jnp.bfloat16)


def backward_kernel(sizes, qkv_ref, q_gain_ref, k_gain_ref, cos_ref, sin_ref, mixed_t_ref, total_ref, grad_ref, out_ref, gain_ref, out_t, queries, keys, keys_t, values, grads, key_sum, value_sum):
    heads, groups, width = sizes
    ratio = heads // groups
    length = qkv_ref.shape[1]
    fill_heads(qkv_ref, q_gain_ref, k_gain_ref, cos_ref, sin_ref, queries, keys, keys_t, values, None, sizes)
    for block in range(heads * width // 128):
        turned = grad_ref[:, pl.ds(block * 128, 128)].astype(jnp.float32).T
        grads[pl.ds(block * 128, 128), :] = turned.astype(jnp.bfloat16)
    key_sum[...] = jnp.zeros_like(key_sum)
    value_sum[...] = jnp.zeros_like(value_sum)
    gain_ref[...] = jnp.zeros_like(gain_ref)
    cosine, sine = cos_ref[...], sin_ref[...]

    def finish(grad_turned, rows, gain, first):
        grad = head_turn_back(grad_turned, cosine, sine)
        unit, inverse = head_norm(qkv_ref[rows, :])
        product = grad * unit
        part = product[:, :128]
        for lane in range(128, length, 128):
            part = part + product[:, lane : lane + 128]
        gain_ref[pl.ds(first, width), :] += part
        scaled = grad * gain
        before = inverse * (scaled - unit * jnp.mean(scaled * unit, axis=0, keepdims=True))
        out_t[rows, :] = before

    @pl.loop(0, heads)
    def _(head):
        group = head // ratio
        rows = pl.ds(head * width, width)
        query_parts = []
        for tile in range(length // TILE):
            count = (tile + 1) * TILE
            columns = pl.ds(tile * TILE, TILE)
            query = queries[head, :, columns]
            grad = grads[rows, columns]
            scores = dot(keys[group, pl.ds(0, count), :], query) - total_ref[pl.ds(head, 1), columns]
            weights = causal_exp(scores, count)
            inner = jnp.sum(
                grad.astype(jnp.float32) * mixed_t_ref[rows, columns].astype(jnp.float32),
                axis=0,
                keepdims=True,
            )
            weight_grad = dot(values[group, pl.ds(0, count), :], grad)
            score_grad = (weights * (weight_grad - inner)).astype(jnp.bfloat16)
            query_parts.append(dot(keys_t[group, :, pl.ds(0, count)], score_grad))
            key_sum[group, pl.ds(0, count), :] += dot_nt(score_grad, query)
            value_sum[group, pl.ds(0, count), :] += dot_nt(weights.astype(jnp.bfloat16), grad)
        query_grad = jnp.concatenate(query_parts, axis=1) * width**-0.5
        finish(query_grad, rows, q_gain_ref[...], 0)

    for group in range(groups):
        key_grad = key_sum[group].T * (1.0 / log2_e)
        finish(key_grad, pl.ds((heads + group) * width, width), k_gain_ref[...], width)
        out_t[pl.ds((heads + groups + group) * width, width), :] = value_sum[group].T

    for block in range(out_t.shape[0] // 128):
        some = pl.ds(block * 128, 128)
        out_ref[:, some] = out_t[some, :].T.astype(jnp.bfloat16)


def attention_forward(qkv_t, q_gain, k_gain, cosine, sine, sizes):
    heads, groups, width = sizes
    length = qkv_t.shape[1]
    bf16, f32 = jnp.bfloat16, jnp.float32
    pairs = heads * length * length
    return pl.pallas_call(
        functools.partial(forward_kernel, sizes),
        out_shape=(
            jax.ShapeDtypeStruct((length, heads * width), bf16),
            jax.ShapeDtypeStruct((heads * width, length), bf16),
            jax.ShapeDtypeStruct((-(-heads // 8) * 8, length), f32),
        ),
        scratch_shapes=[
            pltpu.VMEM((heads, width, length), bf16),
            pltpu.VMEM((groups, length, width), bf16),
            pltpu.VMEM((groups, width, length), bf16),
            pltpu.VMEM((heads * width, length), f32),
        ],
        compiler_params=pltpu.CompilerParams(vmem_limit_bytes=32 * 2**20),
        cost_estimate=pl.CostEstimate(
            flops=8 * pairs * width, bytes_accessed=6 * 2**20, transcendentals=pairs
        ),
    )(qkv_t, q_gain, k_gain, cosine, sine)


def attention_backward(qkv_t, q_gain, k_gain, cosine, sine, mixed_t, total, mixed_grad, sizes):
    heads, groups, width = sizes
    length = qkv_t.shape[1]
    bf16, f32 = jnp.bfloat16, jnp.float32
    pairs = heads * length * length
    return pl.pallas_call(
        functools.partial(backward_kernel, sizes),
        out_shape=(
            jax.ShapeDtypeStruct(qkv_t.shape[::-1], bf16),
            jax.ShapeDtypeStruct((2 * width, 128), f32),
        ),
        scratch_shapes=[
            pltpu.VMEM(qkv_t.shape, f32),
            pltpu.VMEM((heads, width, length), bf16),
            pltpu.VMEM((groups, length, width), bf16),
            pltpu.VMEM((groups, width, length), bf16),
            pltpu.VMEM((groups, length, width), bf16),
            pltpu.VMEM((heads * width, length), bf16),
            pltpu.VMEM((groups, length, width), f32),
            pltpu.VMEM((groups, length, width), f32),
        ],
        compiler_params=pltpu.CompilerParams(vmem_limit_bytes=40 * 2**20),
        cost_estimate=pl.CostEstimate(flops=0, bytes_accessed=2**20, transcendentals=0),
    )(qkv_t, q_gain, k_gain, cosine, sine, mixed_t, total, mixed_grad)


def hidden_kernel(size, ids_ref, *refs):
    pieces, chunks, refs = refs[:4], refs[4 : 4 + 2 * size], refs[4 + 2 * size :]
    slope_ref, silu_ref, hidden_ref, gate_out, up_out, tokens, gate, up, *sems = refs
    row_sems, in_sems, out_sems = sems
    step = pl.program_id(0)
    steps = pl.num_programs(0)
    rows = chunks[0].shape[0]
    piece = pieces[0].shape[0]

    @pl.when(step == 0)
    def _():
        copies = [
            pltpu.make_async_copy(
                source, tokens.at[pl.ds(index * piece, piece), :], row_sems.at[index]
            )
            for index, source in enumerate(pieces)
        ]
        for copy in copies:
            copy.start()

        @pl.loop(0, steps)
        def _(tile):
            columns = pl.ds(pl.multiple_of(tile * TILE, TILE), TILE)
            for which, target in ((0, gate), (1, up)):
                for index in range(size):
                    first = pl.multiple_of(ids_ref[which, index] * rows, 16)
                    pltpu.make_async_copy(
                        chunks[which * size + index].at[:, columns],
                        target.at[pl.ds(first, rows), columns],
                        in_sems.at[which, tile],
                    ).start()

        for copy in copies:
            copy.wait()

    columns = pl.ds(pl.multiple_of(step * TILE, TILE), TILE)
    for which, target, result in ((0, gate, gate_out), (1, up, up_out)):
        part = target.at[:, columns]
        pltpu.make_async_copy(part, part, in_sems.at[which, step]).wait()
        pltpu.make_async_copy(part, result.at[:, columns], out_sems.at[which, step]).start()
    for half in range(2):
        some = pl.ds(half * 2 * piece, 2 * piece)
        gate_act = dot(tokens[some, :], gate[:, columns])
        up_act = dot(tokens[some, :], up[:, columns])
        sigmoid = 0.5 + 0.5 * jnp.tanh(0.5 * gate_act)
        silu = gate_act * sigmoid
        hidden_ref[some, :] = (silu * up_act).astype(hidden_ref.dtype)
        silu_ref[some, :] = silu.astype(silu_ref.dtype)
        slope_ref[some, :] = (up_act * sigmoid * (1.0 + gate_act * (1.0 - sigmoid))).astype(
            slope_ref.dtype
        )

    @pl.when(step == steps - 1)
    def _():
        @pl.loop(0, steps)
        def _(tile):
            columns = pl.ds(pl.multiple_of(tile * TILE, TILE), TILE)
            for which, target, result in ((0, gate, gate_out), (1, up, up_out)):
                pltpu.make_async_copy(
                    target.at[:, columns], result.at[:, columns], out_sems.at[which, tile]
                ).wait()


def ffn_hidden(pieces, gate_chunks, up_chunks, ids):
    size = len(gate_chunks)
    part, columns = gate_chunks[0].shape
    piece, width = pieces[0].shape
    length = 4 * piece
    bf16 = jnp.bfloat16
    tall = pl.BlockSpec((length, TILE), lambda i, ids: (0, i))
    act = jax.ShapeDtypeStruct((length, columns), bf16)
    weight = jax.ShapeDtypeStruct((width, columns), bf16)
    anywhere = pl.BlockSpec(memory_space=pl.ANY)
    return pl.pallas_call(
        functools.partial(hidden_kernel, size),
        grid_spec=pltpu.PrefetchScalarGridSpec(
            num_scalar_prefetch=1,
            grid=(columns // TILE,),
            in_specs=[anywhere] * (4 + 2 * size),
            out_specs=[tall, tall, tall, anywhere, anywhere],
            scratch_shapes=[
                pltpu.VMEM((length, width), bf16),
                pltpu.VMEM((width, columns), bf16),
                pltpu.VMEM((width, columns), bf16),
                pltpu.SemaphoreType.DMA((4,)),
                pltpu.SemaphoreType.DMA((2, columns // TILE)),
                pltpu.SemaphoreType.DMA((2, columns // TILE)),
            ],
        ),
        out_shape=(act, act, act, weight, weight),
        compiler_params=pltpu.CompilerParams(vmem_limit_bytes=56 * 2**20),
        cost_estimate=pl.CostEstimate(
            flops=4 * length * width * columns,
            bytes_accessed=36 * 2**20,
            transcendentals=length * columns,
        ),
    )(ids, *pieces, *gate_chunks, *up_chunks)


def hidden_grad_kernel(size, owners_ref, grad_ref, slope_ref, silu_ref, *refs):
    chunks, refs = refs[: 2 * size], refs[2 * size :]
    gate_out, up_out, down_out, down, in_sems, out_sem = refs
    step = pl.program_id(0)
    rows = chunks[0].shape[0]

    @pl.when(step == 0)
    def _():
        copies = []
        for which in range(2):
            for index in range(size):
                first = pl.multiple_of((2 * owners_ref[which, index] + which) * rows, 16)
                copies.append(
                    pltpu.make_async_copy(
                        chunks[which * size + index],
                        down.at[pl.ds(first, rows), :],
                        in_sems.at[which, index],
                    )
                )
        for copy in copies:
            copy.start()
        for copy in copies:
            copy.wait()
        pltpu.make_async_copy(down, down_out, out_sem).start()

    weight = down[pl.ds(pl.multiple_of(step * TILE, TILE), TILE), :]
    hidden_grad = dot_nt(grad_ref[...], weight)
    gate_out[...] = (hidden_grad * slope_ref[...].astype(jnp.float32)).astype(jnp.bfloat16)
    up_out[...] = (hidden_grad * silu_ref[...].astype(jnp.float32)).astype(jnp.bfloat16)

    @pl.when(step == pl.num_programs(0) - 1)
    def _():
        pltpu.make_async_copy(down, down_out, out_sem).wait()


def ffn_hidden_grad(out_grad, slope, silu, ahead, behind, owners):
    size = len(ahead)
    length, width = out_grad.shape
    columns = slope.shape[1]
    bf16 = jnp.bfloat16
    tall = pl.BlockSpec((length, TILE), lambda i, owners: (0, i))
    anywhere = pl.BlockSpec(memory_space=pl.ANY)
    act = jax.ShapeDtypeStruct((length, columns), bf16)
    weight = (2 * size * ahead[0].shape[0], width)
    return pl.pallas_call(
        functools.partial(hidden_grad_kernel, size),
        grid_spec=pltpu.PrefetchScalarGridSpec(
            num_scalar_prefetch=1,
            grid=(columns // TILE,),
            in_specs=[pl.BlockSpec((length, width), lambda i, owners: (0, 0)), tall, tall]
            + [anywhere] * (2 * size),
            out_specs=[tall, tall, anywhere],
            scratch_shapes=[
                pltpu.VMEM(weight, bf16),
                pltpu.SemaphoreType.DMA((2, size)),
                pltpu.SemaphoreType.DMA,
            ],
        ),
        out_shape=(act, act, jax.ShapeDtypeStruct(weight, bf16)),
        compiler_params=pltpu.CompilerParams(vmem_limit_bytes=56 * 2**20),
        cost_estimate=pl.CostEstimate(flops=0, bytes_accessed=2**20, transcendentals=0),
    )(owners, out_grad, slope, silu, *ahead, *behind)


def rows_grad_kernel(gate_grad_ref, up_grad_ref, gate_ref, up_ref, own_ref, other_ref, sent_ref):
    piece = own_ref.shape[0]
    total = dot_nt(gate_grad_ref[...], gate_ref[...]) + dot_nt(up_grad_ref[...], up_ref[...])
    total = total.astype(jnp.bfloat16)
    own_ref[...] = total[:piece]
    other_ref[...] = total[piece : 2 * piece]
    sent_ref[...] = total[2 * piece :]


def ffn_rows_grad(gate_grad, up_grad, gate, up):
    length, columns = gate_grad.shape
    width = gate.shape[0]
    piece = length // 4
    bf16 = jnp.bfloat16
    whole = pl.BlockSpec((length, columns), lambda i: (0, 0))
    weight = pl.BlockSpec((TILE, columns), lambda i: (i, 0))
    part = pl.BlockSpec((piece, TILE), lambda i: (0, i))
    return pl.pallas_call(
        rows_grad_kernel,
        grid=(width // TILE,),
        in_specs=[whole, whole, weight, weight],
        out_specs=[part, part, pl.BlockSpec((2 * piece, TILE), lambda i: (0, i))],
        out_shape=(
            jax.ShapeDtypeStruct((piece, width), bf16),
            jax.ShapeDtypeStruct((piece, width), bf16),
            jax.ShapeDtypeStruct((2 * piece, width), bf16),
        ),
        compiler_params=pltpu.CompilerParams(vmem_limit_bytes=56 * 2**20),
        cost_estimate=pl.CostEstimate(flops=0, bytes_accessed=2**20, transcendentals=0),
    )(gate_grad, up_grad, gate, up)


def lay_kernel(size, sizes, owners_ref, *refs):
    chunks, refs = refs[: 2 * size], refs[2 * size :]
    qkv_out, out_out, gains_out, sems = refs
    rows, top, qkv_columns, columns = sizes
    copies = []
    for which, count in ((0, top), (1, rows - top)):
        for index in range(size):
            chunk = chunks[which * size + index]
            owner = owners_ref[which, index]
            first = pl.multiple_of(owner * rows + which * top, 16)
            target = pl.ds(first, count)
            pairs = [
                (chunk.at[pl.ds(0, count), pl.ds(0, qkv_columns)], qkv_out.at[target, :]),
                (
                    chunk.at[pl.ds(0, count), pl.ds(qkv_columns, columns - qkv_columns)],
                    out_out.at[target, :],
                ),
            ]
            if which:
                pairs.append((chunk.at[pl.ds(count, 16), :], gains_out.at[owner]))
            for kind, (source, place) in enumerate(pairs):
                copies.append(pltpu.make_async_copy(source, place, sems.at[kind, which, index]))
    for copy in copies:
        copy.start()
    for copy in copies:
        copy.wait()


def lay_attention(ahead, behind, owners, rows, qkv_columns):
    size = len(ahead)
    top, columns = ahead[0].shape
    bf16 = jnp.bfloat16
    anywhere = pl.BlockSpec(memory_space=pl.ANY)
    return pl.pallas_call(
        functools.partial(lay_kernel, size, (rows, top, qkv_columns, columns)),
        grid_spec=pltpu.PrefetchScalarGridSpec(
            num_scalar_prefetch=1,
            grid=(1,),
            in_specs=[anywhere] * (2 * size),
            out_specs=[pl.BlockSpec(memory_space=pltpu.VMEM)] * 3,
            scratch_shapes=[pltpu.SemaphoreType.DMA((3, 2, size))],
        ),
        out_shape=(
            jax.ShapeDtypeStruct((size * rows, qkv_columns), bf16),
            jax.ShapeDtypeStruct((size * rows, columns - qkv_columns), bf16),
            jax.ShapeDtypeStruct((size, 16, columns), bf16),
        ),
        cost_estimate=pl.CostEstimate(flops=0, bytes_accessed=7 * 2**20, transcendentals=0),
    )(owners, *ahead, *behind)


def pick_kernel(sizes, index_ref, gate_ref, up_ref, gate_out, up_out):
    size, part, window = sizes
    rows = gate_ref.shape[0]
    for source, target in ((gate_ref, gate_out), (up_ref, up_out)):
        for index in range(4):
            count = min(window, part - index * window)

            @pl.when(index_ref[0] == index)
            def _():
                parts = []
                for owner in range(size):
                    first = owner * part + index * window
                    low, high = first // 128 * 128, -(-(first + count) // 128) * 128
                    wide = source[:, low:high].astype(jnp.float32)
                    parts.append(wide[:, first - low : first - low + count])
                    if count < window:
                        parts.append(jnp.zeros((rows, window - count), jnp.float32))
                target[...] = jnp.concatenate(parts, axis=1).astype(target.dtype)


def pick_hidden(gate, up, seq_index, size, part, window):
    rows, columns = gate.shape
    block = 48 if rows % 48 == 0 else rows
    wide = pl.BlockSpec((block, columns), lambda i, index: (i, 0))
    narrow = pl.BlockSpec((block, size * window), lambda i, index: (i, 0))
    out = jax.ShapeDtypeStruct((rows, size * window), gate.dtype)
    return pl.pallas_call(
        functools.partial(pick_kernel, (size, part, window)),
        grid_spec=pltpu.PrefetchScalarGridSpec(
            num_scalar_prefetch=1,
            grid=(rows // block,),
            in_specs=[wide, wide],
            out_specs=[narrow, narrow],
        ),
        out_shape=(out, out),
        compiler_params=pltpu.CompilerParams(vmem_limit_bytes=32 * 2**20),
        cost_estimate=pl.CostEstimate(flops=0, bytes_accessed=8 * 2**20, transcendentals=0),
    )(jnp.reshape(seq_index, (1,)).astype(jnp.int32), gate, up)


def spread_kernel(sizes, index_ref, own_ref, other_ref, near_ref, far_ref, out_ref, parts):
    size, part, window = sizes
    me = index_ref[0]
    parts[me] = own_ref[...]
    parts[me ^ 2] = other_ref[...]
    parts[me ^ 1] = near_ref[...]
    parts[me ^ 3] = far_ref[...]
    pieces = []
    for owner in range(size):
        for index in range(4):
            count = min(window, part - index * window)
            first = owner * window
            low, high = first // 128 * 128, -(-(first + count) // 128) * 128
            wide = parts[index, :, low:high].astype(jnp.float32)
            pieces.append(wide[:, first - low : first - low + count])
    out_ref[...] = jnp.concatenate(pieces, axis=1)


def spread_hidden(pieces, which, seq_index, size, part, window):
    _, rows, columns = pieces[0].shape
    block = 48 if rows % 48 == 0 else rows
    narrow = pl.BlockSpec((None, block, columns), lambda i, index: (which, i, 0))
    return pl.pallas_call(
        functools.partial(spread_kernel, (size, part, window)),
        grid_spec=pltpu.PrefetchScalarGridSpec(
            num_scalar_prefetch=1,
            grid=(rows // block,),
            in_specs=[narrow] * 4,
            out_specs=pl.BlockSpec((block, size * part), lambda i, index: (i, 0)),
            scratch_shapes=[pltpu.VMEM((4, block, columns), pieces[0].dtype)],
        ),
        out_shape=jax.ShapeDtypeStruct((rows, size * part), jnp.float32),
        compiler_params=pltpu.CompilerParams(vmem_limit_bytes=32 * 2**20),
        cost_estimate=pl.CostEstimate(flops=0, bytes_accessed=64 * 2**20, transcendentals=0),
    )(jnp.reshape(seq_index, (1,)), *pieces)


def norm_forward(values, gain):
    inverse = lax.rsqrt(jnp.mean(values * values, axis=-1, keepdims=True) + norm_epsilon)
    unit = values * inverse
    return (unit * gain, unit, inverse)


def norm_backward(grad_in, unit, inverse, gain):
    scaled = grad_in * gain
    return inverse * (scaled - unit * jnp.mean(scaled * unit, axis=-1, keepdims=True))


def transpose_dot(left, right):
    return lax.dot_general(
        left, right, (((0,), (0,)), ((), ())), preferred_element_type=jnp.float32
    )


def by_rows(values):
    return with_layout_constraint(values, Layout(major_to_minor=(0, 1)))


def dot_transposed(left, right):
    return lax.dot_general(
        left, right, (((1,), (1,)), ((), ())), preferred_element_type=jnp.float32
    )


def split_rows(rows):
    return (rows // 32) * 16


def ring_ids(size):
    return list(range(0, size, 2)) + [i for i in range(size - 1, 0, -1) if i % 2]


def ring_perms(size):
    ids = ring_ids(size)
    forward = [(ids[i], ids[(i + 1) % size]) for i in range(size)]
    return forward, [(b, a) for a, b in forward]


def ring_owners(size):
    ids = ring_ids(size)
    table = np.zeros((size, 4, size), np.int32)
    for place, device in enumerate(ids):
        for step in range(size):
            table[device, 0, step] = ids[(place - step) % size]
            table[device, 1, step] = ids[(place + step) % size]
            table[device, 2, step] = ids[(place - 1 - step) % size]
            table[device, 3, step] = ids[(place + 1 + step) % size]
    return lax.dynamic_index_in_dim(
        jnp.asarray(table), lax.axis_index("fsdp").astype(jnp.uint32), 0, keepdims=False
    )


def after(value, *needed):
    return lax.optimization_barrier((value, *needed))[0] if needed else value


class GatherRing:
    def __init__(self, ahead, behind, size):
        self.perms = ring_perms(size)
        self.ahead, self.behind = [ahead], [behind]

    def step(self, first=(), last=()):
        forward, backward = self.perms
        ahead = lax.ppermute(after(self.ahead[-1], *first), "fsdp", forward)
        behind = lax.ppermute(after(self.behind[-1], *first), "fsdp", backward)
        self.ahead.append(after(ahead, *last))
        self.behind.append(after(behind, *last))


class ScatterRing:
    def __init__(self, way, blocks, size, owners, rows=None):
        self.perm = ring_perms(size)[way]
        self.owners = lax.squeeze(lax.slice_in_dim(owners, 2 + way, 3 + way), (0,)).astype(
            jnp.uint32
        )
        self.blocks, self.count = blocks, 0
        self.first, self.last = rows or (0, blocks.shape[1])
        self.sum = self.own().astype(jnp.bfloat16)

    def own(self):
        owner = lax.squeeze(lax.slice_in_dim(self.owners, self.count, self.count + 1), (0,))
        zero = jnp.uint32(0)
        shape = (1, self.last - self.first, self.blocks.shape[2])
        start = (owner, jnp.uint32(self.first), zero)
        return lax.dynamic_slice(self.blocks, start, shape)[0].astype(jnp.float32)

    def step(self, *needed):
        came = after(lax.ppermute(self.sum, "fsdp", self.perm), *needed)
        self.count += 1
        self.sum = (came.astype(jnp.float32) + self.own()).astype(jnp.bfloat16)
        return self.sum


def exchange(values, mask):
    return lax.ppermute(values, "seq", [(i, i ^ mask) for i in range(4)])


def gather_seq(block, *needed):
    block = after(block, *needed)
    other = exchange(block, 2)
    return [block, other, exchange(block, 1), exchange(other, 1)]


def in_order(pieces, seq_index):
    high, low = seq_index // 2, seq_index % 2

    def pick(first, second, flag):
        return jnp.where(flag == 0, first, second), jnp.where(flag == 0, second, first)

    mine = pick(pieces[0], pieces[1], high)
    theirs = pick(pieces[2], pieces[3], high)
    return [*pick(mine[0], theirs[0], low), *pick(mine[1], theirs[1], low)]


def scatter_seq(own, other, there):
    rows = own.shape[0]
    came = exchange(there, 1).astype(jnp.float32)
    sent = (other.astype(jnp.float32) + came[rows:]).astype(jnp.bfloat16)
    near = own.astype(jnp.float32) + came[:rows]
    return near + exchange(sent, 2).astype(jnp.float32), sent


def swap(blocks):
    return lax.all_to_all(blocks, "seq", split_axis=0, concat_axis=0, tiled=True)


def side_by_side(blocks):
    return blocks.transpose(1, 0, 2).reshape(blocks.shape[1], -1)


def apart(values):
    return values.reshape(values.shape[0], 4, -1).transpose(1, 0, 2)


def body(
    tokens,
    norm_gain,
    query_weight,
    key_weight,
    value_weight,
    query_gain,
    key_gain,
    out_weight,
    ffn_gain,
    gate_weight,
    up_weight,
    down_weight,
    cotangent,
):
    bf16, f32 = jnp.bfloat16, jnp.float32
    size = lax.axis_size("fsdp")
    seq_index = lax.axis_index("seq")
    owners = ring_owners(size)
    own_rows, width = query_weight.shape
    head_part = query_gain.shape[0]
    head_width = head_part * size
    query_columns = width // 4
    key_columns = key_weight.shape[1] // 4
    ff_part = down_weight.shape[0]
    window = -(-ff_part // 64) * 16

    def columns_of(weight, count):
        return lax.dynamic_slice_in_dim(weight, seq_index.astype(jnp.uint32) * count, count, 1)

    def hidden_rows(weight):
        tall = jnp.pad(weight, ((0, 4 * window - ff_part), (0, 0)))
        return lax.dynamic_slice_in_dim(tall, seq_index.astype(jnp.uint32) * window, window, 0)

    gains = jnp.concatenate([norm_gain, ffn_gain, query_gain, key_gain])
    gain_count = gains.shape[0]
    qkv_columns = query_columns + 2 * key_columns
    packed_columns = qkv_columns + query_columns
    gain_rows = jnp.pad(gains[None], ((0, 15), (0, packed_columns - gain_count)))
    packed = jnp.concatenate(
        [
            columns_of(query_weight, query_columns),
            columns_of(key_weight, key_columns),
            columns_of(value_weight, key_columns),
            columns_of(out_weight, query_columns),
        ],
        axis=1,
    )
    top = split_rows(own_rows + 16)
    first_ring = GatherRing(
        packed[:top], jnp.concatenate([packed[top:], gain_rows], axis=0), size
    )
    for _ in range(size - 1):
        first_ring.step()
    ffn_ring = GatherRing(
        *pick_hidden(gate_weight, up_weight, seq_index, size, ff_part, window), size
    )
    down_rows = hidden_rows(down_weight)
    def advance(rings, *needed):
        for way in rings:
            if way.count < size - 1:
                way.step(*needed)

    for step in range(1, size):
        ffn_ring.step((first_ring.ahead[2],) if step == 1 else ())
    down_ring = GatherRing(down_rows[: window // 2], down_rows[window // 2 :], size)
    for step in range(1, size - 2):
        lag = min(step + 2, size - 1)
        down_ring.step((ffn_ring.ahead[lag], ffn_ring.behind[lag]))

    qkv_all, out_part, gains_all = lay_attention(
        first_ring.ahead, first_ring.behind, owners, own_rows, qkv_columns
    )
    gains_all = gains_all[:, 0].astype(f32)
    first_gain = gains_all[:, :own_rows].reshape(-1)
    second_gain = gains_all[:, own_rows : 2 * own_rows].reshape(-1)
    q_gain_f = gains_all[:, 2 * own_rows : 2 * own_rows + head_part].reshape(-1)
    k_gain_f = gains_all[:, 2 * own_rows + head_part : 2 * (own_rows + head_part)].reshape(-1)

    inputs = tokens[0]
    tok_rows = inputs.shape[0]
    length = 4 * tok_rows
    input_blocks = gather_seq(inputs)
    inputs_all = jnp.concatenate(in_order(input_blocks, seq_index), axis=0).astype(f32)
    out_grad = cotangent[0]
    grad_blocks = gather_seq(out_grad, input_blocks[1])
    out_grad_all = jnp.concatenate(grad_blocks, axis=0)


    out_other = exchange(after(out_part, input_blocks[1]), 2)
    normed, _, _ = norm_forward(inputs_all, first_gain)
    normed_low = after(normed.astype(bf16), grad_blocks[1])
    qkv_t = lax.dot_general(
        qkv_all, normed_low, (((0,), (1,)), ((), ())), preferred_element_type=f32
    )
    sizes = (query_columns // head_width, key_columns // head_width, head_width)
    cosine, sine = rope_rows(length, head_width)
    tables = (q_gain_f[:, None], k_gain_f[:, None], cosine, sine)
    mixed_heads, mixed_t, totals = attention_forward(qkv_t, *tables, sizes)
    mixed = side_by_side(swap(mixed_heads.reshape(4, tok_rows, query_columns)))
    out_other = after(out_other, mixed_heads)
    out_blocks = [out_part, out_other, exchange(out_part, 1), exchange(out_other, 1)]
    out_all = jnp.concatenate(in_order(out_blocks, seq_index), axis=1)
    attended = jnp.dot(mixed, out_all, preferred_element_type=f32)
    middle = inputs.astype(f32) + attended
    normed_two, middle_unit, middle_inverse = norm_forward(middle, second_gain)
    normed_two_low = normed_two.astype(bf16)
    normed_blocks = gather_seq(normed_two_low)
    normed_two_all = jnp.concatenate(normed_blocks, axis=0)
    mixed_all = jnp.concatenate(
        in_order(gather_seq(mixed_heads, normed_blocks[1]), seq_index), axis=1
    )

    slope, silu, hidden, gate_all, up_all = ffn_hidden(
        [after(normed_blocks[0], down_ring.ahead[-1], down_ring.behind[-1]), *normed_blocks[1:]],
        ffn_ring.ahead,
        ffn_ring.behind,
        owners,
    )
    down_ring.step((), (hidden,))
    hidden = after(hidden, down_ring.ahead[-1], down_ring.behind[-1])
    down_ring.step()
    down_weight_grad = transpose_dot(hidden, out_grad_all).astype(bf16)
    down_blocks = after(
        down_weight_grad, down_ring.ahead[-1], down_ring.behind[-1]
    ).reshape(size, window, width)
    down_sums = (ScatterRing(0, down_blocks, size, owners),)
    gate_grad, up_grad, down_all = ffn_hidden_grad(
        after(out_grad_all, *(way.sum for way in down_sums)),
        slope,
        silu,
        down_ring.ahead,
        down_ring.behind,
        owners,
    )
    advance(down_sums, gate_grad)
    gate_weight_grad = transpose_dot(
        after(normed_two_all, *(way.sum for way in down_sums)), gate_grad
    ).astype(bf16)
    gate_sums = ScatterRing(
        0, gate_weight_grad.reshape(size, own_rows, size * window), size, owners
    )
    up_weight_grad = transpose_dot(after(normed_two_all, gate_sums.sum), up_grad).astype(bf16)
    up_sums = ScatterRing(1, up_weight_grad.reshape(size, own_rows, size * window), size, owners)
    ffn_sums = (gate_sums, up_sums)
    normed_parts = ffn_rows_grad(after(gate_grad, up_sums.sum), up_grad, gate_all, up_all)
    advance(ffn_sums, normed_parts[0])
    normed_two_grad, half_sum = scatter_seq(
        *normed_parts[:2], after(normed_parts[2], gate_sums.sum)
    )
    advance(ffn_sums, half_sum)
    ffn_gain_grad = jnp.sum(normed_two_grad * middle_unit, axis=0)
    middle_grad = out_grad.astype(f32) + norm_backward(
        normed_two_grad, middle_unit, middle_inverse, second_gain
    )
    attended_low = middle_grad.astype(bf16)
    mixed_grad = dot_transposed(attended_low, out_all).astype(bf16)
    advance(ffn_sums, mixed_grad)
    advance(down_sums, mixed_grad)
    mixed_grad_heads = after(
        swap(apart(mixed_grad)), gate_sums.sum, up_sums.sum, down_sums[0].sum
    ).reshape(
        length, query_columns
    )
    qkv_grad, head_gains = attention_backward(
        qkv_t, *tables, mixed_t, totals, mixed_grad_heads, sizes
    )
    attended_columns = after(
        swap(apart(after(attended_low, mixed_grad_heads))), qkv_grad
    ).reshape(length, query_columns)
    out_weight_grad = by_rows(transpose_dot(mixed_all, attended_columns).astype(bf16))
    advance(ffn_sums, qkv_grad)
    advance(down_sums, qkv_grad)
    qkv_grad = after(qkv_grad, gate_sums.sum, up_sums.sum)
    head_gains = jnp.sum(head_gains, axis=1)
    query_gain_grad, key_gain_grad = head_gains[:head_width], head_gains[head_width:]
    qkv_weight_grad = transpose_dot(normed_low, qkv_grad)
    norm_gain_grad = jnp.sum(qkv_weight_grad * qkv_all.astype(f32), axis=1) / first_gain
    qkv_weight_grad = by_rows(qkv_weight_grad.astype(bf16))
    normed_partial = dot_transposed(qkv_grad, qkv_all)
    partial_blocks = normed_partial.astype(bf16).reshape(4, tok_rows, width)

    def partial_of(mask):
        index = (seq_index ^ mask).astype(jnp.uint32)
        return lax.dynamic_index_in_dim(partial_blocks, index, 0, keepdims=False)

    normed_grad, normed_sent = scatter_seq(
        partial_of(0),
        partial_of(2),
        jnp.concatenate([partial_of(1), partial_of(3)], axis=0),
    )
    _, own_unit, own_inverse = norm_forward(inputs.astype(f32), first_gain)
    inputs_grad = middle_grad + norm_backward(normed_grad, own_unit, own_inverse, first_gain)

    gain_grads = jnp.concatenate(
        [
            norm_gain_grad.reshape(size, -1),
            ffn_gain_grad.reshape(size, -1),
            query_gain_grad.reshape(size, -1),
            key_gain_grad.reshape(size, -1),
        ],
        axis=1,
    )
    gain_blocks = jnp.pad(
        gain_grads[:, None], ((0, 0), (0, 15), (0, packed_columns - gain_count))
    )
    packed_blocks = jnp.concatenate([qkv_weight_grad, out_weight_grad], axis=1).reshape(
        size, own_rows, packed_columns
    )
    packed_blocks = jnp.concatenate([packed_blocks, gain_blocks.astype(bf16)], axis=1)
    last_sums = (ScatterRing(1, packed_blocks, size, owners),)
    advance(ffn_sums, last_sums[0].sum)
    down_partial = jnp.dot(
        after(hidden, gate_sums.sum), down_all, preferred_element_type=f32
    ).astype(bf16)
    down_sum, down_sent = scatter_seq(
        down_partial[:tok_rows],
        down_partial[tok_rows : 2 * tok_rows],
        down_partial[2 * tok_rows :],
    )
    advance(down_sums, gate_sums.sum)
    advance(last_sums, gate_sums.sum, up_sums.sum)
    pins = [(normed_grad, down_sent), (normed_sent,)]
    while gate_sums.count < size - 1:
        advance(ffn_sums, last_sums[0].sum, *(pins.pop() if pins else ()))
        advance(down_sums, gate_sums.sum, up_sums.sum)
        advance(last_sums, gate_sums.sum, up_sums.sum)
    both = jnp.stack([gate_sums.sum, up_sums.sum])
    ffn_blocks = gather_seq(both)
    pins = [(both,), (down_sum,), (), (ffn_blocks[1],)]
    while last_sums[0].count < size - 1 or down_sums[0].count < size - 1:
        needed = pins.pop(0) if pins else ()
        advance(down_sums, *needed)
        advance(last_sums, *needed)
    down_pieces = gather_seq(down_sums[0].sum)
    packed_share = last_sums[0].sum
    output = middle + down_sum
    down_full = jnp.concatenate(in_order(down_pieces, seq_index), axis=0)[
        :ff_part
    ].astype(f32)
    gate_full, up_full = (
        spread_hidden(ffn_blocks, which, seq_index, size, ff_part, window) for which in range(2)
    )
    packs = in_order(gather_seq(packed_share), seq_index)

    def unpack(first, count):
        return jnp.concatenate(
            [p[:own_rows, first : first + count] for p in packs], axis=1
        ).astype(f32)

    gain_sum = sum(p[own_rows, :gain_count].astype(f32) for p in packs)
    return (
        output[None].astype(bf16),
        inputs_grad[None].astype(bf16),
        gain_sum[:own_rows],
        unpack(0, query_columns),
        unpack(query_columns, key_columns),
        unpack(query_columns + key_columns, key_columns),
        gain_sum[2 * own_rows : 2 * own_rows + head_part],
        gain_sum[2 * own_rows + head_part :],
        unpack(qkv_columns, query_columns),
        gain_sum[own_rows : 2 * own_rows],
        gate_full,
        up_full,
        down_full,
    )


def solution(mesh):
    in_specs = (
        P("fsdp", "seq", None),
        P("fsdp"),
        P("fsdp", None),
        P("fsdp", None),
        P("fsdp", None),
        P("fsdp"),
        P("fsdp"),
        P("fsdp", None),
        P("fsdp"),
        P("fsdp", None),
        P("fsdp", None),
        P("fsdp", None),
        P("fsdp", "seq", None),
    )
    out_specs = (
        P("fsdp", "seq", None),
        P("fsdp", "seq", None),
        P("fsdp"),
        P("fsdp", None),
        P("fsdp", None),
        P("fsdp", None),
        P("fsdp"),
        P("fsdp"),
        P("fsdp", None),
        P("fsdp"),
        P("fsdp", None),
        P("fsdp", None),
        P("fsdp", None),
    )
    return jax.shard_map(body, mesh=mesh, in_specs=in_specs, out_specs=out_specs, check_vma=False)
```

```python
import functools
import math

import jax
import jax.numpy as jnp
import numpy as np
from jax import lax
from jax.experimental import pallas as pl
from jax.experimental.layout import Layout, with_layout_constraint
from jax.experimental.pallas import tpu as pltpu
from jax.sharding import PartitionSpec as P

norm_epsilon = 1e-05
TILE = 256
log2_e = math.log2(math.e)


def rope_rows(length, width):
    half_width = width // 2
    inverse = jnp.exp(
        jnp.arange(half_width, dtype=jnp.float32) * (-2.0 * math.log(1000000.0) / width)
    )
    angles = inverse[:, None] * jnp.arange(length, dtype=jnp.int32).astype(jnp.float32)[None, :]
    return jnp.cos(angles), jnp.sin(angles)


def head_norm(values):
    inverse = lax.rsqrt(jnp.mean(values * values, axis=0, keepdims=True) + norm_epsilon)
    return values * inverse, inverse


def head_turn(values, cosine, sine):
    half = values.shape[0] // 2
    first, second = values[:half], values[half:]
    return jnp.concatenate(
        [first * cosine - second * sine, second * cosine + first * sine], axis=0
    )


def head_turn_back(values, cosine, sine):
    half = values.shape[0] // 2
    first, second = values[:half], values[half:]
    return jnp.concatenate(
        [first * cosine + second * sine, second * cosine - first * sine], axis=0
    )


def fill_heads(qkv_ref, q_gain_ref, k_gain_ref, cos_ref, sin_ref, queries, keys, keys_t, values, values_t, sizes):
    heads, groups, width = sizes
    cosine, sine = cos_ref[...], sin_ref[...]

    @pl.loop(0, heads)
    def _(head):
        unit, _ = head_norm(qkv_ref[pl.ds(head * width, width), :])
        turned = head_turn(unit * q_gain_ref[...], cosine, sine)
        queries[head] = (turned * (width**-0.5 * log2_e)).astype(jnp.bfloat16)

    @pl.loop(0, groups)
    def _(group):
        unit, _ = head_norm(qkv_ref[pl.ds((heads + group) * width, width), :])
        turned = head_turn(unit * k_gain_ref[...], cosine, sine)
        keys[group] = turned.T.astype(jnp.bfloat16)
        if keys_t is not None:
            keys_t[group] = turned.astype(jnp.bfloat16)
        value = qkv_ref[pl.ds((heads + groups + group) * width, width), :]
        if values is not None:
            values[group] = value.T.astype(jnp.bfloat16)
        if values_t is not None:
            values_t[group] = value.astype(jnp.bfloat16)


def diagonal_mask():
    key_place = lax.broadcasted_iota(jnp.int32, (TILE, TILE), 0)
    query_place = lax.broadcasted_iota(jnp.int32, (TILE, TILE), 1)
    return key_place <= query_place


def causal_exp(scores, count):
    weights = jnp.exp2(scores)
    last = jnp.where(diagonal_mask(), weights[count - TILE :], 0.0)
    if count == TILE:
        return last
    return jnp.concatenate([weights[: count - TILE], last], axis=0)


def dot(left, right):
    return jnp.dot(left, right, preferred_element_type=jnp.float32)


def dot_nt(left, right):
    return lax.dot_general(
        left, right, (((1,), (1,)), ((), ())), preferred_element_type=jnp.float32
    )


def forward_kernel(sizes, qkv_ref, q_gain_ref, k_gain_ref, cos_ref, sin_ref, mixed_ref, mixed_t_ref, total_ref, queries, keys, values_t, mixed_f):
    heads, groups, width = sizes
    ratio = heads // groups
    length = qkv_ref.shape[1]
    fill_heads(qkv_ref, q_gain_ref, k_gain_ref, cos_ref, sin_ref, queries, keys, None, None, values_t, sizes)

    @pl.loop(0, heads)
    def _(head):
        group = head // ratio
        for tile in range(length // TILE):
            count = (tile + 1) * TILE
            columns = pl.ds(tile * TILE, TILE)
            scores = dot(keys[group, pl.ds(0, count), :], queries[head, :, columns])
            weights = causal_exp(scores, count)
            total = jnp.sum(weights, axis=0, keepdims=True)
            result = dot(values_t[group, :, pl.ds(0, count)], weights.astype(jnp.bfloat16))
            mixed_f[pl.ds(head * width, width), columns] = result * (1.0 / total)
            total_ref[pl.ds(head, 1), columns] = jnp.log2(total)

    for block in range(heads * width // 128):
        rows = mixed_f[pl.ds(block * 128, 128), :]
        mixed_t_ref[pl.ds(block * 128, 128), :] = rows.astype(jnp.bfloat16)
        mixed_ref[:, pl.ds(block * 128, 128)] = rows.T.astype(jnp.bfloat16)


def backward_kernel(sizes, qkv_ref, q_gain_ref, k_gain_ref, cos_ref, sin_ref, mixed_t_ref, total_ref, grad_ref, out_ref, gain_ref, out_t, queries, keys, keys_t, values, grads, key_sum, value_sum):
    heads, groups, width = sizes
    ratio = heads // groups
    length = qkv_ref.shape[1]
    fill_heads(qkv_ref, q_gain_ref, k_gain_ref, cos_ref, sin_ref, queries, keys, keys_t, values, None, sizes)
    for block in range(heads * width // 128):
        turned = grad_ref[:, pl.ds(block * 128, 128)].astype(jnp.float32).T
        grads[pl.ds(block * 128, 128), :] = turned.astype(jnp.bfloat16)
    key_sum[...] = jnp.zeros_like(key_sum)
    value_sum[...] = jnp.zeros_like(value_sum)
    gain_ref[...] = jnp.zeros_like(gain_ref)
    cosine, sine = cos_ref[...], sin_ref[...]

    def finish(grad_turned, rows, gain, first):
        grad = head_turn_back(grad_turned, cosine, sine)
        unit, inverse = head_norm(qkv_ref[rows, :])
        product = grad * unit
        part = product[:, :128]
        for lane in range(128, length, 128):
            part = part + product[:, lane : lane + 128]
        gain_ref[pl.ds(first, width), :] += part
        scaled = grad * gain
        before = inverse * (scaled - unit * jnp.mean(scaled * unit, axis=0, keepdims=True))
        out_t[rows, :] = before

    @pl.loop(0, heads)
    def _(head):
        group = head // ratio
        rows = pl.ds(head * width, width)
        query_parts = []
        for tile in range(length // TILE):
            count = (tile + 1) * TILE
            columns = pl.ds(tile * TILE, TILE)
            query = queries[head, :, columns]
            grad = grads[rows, columns]
            scores = dot(keys[group, pl.ds(0, count), :], query) - total_ref[pl.ds(head, 1), columns]
            weights = causal_exp(scores, count)
            inner = jnp.sum(
                grad.astype(jnp.float32) * mixed_t_ref[rows, columns].astype(jnp.float32),
                axis=0,
                keepdims=True,
            )
            weight_grad = dot(values[group, pl.ds(0, count), :], grad)
            score_grad = (weights * (weight_grad - inner)).astype(jnp.bfloat16)
            query_parts.append(dot(keys_t[group, :, pl.ds(0, count)], score_grad))
            key_sum[group, pl.ds(0, count), :] += dot_nt(score_grad, query)
            value_sum[group, pl.ds(0, count), :] += dot_nt(weights.astype(jnp.bfloat16), grad)
        query_grad = jnp.concatenate(query_parts, axis=1) * width**-0.5
        finish(query_grad, rows, q_gain_ref[...], 0)

    for group in range(groups):
        key_grad = key_sum[group].T * (1.0 / log2_e)
        finish(key_grad, pl.ds((heads + group) * width, width), k_gain_ref[...], width)
        out_t[pl.ds((heads + groups + group) * width, width), :] = value_sum[group].T

    for block in range(out_t.shape[0] // 128):
        some = pl.ds(block * 128, 128)
        out_ref[:, some] = out_t[some, :].T.astype(jnp.bfloat16)


def attention_forward(qkv_t, q_gain, k_gain, cosine, sine, sizes):
    heads, groups, width = sizes
    length = qkv_t.shape[1]
    bf16, f32 = jnp.bfloat16, jnp.float32
    pairs = heads * length * length
    return pl.pallas_call(
        functools.partial(forward_kernel, sizes),
        out_shape=(
            jax.ShapeDtypeStruct((length, heads * width), bf16),
            jax.ShapeDtypeStruct((heads * width, length), bf16),
            jax.ShapeDtypeStruct((-(-heads // 8) * 8, length), f32),
        ),
        scratch_shapes=[
            pltpu.VMEM((heads, width, length), bf16),
            pltpu.VMEM((groups, length, width), bf16),
            pltpu.VMEM((groups, width, length), bf16),
            pltpu.VMEM((heads * width, length), f32),
        ],
        compiler_params=pltpu.CompilerParams(vmem_limit_bytes=32 * 2**20),
        cost_estimate=pl.CostEstimate(
            flops=8 * pairs * width, bytes_accessed=6 * 2**20, transcendentals=pairs
        ),
    )(qkv_t, q_gain, k_gain, cosine, sine)


def attention_backward(qkv_t, q_gain, k_gain, cosine, sine, mixed_t, total, mixed_grad, sizes):
    heads, groups, width = sizes
    length = qkv_t.shape[1]
    bf16, f32 = jnp.bfloat16, jnp.float32
    pairs = heads * length * length
    return pl.pallas_call(
        functools.partial(backward_kernel, sizes),
        out_shape=(
            jax.ShapeDtypeStruct(qkv_t.shape[::-1], bf16),
            jax.ShapeDtypeStruct((2 * width, 128), f32),
        ),
        scratch_shapes=[
            pltpu.VMEM(qkv_t.shape, f32),
            pltpu.VMEM((heads, width, length), bf16),
            pltpu.VMEM((groups, length, width), bf16),
            pltpu.VMEM((groups, width, length), bf16),
            pltpu.VMEM((groups, length, width), bf16),
            pltpu.VMEM((heads * width, length), bf16),
            pltpu.VMEM((groups, length, width), f32),
            pltpu.VMEM((groups, length, width), f32),
        ],
        compiler_params=pltpu.CompilerParams(vmem_limit_bytes=40 * 2**20),
        cost_estimate=pl.CostEstimate(flops=0, bytes_accessed=2**20, transcendentals=0),
    )(qkv_t, q_gain, k_gain, cosine, sine, mixed_t, total, mixed_grad)


def hidden_kernel(size, ids_ref, *refs):
    pieces, chunks, refs = refs[:4], refs[4 : 4 + 2 * size], refs[4 + 2 * size :]
    slope_ref, silu_ref, hidden_ref, gate_out, up_out, tokens, gate, up, *sems = refs
    row_sems, in_sems, out_sems = sems
    step = pl.program_id(0)
    steps = pl.num_programs(0)
    rows = chunks[0].shape[0]
    piece = pieces[0].shape[0]

    @pl.when(step == 0)
    def _():
        copies = [
            pltpu.make_async_copy(
                source, tokens.at[pl.ds(index * piece, piece), :], row_sems.at[index]
            )
            for index, source in enumerate(pieces)
        ]
        for copy in copies:
            copy.start()

        @pl.loop(0, steps)
        def _(tile):
            columns = pl.ds(pl.multiple_of(tile * TILE, TILE), TILE)
            for which, target in ((0, gate), (1, up)):
                for index in range(size):
                    first = pl.multiple_of(ids_ref[which, index] * rows, 16)
                    pltpu.make_async_copy(
                        chunks[which * size + index].at[:, columns],
                        target.at[pl.ds(first, rows), columns],
                        in_sems.at[which, tile],
                    ).start()

        for copy in copies:
            copy.wait()

    columns = pl.ds(pl.multiple_of(step * TILE, TILE), TILE)
    for which, target, result in ((0, gate, gate_out), (1, up, up_out)):
        part = target.at[:, columns]
        pltpu.make_async_copy(part, part, in_sems.at[which, step]).wait()
        pltpu.make_async_copy(part, result.at[:, columns], out_sems.at[which, step]).start()
    for half in range(2):
        some = pl.ds(half * 2 * piece, 2 * piece)
        gate_act = dot(tokens[some, :], gate[:, columns])
        up_act = dot(tokens[some, :], up[:, columns])
        sigmoid = 0.5 + 0.5 * jnp.tanh(0.5 * gate_act)
        silu = gate_act * sigmoid
        hidden_ref[some, :] = (silu * up_act).astype(hidden_ref.dtype)
        silu_ref[some, :] = silu.astype(silu_ref.dtype)
        slope_ref[some, :] = (up_act * sigmoid * (1.0 + gate_act * (1.0 - sigmoid))).astype(
            slope_ref.dtype
        )

    @pl.when(step == steps - 1)
    def _():
        @pl.loop(0, steps)
        def _(tile):
            columns = pl.ds(pl.multiple_of(tile * TILE, TILE), TILE)
            for which, target, result in ((0, gate, gate_out), (1, up, up_out)):
                pltpu.make_async_copy(
                    target.at[:, columns], result.at[:, columns], out_sems.at[which, tile]
                ).wait()


def ffn_hidden(pieces, gate_chunks, up_chunks, ids):
    size = len(gate_chunks)
    part, columns = gate_chunks[0].shape
    piece, width = pieces[0].shape
    length = 4 * piece
    bf16 = jnp.bfloat16
    tall = pl.BlockSpec((length, TILE), lambda i, ids: (0, i))
    act = jax.ShapeDtypeStruct((length, columns), bf16)
    weight = jax.ShapeDtypeStruct((width, columns), bf16)
    anywhere = pl.BlockSpec(memory_space=pl.ANY)
    return pl.pallas_call(
        functools.partial(hidden_kernel, size),
        grid_spec=pltpu.PrefetchScalarGridSpec(
            num_scalar_prefetch=1,
            grid=(columns // TILE,),
            in_specs=[anywhere] * (4 + 2 * size),
            out_specs=[tall, tall, tall, anywhere, anywhere],
            scratch_shapes=[
                pltpu.VMEM((length, width), bf16),
                pltpu.VMEM((width, columns), bf16),
                pltpu.VMEM((width, columns), bf16),
                pltpu.SemaphoreType.DMA((4,)),
                pltpu.SemaphoreType.DMA((2, columns // TILE)),
                pltpu.SemaphoreType.DMA((2, columns // TILE)),
            ],
        ),
        out_shape=(act, act, act, weight, weight),
        compiler_params=pltpu.CompilerParams(vmem_limit_bytes=56 * 2**20),
        cost_estimate=pl.CostEstimate(
            flops=4 * length * width * columns,
            bytes_accessed=36 * 2**20,
            transcendentals=length * columns,
        ),
    )(ids, *pieces, *gate_chunks, *up_chunks)


def hidden_grad_kernel(size, owners_ref, grad_ref, slope_ref, silu_ref, *refs):
    chunks, refs = refs[: 2 * size], refs[2 * size :]
    gate_out, up_out, down_out, down, in_sems, out_sem = refs
    step = pl.program_id(0)
    rows = chunks[0].shape[0]

    @pl.when(step == 0)
    def _():
        copies = []
        for which in range(2):
            for index in range(size):
                first = pl.multiple_of((2 * owners_ref[which, index] + which) * rows, 16)
                copies.append(
                    pltpu.make_async_copy(
                        chunks[which * size + index],
                        down.at[pl.ds(first, rows), :],
                        in_sems.at[which, index],
                    )
                )
        for copy in copies:
            copy.start()
        for copy in copies:
            copy.wait()
        pltpu.make_async_copy(down, down_out, out_sem).start()

    weight = down[pl.ds(pl.multiple_of(step * TILE, TILE), TILE), :]
    hidden_grad = dot_nt(grad_ref[...], weight)
    gate_out[...] = (hidden_grad * slope_ref[...].astype(jnp.float32)).astype(jnp.bfloat16)
    up_out[...] = (hidden_grad * silu_ref[...].astype(jnp.float32)).astype(jnp.bfloat16)

    @pl.when(step == pl.num_programs(0) - 1)
    def _():
        pltpu.make_async_copy(down, down_out, out_sem).wait()


def ffn_hidden_grad(out_grad, slope, silu, ahead, behind, owners):
    size = len(ahead)
    length, width = out_grad.shape
    columns = slope.shape[1]
    bf16 = jnp.bfloat16
    tall = pl.BlockSpec((length, TILE), lambda i, owners: (0, i))
    anywhere = pl.BlockSpec(memory_space=pl.ANY)
    act = jax.ShapeDtypeStruct((length, columns), bf16)
    weight = (2 * size * ahead[0].shape[0], width)
    return pl.pallas_call(
        functools.partial(hidden_grad_kernel, size),
        grid_spec=pltpu.PrefetchScalarGridSpec(
            num_scalar_prefetch=1,
            grid=(columns // TILE,),
            in_specs=[pl.BlockSpec((length, width), lambda i, owners: (0, 0)), tall, tall]
            + [anywhere] * (2 * size),
            out_specs=[tall, tall, anywhere],
            scratch_shapes=[
                pltpu.VMEM(weight, bf16),
                pltpu.SemaphoreType.DMA((2, size)),
                pltpu.SemaphoreType.DMA,
            ],
        ),
        out_shape=(act, act, jax.ShapeDtypeStruct(weight, bf16)),
        compiler_params=pltpu.CompilerParams(vmem_limit_bytes=56 * 2**20),
        cost_estimate=pl.CostEstimate(flops=0, bytes_accessed=2**20, transcendentals=0),
    )(owners, out_grad, slope, silu, *ahead, *behind)


def rows_grad_kernel(gate_grad_ref, up_grad_ref, gate_ref, up_ref, own_ref, other_ref, sent_ref):
    piece = own_ref.shape[0]
    total = dot_nt(gate_grad_ref[...], gate_ref[...]) + dot_nt(up_grad_ref[...], up_ref[...])
    total = total.astype(jnp.bfloat16)
    own_ref[...] = total[:piece]
    other_ref[...] = total[piece : 2 * piece]
    sent_ref[...] = total[2 * piece :]


def ffn_rows_grad(gate_grad, up_grad, gate, up):
    length, columns = gate_grad.shape
    width = gate.shape[0]
    piece = length // 4
    bf16 = jnp.bfloat16
    whole = pl.BlockSpec((length, columns), lambda i: (0, 0))
    weight = pl.BlockSpec((TILE, columns), lambda i: (i, 0))
    part = pl.BlockSpec((piece, TILE), lambda i: (0, i))
    return pl.pallas_call(
        rows_grad_kernel,
        grid=(width // TILE,),
        in_specs=[whole, whole, weight, weight],
        out_specs=[part, part, pl.BlockSpec((2 * piece, TILE), lambda i: (0, i))],
        out_shape=(
            jax.ShapeDtypeStruct((piece, width), bf16),
            jax.ShapeDtypeStruct((piece, width), bf16),
            jax.ShapeDtypeStruct((2 * piece, width), bf16),
        ),
        compiler_params=pltpu.CompilerParams(vmem_limit_bytes=56 * 2**20),
        cost_estimate=pl.CostEstimate(flops=0, bytes_accessed=2**20, transcendentals=0),
    )(gate_grad, up_grad, gate, up)


def lay_kernel(size, sizes, owners_ref, *refs):
    chunks, refs = refs[: 2 * size], refs[2 * size :]
    qkv_out, out_out, gains_out, sems = refs
    rows, top, qkv_columns, columns = sizes
    copies = []
    for which, count in ((0, top), (1, rows - top)):
        for index in range(size):
            chunk = chunks[which * size + index]
            owner = owners_ref[which, index]
            first = pl.multiple_of(owner * rows + which * top, 16)
            target = pl.ds(first, count)
            pairs = [
                (chunk.at[pl.ds(0, count), pl.ds(0, qkv_columns)], qkv_out.at[target, :]),
                (
                    chunk.at[pl.ds(0, count), pl.ds(qkv_columns, columns - qkv_columns)],
                    out_out.at[target, :],
                ),
            ]
            if which:
                pairs.append((chunk.at[pl.ds(count, 16), :], gains_out.at[owner]))
            for kind, (source, place) in enumerate(pairs):
                copies.append(pltpu.make_async_copy(source, place, sems.at[kind, which, index]))
    for copy in copies:
        copy.start()
    for copy in copies:
        copy.wait()


def lay_attention(ahead, behind, owners, rows, qkv_columns):
    size = len(ahead)
    top, columns = ahead[0].shape
    bf16 = jnp.bfloat16
    anywhere = pl.BlockSpec(memory_space=pl.ANY)
    return pl.pallas_call(
        functools.partial(lay_kernel, size, (rows, top, qkv_columns, columns)),
        grid_spec=pltpu.PrefetchScalarGridSpec(
            num_scalar_prefetch=1,
            grid=(1,),
            in_specs=[anywhere] * (2 * size),
            out_specs=[pl.BlockSpec(memory_space=pltpu.VMEM)] * 3,
            scratch_shapes=[pltpu.SemaphoreType.DMA((3, 2, size))],
        ),
        out_shape=(
            jax.ShapeDtypeStruct((size * rows, qkv_columns), bf16),
            jax.ShapeDtypeStruct((size * rows, columns - qkv_columns), bf16),
            jax.ShapeDtypeStruct((size, 16, columns), bf16),
        ),
        cost_estimate=pl.CostEstimate(flops=0, bytes_accessed=7 * 2**20, transcendentals=0),
    )(owners, *ahead, *behind)


def pick_kernel(sizes, index_ref, gate_ref, up_ref, gate_out, up_out):
    size, part, window = sizes
    rows = gate_ref.shape[0]
    for source, target in ((gate_ref, gate_out), (up_ref, up_out)):
        for index in range(4):
            count = min(window, part - index * window)

            @pl.when(index_ref[0] == index)
            def _():
                parts = []
                for owner in range(size):
                    first = owner * part + index * window
                    low, high = first // 128 * 128, -(-(first + count) // 128) * 128
                    wide = source[:, low:high].astype(jnp.float32)
                    parts.append(wide[:, first - low : first - low + count])
                    if count < window:
                        parts.append(jnp.zeros((rows, window - count), jnp.float32))
                target[...] = jnp.concatenate(parts, axis=1).astype(target.dtype)


def pick_hidden(gate, up, seq_index, size, part, window):
    rows, columns = gate.shape
    block = 48 if rows % 48 == 0 else rows
    wide = pl.BlockSpec((block, columns), lambda i, index: (i, 0))
    narrow = pl.BlockSpec((block, size * window), lambda i, index: (i, 0))
    out = jax.ShapeDtypeStruct((rows, size * window), gate.dtype)
    return pl.pallas_call(
        functools.partial(pick_kernel, (size, part, window)),
        grid_spec=pltpu.PrefetchScalarGridSpec(
            num_scalar_prefetch=1,
            grid=(rows // block,),
            in_specs=[wide, wide],
            out_specs=[narrow, narrow],
        ),
        out_shape=(out, out),
        compiler_params=pltpu.CompilerParams(vmem_limit_bytes=32 * 2**20),
        cost_estimate=pl.CostEstimate(flops=0, bytes_accessed=8 * 2**20, transcendentals=0),
    )(jnp.reshape(seq_index, (1,)).astype(jnp.int32), gate, up)


def spread_kernel(sizes, index_ref, own_ref, other_ref, near_ref, far_ref, out_ref, parts):
    size, part, window = sizes
    me = index_ref[0]
    parts[me] = own_ref[...]
    parts[me ^ 2] = other_ref[...]
    parts[me ^ 1] = near_ref[...]
    parts[me ^ 3] = far_ref[...]
    pieces = []
    for owner in range(size):
        for index in range(4):
            count = min(window, part - index * window)
            first = owner * window
            low, high = first // 128 * 128, -(-(first + count) // 128) * 128
            wide = parts[index, :, low:high].astype(jnp.float32)
            pieces.append(wide[:, first - low : first - low + count])
    out_ref[...] = jnp.concatenate(pieces, axis=1)


def spread_hidden(pieces, which, seq_index, size, part, window):
    _, rows, columns = pieces[0].shape
    block = 48 if rows % 48 == 0 else rows
    narrow = pl.BlockSpec((None, block, columns), lambda i, index: (which, i, 0))
    return pl.pallas_call(
        functools.partial(spread_kernel, (size, part, window)),
        grid_spec=pltpu.PrefetchScalarGridSpec(
            num_scalar_prefetch=1,
            grid=(rows // block,),
            in_specs=[narrow] * 4,
            out_specs=pl.BlockSpec((block, size * part), lambda i, index: (i, 0)),
            scratch_shapes=[pltpu.VMEM((4, block, columns), pieces[0].dtype)],
        ),
        out_shape=jax.ShapeDtypeStruct((rows, size * part), jnp.float32),
        compiler_params=pltpu.CompilerParams(vmem_limit_bytes=32 * 2**20),
        cost_estimate=pl.CostEstimate(flops=0, bytes_accessed=64 * 2**20, transcendentals=0),
    )(jnp.reshape(seq_index, (1,)), *pieces)


def norm_forward(values, gain):
    inverse = lax.rsqrt(jnp.mean(values * values, axis=-1, keepdims=True) + norm_epsilon)
    unit = values * inverse
    return (unit * gain, unit, inverse)


def norm_backward(grad_in, unit, inverse, gain):
    scaled = grad_in * gain
    return inverse * (scaled - unit * jnp.mean(scaled * unit, axis=-1, keepdims=True))


def transpose_dot(left, right):
    return lax.dot_general(
        left, right, (((0,), (0,)), ((), ())), preferred_element_type=jnp.float32
    )


def by_rows(values):
    return with_layout_constraint(values, Layout(major_to_minor=(0, 1)))


def dot_transposed(left, right):
    return lax.dot_general(
        left, right, (((1,), (1,)), ((), ())), preferred_element_type=jnp.float32
    )


def split_rows(rows):
    return (rows // 32) * 16


def ring_ids(size):
    return list(range(0, size, 2)) + [i for i in range(size - 1, 0, -1) if i % 2]


def ring_perms(size):
    ids = ring_ids(size)
    forward = [(ids[i], ids[(i + 1) % size]) for i in range(size)]
    return forward, [(b, a) for a, b in forward]


def ring_owners(size):
    ids = ring_ids(size)
    table = np.zeros((size, 4, size), np.int32)
    for place, device in enumerate(ids):
        for step in range(size):
            table[device, 0, step] = ids[(place - step) % size]
            table[device, 1, step] = ids[(place + step) % size]
            table[device, 2, step] = ids[(place - 1 - step) % size]
            table[device, 3, step] = ids[(place + 1 + step) % size]
    return lax.dynamic_index_in_dim(
        jnp.asarray(table), lax.axis_index("fsdp").astype(jnp.uint32), 0, keepdims=False
    )


def after(value, *needed):
    return lax.optimization_barrier((value, *needed))[0] if needed else value


class GatherRing:
    def __init__(self, ahead, behind, size):
        self.perms = ring_perms(size)
        self.ahead, self.behind = [ahead], [behind]

    def step(self, first=(), last=()):
        forward, backward = self.perms
        ahead = lax.ppermute(after(self.ahead[-1], *first), "fsdp", forward)
        behind = lax.ppermute(after(self.behind[-1], *first), "fsdp", backward)
        self.ahead.append(after(ahead, *last))
        self.behind.append(after(behind, *last))


class ScatterRing:
    def __init__(self, way, blocks, size, owners, rows=None):
        self.perm = ring_perms(size)[way]
        self.owners = lax.squeeze(lax.slice_in_dim(owners, 2 + way, 3 + way), (0,)).astype(
            jnp.uint32
        )
        self.blocks, self.count = blocks, 0
        self.first, self.last = rows or (0, blocks.shape[1])
        self.sum = self.own().astype(jnp.bfloat16)

    def own(self):
        owner = lax.squeeze(lax.slice_in_dim(self.owners, self.count, self.count + 1), (0,))
        zero = jnp.uint32(0)
        shape = (1, self.last - self.first, self.blocks.shape[2])
        start = (owner, jnp.uint32(self.first), zero)
        return lax.dynamic_slice(self.blocks, start, shape)[0].astype(jnp.float32)

    def step(self, *needed):
        came = after(lax.ppermute(self.sum, "fsdp", self.perm), *needed)
        self.count += 1
        self.sum = (came.astype(jnp.float32) + self.own()).astype(jnp.bfloat16)
        return self.sum


def exchange(values, mask):
    return lax.ppermute(values, "seq", [(i, i ^ mask) for i in range(4)])


def gather_seq(block, *needed):
    block = after(block, *needed)
    other = exchange(block, 2)
    return [block, other, exchange(block, 1), exchange(other, 1)]


def in_order(pieces, seq_index):
    high, low = seq_index // 2, seq_index % 2

    def pick(first, second, flag):
        return jnp.where(flag == 0, first, second), jnp.where(flag == 0, second, first)

    mine = pick(pieces[0], pieces[1], high)
    theirs = pick(pieces[2], pieces[3], high)
    return [*pick(mine[0], theirs[0], low), *pick(mine[1], theirs[1], low)]


def scatter_seq(own, other, there):
    rows = own.shape[0]
    came = exchange(there, 1).astype(jnp.float32)
    sent = (other.astype(jnp.float32) + came[rows:]).astype(jnp.bfloat16)
    near = own.astype(jnp.float32) + came[:rows]
    return near + exchange(sent, 2).astype(jnp.float32), sent


def swap(blocks):
    return lax.all_to_all(blocks, "seq", split_axis=0, concat_axis=0, tiled=True)


def side_by_side(blocks):
    return blocks.transpose(1, 0, 2).reshape(blocks.shape[1], -1)


def apart(values):
    return values.reshape(values.shape[0], 4, -1).transpose(1, 0, 2)


def body(
    tokens,
    norm_gain,
    query_weight,
    key_weight,
    value_weight,
    query_gain,
    key_gain,
    out_weight,
    ffn_gain,
    gate_weight,
    up_weight,
    down_weight,
    cotangent,
):
    bf16, f32 = jnp.bfloat16, jnp.float32
    size = lax.axis_size("fsdp")
    seq_index = lax.axis_index("seq")
    owners = ring_owners(size)
    own_rows, width = query_weight.shape
    head_part = query_gain.shape[0]
    head_width = head_part * size
    query_columns = width // 4
    key_columns = key_weight.shape[1] // 4
    ff_part = down_weight.shape[0]
    window = -(-ff_part // 64) * 16

    def columns_of(weight, count):
        return lax.dynamic_slice_in_dim(weight, seq_index.astype(jnp.uint32) * count, count, 1)

    def hidden_rows(weight):
        tall = jnp.pad(weight, ((0, 4 * window - ff_part), (0, 0)))
        return lax.dynamic_slice_in_dim(tall, seq_index.astype(jnp.uint32) * window, window, 0)

    gains = jnp.concatenate([norm_gain, ffn_gain, query_gain, key_gain])
    gain_count = gains.shape[0]
    qkv_columns = query_columns + 2 * key_columns
    packed_columns = qkv_columns + query_columns
    gain_rows = jnp.pad(gains[None], ((0, 15), (0, packed_columns - gain_count)))
    packed = jnp.concatenate(
        [
            columns_of(query_weight, query_columns),
            columns_of(key_weight, key_columns),
            columns_of(value_weight, key_columns),
            columns_of(out_weight, query_columns),
        ],
        axis=1,
    )
    top = split_rows(own_rows + 16)
    first_ring = GatherRing(
        packed[:top], jnp.concatenate([packed[top:], gain_rows], axis=0), size
    )
    for _ in range(size - 1):
        first_ring.step()
    ffn_ring = GatherRing(
        *pick_hidden(gate_weight, up_weight, seq_index, size, ff_part, window), size
    )
    down_rows = hidden_rows(down_weight)
    def advance(rings, *needed):
        for way in rings:
            if way.count < size - 1:
                way.step(*needed)

    for step in range(1, size):
        ffn_ring.step((first_ring.ahead[2],) if step == 1 else ())
    down_ring = GatherRing(down_rows[: window // 2], down_rows[window // 2 :], size)
    for step in range(1, size - 2):
        lag = min(step + 2, size - 1)
        down_ring.step((ffn_ring.ahead[lag], ffn_ring.behind[lag]))

    qkv_all, out_part, gains_all = lay_attention(
        first_ring.ahead, first_ring.behind, owners, own_rows, qkv_columns
    )
    gains_all = gains_all[:, 0].astype(f32)
    first_gain = gains_all[:, :own_rows].reshape(-1)
    second_gain = gains_all[:, own_rows : 2 * own_rows].reshape(-1)
    q_gain_f = gains_all[:, 2 * own_rows : 2 * own_rows + head_part].reshape(-1)
    k_gain_f = gains_all[:, 2 * own_rows + head_part : 2 * (own_rows + head_part)].reshape(-1)

    inputs = tokens[0]
    tok_rows = inputs.shape[0]
    length = 4 * tok_rows
    input_blocks = gather_seq(inputs)
    inputs_all = jnp.concatenate(in_order(input_blocks, seq_index), axis=0).astype(f32)
    out_grad = cotangent[0]
    grad_blocks = gather_seq(out_grad, input_blocks[1])
    out_grad_all = jnp.concatenate(grad_blocks, axis=0)


    out_other = exchange(after(out_part, input_blocks[1]), 2)
    normed, _, _ = norm_forward(inputs_all, first_gain)
    normed_low = after(normed.astype(bf16), grad_blocks[1])
    qkv_t = lax.dot_general(
        qkv_all, normed_low, (((0,), (1,)), ((), ())), preferred_element_type=f32
    )
    sizes = (query_columns // head_width, key_columns // head_width, head_width)
    cosine, sine = rope_rows(length, head_width)
    tables = (q_gain_f[:, None], k_gain_f[:, None], cosine, sine)
    mixed_heads, mixed_t, totals = attention_forward(qkv_t, *tables, sizes)
    mixed = side_by_side(swap(mixed_heads.reshape(4, tok_rows, query_columns)))
    out_other = after(out_other, mixed_heads)
    out_blocks = [out_part, out_other, exchange(out_part, 1), exchange(out_other, 1)]
    out_all = jnp.concatenate(in_order(out_blocks, seq_index), axis=1)
    attended = jnp.dot(mixed, out_all, preferred_element_type=f32)
    middle = inputs.astype(f32) + attended
    normed_two, middle_unit, middle_inverse = norm_forward(middle, second_gain)
    normed_two_low = normed_two.astype(bf16)
    normed_blocks = gather_seq(normed_two_low)
    normed_two_all = jnp.concatenate(normed_blocks, axis=0)
    mixed_other = exchange(after(mixed_heads, normed_blocks[1]), 2)

    slope, silu, hidden, gate_all, up_all = ffn_hidden(
        [after(normed_blocks[0], down_ring.ahead[-1], down_ring.behind[-1]), *normed_blocks[1:]],
        ffn_ring.ahead,
        ffn_ring.behind,
        owners,
    )
    down_ring.step((), (hidden,))
    hidden = after(hidden, down_ring.ahead[-1], down_ring.behind[-1])
    down_ring.step()
    down_weight_grad = transpose_dot(hidden, out_grad_all).astype(bf16)
    down_blocks = after(
        down_weight_grad, down_ring.ahead[-1], down_ring.behind[-1]
    ).reshape(size, window, width)
    down_sums = (ScatterRing(0, down_blocks, size, owners),)
    gate_grad, up_grad, down_all = ffn_hidden_grad(
        after(out_grad_all, *(way.sum for way in down_sums)),
        slope,
        silu,
        down_ring.ahead,
        down_ring.behind,
        owners,
    )
    advance(down_sums, gate_grad)
    gate_weight_grad = transpose_dot(after(normed_two_all, down_sums[0].sum), gate_grad).astype(bf16)
    gate_sums = ScatterRing(
        0, gate_weight_grad.reshape(size, own_rows, size * window), size, owners
    )
    up_weight_grad = transpose_dot(after(normed_two_all, gate_sums.sum), up_grad).astype(bf16)
    up_sums = ScatterRing(1, up_weight_grad.reshape(size, own_rows, size * window), size, owners)
    ffn_sums = (gate_sums, up_sums)
    normed_parts = ffn_rows_grad(
        after(gate_grad, up_sums.sum, mixed_other), up_grad, gate_all, up_all
    )
    mixed_blocks = [mixed_heads, mixed_other, exchange(mixed_heads, 1), exchange(mixed_other, 1)]
    mixed_all = jnp.concatenate(in_order(mixed_blocks, seq_index), axis=1)
    advance(ffn_sums, normed_parts[0])
    normed_two_grad, half_sum = scatter_seq(
        *normed_parts[:2], after(normed_parts[2], gate_sums.sum)
    )
    advance(ffn_sums, normed_two_grad)
    ffn_gain_grad = jnp.sum(normed_two_grad * middle_unit, axis=0)
    middle_grad = out_grad.astype(f32) + norm_backward(
        normed_two_grad, middle_unit, middle_inverse, second_gain
    )
    attended_low = middle_grad.astype(bf16)
    mixed_grad = dot_transposed(attended_low, out_all).astype(bf16)
    advance(ffn_sums, mixed_grad)
    down_sums[0].sum = after(down_sums[0].sum, mixed_grad)
    mixed_grad_heads = after(swap(apart(mixed_grad)), gate_sums.sum, up_sums.sum).reshape(
        length, query_columns
    )
    qkv_grad, head_gains = attention_backward(
        qkv_t, *tables, mixed_t, totals, mixed_grad_heads, sizes
    )
    attended_columns = after(
        swap(apart(after(attended_low, mixed_grad_heads))), qkv_grad
    ).reshape(length, query_columns)
    out_weight_grad = by_rows(transpose_dot(mixed_all, attended_columns).astype(bf16))
    advance(ffn_sums, qkv_grad)
    advance(down_sums, qkv_grad)
    qkv_grad = after(qkv_grad, gate_sums.sum, up_sums.sum)
    head_gains = jnp.sum(head_gains, axis=1)
    query_gain_grad, key_gain_grad = head_gains[:head_width], head_gains[head_width:]
    qkv_weight_grad = transpose_dot(normed_low, qkv_grad)
    norm_gain_grad = jnp.sum(qkv_weight_grad * qkv_all.astype(f32), axis=1) / first_gain
    qkv_weight_grad = by_rows(qkv_weight_grad.astype(bf16))
    normed_partial = dot_transposed(qkv_grad, qkv_all)
    partial_blocks = normed_partial.astype(bf16).reshape(4, tok_rows, width)

    def partial_of(mask):
        index = (seq_index ^ mask).astype(jnp.uint32)
        return lax.dynamic_index_in_dim(partial_blocks, index, 0, keepdims=False)

    normed_grad, normed_sent = scatter_seq(
        partial_of(0),
        partial_of(2),
        jnp.concatenate([partial_of(1), partial_of(3)], axis=0),
    )
    _, own_unit, own_inverse = norm_forward(inputs.astype(f32), first_gain)
    inputs_grad = middle_grad + norm_backward(normed_grad, own_unit, own_inverse, first_gain)

    gain_grads = jnp.concatenate(
        [
            norm_gain_grad.reshape(size, -1),
            ffn_gain_grad.reshape(size, -1),
            query_gain_grad.reshape(size, -1),
            key_gain_grad.reshape(size, -1),
        ],
        axis=1,
    )
    gain_blocks = jnp.pad(
        gain_grads[:, None], ((0, 0), (0, 15), (0, packed_columns - gain_count))
    )
    packed_blocks = jnp.concatenate([qkv_weight_grad, out_weight_grad], axis=1).reshape(
        size, own_rows, packed_columns
    )
    packed_blocks = jnp.concatenate([packed_blocks, gain_blocks.astype(bf16)], axis=1)
    last_sums = (ScatterRing(1, packed_blocks, size, owners),)
    advance(ffn_sums, last_sums[0].sum, normed_sent)
    down_partial = jnp.dot(
        after(hidden, gate_sums.sum), down_all, preferred_element_type=f32
    ).astype(bf16)
    down_sum, down_sent = scatter_seq(
        down_partial[:tok_rows],
        down_partial[tok_rows : 2 * tok_rows],
        down_partial[2 * tok_rows :],
    )
    advance(down_sums, gate_sums.sum)
    advance(last_sums, gate_sums.sum, up_sums.sum)
    pins = [(down_sum,), (normed_grad, down_sent)]
    while gate_sums.count < size - 1:
        advance(ffn_sums, last_sums[0].sum, *(pins.pop() if pins else ()))
        advance(down_sums, gate_sums.sum, up_sums.sum)
        advance(last_sums, gate_sums.sum, up_sums.sum)
    both = jnp.stack([gate_sums.sum, up_sums.sum])
    ffn_blocks = gather_seq(both)
    pins = [(both,), (both,)]
    while last_sums[0].count < size - 1 or down_sums[0].count < size - 1:
        needed = pins.pop(0) if pins else ()
        advance(down_sums, *needed)
        advance(last_sums, *needed)
    down_pieces = gather_seq(down_sums[0].sum)
    packed_share = last_sums[0].sum
    output = middle + down_sum
    down_full = jnp.concatenate(in_order(down_pieces, seq_index), axis=0)[
        :ff_part
    ].astype(f32)
    gate_full, up_full = (
        spread_hidden(ffn_blocks, which, seq_index, size, ff_part, window) for which in range(2)
    )
    packs = [
        after(piece, gate_full, up_full)
        for piece in in_order(gather_seq(packed_share), seq_index)
    ]

    def unpack(first, count):
        return jnp.concatenate(
            [p[:own_rows, first : first + count] for p in packs], axis=1
        ).astype(f32)

    gain_sum = sum(p[own_rows, :gain_count].astype(f32) for p in packs)
    return (
        output[None].astype(bf16),
        inputs_grad[None].astype(bf16),
        gain_sum[:own_rows],
        unpack(0, query_columns),
        unpack(query_columns, key_columns),
        unpack(query_columns + key_columns, key_columns),
        gain_sum[2 * own_rows : 2 * own_rows + head_part],
        gain_sum[2 * own_rows + head_part :],
        unpack(qkv_columns, query_columns),
        gain_sum[own_rows : 2 * own_rows],
        gate_full,
        up_full,
        down_full,
    )


def solution(mesh):
    in_specs = (
        P("fsdp", "seq", None),
        P("fsdp"),
        P("fsdp", None),
        P("fsdp", None),
        P("fsdp", None),
        P("fsdp"),
        P("fsdp"),
        P("fsdp", None),
        P("fsdp"),
        P("fsdp", None),
        P("fsdp", None),
        P("fsdp", None),
        P("fsdp", "seq", None),
    )
    out_specs = (
        P("fsdp", "seq", None),
        P("fsdp", "seq", None),
        P("fsdp"),
        P("fsdp", None),
        P("fsdp", None),
        P("fsdp", None),
        P("fsdp"),
        P("fsdp"),
        P("fsdp", None),
        P("fsdp"),
        P("fsdp", None),
        P("fsdp", None),
        P("fsdp", None),
    )
    return jax.shard_map(body, mesh=mesh, in_specs=in_specs, out_specs=out_specs, check_vma=False)
```

```python
import functools
import math

import jax
import jax.numpy as jnp
import numpy as np
from jax import lax
from jax.experimental import pallas as pl
from jax.experimental.layout import Layout, with_layout_constraint
from jax.experimental.pallas import tpu as pltpu
from jax.sharding import PartitionSpec as P

norm_epsilon = 1e-05
TILE = 256
log2_e = math.log2(math.e)


def rope_rows(length, width):
    half_width = width // 2
    inverse = jnp.exp(
        jnp.arange(half_width, dtype=jnp.float32) * (-2.0 * math.log(1000000.0) / width)
    )
    angles = inverse[:, None] * jnp.arange(length, dtype=jnp.int32).astype(jnp.float32)[None, :]
    return jnp.cos(angles), jnp.sin(angles)


def head_norm(values):
    inverse = lax.rsqrt(jnp.mean(values * values, axis=0, keepdims=True) + norm_epsilon)
    return values * inverse, inverse


def head_turn(values, cosine, sine):
    half = values.shape[0] // 2
    first, second = values[:half], values[half:]
    return jnp.concatenate(
        [first * cosine - second * sine, second * cosine + first * sine], axis=0
    )


def head_turn_back(values, cosine, sine):
    half = values.shape[0] // 2
    first, second = values[:half], values[half:]
    return jnp.concatenate(
        [first * cosine + second * sine, second * cosine - first * sine], axis=0
    )


def fill_heads(qkv_ref, q_gain_ref, k_gain_ref, cos_ref, sin_ref, queries, keys, keys_t, values, values_t, sizes):
    heads, groups, width = sizes
    cosine, sine = cos_ref[...], sin_ref[...]

    @pl.loop(0, heads)
    def _(head):
        unit, _ = head_norm(qkv_ref[pl.ds(head * width, width), :])
        turned = head_turn(unit * q_gain_ref[...], cosine, sine)
        queries[head] = (turned * (width**-0.5 * log2_e)).astype(jnp.bfloat16)

    @pl.loop(0, groups)
    def _(group):
        unit, _ = head_norm(qkv_ref[pl.ds((heads + group) * width, width), :])
        turned = head_turn(unit * k_gain_ref[...], cosine, sine)
        keys[group] = turned.T.astype(jnp.bfloat16)
        if keys_t is not None:
            keys_t[group] = turned.astype(jnp.bfloat16)
        value = qkv_ref[pl.ds((heads + groups + group) * width, width), :]
        if values is not None:
            values[group] = value.T.astype(jnp.bfloat16)
        if values_t is not None:
            values_t[group] = value.astype(jnp.bfloat16)


def diagonal_mask():
    key_place = lax.broadcasted_iota(jnp.int32, (TILE, TILE), 0)
    query_place = lax.broadcasted_iota(jnp.int32, (TILE, TILE), 1)
    return key_place <= query_place


def causal_exp(scores, count):
    weights = jnp.exp2(scores)
    last = jnp.where(diagonal_mask(), weights[count - TILE :], 0.0)
    if count == TILE:
        return last
    return jnp.concatenate([weights[: count - TILE], last], axis=0)


def dot(left, right):
    return jnp.dot(left, right, preferred_element_type=jnp.float32)


def dot_nt(left, right):
    return lax.dot_general(
        left, right, (((1,), (1,)), ((), ())), preferred_element_type=jnp.float32
    )


def forward_kernel(sizes, qkv_ref, q_gain_ref, k_gain_ref, cos_ref, sin_ref, mixed_ref, mixed_t_ref, total_ref, queries, keys, values_t, mixed_f):
    heads, groups, width = sizes
    ratio = heads // groups
    length = qkv_ref.shape[1]
    fill_heads(qkv_ref, q_gain_ref, k_gain_ref, cos_ref, sin_ref, queries, keys, None, None, values_t, sizes)

    @pl.loop(0, heads)
    def _(head):
        group = head // ratio
        for tile in range(length // TILE):
            count = (tile + 1) * TILE
            columns = pl.ds(tile * TILE, TILE)
            scores = dot(keys[group, pl.ds(0, count), :], queries[head, :, columns])
            weights = causal_exp(scores, count)
            total = jnp.sum(weights, axis=0, keepdims=True)
            result = dot(values_t[group, :, pl.ds(0, count)], weights.astype(jnp.bfloat16))
            mixed_f[pl.ds(head * width, width), columns] = result * (1.0 / total)
            total_ref[pl.ds(head, 1), columns] = jnp.log2(total)

    for block in range(heads * width // 128):
        rows = mixed_f[pl.ds(block * 128, 128), :]
        mixed_t_ref[pl.ds(block * 128, 128), :] = rows.astype(jnp.bfloat16)
        mixed_ref[:, pl.ds(block * 128, 128)] = rows.T.astype(jnp.bfloat16)


def backward_kernel(sizes, qkv_ref, q_gain_ref, k_gain_ref, cos_ref, sin_ref, mixed_t_ref, total_ref, grad_ref, out_ref, gain_ref, out_t, queries, keys, keys_t, values, grads, key_sum, value_sum):
    heads, groups, width = sizes
    ratio = heads // groups
    length = qkv_ref.shape[1]
    fill_heads(qkv_ref, q_gain_ref, k_gain_ref, cos_ref, sin_ref, queries, keys, keys_t, values, None, sizes)
    for block in range(heads * width // 128):
        turned = grad_ref[:, pl.ds(block * 128, 128)].astype(jnp.float32).T
        grads[pl.ds(block * 128, 128), :] = turned.astype(jnp.bfloat16)
    key_sum[...] = jnp.zeros_like(key_sum)
    value_sum[...] = jnp.zeros_like(value_sum)
    gain_ref[...] = jnp.zeros_like(gain_ref)
    cosine, sine = cos_ref[...], sin_ref[...]

    def finish(grad_turned, rows, gain, first):
        grad = head_turn_back(grad_turned, cosine, sine)
        unit, inverse = head_norm(qkv_ref[rows, :])
        product = grad * unit
        part = product[:, :128]
        for lane in range(128, length, 128):
            part = part + product[:, lane : lane + 128]
        gain_ref[pl.ds(first, width), :] += part
        scaled = grad * gain
        before = inverse * (scaled - unit * jnp.mean(scaled * unit, axis=0, keepdims=True))
        out_t[rows, :] = before

    @pl.loop(0, heads)
    def _(head):
        group = head // ratio
        rows = pl.ds(head * width, width)
        query_parts = []
        for tile in range(length // TILE):
            count = (tile + 1) * TILE
            columns = pl.ds(tile * TILE, TILE)
            query = queries[head, :, columns]
            grad = grads[rows, columns]
            scores = dot(keys[group, pl.ds(0, count), :], query) - total_ref[pl.ds(head, 1), columns]
            weights = causal_exp(scores, count)
            inner = jnp.sum(
                grad.astype(jnp.float32) * mixed_t_ref[rows, columns].astype(jnp.float32),
                axis=0,
                keepdims=True,
            )
            weight_grad = dot(values[group, pl.ds(0, count), :], grad)
            score_grad = (weights * (weight_grad - inner)).astype(jnp.bfloat16)
            query_parts.append(dot(keys_t[group, :, pl.ds(0, count)], score_grad))
            key_sum[group, pl.ds(0, count), :] += dot_nt(score_grad, query)
            value_sum[group, pl.ds(0, count), :] += dot_nt(weights.astype(jnp.bfloat16), grad)
        query_grad = jnp.concatenate(query_parts, axis=1) * width**-0.5
        finish(query_grad, rows, q_gain_ref[...], 0)

    for group in range(groups):
        key_grad = key_sum[group].T * (1.0 / log2_e)
        finish(key_grad, pl.ds((heads + group) * width, width), k_gain_ref[...], width)
        out_t[pl.ds((heads + groups + group) * width, width), :] = value_sum[group].T

    for block in range(out_t.shape[0] // 128):
        some = pl.ds(block * 128, 128)
        out_ref[:, some] = out_t[some, :].T.astype(jnp.bfloat16)


def attention_forward(qkv_t, q_gain, k_gain, cosine, sine, sizes):
    heads, groups, width = sizes
    length = qkv_t.shape[1]
    bf16, f32 = jnp.bfloat16, jnp.float32
    pairs = heads * length * length
    return pl.pallas_call(
        functools.partial(forward_kernel, sizes),
        out_shape=(
            jax.ShapeDtypeStruct((length, heads * width), bf16),
            jax.ShapeDtypeStruct((heads * width, length), bf16),
            jax.ShapeDtypeStruct((-(-heads // 8) * 8, length), f32),
        ),
        scratch_shapes=[
            pltpu.VMEM((heads, width, length), bf16),
            pltpu.VMEM((groups, length, width), bf16),
            pltpu.VMEM((groups, width, length), bf16),
            pltpu.VMEM((heads * width, length), f32),
        ],
        compiler_params=pltpu.CompilerParams(vmem_limit_bytes=32 * 2**20),
        cost_estimate=pl.CostEstimate(
            flops=8 * pairs * width, bytes_accessed=6 * 2**20, transcendentals=pairs
        ),
    )(qkv_t, q_gain, k_gain, cosine, sine)


def attention_backward(qkv_t, q_gain, k_gain, cosine, sine, mixed_t, total, mixed_grad, sizes):
    heads, groups, width = sizes
    length = qkv_t.shape[1]
    bf16, f32 = jnp.bfloat16, jnp.float32
    pairs = heads * length * length
    return pl.pallas_call(
        functools.partial(backward_kernel, sizes),
        out_shape=(
            jax.ShapeDtypeStruct(qkv_t.shape[::-1], bf16),
            jax.ShapeDtypeStruct((2 * width, 128), f32),
        ),
        scratch_shapes=[
            pltpu.VMEM(qkv_t.shape, f32),
            pltpu.VMEM((heads, width, length), bf16),
            pltpu.VMEM((groups, length, width), bf16),
            pltpu.VMEM((groups, width, length), bf16),
            pltpu.VMEM((groups, length, width), bf16),
            pltpu.VMEM((heads * width, length), bf16),
            pltpu.VMEM((groups, length, width), f32),
            pltpu.VMEM((groups, length, width), f32),
        ],
        compiler_params=pltpu.CompilerParams(vmem_limit_bytes=40 * 2**20),
        cost_estimate=pl.CostEstimate(flops=0, bytes_accessed=2**20, transcendentals=0),
    )(qkv_t, q_gain, k_gain, cosine, sine, mixed_t, total, mixed_grad)


def hidden_kernel(size, ids_ref, *refs):
    pieces, chunks, refs = refs[:4], refs[4 : 4 + 2 * size], refs[4 + 2 * size :]
    slope_ref, silu_ref, hidden_ref, gate_out, up_out, tokens, gate, up, *sems = refs
    row_sems, in_sems, out_sems = sems
    step = pl.program_id(0)
    steps = pl.num_programs(0)
    rows = chunks[0].shape[0]
    piece = pieces[0].shape[0]

    @pl.when(step == 0)
    def _():
        copies = [
            pltpu.make_async_copy(
                source, tokens.at[pl.ds(index * piece, piece), :], row_sems.at[index]
            )
            for index, source in enumerate(pieces)
        ]
        for copy in copies:
            copy.start()

        @pl.loop(0, steps)
        def _(tile):
            columns = pl.ds(pl.multiple_of(tile * TILE, TILE), TILE)
            for which, target in ((0, gate), (1, up)):
                for index in range(size):
                    first = pl.multiple_of(ids_ref[which, index] * rows, 16)
                    pltpu.make_async_copy(
                        chunks[which * size + index].at[:, columns],
                        target.at[pl.ds(first, rows), columns],
                        in_sems.at[which, tile],
                    ).start()

        for copy in copies:
            copy.wait()

    columns = pl.ds(pl.multiple_of(step * TILE, TILE), TILE)
    for which, target, result in ((0, gate, gate_out), (1, up, up_out)):
        part = target.at[:, columns]
        pltpu.make_async_copy(part, part, in_sems.at[which, step]).wait()
        pltpu.make_async_copy(part, result.at[:, columns], out_sems.at[which, step]).start()
    for half in range(2):
        some = pl.ds(half * 2 * piece, 2 * piece)
        gate_act = dot(tokens[some, :], gate[:, columns])
        up_act = dot(tokens[some, :], up[:, columns])
        sigmoid = 0.5 + 0.5 * jnp.tanh(0.5 * gate_act)
        silu = gate_act * sigmoid
        hidden_ref[some, :] = (silu * up_act).astype(hidden_ref.dtype)
        silu_ref[some, :] = silu.astype(silu_ref.dtype)
        slope_ref[some, :] = (up_act * sigmoid * (1.0 + gate_act * (1.0 - sigmoid))).astype(
            slope_ref.dtype
        )

    @pl.when(step == steps - 1)
    def _():
        @pl.loop(0, steps)
        def _(tile):
            columns = pl.ds(pl.multiple_of(tile * TILE, TILE), TILE)
            for which, target, result in ((0, gate, gate_out), (1, up, up_out)):
                pltpu.make_async_copy(
                    target.at[:, columns], result.at[:, columns], out_sems.at[which, tile]
                ).wait()


def ffn_hidden(pieces, gate_chunks, up_chunks, ids):
    size = len(gate_chunks)
    part, columns = gate_chunks[0].shape
    piece, width = pieces[0].shape
    length = 4 * piece
    bf16 = jnp.bfloat16
    tall = pl.BlockSpec((length, TILE), lambda i, ids: (0, i))
    act = jax.ShapeDtypeStruct((length, columns), bf16)
    weight = jax.ShapeDtypeStruct((width, columns), bf16)
    anywhere = pl.BlockSpec(memory_space=pl.ANY)
    return pl.pallas_call(
        functools.partial(hidden_kernel, size),
        grid_spec=pltpu.PrefetchScalarGridSpec(
            num_scalar_prefetch=1,
            grid=(columns // TILE,),
            in_specs=[anywhere] * (4 + 2 * size),
            out_specs=[tall, tall, tall, anywhere, anywhere],
            scratch_shapes=[
                pltpu.VMEM((length, width), bf16),
                pltpu.VMEM((width, columns), bf16),
                pltpu.VMEM((width, columns), bf16),
                pltpu.SemaphoreType.DMA((4,)),
                pltpu.SemaphoreType.DMA((2, columns // TILE)),
                pltpu.SemaphoreType.DMA((2, columns // TILE)),
            ],
        ),
        out_shape=(act, act, act, weight, weight),
        compiler_params=pltpu.CompilerParams(vmem_limit_bytes=56 * 2**20),
        cost_estimate=pl.CostEstimate(
            flops=4 * length * width * columns,
            bytes_accessed=36 * 2**20,
            transcendentals=length * columns,
        ),
    )(ids, *pieces, *gate_chunks, *up_chunks)


def hidden_grad_kernel(size, owners_ref, grad_ref, slope_ref, silu_ref, *refs):
    chunks, refs = refs[: 2 * size], refs[2 * size :]
    gate_out, up_out, down_out, down, in_sems, out_sem = refs
    step = pl.program_id(0)
    rows = chunks[0].shape[0]

    @pl.when(step == 0)
    def _():
        copies = []
        for which in range(2):
            for index in range(size):
                first = pl.multiple_of((2 * owners_ref[which, index] + which) * rows, 16)
                copies.append(
                    pltpu.make_async_copy(
                        chunks[which * size + index],
                        down.at[pl.ds(first, rows), :],
                        in_sems.at[which, index],
                    )
                )
        for copy in copies:
            copy.start()
        for copy in copies:
            copy.wait()
        pltpu.make_async_copy(down, down_out, out_sem).start()

    weight = down[pl.ds(pl.multiple_of(step * TILE, TILE), TILE), :]
    hidden_grad = dot_nt(grad_ref[...], weight)
    gate_out[...] = (hidden_grad * slope_ref[...].astype(jnp.float32)).astype(jnp.bfloat16)
    up_out[...] = (hidden_grad * silu_ref[...].astype(jnp.float32)).astype(jnp.bfloat16)

    @pl.when(step == pl.num_programs(0) - 1)
    def _():
        pltpu.make_async_copy(down, down_out, out_sem).wait()


def ffn_hidden_grad(out_grad, slope, silu, ahead, behind, owners):
    size = len(ahead)
    length, width = out_grad.shape
    columns = slope.shape[1]
    bf16 = jnp.bfloat16
    tall = pl.BlockSpec((length, TILE), lambda i, owners: (0, i))
    anywhere = pl.BlockSpec(memory_space=pl.ANY)
    act = jax.ShapeDtypeStruct((length, columns), bf16)
    weight = (2 * size * ahead[0].shape[0], width)
    return pl.pallas_call(
        functools.partial(hidden_grad_kernel, size),
        grid_spec=pltpu.PrefetchScalarGridSpec(
            num_scalar_prefetch=1,
            grid=(columns // TILE,),
            in_specs=[pl.BlockSpec((length, width), lambda i, owners: (0, 0)), tall, tall]
            + [anywhere] * (2 * size),
            out_specs=[tall, tall, anywhere],
            scratch_shapes=[
                pltpu.VMEM(weight, bf16),
                pltpu.SemaphoreType.DMA((2, size)),
                pltpu.SemaphoreType.DMA,
            ],
        ),
        out_shape=(act, act, jax.ShapeDtypeStruct(weight, bf16)),
        compiler_params=pltpu.CompilerParams(vmem_limit_bytes=56 * 2**20),
        cost_estimate=pl.CostEstimate(flops=0, bytes_accessed=2**20, transcendentals=0),
    )(owners, out_grad, slope, silu, *ahead, *behind)


def rows_grad_kernel(gate_grad_ref, up_grad_ref, gate_ref, up_ref, own_ref, other_ref, sent_ref):
    piece = own_ref.shape[0]
    total = dot_nt(gate_grad_ref[...], gate_ref[...]) + dot_nt(up_grad_ref[...], up_ref[...])
    total = total.astype(jnp.bfloat16)
    own_ref[...] = total[:piece]
    other_ref[...] = total[piece : 2 * piece]
    sent_ref[...] = total[2 * piece :]


def ffn_rows_grad(gate_grad, up_grad, gate, up):
    length, columns = gate_grad.shape
    width = gate.shape[0]
    piece = length // 4
    bf16 = jnp.bfloat16
    whole = pl.BlockSpec((length, columns), lambda i: (0, 0))
    weight = pl.BlockSpec((TILE, columns), lambda i: (i, 0))
    part = pl.BlockSpec((piece, TILE), lambda i: (0, i))
    return pl.pallas_call(
        rows_grad_kernel,
        grid=(width // TILE,),
        in_specs=[whole, whole, weight, weight],
        out_specs=[part, part, pl.BlockSpec((2 * piece, TILE), lambda i: (0, i))],
        out_shape=(
            jax.ShapeDtypeStruct((piece, width), bf16),
            jax.ShapeDtypeStruct((piece, width), bf16),
            jax.ShapeDtypeStruct((2 * piece, width), bf16),
        ),
        compiler_params=pltpu.CompilerParams(vmem_limit_bytes=56 * 2**20),
        cost_estimate=pl.CostEstimate(flops=0, bytes_accessed=2**20, transcendentals=0),
    )(gate_grad, up_grad, gate, up)


def lay_kernel(size, sizes, owners_ref, *refs):
    chunks, refs = refs[: 2 * size], refs[2 * size :]
    qkv_out, out_out, gains_out, sems = refs
    rows, top, qkv_columns, columns = sizes
    copies = []
    for which, count in ((0, top), (1, rows - top)):
        for index in range(size):
            chunk = chunks[which * size + index]
            owner = owners_ref[which, index]
            first = pl.multiple_of(owner * rows + which * top, 16)
            target = pl.ds(first, count)
            pairs = [
                (chunk.at[pl.ds(0, count), pl.ds(0, qkv_columns)], qkv_out.at[target, :]),
                (
                    chunk.at[pl.ds(0, count), pl.ds(qkv_columns, columns - qkv_columns)],
                    out_out.at[target, :],
                ),
            ]
            if which:
                pairs.append((chunk.at[pl.ds(count, 16), :], gains_out.at[owner]))
            for kind, (source, place) in enumerate(pairs):
                copies.append(pltpu.make_async_copy(source, place, sems.at[kind, which, index]))
    for copy in copies:
        copy.start()
    for copy in copies:
        copy.wait()


def lay_attention(ahead, behind, owners, rows, qkv_columns):
    size = len(ahead)
    top, columns = ahead[0].shape
    bf16 = jnp.bfloat16
    anywhere = pl.BlockSpec(memory_space=pl.ANY)
    return pl.pallas_call(
        functools.partial(lay_kernel, size, (rows, top, qkv_columns, columns)),
        grid_spec=pltpu.PrefetchScalarGridSpec(
            num_scalar_prefetch=1,
            grid=(1,),
            in_specs=[anywhere] * (2 * size),
            out_specs=[pl.BlockSpec(memory_space=pltpu.VMEM)] * 3,
            scratch_shapes=[pltpu.SemaphoreType.DMA((3, 2, size))],
        ),
        out_shape=(
            jax.ShapeDtypeStruct((size * rows, qkv_columns), bf16),
            jax.ShapeDtypeStruct((size * rows, columns - qkv_columns), bf16),
            jax.ShapeDtypeStruct((size, 16, columns), bf16),
        ),
        cost_estimate=pl.CostEstimate(flops=0, bytes_accessed=7 * 2**20, transcendentals=0),
    )(owners, *ahead, *behind)


def pick_kernel(sizes, index_ref, gate_ref, up_ref, gate_out, up_out):
    size, part, window = sizes
    rows = gate_ref.shape[0]
    for source, target in ((gate_ref, gate_out), (up_ref, up_out)):
        for index in range(4):
            count = min(window, part - index * window)

            @pl.when(index_ref[0] == index)
            def _():
                parts = []
                for owner in range(size):
                    first = owner * part + index * window
                    low, high = first // 128 * 128, -(-(first + count) // 128) * 128
                    wide = source[:, low:high].astype(jnp.float32)
                    parts.append(wide[:, first - low : first - low + count])
                    if count < window:
                        parts.append(jnp.zeros((rows, window - count), jnp.float32))
                target[...] = jnp.concatenate(parts, axis=1).astype(target.dtype)


def pick_hidden(gate, up, seq_index, size, part, window):
    rows, columns = gate.shape
    block = 48 if rows % 48 == 0 else rows
    wide = pl.BlockSpec((block, columns), lambda i, index: (i, 0))
    narrow = pl.BlockSpec((block, size * window), lambda i, index: (i, 0))
    out = jax.ShapeDtypeStruct((rows, size * window), gate.dtype)
    return pl.pallas_call(
        functools.partial(pick_kernel, (size, part, window)),
        grid_spec=pltpu.PrefetchScalarGridSpec(
            num_scalar_prefetch=1,
            grid=(rows // block,),
            in_specs=[wide, wide],
            out_specs=[narrow, narrow],
        ),
        out_shape=(out, out),
        compiler_params=pltpu.CompilerParams(vmem_limit_bytes=32 * 2**20),
        cost_estimate=pl.CostEstimate(flops=0, bytes_accessed=8 * 2**20, transcendentals=0),
    )(jnp.reshape(seq_index, (1,)).astype(jnp.int32), gate, up)


def spread_kernel(sizes, index_ref, own_ref, other_ref, near_ref, far_ref, out_ref, parts):
    size, part, window = sizes
    me = index_ref[0]
    parts[me] = own_ref[...]
    parts[me ^ 2] = other_ref[...]
    parts[me ^ 1] = near_ref[...]
    parts[me ^ 3] = far_ref[...]
    pieces = []
    for owner in range(size):
        for index in range(4):
            count = min(window, part - index * window)
            first = owner * window
            low, high = first // 128 * 128, -(-(first + count) // 128) * 128
            wide = parts[index, :, low:high].astype(jnp.float32)
            pieces.append(wide[:, first - low : first - low + count])
    out_ref[...] = jnp.concatenate(pieces, axis=1)


def spread_hidden(pieces, which, seq_index, size, part, window):
    _, rows, columns = pieces[0].shape
    block = 48 if rows % 48 == 0 else rows
    narrow = pl.BlockSpec((None, block, columns), lambda i, index: (which, i, 0))
    return pl.pallas_call(
        functools.partial(spread_kernel, (size, part, window)),
        grid_spec=pltpu.PrefetchScalarGridSpec(
            num_scalar_prefetch=1,
            grid=(rows // block,),
            in_specs=[narrow] * 4,
            out_specs=pl.BlockSpec((block, size * part), lambda i, index: (i, 0)),
            scratch_shapes=[pltpu.VMEM((4, block, columns), pieces[0].dtype)],
        ),
        out_shape=jax.ShapeDtypeStruct((rows, size * part), jnp.float32),
        compiler_params=pltpu.CompilerParams(vmem_limit_bytes=32 * 2**20),
        cost_estimate=pl.CostEstimate(flops=0, bytes_accessed=64 * 2**20, transcendentals=0),
    )(jnp.reshape(seq_index, (1,)), *pieces)


def norm_forward(values, gain):
    inverse = lax.rsqrt(jnp.mean(values * values, axis=-1, keepdims=True) + norm_epsilon)
    unit = values * inverse
    return (unit * gain, unit, inverse)


def norm_backward(grad_in, unit, inverse, gain):
    scaled = grad_in * gain
    return inverse * (scaled - unit * jnp.mean(scaled * unit, axis=-1, keepdims=True))


def transpose_dot(left, right):
    return lax.dot_general(
        left, right, (((0,), (0,)), ((), ())), preferred_element_type=jnp.float32
    )


def by_rows(values):
    return with_layout_constraint(values, Layout(major_to_minor=(0, 1)))


def dot_transposed(left, right):
    return lax.dot_general(
        left, right, (((1,), (1,)), ((), ())), preferred_element_type=jnp.float32
    )


def split_rows(rows):
    return (rows // 32) * 16


def ring_ids(size):
    return list(range(0, size, 2)) + [i for i in range(size - 1, 0, -1) if i % 2]


def ring_perms(size):
    ids = ring_ids(size)
    forward = [(ids[i], ids[(i + 1) % size]) for i in range(size)]
    return forward, [(b, a) for a, b in forward]


def ring_owners(size):
    ids = ring_ids(size)
    table = np.zeros((size, 4, size), np.int32)
    for place, device in enumerate(ids):
        for step in range(size):
            table[device, 0, step] = ids[(place - step) % size]
            table[device, 1, step] = ids[(place + step) % size]
            table[device, 2, step] = ids[(place - 1 - step) % size]
            table[device, 3, step] = ids[(place + 1 + step) % size]
    return lax.dynamic_index_in_dim(
        jnp.asarray(table), lax.axis_index("fsdp").astype(jnp.uint32), 0, keepdims=False
    )


def after(value, *needed):
    return lax.optimization_barrier((value, *needed))[0] if needed else value


class GatherRing:
    def __init__(self, ahead, behind, size):
        self.perms = ring_perms(size)
        self.ahead, self.behind = [ahead], [behind]

    def step(self, first=(), last=()):
        forward, backward = self.perms
        ahead = lax.ppermute(after(self.ahead[-1], *first), "fsdp", forward)
        behind = lax.ppermute(after(self.behind[-1], *first), "fsdp", backward)
        self.ahead.append(after(ahead, *last))
        self.behind.append(after(behind, *last))


class ScatterRing:
    def __init__(self, way, blocks, size, owners, rows=None):
        self.perm = ring_perms(size)[way]
        self.owners = lax.squeeze(lax.slice_in_dim(owners, 2 + way, 3 + way), (0,)).astype(
            jnp.uint32
        )
        self.blocks, self.count = blocks, 0
        self.first, self.last = rows or (0, blocks.shape[1])
        self.sum = self.own().astype(jnp.bfloat16)

    def own(self):
        owner = lax.squeeze(lax.slice_in_dim(self.owners, self.count, self.count + 1), (0,))
        zero = jnp.uint32(0)
        shape = (1, self.last - self.first, self.blocks.shape[2])
        start = (owner, jnp.uint32(self.first), zero)
        return lax.dynamic_slice(self.blocks, start, shape)[0].astype(jnp.float32)

    def step(self, *needed):
        came = after(lax.ppermute(self.sum, "fsdp", self.perm), *needed)
        self.count += 1
        self.sum = (came.astype(jnp.float32) + self.own()).astype(jnp.bfloat16)
        return self.sum


def exchange(values, mask):
    return lax.ppermute(values, "seq", [(i, i ^ mask) for i in range(4)])


def gather_seq(block, *needed):
    block = after(block, *needed)
    other = exchange(block, 2)
    return [block, other, exchange(block, 1), exchange(other, 1)]


def in_order(pieces, seq_index):
    high, low = seq_index // 2, seq_index % 2

    def pick(first, second, flag):
        return jnp.where(flag == 0, first, second), jnp.where(flag == 0, second, first)

    mine = pick(pieces[0], pieces[1], high)
    theirs = pick(pieces[2], pieces[3], high)
    return [*pick(mine[0], theirs[0], low), *pick(mine[1], theirs[1], low)]


def scatter_seq(own, other, there):
    rows = own.shape[0]
    came = exchange(there, 1).astype(jnp.float32)
    sent = (other.astype(jnp.float32) + came[rows:]).astype(jnp.bfloat16)
    near = own.astype(jnp.float32) + came[:rows]
    return near + exchange(sent, 2).astype(jnp.float32), sent


def swap(blocks):
    return lax.all_to_all(blocks, "seq", split_axis=0, concat_axis=0, tiled=True)


def side_by_side(blocks):
    return blocks.transpose(1, 0, 2).reshape(blocks.shape[1], -1)


def apart(values):
    return values.reshape(values.shape[0], 4, -1).transpose(1, 0, 2)


def body(
    tokens,
    norm_gain,
    query_weight,
    key_weight,
    value_weight,
    query_gain,
    key_gain,
    out_weight,
    ffn_gain,
    gate_weight,
    up_weight,
    down_weight,
    cotangent,
):
    bf16, f32 = jnp.bfloat16, jnp.float32
    size = lax.axis_size("fsdp")
    seq_index = lax.axis_index("seq")
    owners = ring_owners(size)
    own_rows, width = query_weight.shape
    head_part = query_gain.shape[0]
    head_width = head_part * size
    query_columns = width // 4
    key_columns = key_weight.shape[1] // 4
    ff_part = down_weight.shape[0]
    window = -(-ff_part // 64) * 16

    def columns_of(weight, count):
        return lax.dynamic_slice_in_dim(weight, seq_index.astype(jnp.uint32) * count, count, 1)

    def hidden_rows(weight):
        tall = jnp.pad(weight, ((0, 4 * window - ff_part), (0, 0)))
        return lax.dynamic_slice_in_dim(tall, seq_index.astype(jnp.uint32) * window, window, 0)

    gains = jnp.concatenate([norm_gain, ffn_gain, query_gain, key_gain])
    gain_count = gains.shape[0]
    qkv_columns = query_columns + 2 * key_columns
    packed_columns = qkv_columns + query_columns
    gain_rows = jnp.pad(gains[None], ((0, 15), (0, packed_columns - gain_count)))
    packed = jnp.concatenate(
        [
            columns_of(query_weight, query_columns),
            columns_of(key_weight, key_columns),
            columns_of(value_weight, key_columns),
            columns_of(out_weight, query_columns),
        ],
        axis=1,
    )
    top = split_rows(own_rows + 16)
    first_ring = GatherRing(
        packed[:top], jnp.concatenate([packed[top:], gain_rows], axis=0), size
    )
    for _ in range(size - 1):
        first_ring.step()
    ffn_ring = GatherRing(
        *pick_hidden(gate_weight, up_weight, seq_index, size, ff_part, window), size
    )
    down_rows = hidden_rows(down_weight)
    def advance(rings, *needed):
        for way in rings:
            if way.count < size - 1:
                way.step(*needed)

    for step in range(1, size):
        ffn_ring.step((first_ring.ahead[2],) if step == 1 else ())
    down_ring = GatherRing(down_rows[: window // 2], down_rows[window // 2 :], size)
    for step in range(1, size - 2):
        lag = min(step + 2, size - 1)
        down_ring.step((ffn_ring.ahead[lag], ffn_ring.behind[lag]))

    qkv_all, out_part, gains_all = lay_attention(
        first_ring.ahead, first_ring.behind, owners, own_rows, qkv_columns
    )
    gains_all = gains_all[:, 0].astype(f32)
    first_gain = gains_all[:, :own_rows].reshape(-1)
    second_gain = gains_all[:, own_rows : 2 * own_rows].reshape(-1)
    q_gain_f = gains_all[:, 2 * own_rows : 2 * own_rows + head_part].reshape(-1)
    k_gain_f = gains_all[:, 2 * own_rows + head_part : 2 * (own_rows + head_part)].reshape(-1)

    inputs = tokens[0]
    tok_rows = inputs.shape[0]
    length = 4 * tok_rows
    input_blocks = gather_seq(inputs)
    inputs_all = jnp.concatenate(in_order(input_blocks, seq_index), axis=0).astype(f32)
    out_grad = cotangent[0]
    grad_blocks = gather_seq(out_grad, input_blocks[1])
    out_grad_all = jnp.concatenate(grad_blocks, axis=0)


    out_other = exchange(after(out_part, input_blocks[1]), 2)
    normed, _, _ = norm_forward(inputs_all, first_gain)
    normed_low = after(normed.astype(bf16), grad_blocks[1])
    qkv_t = lax.dot_general(
        qkv_all, normed_low, (((0,), (1,)), ((), ())), preferred_element_type=f32
    )
    sizes = (query_columns // head_width, key_columns // head_width, head_width)
    cosine, sine = rope_rows(length, head_width)
    tables = (q_gain_f[:, None], k_gain_f[:, None], cosine, sine)
    mixed_heads, mixed_t, totals = attention_forward(qkv_t, *tables, sizes)
    mixed = side_by_side(swap(mixed_heads.reshape(4, tok_rows, query_columns)))
    out_other = after(out_other, mixed_heads)
    out_blocks = [out_part, out_other, exchange(out_part, 1), exchange(out_other, 1)]
    out_all = jnp.concatenate(in_order(out_blocks, seq_index), axis=1)
    attended = jnp.dot(mixed, out_all, preferred_element_type=f32)
    middle = inputs.astype(f32) + attended
    normed_two, middle_unit, middle_inverse = norm_forward(middle, second_gain)
    normed_two_low = normed_two.astype(bf16)
    normed_blocks = gather_seq(normed_two_low)
    normed_two_all = jnp.concatenate(normed_blocks, axis=0)
    mixed_other = exchange(after(mixed_heads, normed_blocks[1]), 2)

    slope, silu, hidden, gate_all, up_all = ffn_hidden(
        [after(normed_blocks[0], down_ring.ahead[-1], down_ring.behind[-1]), *normed_blocks[1:]],
        ffn_ring.ahead,
        ffn_ring.behind,
        owners,
    )
    down_ring.step((), (hidden,))
    hidden = after(hidden, down_ring.ahead[-1], down_ring.behind[-1])
    down_ring.step()
    down_weight_grad = transpose_dot(hidden, out_grad_all).astype(bf16)
    down_blocks = after(
        down_weight_grad, down_ring.ahead[-1], down_ring.behind[-1]
    ).reshape(size, window, width)
    down_sums = (ScatterRing(0, down_blocks, size, owners),)
    gate_grad, up_grad, down_all = ffn_hidden_grad(
        after(out_grad_all, *(way.sum for way in down_sums)),
        slope,
        silu,
        down_ring.ahead,
        down_ring.behind,
        owners,
    )
    advance(down_sums, gate_grad)
    gate_weight_grad = transpose_dot(after(normed_two_all, down_sums[0].sum), gate_grad).astype(bf16)
    gate_sums = ScatterRing(
        0, gate_weight_grad.reshape(size, own_rows, size * window), size, owners
    )
    up_weight_grad = transpose_dot(after(normed_two_all, gate_sums.sum), up_grad).astype(bf16)
    up_sums = ScatterRing(1, up_weight_grad.reshape(size, own_rows, size * window), size, owners)
    ffn_sums = (gate_sums, up_sums)
    advance(down_sums, up_sums.sum)
    normed_parts = ffn_rows_grad(
        after(gate_grad, up_sums.sum, mixed_other, down_sums[0].sum), up_grad, gate_all, up_all
    )
    mixed_blocks = [mixed_heads, mixed_other, exchange(mixed_heads, 1), exchange(mixed_other, 1)]
    mixed_all = jnp.concatenate(in_order(mixed_blocks, seq_index), axis=1)
    advance(ffn_sums, normed_parts[0])
    normed_two_grad, half_sum = scatter_seq(
        *normed_parts[:2], after(normed_parts[2], gate_sums.sum, up_sums.sum)
    )
    advance(ffn_sums, normed_two_grad)
    ffn_gain_grad = jnp.sum(normed_two_grad * middle_unit, axis=0)
    middle_grad = out_grad.astype(f32) + norm_backward(
        normed_two_grad, middle_unit, middle_inverse, second_gain
    )
    attended_low = middle_grad.astype(bf16)
    mixed_grad = dot_transposed(attended_low, out_all).astype(bf16)
    advance(ffn_sums, mixed_grad)
    down_sums[0].sum = after(down_sums[0].sum, mixed_grad)
    mixed_grad_heads = after(swap(apart(mixed_grad)), gate_sums.sum, up_sums.sum).reshape(
        length, query_columns
    )
    qkv_grad, head_gains = attention_backward(
        qkv_t, *tables, mixed_t, totals, mixed_grad_heads, sizes
    )
    attended_columns = after(
        swap(apart(after(attended_low, mixed_grad_heads))), qkv_grad
    ).reshape(length, query_columns)
    out_weight_grad = by_rows(transpose_dot(mixed_all, attended_columns).astype(bf16))
    advance(ffn_sums, qkv_grad)
    advance(down_sums, qkv_grad)
    qkv_grad = after(qkv_grad, gate_sums.sum, up_sums.sum)
    head_gains = jnp.sum(head_gains, axis=1)
    query_gain_grad, key_gain_grad = head_gains[:head_width], head_gains[head_width:]
    qkv_weight_grad = transpose_dot(normed_low, qkv_grad)
    norm_gain_grad = jnp.sum(qkv_weight_grad * qkv_all.astype(f32), axis=1) / first_gain
    qkv_weight_grad = by_rows(qkv_weight_grad.astype(bf16))
    normed_partial = dot_transposed(qkv_grad, qkv_all)
    partial_blocks = normed_partial.astype(bf16).reshape(4, tok_rows, width)

    def partial_of(mask):
        index = (seq_index ^ mask).astype(jnp.uint32)
        return lax.dynamic_index_in_dim(partial_blocks, index, 0, keepdims=False)

    normed_grad, normed_sent = scatter_seq(
        partial_of(0),
        partial_of(2),
        jnp.concatenate([partial_of(1), partial_of(3)], axis=0),
    )
    _, own_unit, own_inverse = norm_forward(inputs.astype(f32), first_gain)
    inputs_grad = middle_grad + norm_backward(normed_grad, own_unit, own_inverse, first_gain)

    gain_grads = jnp.concatenate(
        [
            norm_gain_grad.reshape(size, -1),
            ffn_gain_grad.reshape(size, -1),
            query_gain_grad.reshape(size, -1),
            key_gain_grad.reshape(size, -1),
        ],
        axis=1,
    )
    gain_blocks = jnp.pad(
        gain_grads[:, None], ((0, 0), (0, 15), (0, packed_columns - gain_count))
    )
    packed_blocks = jnp.concatenate([qkv_weight_grad, out_weight_grad], axis=1).reshape(
        size, own_rows, packed_columns
    )
    packed_blocks = jnp.concatenate([packed_blocks, gain_blocks.astype(bf16)], axis=1)
    last_sums = (ScatterRing(1, packed_blocks, size, owners),)
    advance(ffn_sums, last_sums[0].sum, normed_sent)
    down_partial = jnp.dot(
        after(hidden, gate_sums.sum), down_all, preferred_element_type=f32
    ).astype(bf16)
    down_sum, down_sent = scatter_seq(
        down_partial[:tok_rows],
        down_partial[tok_rows : 2 * tok_rows],
        down_partial[2 * tok_rows :],
    )
    advance(down_sums, gate_sums.sum)
    advance(last_sums, gate_sums.sum, up_sums.sum)
    pins = [(down_sum,), (normed_grad, down_sent)]
    while gate_sums.count < size - 1:
        advance(ffn_sums, last_sums[0].sum, *(pins.pop() if pins else ()))
        advance(down_sums, gate_sums.sum, up_sums.sum)
        advance(last_sums, gate_sums.sum, up_sums.sum)
    both = jnp.stack([gate_sums.sum, up_sums.sum])
    ffn_blocks = gather_seq(both)
    pins = [(both,), (both,)]
    while last_sums[0].count < size - 1 or down_sums[0].count < size - 1:
        needed = pins.pop(0) if pins else ()
        advance(down_sums, *needed)
        advance(last_sums, *needed)
    down_pieces = gather_seq(down_sums[0].sum)
    packed_share = last_sums[0].sum
    output = middle + down_sum
    down_full = jnp.concatenate(in_order(down_pieces, seq_index), axis=0)[
        :ff_part
    ].astype(f32)
    gate_full, up_full = (
        spread_hidden(ffn_blocks, which, seq_index, size, ff_part, window) for which in range(2)
    )
    packs = [
        after(piece, gate_full, up_full)
        for piece in in_order(gather_seq(packed_share), seq_index)
    ]

    def unpack(first, count):
        return jnp.concatenate(
            [p[:own_rows, first : first + count] for p in packs], axis=1
        ).astype(f32)

    gain_sum = sum(p[own_rows, :gain_count].astype(f32) for p in packs)
    return (
        output[None].astype(bf16),
        inputs_grad[None].astype(bf16),
        gain_sum[:own_rows],
        unpack(0, query_columns),
        unpack(query_columns, key_columns),
        unpack(query_columns + key_columns, key_columns),
        gain_sum[2 * own_rows : 2 * own_rows + head_part],
        gain_sum[2 * own_rows + head_part :],
        unpack(qkv_columns, query_columns),
        gain_sum[own_rows : 2 * own_rows],
        gate_full,
        up_full,
        down_full,
    )


def solution(mesh):
    in_specs = (
        P("fsdp", "seq", None),
        P("fsdp"),
        P("fsdp", None),
        P("fsdp", None),
        P("fsdp", None),
        P("fsdp"),
        P("fsdp"),
        P("fsdp", None),
        P("fsdp"),
        P("fsdp", None),
        P("fsdp", None),
        P("fsdp", None),
        P("fsdp", "seq", None),
    )
    out_specs = (
        P("fsdp", "seq", None),
        P("fsdp", "seq", None),
        P("fsdp"),
        P("fsdp", None),
        P("fsdp", None),
        P("fsdp", None),
        P("fsdp"),
        P("fsdp"),
        P("fsdp", None),
        P("fsdp"),
        P("fsdp", None),
        P("fsdp", None),
        P("fsdp", None),
    )
    return jax.shard_map(body, mesh=mesh, in_specs=in_specs, out_specs=out_specs, check_vma=False)
```

```python
import functools
import math

import jax
import jax.numpy as jnp
import numpy as np
from jax import lax
from jax.experimental import pallas as pl
from jax.experimental.layout import Layout, with_layout_constraint
from jax.experimental.pallas import tpu as pltpu
from jax.sharding import PartitionSpec as P

norm_epsilon = 1e-05
TILE = 256
log2_e = math.log2(math.e)


def rope_rows(length, width):
    half_width = width // 2
    inverse = jnp.exp(
        jnp.arange(half_width, dtype=jnp.float32) * (-2.0 * math.log(1000000.0) / width)
    )
    angles = inverse[:, None] * jnp.arange(length, dtype=jnp.int32).astype(jnp.float32)[None, :]
    return jnp.cos(angles), jnp.sin(angles)


def head_norm(values):
    inverse = lax.rsqrt(jnp.mean(values * values, axis=0, keepdims=True) + norm_epsilon)
    return values * inverse, inverse


def head_turn(values, cosine, sine):
    half = values.shape[0] // 2
    first, second = values[:half], values[half:]
    return jnp.concatenate(
        [first * cosine - second * sine, second * cosine + first * sine], axis=0
    )


def head_turn_back(values, cosine, sine):
    half = values.shape[0] // 2
    first, second = values[:half], values[half:]
    return jnp.concatenate(
        [first * cosine + second * sine, second * cosine - first * sine], axis=0
    )


def fill_heads(qkv_ref, q_gain_ref, k_gain_ref, cos_ref, sin_ref, queries, keys, keys_t, values, values_t, sizes):
    heads, groups, width = sizes
    cosine, sine = cos_ref[...], sin_ref[...]

    @pl.loop(0, heads)
    def _(head):
        unit, _ = head_norm(qkv_ref[pl.ds(head * width, width), :])
        turned = head_turn(unit * q_gain_ref[...], cosine, sine)
        queries[head] = (turned * (width**-0.5 * log2_e)).astype(jnp.bfloat16)

    @pl.loop(0, groups)
    def _(group):
        unit, _ = head_norm(qkv_ref[pl.ds((heads + group) * width, width), :])
        turned = head_turn(unit * k_gain_ref[...], cosine, sine)
        keys[group] = turned.T.astype(jnp.bfloat16)
        if keys_t is not None:
            keys_t[group] = turned.astype(jnp.bfloat16)
        value = qkv_ref[pl.ds((heads + groups + group) * width, width), :]
        if values is not None:
            values[group] = value.T.astype(jnp.bfloat16)
        if values_t is not None:
            values_t[group] = value.astype(jnp.bfloat16)


def diagonal_mask():
    key_place = lax.broadcasted_iota(jnp.int32, (TILE, TILE), 0)
    query_place = lax.broadcasted_iota(jnp.int32, (TILE, TILE), 1)
    return key_place <= query_place


def causal_exp(scores, count):
    weights = jnp.exp2(scores)
    last = jnp.where(diagonal_mask(), weights[count - TILE :], 0.0)
    if count == TILE:
        return last
    return jnp.concatenate([weights[: count - TILE], last], axis=0)


def dot(left, right):
    return jnp.dot(left, right, preferred_element_type=jnp.float32)


def dot_nt(left, right):
    return lax.dot_general(
        left, right, (((1,), (1,)), ((), ())), preferred_element_type=jnp.float32
    )


def forward_kernel(sizes, qkv_ref, q_gain_ref, k_gain_ref, cos_ref, sin_ref, mixed_ref, mixed_t_ref, total_ref, queries, keys, values_t, mixed_f):
    heads, groups, width = sizes
    ratio = heads // groups
    length = qkv_ref.shape[1]
    fill_heads(qkv_ref, q_gain_ref, k_gain_ref, cos_ref, sin_ref, queries, keys, None, None, values_t, sizes)

    @pl.loop(0, heads)
    def _(head):
        group = head // ratio
        for tile in range(length // TILE):
            count = (tile + 1) * TILE
            columns = pl.ds(tile * TILE, TILE)
            scores = dot(keys[group, pl.ds(0, count), :], queries[head, :, columns])
            weights = causal_exp(scores, count)
            total = jnp.sum(weights, axis=0, keepdims=True)
            result = dot(values_t[group, :, pl.ds(0, count)], weights.astype(jnp.bfloat16))
            mixed_f[pl.ds(head * width, width), columns] = result * (1.0 / total)
            total_ref[pl.ds(head, 1), columns] = jnp.log2(total)

    for block in range(heads * width // 128):
        rows = mixed_f[pl.ds(block * 128, 128), :]
        mixed_t_ref[pl.ds(block * 128, 128), :] = rows.astype(jnp.bfloat16)
        mixed_ref[:, pl.ds(block * 128, 128)] = rows.T.astype(jnp.bfloat16)


def backward_kernel(sizes, qkv_ref, q_gain_ref, k_gain_ref, cos_ref, sin_ref, mixed_t_ref, total_ref, grad_ref, out_ref, gain_ref, out_t, queries, keys, keys_t, values, grads, key_sum, value_sum):
    heads, groups, width = sizes
    ratio = heads // groups
    length = qkv_ref.shape[1]
    fill_heads(qkv_ref, q_gain_ref, k_gain_ref, cos_ref, sin_ref, queries, keys, keys_t, values, None, sizes)
    for block in range(heads * width // 128):
        turned = grad_ref[:, pl.ds(block * 128, 128)].astype(jnp.float32).T
        grads[pl.ds(block * 128, 128), :] = turned.astype(jnp.bfloat16)
    key_sum[...] = jnp.zeros_like(key_sum)
    value_sum[...] = jnp.zeros_like(value_sum)
    gain_ref[...] = jnp.zeros_like(gain_ref)
    cosine, sine = cos_ref[...], sin_ref[...]

    def finish(grad_turned, rows, gain, first):
        grad = head_turn_back(grad_turned, cosine, sine)
        unit, inverse = head_norm(qkv_ref[rows, :])
        product = grad * unit
        part = product[:, :128]
        for lane in range(128, length, 128):
            part = part + product[:, lane : lane + 128]
        gain_ref[pl.ds(first, width), :] += part
        scaled = grad * gain
        before = inverse * (scaled - unit * jnp.mean(scaled * unit, axis=0, keepdims=True))
        out_t[rows, :] = before

    @pl.loop(0, heads)
    def _(head):
        group = head // ratio
        rows = pl.ds(head * width, width)
        query_parts = []
        for tile in range(length // TILE):
            count = (tile + 1) * TILE
            columns = pl.ds(tile * TILE, TILE)
            query = queries[head, :, columns]
            grad = grads[rows, columns]
            scores = dot(keys[group, pl.ds(0, count), :], query) - total_ref[pl.ds(head, 1), columns]
            weights = causal_exp(scores, count)
            inner = jnp.sum(
                grad.astype(jnp.float32) * mixed_t_ref[rows, columns].astype(jnp.float32),
                axis=0,
                keepdims=True,
            )
            weight_grad = dot(values[group, pl.ds(0, count), :], grad)
            score_grad = (weights * (weight_grad - inner)).astype(jnp.bfloat16)
            query_parts.append(dot(keys_t[group, :, pl.ds(0, count)], score_grad))
            key_sum[group, pl.ds(0, count), :] += dot_nt(score_grad, query)
            value_sum[group, pl.ds(0, count), :] += dot_nt(weights.astype(jnp.bfloat16), grad)
        query_grad = jnp.concatenate(query_parts, axis=1) * width**-0.5
        finish(query_grad, rows, q_gain_ref[...], 0)

    for group in range(groups):
        key_grad = key_sum[group].T * (1.0 / log2_e)
        finish(key_grad, pl.ds((heads + group) * width, width), k_gain_ref[...], width)
        out_t[pl.ds((heads + groups + group) * width, width), :] = value_sum[group].T

    for block in range(out_t.shape[0] // 128):
        some = pl.ds(block * 128, 128)
        out_ref[:, some] = out_t[some, :].T.astype(jnp.bfloat16)


def attention_forward(qkv_t, q_gain, k_gain, cosine, sine, sizes):
    heads, groups, width = sizes
    length = qkv_t.shape[1]
    bf16, f32 = jnp.bfloat16, jnp.float32
    pairs = heads * length * length
    return pl.pallas_call(
        functools.partial(forward_kernel, sizes),
        out_shape=(
            jax.ShapeDtypeStruct((length, heads * width), bf16),
            jax.ShapeDtypeStruct((heads * width, length), bf16),
            jax.ShapeDtypeStruct((-(-heads // 8) * 8, length), f32),
        ),
        scratch_shapes=[
            pltpu.VMEM((heads, width, length), bf16),
            pltpu.VMEM((groups, length, width), bf16),
            pltpu.VMEM((groups, width, length), bf16),
            pltpu.VMEM((heads * width, length), f32),
        ],
        compiler_params=pltpu.CompilerParams(vmem_limit_bytes=32 * 2**20),
        cost_estimate=pl.CostEstimate(
            flops=8 * pairs * width, bytes_accessed=6 * 2**20, transcendentals=pairs
        ),
    )(qkv_t, q_gain, k_gain, cosine, sine)


def attention_backward(qkv_t, q_gain, k_gain, cosine, sine, mixed_t, total, mixed_grad, sizes):
    heads, groups, width = sizes
    length = qkv_t.shape[1]
    bf16, f32 = jnp.bfloat16, jnp.float32
    pairs = heads * length * length
    return pl.pallas_call(
        functools.partial(backward_kernel, sizes),
        out_shape=(
            jax.ShapeDtypeStruct(qkv_t.shape[::-1], bf16),
            jax.ShapeDtypeStruct((2 * width, 128), f32),
        ),
        scratch_shapes=[
            pltpu.VMEM(qkv_t.shape, f32),
            pltpu.VMEM((heads, width, length), bf16),
            pltpu.VMEM((groups, length, width), bf16),
            pltpu.VMEM((groups, width, length), bf16),
            pltpu.VMEM((groups, length, width), bf16),
            pltpu.VMEM((heads * width, length), bf16),
            pltpu.VMEM((groups, length, width), f32),
            pltpu.VMEM((groups, length, width), f32),
        ],
        compiler_params=pltpu.CompilerParams(vmem_limit_bytes=40 * 2**20),
        cost_estimate=pl.CostEstimate(flops=0, bytes_accessed=2**20, transcendentals=0),
    )(qkv_t, q_gain, k_gain, cosine, sine, mixed_t, total, mixed_grad)


def hidden_kernel(size, ids_ref, *refs):
    pieces, chunks, refs = refs[:4], refs[4 : 4 + 2 * size], refs[4 + 2 * size :]
    slope_ref, silu_ref, hidden_ref, gate_out, up_out, tokens, gate, up, *sems = refs
    row_sems, in_sems, out_sems = sems
    step = pl.program_id(0)
    steps = pl.num_programs(0)
    rows = chunks[0].shape[0]
    piece = pieces[0].shape[0]

    @pl.when(step == 0)
    def _():
        copies = [
            pltpu.make_async_copy(
                source, tokens.at[pl.ds(index * piece, piece), :], row_sems.at[index]
            )
            for index, source in enumerate(pieces)
        ]
        for copy in copies:
            copy.start()

        @pl.loop(0, steps)
        def _(tile):
            columns = pl.ds(pl.multiple_of(tile * TILE, TILE), TILE)
            for which, target in ((0, gate), (1, up)):
                for index in range(size):
                    first = pl.multiple_of(ids_ref[which, index] * rows, 16)
                    pltpu.make_async_copy(
                        chunks[which * size + index].at[:, columns],
                        target.at[pl.ds(first, rows), columns],
                        in_sems.at[which, tile],
                    ).start()

        for copy in copies:
            copy.wait()

    columns = pl.ds(pl.multiple_of(step * TILE, TILE), TILE)
    for which, target, result in ((0, gate, gate_out), (1, up, up_out)):
        part = target.at[:, columns]
        pltpu.make_async_copy(part, part, in_sems.at[which, step]).wait()
        pltpu.make_async_copy(part, result.at[:, columns], out_sems.at[which, step]).start()
    for half in range(2):
        some = pl.ds(half * 2 * piece, 2 * piece)
        gate_act = dot(tokens[some, :], gate[:, columns])
        up_act = dot(tokens[some, :], up[:, columns])
        sigmoid = 0.5 + 0.5 * jnp.tanh(0.5 * gate_act)
        silu = gate_act * sigmoid
        hidden_ref[some, :] = (silu * up_act).astype(hidden_ref.dtype)
        silu_ref[some, :] = silu.astype(silu_ref.dtype)
        slope_ref[some, :] = (up_act * sigmoid * (1.0 + gate_act * (1.0 - sigmoid))).astype(
            slope_ref.dtype
        )

    @pl.when(step == steps - 1)
    def _():
        @pl.loop(0, steps)
        def _(tile):
            columns = pl.ds(pl.multiple_of(tile * TILE, TILE), TILE)
            for which, target, result in ((0, gate, gate_out), (1, up, up_out)):
                pltpu.make_async_copy(
                    target.at[:, columns], result.at[:, columns], out_sems.at[which, tile]
                ).wait()


def ffn_hidden(pieces, gate_chunks, up_chunks, ids):
    size = len(gate_chunks)
    part, columns = gate_chunks[0].shape
    piece, width = pieces[0].shape
    length = 4 * piece
    bf16 = jnp.bfloat16
    tall = pl.BlockSpec((length, TILE), lambda i, ids: (0, i))
    act = jax.ShapeDtypeStruct((length, columns), bf16)
    weight = jax.ShapeDtypeStruct((width, columns), bf16)
    anywhere = pl.BlockSpec(memory_space=pl.ANY)
    return pl.pallas_call(
        functools.partial(hidden_kernel, size),
        grid_spec=pltpu.PrefetchScalarGridSpec(
            num_scalar_prefetch=1,
            grid=(columns // TILE,),
            in_specs=[anywhere] * (4 + 2 * size),
            out_specs=[tall, tall, tall, anywhere, anywhere],
            scratch_shapes=[
                pltpu.VMEM((length, width), bf16),
                pltpu.VMEM((width, columns), bf16),
                pltpu.VMEM((width, columns), bf16),
                pltpu.SemaphoreType.DMA((4,)),
                pltpu.SemaphoreType.DMA((2, columns // TILE)),
                pltpu.SemaphoreType.DMA((2, columns // TILE)),
            ],
        ),
        out_shape=(act, act, act, weight, weight),
        compiler_params=pltpu.CompilerParams(vmem_limit_bytes=56 * 2**20),
        cost_estimate=pl.CostEstimate(
            flops=4 * length * width * columns,
            bytes_accessed=36 * 2**20,
            transcendentals=length * columns,
        ),
    )(ids, *pieces, *gate_chunks, *up_chunks)


def hidden_grad_kernel(size, owners_ref, grad_ref, slope_ref, silu_ref, *refs):
    chunks, refs = refs[: 2 * size], refs[2 * size :]
    gate_out, up_out, down_out, down, in_sems, out_sem = refs
    step = pl.program_id(0)
    rows = chunks[0].shape[0]

    @pl.when(step == 0)
    def _():
        copies = []
        for which in range(2):
            for index in range(size):
                first = pl.multiple_of((2 * owners_ref[which, index] + which) * rows, 16)
                copies.append(
                    pltpu.make_async_copy(
                        chunks[which * size + index],
                        down.at[pl.ds(first, rows), :],
                        in_sems.at[which, index],
                    )
                )
        for copy in copies:
            copy.start()
        for copy in copies:
            copy.wait()
        pltpu.make_async_copy(down, down_out, out_sem).start()

    weight = down[pl.ds(pl.multiple_of(step * TILE, TILE), TILE), :]
    hidden_grad = dot_nt(grad_ref[...], weight)
    gate_out[...] = (hidden_grad * slope_ref[...].astype(jnp.float32)).astype(jnp.bfloat16)
    up_out[...] = (hidden_grad * silu_ref[...].astype(jnp.float32)).astype(jnp.bfloat16)

    @pl.when(step == pl.num_programs(0) - 1)
    def _():
        pltpu.make_async_copy(down, down_out, out_sem).wait()


def ffn_hidden_grad(out_grad, slope, silu, ahead, behind, owners):
    size = len(ahead)
    length, width = out_grad.shape
    columns = slope.shape[1]
    bf16 = jnp.bfloat16
    tall = pl.BlockSpec((length, TILE), lambda i, owners: (0, i))
    anywhere = pl.BlockSpec(memory_space=pl.ANY)
    act = jax.ShapeDtypeStruct((length, columns), bf16)
    weight = (2 * size * ahead[0].shape[0], width)
    return pl.pallas_call(
        functools.partial(hidden_grad_kernel, size),
        grid_spec=pltpu.PrefetchScalarGridSpec(
            num_scalar_prefetch=1,
            grid=(columns // TILE,),
            in_specs=[pl.BlockSpec((length, width), lambda i, owners: (0, 0)), tall, tall]
            + [anywhere] * (2 * size),
            out_specs=[tall, tall, anywhere],
            scratch_shapes=[
                pltpu.VMEM(weight, bf16),
                pltpu.SemaphoreType.DMA((2, size)),
                pltpu.SemaphoreType.DMA,
            ],
        ),
        out_shape=(act, act, jax.ShapeDtypeStruct(weight, bf16)),
        compiler_params=pltpu.CompilerParams(vmem_limit_bytes=56 * 2**20),
        cost_estimate=pl.CostEstimate(flops=0, bytes_accessed=2**20, transcendentals=0),
    )(owners, out_grad, slope, silu, *ahead, *behind)


def rows_grad_kernel(gate_grad_ref, up_grad_ref, gate_ref, up_ref, own_ref, other_ref, sent_ref):
    piece = own_ref.shape[0]
    total = dot_nt(gate_grad_ref[...], gate_ref[...]) + dot_nt(up_grad_ref[...], up_ref[...])
    total = total.astype(jnp.bfloat16)
    own_ref[...] = total[:piece]
    other_ref[...] = total[piece : 2 * piece]
    sent_ref[...] = total[2 * piece :]


def ffn_rows_grad(gate_grad, up_grad, gate, up):
    length, columns = gate_grad.shape
    width = gate.shape[0]
    piece = length // 4
    bf16 = jnp.bfloat16
    whole = pl.BlockSpec((length, columns), lambda i: (0, 0))
    weight = pl.BlockSpec((TILE, columns), lambda i: (i, 0))
    part = pl.BlockSpec((piece, TILE), lambda i: (0, i))
    return pl.pallas_call(
        rows_grad_kernel,
        grid=(width // TILE,),
        in_specs=[whole, whole, weight, weight],
        out_specs=[part, part, pl.BlockSpec((2 * piece, TILE), lambda i: (0, i))],
        out_shape=(
            jax.ShapeDtypeStruct((piece, width), bf16),
            jax.ShapeDtypeStruct((piece, width), bf16),
            jax.ShapeDtypeStruct((2 * piece, width), bf16),
        ),
        compiler_params=pltpu.CompilerParams(vmem_limit_bytes=56 * 2**20),
        cost_estimate=pl.CostEstimate(flops=0, bytes_accessed=2**20, transcendentals=0),
    )(gate_grad, up_grad, gate, up)


def lay_kernel(size, sizes, owners_ref, *refs):
    chunks, refs = refs[: 2 * size], refs[2 * size :]
    qkv_out, out_out, gains_out, sems = refs
    rows, top, qkv_columns, columns = sizes
    copies = []
    for which, count in ((0, top), (1, rows - top)):
        for index in range(size):
            chunk = chunks[which * size + index]
            owner = owners_ref[which, index]
            first = pl.multiple_of(owner * rows + which * top, 16)
            target = pl.ds(first, count)
            pairs = [
                (chunk.at[pl.ds(0, count), pl.ds(0, qkv_columns)], qkv_out.at[target, :]),
                (
                    chunk.at[pl.ds(0, count), pl.ds(qkv_columns, columns - qkv_columns)],
                    out_out.at[target, :],
                ),
            ]
            if which:
                pairs.append((chunk.at[pl.ds(count, 16), :], gains_out.at[owner]))
            for kind, (source, place) in enumerate(pairs):
                copies.append(pltpu.make_async_copy(source, place, sems.at[kind, which, index]))
    for copy in copies:
        copy.start()
    for copy in copies:
        copy.wait()


def lay_attention(ahead, behind, owners, rows, qkv_columns):
    size = len(ahead)
    top, columns = ahead[0].shape
    bf16 = jnp.bfloat16
    anywhere = pl.BlockSpec(memory_space=pl.ANY)
    return pl.pallas_call(
        functools.partial(lay_kernel, size, (rows, top, qkv_columns, columns)),
        grid_spec=pltpu.PrefetchScalarGridSpec(
            num_scalar_prefetch=1,
            grid=(1,),
            in_specs=[anywhere] * (2 * size),
            out_specs=[pl.BlockSpec(memory_space=pltpu.VMEM)] * 3,
            scratch_shapes=[pltpu.SemaphoreType.DMA((3, 2, size))],
        ),
        out_shape=(
            jax.ShapeDtypeStruct((size * rows, qkv_columns), bf16),
            jax.ShapeDtypeStruct((size * rows, columns - qkv_columns), bf16),
            jax.ShapeDtypeStruct((size, 16, columns), bf16),
        ),
        cost_estimate=pl.CostEstimate(flops=0, bytes_accessed=7 * 2**20, transcendentals=0),
    )(owners, *ahead, *behind)


def pick_kernel(sizes, index_ref, gate_ref, up_ref, gate_out, up_out):
    size, part, window = sizes
    rows = gate_ref.shape[0]
    for source, target in ((gate_ref, gate_out), (up_ref, up_out)):
        for index in range(4):
            count = min(window, part - index * window)

            @pl.when(index_ref[0] == index)
            def _():
                parts = []
                for owner in range(size):
                    first = owner * part + index * window
                    low, high = first // 128 * 128, -(-(first + count) // 128) * 128
                    wide = source[:, low:high].astype(jnp.float32)
                    parts.append(wide[:, first - low : first - low + count])
                    if count < window:
                        parts.append(jnp.zeros((rows, window - count), jnp.float32))
                target[...] = jnp.concatenate(parts, axis=1).astype(target.dtype)


def pick_hidden(gate, up, seq_index, size, part, window):
    rows, columns = gate.shape
    block = 48 if rows % 48 == 0 else rows
    wide = pl.BlockSpec((block, columns), lambda i, index: (i, 0))
    narrow = pl.BlockSpec((block, size * window), lambda i, index: (i, 0))
    out = jax.ShapeDtypeStruct((rows, size * window), gate.dtype)
    return pl.pallas_call(
        functools.partial(pick_kernel, (size, part, window)),
        grid_spec=pltpu.PrefetchScalarGridSpec(
            num_scalar_prefetch=1,
            grid=(rows // block,),
            in_specs=[wide, wide],
            out_specs=[narrow, narrow],
        ),
        out_shape=(out, out),
        compiler_params=pltpu.CompilerParams(vmem_limit_bytes=32 * 2**20),
        cost_estimate=pl.CostEstimate(flops=0, bytes_accessed=8 * 2**20, transcendentals=0),
    )(jnp.reshape(seq_index, (1,)).astype(jnp.int32), gate, up)


def spread_kernel(sizes, index_ref, own_ref, other_ref, near_ref, far_ref, out_ref, parts):
    size, part, window = sizes
    me = index_ref[0]
    parts[me] = own_ref[...]
    parts[me ^ 2] = other_ref[...]
    parts[me ^ 1] = near_ref[...]
    parts[me ^ 3] = far_ref[...]
    pieces = []
    for owner in range(size):
        for index in range(4):
            count = min(window, part - index * window)
            first = owner * window
            low, high = first // 128 * 128, -(-(first + count) // 128) * 128
            wide = parts[index, :, low:high].astype(jnp.float32)
            pieces.append(wide[:, first - low : first - low + count])
    out_ref[...] = jnp.concatenate(pieces, axis=1)


def spread_hidden(pieces, which, seq_index, size, part, window):
    _, rows, columns = pieces[0].shape
    block = 48 if rows % 48 == 0 else rows
    narrow = pl.BlockSpec((None, block, columns), lambda i, index: (which, i, 0))
    return pl.pallas_call(
        functools.partial(spread_kernel, (size, part, window)),
        grid_spec=pltpu.PrefetchScalarGridSpec(
            num_scalar_prefetch=1,
            grid=(rows // block,),
            in_specs=[narrow] * 4,
            out_specs=pl.BlockSpec((block, size * part), lambda i, index: (i, 0)),
            scratch_shapes=[pltpu.VMEM((4, block, columns), pieces[0].dtype)],
        ),
        out_shape=jax.ShapeDtypeStruct((rows, size * part), jnp.float32),
        compiler_params=pltpu.CompilerParams(vmem_limit_bytes=32 * 2**20),
        cost_estimate=pl.CostEstimate(flops=0, bytes_accessed=64 * 2**20, transcendentals=0),
    )(jnp.reshape(seq_index, (1,)), *pieces)


def norm_forward(values, gain):
    inverse = lax.rsqrt(jnp.mean(values * values, axis=-1, keepdims=True) + norm_epsilon)
    unit = values * inverse
    return (unit * gain, unit, inverse)


def norm_backward(grad_in, unit, inverse, gain):
    scaled = grad_in * gain
    return inverse * (scaled - unit * jnp.mean(scaled * unit, axis=-1, keepdims=True))


def transpose_dot(left, right):
    return lax.dot_general(
        left, right, (((0,), (0,)), ((), ())), preferred_element_type=jnp.float32
    )


def by_rows(values):
    return with_layout_constraint(values, Layout(major_to_minor=(0, 1)))


def dot_transposed(left, right):
    return lax.dot_general(
        left, right, (((1,), (1,)), ((), ())), preferred_element_type=jnp.float32
    )


def split_rows(rows):
    return (rows // 32) * 16


def ring_ids(size):
    return list(range(0, size, 2)) + [i for i in range(size - 1, 0, -1) if i % 2]


def ring_perms(size):
    ids = ring_ids(size)
    forward = [(ids[i], ids[(i + 1) % size]) for i in range(size)]
    return forward, [(b, a) for a, b in forward]


def ring_owners(size):
    ids = ring_ids(size)
    table = np.zeros((size, 4, size), np.int32)
    for place, device in enumerate(ids):
        for step in range(size):
            table[device, 0, step] = ids[(place - step) % size]
            table[device, 1, step] = ids[(place + step) % size]
            table[device, 2, step] = ids[(place - 1 - step) % size]
            table[device, 3, step] = ids[(place + 1 + step) % size]
    return lax.dynamic_index_in_dim(
        jnp.asarray(table), lax.axis_index("fsdp").astype(jnp.uint32), 0, keepdims=False
    )


def after(value, *needed):
    return lax.optimization_barrier((value, *needed))[0] if needed else value


class GatherRing:
    def __init__(self, ahead, behind, size):
        self.perms = ring_perms(size)
        self.ahead, self.behind = [ahead], [behind]

    def step(self, first=(), last=()):
        forward, backward = self.perms
        ahead = lax.ppermute(after(self.ahead[-1], *first), "fsdp", forward)
        behind = lax.ppermute(after(self.behind[-1], *first), "fsdp", backward)
        self.ahead.append(after(ahead, *last))
        self.behind.append(after(behind, *last))


class ScatterRing:
    def __init__(self, way, blocks, size, owners, rows=None):
        self.perm = ring_perms(size)[way]
        self.owners = lax.squeeze(lax.slice_in_dim(owners, 2 + way, 3 + way), (0,)).astype(
            jnp.uint32
        )
        self.blocks, self.count = blocks, 0
        self.first, self.last = rows or (0, blocks.shape[1])
        self.sum = self.own().astype(jnp.bfloat16)

    def own(self):
        owner = lax.squeeze(lax.slice_in_dim(self.owners, self.count, self.count + 1), (0,))
        zero = jnp.uint32(0)
        shape = (1, self.last - self.first, self.blocks.shape[2])
        start = (owner, jnp.uint32(self.first), zero)
        return lax.dynamic_slice(self.blocks, start, shape)[0].astype(jnp.float32)

    def step(self, *needed):
        came = after(lax.ppermute(self.sum, "fsdp", self.perm), *needed)
        self.count += 1
        self.sum = (came.astype(jnp.float32) + self.own()).astype(jnp.bfloat16)
        return self.sum


def exchange(values, mask):
    return lax.ppermute(values, "seq", [(i, i ^ mask) for i in range(4)])


def gather_seq(block, *needed):
    block = after(block, *needed)
    other = exchange(block, 2)
    return [block, other, exchange(block, 1), exchange(other, 1)]


def in_order(pieces, seq_index):
    high, low = seq_index // 2, seq_index % 2

    def pick(first, second, flag):
        return jnp.where(flag == 0, first, second), jnp.where(flag == 0, second, first)

    mine = pick(pieces[0], pieces[1], high)
    theirs = pick(pieces[2], pieces[3], high)
    return [*pick(mine[0], theirs[0], low), *pick(mine[1], theirs[1], low)]


def scatter_seq(own, other, there):
    rows = own.shape[0]
    came = exchange(there, 1).astype(jnp.float32)
    sent = (other.astype(jnp.float32) + came[rows:]).astype(jnp.bfloat16)
    near = own.astype(jnp.float32) + came[:rows]
    return near + exchange(sent, 2).astype(jnp.float32), sent


def swap(blocks):
    return lax.all_to_all(blocks, "seq", split_axis=0, concat_axis=0, tiled=True)


def side_by_side(blocks):
    return blocks.transpose(1, 0, 2).reshape(blocks.shape[1], -1)


def apart(values):
    return values.reshape(values.shape[0], 4, -1).transpose(1, 0, 2)


def body(
    tokens,
    norm_gain,
    query_weight,
    key_weight,
    value_weight,
    query_gain,
    key_gain,
    out_weight,
    ffn_gain,
    gate_weight,
    up_weight,
    down_weight,
    cotangent,
):
    bf16, f32 = jnp.bfloat16, jnp.float32
    size = lax.axis_size("fsdp")
    seq_index = lax.axis_index("seq")
    owners = ring_owners(size)
    own_rows, width = query_weight.shape
    head_part = query_gain.shape[0]
    head_width = head_part * size
    query_columns = width // 4
    key_columns = key_weight.shape[1] // 4
    ff_part = down_weight.shape[0]
    window = -(-ff_part // 64) * 16

    def columns_of(weight, count):
        return lax.dynamic_slice_in_dim(weight, seq_index.astype(jnp.uint32) * count, count, 1)

    def hidden_rows(weight):
        tall = jnp.pad(weight, ((0, 4 * window - ff_part), (0, 0)))
        return lax.dynamic_slice_in_dim(tall, seq_index.astype(jnp.uint32) * window, window, 0)

    gains = jnp.concatenate([norm_gain, ffn_gain, query_gain, key_gain])
    gain_count = gains.shape[0]
    qkv_columns = query_columns + 2 * key_columns
    packed_columns = qkv_columns + query_columns
    gain_rows = jnp.pad(gains[None], ((0, 15), (0, packed_columns - gain_count)))
    packed = jnp.concatenate(
        [
            columns_of(query_weight, query_columns),
            columns_of(key_weight, key_columns),
            columns_of(value_weight, key_columns),
            columns_of(out_weight, query_columns),
        ],
        axis=1,
    )
    top = split_rows(own_rows + 16)
    first_ring = GatherRing(
        packed[:top], jnp.concatenate([packed[top:], gain_rows], axis=0), size
    )
    for _ in range(size - 1):
        first_ring.step()
    ffn_ring = GatherRing(
        *pick_hidden(gate_weight, up_weight, seq_index, size, ff_part, window), size
    )
    down_rows = hidden_rows(down_weight)
    def advance(rings, *needed):
        for way in rings:
            if way.count < size - 1:
                way.step(*needed)

    for step in range(1, size):
        ffn_ring.step((first_ring.ahead[2],) if step == 1 else ())
    down_ring = GatherRing(down_rows[: window // 2], down_rows[window // 2 :], size)
    for step in range(1, size - 2):
        lag = min(step + 2, size - 1)
        down_ring.step((ffn_ring.ahead[lag], ffn_ring.behind[lag]))

    qkv_all, out_part, gains_all = lay_attention(
        first_ring.ahead, first_ring.behind, owners, own_rows, qkv_columns
    )
    gains_all = gains_all[:, 0].astype(f32)
    first_gain = gains_all[:, :own_rows].reshape(-1)
    second_gain = gains_all[:, own_rows : 2 * own_rows].reshape(-1)
    q_gain_f = gains_all[:, 2 * own_rows : 2 * own_rows + head_part].reshape(-1)
    k_gain_f = gains_all[:, 2 * own_rows + head_part : 2 * (own_rows + head_part)].reshape(-1)

    inputs = tokens[0]
    tok_rows = inputs.shape[0]
    length = 4 * tok_rows
    input_blocks = gather_seq(inputs)
    inputs_all = jnp.concatenate(in_order(input_blocks, seq_index), axis=0).astype(f32)
    out_grad = cotangent[0]
    grad_blocks = gather_seq(out_grad, input_blocks[1])
    out_grad_all = jnp.concatenate(grad_blocks, axis=0)


    out_other = exchange(after(out_part, input_blocks[1]), 2)
    normed, _, _ = norm_forward(inputs_all, first_gain)
    normed_low = after(normed.astype(bf16), grad_blocks[1])
    qkv_t = lax.dot_general(
        qkv_all, normed_low, (((0,), (1,)), ((), ())), preferred_element_type=f32
    )
    sizes = (query_columns // head_width, key_columns // head_width, head_width)
    cosine, sine = rope_rows(length, head_width)
    tables = (q_gain_f[:, None], k_gain_f[:, None], cosine, sine)
    mixed_heads, mixed_t, totals = attention_forward(qkv_t, *tables, sizes)
    mixed = side_by_side(swap(mixed_heads.reshape(4, tok_rows, query_columns)))
    out_other = after(out_other, mixed_heads)
    out_blocks = [out_part, out_other, exchange(out_part, 1), exchange(out_other, 1)]
    out_all = jnp.concatenate(in_order(out_blocks, seq_index), axis=1)
    attended = jnp.dot(mixed, out_all, preferred_element_type=f32)
    middle = inputs.astype(f32) + attended
    normed_two, middle_unit, middle_inverse = norm_forward(middle, second_gain)
    normed_two_low = normed_two.astype(bf16)
    normed_blocks = gather_seq(normed_two_low)
    normed_two_all = jnp.concatenate(normed_blocks, axis=0)
    mixed_other = exchange(after(mixed_heads, normed_blocks[1]), 2)

    slope, silu, hidden, gate_all, up_all = ffn_hidden(
        [after(normed_blocks[0], down_ring.ahead[-1], down_ring.behind[-1]), *normed_blocks[1:]],
        ffn_ring.ahead,
        ffn_ring.behind,
        owners,
    )
    down_ring.step((), (hidden,))
    hidden = after(hidden, down_ring.ahead[-1], down_ring.behind[-1])
    down_ring.step()
    down_weight_grad = transpose_dot(hidden, out_grad_all).astype(bf16)
    down_blocks = after(
        down_weight_grad, down_ring.ahead[-1], down_ring.behind[-1]
    ).reshape(size, window, width)
    down_sums = (ScatterRing(0, down_blocks, size, owners),)
    gate_grad, up_grad, down_all = ffn_hidden_grad(
        after(out_grad_all, *(way.sum for way in down_sums)),
        slope,
        silu,
        down_ring.ahead,
        down_ring.behind,
        owners,
    )
    advance(down_sums, gate_grad)
    gate_weight_grad = transpose_dot(after(normed_two_all, down_sums[0].sum), gate_grad).astype(bf16)
    gate_sums = ScatterRing(
        0, gate_weight_grad.reshape(size, own_rows, size * window), size, owners
    )
    up_weight_grad = transpose_dot(after(normed_two_all, gate_sums.sum), up_grad).astype(bf16)
    up_sums = ScatterRing(1, up_weight_grad.reshape(size, own_rows, size * window), size, owners)
    ffn_sums = (gate_sums, up_sums)
    advance(down_sums, up_sums.sum)
    normed_parts = ffn_rows_grad(
        after(gate_grad, up_sums.sum, mixed_other, down_sums[0].sum), up_grad, gate_all, up_all
    )
    mixed_blocks = [mixed_heads, mixed_other, exchange(mixed_heads, 1), exchange(mixed_other, 1)]
    mixed_all = jnp.concatenate(in_order(mixed_blocks, seq_index), axis=1)
    advance(ffn_sums, normed_parts[0])
    normed_two_grad, half_sum = scatter_seq(
        *normed_parts[:2], after(normed_parts[2], gate_sums.sum, up_sums.sum)
    )
    advance(ffn_sums, normed_two_grad)
    ffn_gain_grad = jnp.sum(normed_two_grad * middle_unit, axis=0)
    middle_grad = out_grad.astype(f32) + norm_backward(
        normed_two_grad, middle_unit, middle_inverse, second_gain
    )
    attended_low = middle_grad.astype(bf16)
    mixed_grad = dot_transposed(attended_low, out_all).astype(bf16)
    advance(ffn_sums, mixed_grad)
    down_sums[0].sum = after(down_sums[0].sum, mixed_grad)
    mixed_grad_heads = after(swap(apart(mixed_grad)), gate_sums.sum, up_sums.sum).reshape(
        length, query_columns
    )
    qkv_grad, head_gains = attention_backward(
        qkv_t, *tables, mixed_t, totals, mixed_grad_heads, sizes
    )
    attended_columns = after(
        swap(apart(after(attended_low, mixed_grad_heads))), qkv_grad
    ).reshape(length, query_columns)
    out_weight_grad = by_rows(transpose_dot(mixed_all, attended_columns).astype(bf16))
    advance(ffn_sums, qkv_grad)
    advance(down_sums, qkv_grad)
    qkv_grad = after(qkv_grad, gate_sums.sum, up_sums.sum)
    head_gains = jnp.sum(head_gains, axis=1)
    query_gain_grad, key_gain_grad = head_gains[:head_width], head_gains[head_width:]
    qkv_weight_grad = transpose_dot(normed_low, qkv_grad)
    norm_gain_grad = jnp.sum(qkv_weight_grad * qkv_all.astype(f32), axis=1) / first_gain
    qkv_weight_grad = by_rows(qkv_weight_grad.astype(bf16))
    normed_partial = dot_transposed(qkv_grad, qkv_all)
    partial_blocks = normed_partial.astype(bf16).reshape(4, tok_rows, width)

    def partial_of(mask):
        index = (seq_index ^ mask).astype(jnp.uint32)
        return lax.dynamic_index_in_dim(partial_blocks, index, 0, keepdims=False)

    normed_grad, normed_sent = scatter_seq(
        partial_of(0),
        partial_of(2),
        jnp.concatenate([partial_of(1), partial_of(3)], axis=0),
    )
    _, own_unit, own_inverse = norm_forward(inputs.astype(f32), first_gain)
    inputs_grad = middle_grad + norm_backward(normed_grad, own_unit, own_inverse, first_gain)

    gain_grads = jnp.concatenate(
        [
            norm_gain_grad.reshape(size, -1),
            ffn_gain_grad.reshape(size, -1),
            query_gain_grad.reshape(size, -1),
            key_gain_grad.reshape(size, -1),
        ],
        axis=1,
    )
    gain_blocks = jnp.pad(
        gain_grads[:, None], ((0, 0), (0, 15), (0, packed_columns - gain_count))
    )
    packed_blocks = jnp.concatenate([qkv_weight_grad, out_weight_grad], axis=1).reshape(
        size, own_rows, packed_columns
    )
    packed_blocks = jnp.concatenate([packed_blocks, gain_blocks.astype(bf16)], axis=1)
    last_sums = (ScatterRing(1, packed_blocks, size, owners),)
    advance(ffn_sums, last_sums[0].sum, normed_sent)
    down_partial = jnp.dot(
        after(hidden, gate_sums.sum), down_all, preferred_element_type=f32
    ).astype(bf16)
    down_sum, down_sent = scatter_seq(
        down_partial[:tok_rows],
        down_partial[tok_rows : 2 * tok_rows],
        down_partial[2 * tok_rows :],
    )
    advance(down_sums, gate_sums.sum)
    advance(last_sums, gate_sums.sum, up_sums.sum)
    pins = [(down_sum,), (normed_grad, down_sent)]
    while gate_sums.count < size - 1:
        advance(ffn_sums, last_sums[0].sum, *(pins.pop() if pins else ()))
        advance(down_sums, gate_sums.sum, up_sums.sum)
        advance(last_sums, gate_sums.sum, up_sums.sum)
    both = jnp.stack([gate_sums.sum, up_sums.sum])
    ffn_blocks = gather_seq(both)
    pins = [(both,), (both,), (ffn_blocks[1],)]
    while last_sums[0].count < size - 1 or down_sums[0].count < size - 1:
        needed = pins.pop(0) if pins else ()
        advance(down_sums, *needed)
        advance(last_sums, *needed)
    packed_share = last_sums[0].sum
    down_share = down_sums[0].sum
    down_other = after(exchange(down_share, 2), packed_share)
    down_pieces = [down_share, down_other, exchange(down_share, 1), exchange(down_other, 1)]
    output = middle + down_sum
    down_full = jnp.concatenate(in_order(down_pieces, seq_index), axis=0)[
        :ff_part
    ].astype(f32)
    gate_full, up_full = (
        spread_hidden(ffn_blocks, which, seq_index, size, ff_part, window) for which in range(2)
    )
    packs = [
        after(piece, gate_full, up_full)
        for piece in in_order(gather_seq(packed_share), seq_index)
    ]

    def unpack(first, count):
        return jnp.concatenate(
            [p[:own_rows, first : first + count] for p in packs], axis=1
        ).astype(f32)

    gain_sum = sum(p[own_rows, :gain_count].astype(f32) for p in packs)
    return (
        output[None].astype(bf16),
        inputs_grad[None].astype(bf16),
        gain_sum[:own_rows],
        unpack(0, query_columns),
        unpack(query_columns, key_columns),
        unpack(query_columns + key_columns, key_columns),
        gain_sum[2 * own_rows : 2 * own_rows + head_part],
        gain_sum[2 * own_rows + head_part :],
        unpack(qkv_columns, query_columns),
        gain_sum[own_rows : 2 * own_rows],
        gate_full,
        up_full,
        down_full,
    )


def solution(mesh):
    in_specs = (
        P("fsdp", "seq", None),
        P("fsdp"),
        P("fsdp", None),
        P("fsdp", None),
        P("fsdp", None),
        P("fsdp"),
        P("fsdp"),
        P("fsdp", None),
        P("fsdp"),
        P("fsdp", None),
        P("fsdp", None),
        P("fsdp", None),
        P("fsdp", "seq", None),
    )
    out_specs = (
        P("fsdp", "seq", None),
        P("fsdp", "seq", None),
        P("fsdp"),
        P("fsdp", None),
        P("fsdp", None),
        P("fsdp", None),
        P("fsdp"),
        P("fsdp"),
        P("fsdp", None),
        P("fsdp"),
        P("fsdp", None),
        P("fsdp", None),
        P("fsdp", None),
    )
    return jax.shard_map(body, mesh=mesh, in_specs=in_specs, out_specs=out_specs, check_vma=False)
```
